32 devices in a mesh: blk: 8 (over z, x), head: 4 (over y, core).
Axes of the slice: x: 2, y: 2, z: 4, core: 2. Of those that a mesh axis runs over, the one named last changes fastest.
Arguments:
- tokens: bfloat16 [8, 2048, 1280], P(None, ('blk', 'head')), may hold values from -6 to 6
- attn_gain: float32 [1280], replicated, may hold values from 0.1 to 1.9
- ffn_gain: float32 [1280], replicated, may hold values from 0.1 to 1.9
- query_weight: bfloat16 [1280, 1280], P('blk', 'head'), may hold values from -0.15625 to 0.15625
- keyval_weight: bfloat16 [2, 1280, 320], P(None, 'blk', 'head'), may hold values from -0.15625 to 0.15625
- output_weight: bfloat16 [1280, 1280], P('blk', 'head'), may hold values from -0.625 to 0.625
- gateup_weight: bfloat16 [2, 1280, 3584], P(None, 'blk', 'head'), may hold values from -0.15625 to 0.15625
- down_weight: bfloat16 [3584, 1280], P('blk', 'head'), may hold values from -0.09375 to 0.09375
- query_down: bfloat16 [8, 1280, 16], replicated, may hold values from -0.15625 to 0.15625
- query_up: bfloat16 [8, 16, 1280], replicated, may hold values from -0.375 to 0.375
- keyval_down: bfloat16 [8, 2, 1280, 16], replicated, may hold values from -0.15625 to 0.15625
- keyval_up: bfloat16 [8, 2, 16, 320], replicated, may hold values from -0.375 to 0.375
- output_down: bfloat16 [8, 1280, 16], replicated, may hold values from -0.15625 to 0.15625
- output_up: bfloat16 [8, 16, 1280], replicated, may hold values from -1.5 to 1.5
- gateup_down: bfloat16 [8, 2, 1280, 16], replicated, may hold values from -0.15625 to 0.15625
- gateup_up: bfloat16 [8, 2, 16, 3584], replicated, may hold values from -0.375 to 0.375
- ffdown_down: bfloat16 [8, 3584, 16], replicated, may hold values from -0.09375 to 0.09375
- ffdown_up: bfloat16 [8, 16, 1280], replicated, may hold values from -0.375 to 0.375
- segment_ids: int32 [8, 2048], replicated, may hold values from 0 to 1, as said below
- real_mask: int32 [8, 2048], replicated, may hold values from 0 to 1, as said below
- adapter_index: int32 [8], replicated, may hold values from 0 to 7, each once
- out_grad: bfloat16 [8, 2048, 1280], P(None, ('blk', 'head')), may hold values from -6 to 6
Outputs:
- output: bfloat16 [8, 2048, 1280], P(None, ('blk', 'head'))
- input_grad: bfloat16 [8, 2048, 1280], P(None, ('blk', 'head'))
- grad_query_down: float32 [8, 1280, 16], replicated
- grad_query_up: float32 [8, 16, 1280], replicated
- grad_keyval_down: float32 [8, 2, 1280, 16], replicated
- grad_keyval_up: float32 [8, 2, 16, 320], replicated
- grad_output_down: float32 [8, 1280, 16], replicated
- grad_output_up: float32 [8, 16, 1280], replicated
- grad_gateup_down: float32 [8, 2, 1280, 16], replicated
- grad_gateup_up: float32 [8, 2, 16, 3584], replicated
- grad_ffdown_down: float32 [8, 3584, 16], replicated
- grad_ffdown_up: float32 [8, 16, 1280], replicated
The draws below stay inside these ranges and needn't reach their ends.
Inputs may be any that keep to these rules, and one draw needn't show every extreme that they name: `segment_ids`: numbers never fall along a sequence and begin at 0 in each; in every draw one sequence is a single document and another reaches the largest number. `real_mask`: each sequence's padding, if any, is a run at its end shorter than 128 positions. `adapter_index`: each adapter serves exactly one sequence.
All inputs are finite; a program needn't handle non-finite values.
Results may differ from the reference program's by a relative error of at most 0.019.
Values may be sent and summed in bfloat16 or wider, within the bound.
A program may use at most 320 MiB of HBM per device.

```python
import math
import jax
import jax.numpy as jnp
from jax import lax

D = 1280
HEADS = 20
KV_HEADS = 5
HEAD_DIM = 64
FF = 3584
RANK = 16
ADAPTERS = 8
SEQS = 8
WINDOW = 1024
SEQ_LEN = 2048


def draw_segment_ids(key, part):
    key = jax.random.fold_in(key, 11)
    first_key, second_key, third_key = jax.random.split(key, 3)
    starts = jax.random.randint(first_key, (SEQS, SEQ_LEN), 0, 2 * WINDOW) == 0
    single = jax.random.randint(second_key, (), 0, SEQS)
    offset = jax.random.randint(third_key, (), 1, SEQS)
    busy = (single + offset) % SEQS
    rows = jnp.arange(SEQS, dtype=jnp.int32)[:, None]
    columns = jnp.arange(SEQ_LEN, dtype=jnp.int32)[None, :]
    forced = (rows == busy) & (columns % WINDOW == 0)
    starts = (starts | forced) & (rows != single) & (columns > 0)
    counted = jnp.cumsum(starts.astype(jnp.int32), axis=1)
    return jnp.minimum(counted, SEQ_LEN // WINDOW - 1).astype(jnp.int32)


def draw_real_mask(key, part):
    key = jax.random.fold_in(key, 12)
    padding = jax.random.randint(key, (SEQS, 1), 0, WINDOW // 8)
    columns = jnp.arange(SEQ_LEN, dtype=jnp.int32)[None, :]
    return (columns < SEQ_LEN - padding).astype(jnp.int32)


def block_levels(stream_key, shape, shards, least, top_value):
    def one(axis_at, shards_of):
        heights = jax.random.uniform(jax.random.fold_in(jax.random.fold_in(stream_key, 6), axis_at), (shards_of,), jnp.float32, least / len(shards), top_value / len(shards))
        return jnp.repeat(jnp.exp(heights), shape[axis_at] // shards_of).reshape((-1,) + (1,) * (len(shape) - axis_at - 1))

    level = one(*shards[0])
    for cut in shards[1:]:
        level = level * one(*cut)
    return level


def noise(key, dims, scale, most, cuts=(), held_as=jnp.bfloat16):
    values = scale * jax.random.normal(key, dims, jnp.float32)
    if cuts:
        values = values * block_levels(key, dims, cuts, -0.22, 0.18)
    return jnp.clip(values, -most, most).astype(held_as)


def setup_inputs(seed: int = 0) -> dict:
    seeds = jax.random.split(jax.random.key(seed), 23)
    return {
        "tokens": noise(seeds[0], (SEQS, SEQ_LEN, D), 1.0, 6.0, ((1, 32),)),
        "attn_gain": jnp.clip(1.0 + 0.18 * jax.random.normal(seeds[1], (D,), jnp.float32), 0.1, 1.9),
        "ffn_gain": jnp.clip(1.0 + 0.18 * jax.random.normal(seeds[2], (D,), jnp.float32), 0.1, 1.9),
        "query_weight": noise(seeds[3], (D, D), D ** -0.5, 0.15625, ((0, 8), (1, 4))),
        "keyval_weight": noise(seeds[4], (2, D, KV_HEADS * HEAD_DIM), D ** -0.5, 0.15625, ((1, 8), (2, 4))),
        "output_weight": noise(seeds[5], (D, D), (D // 16) ** -0.5, 0.625, ((0, 8), (1, 4))),
        "gateup_weight": noise(seeds[6], (2, D, FF), D ** -0.5, 0.15625, ((1, 8), (2, 4))),
        "down_weight": noise(seeds[7], (FF, D), FF ** -0.5, 0.09375, ((0, 8), (1, 4))),
        "query_down": noise(seeds[8], (ADAPTERS, D, RANK), D ** -0.5, 0.15625),
        "query_up": noise(seeds[9], (ADAPTERS, RANK, D), (16 * RANK) ** -0.5, 0.375),
        "keyval_down": noise(seeds[10], (ADAPTERS, 2, D, RANK), D ** -0.5, 0.15625),
        "keyval_up": noise(seeds[11], (ADAPTERS, 2, RANK, KV_HEADS * HEAD_DIM), (16 * RANK) ** -0.5, 0.375),
        "output_down": noise(seeds[12], (ADAPTERS, D, RANK), D ** -0.5, 0.15625),
        "output_up": noise(seeds[13], (ADAPTERS, RANK, D), RANK ** -0.5, 1.5),
        "gateup_down": noise(seeds[14], (ADAPTERS, 2, D, RANK), D ** -0.5, 0.15625),
        "gateup_up": noise(seeds[15], (ADAPTERS, 2, RANK, FF), (16 * RANK) ** -0.5, 0.375),
        "ffdown_down": noise(seeds[16], (ADAPTERS, FF, RANK), FF ** -0.5, 0.09375),
        "ffdown_up": noise(seeds[17], (ADAPTERS, RANK, D), (16 * RANK) ** -0.5, 0.375),
        "segment_ids": draw_segment_ids(jax.random.fold_in(seeds[22], 71), 0),
        "real_mask": draw_real_mask(jax.random.fold_in(seeds[22], 71), 0),
        "adapter_index": jax.random.permutation(seeds[20], ADAPTERS).astype(jnp.int32),
        "out_grad": noise(seeds[21], (SEQS, SEQ_LEN, D), 1.0, 6.0, ((1, 32),)),
    }


EPSILON = 1e-05
ROPE_BASE = 10000.0
ADAPTER_SCALE = 2.0
MASKED = -1e+30

@jax.custom_vjp
def low(v):
    return lax.optimization_barrier(v.astype(jnp.bfloat16)).astype(jnp.float32)

@jax.custom_vjp
def low_back(v):
    return v

def low_keep(v):
    return (low(v), None)

def low_pass(kept, grad):
    return (grad,)

def back_keep(v):
    return (v, None)

def back_low(kept, grad):
    return (low(grad),)
low.defvjp(low_keep, low_pass)
low_back.defvjp(back_keep, back_low)

def rms_scale(values, gain):
    return values * lax.rsqrt(lax.optimization_barrier(jnp.mean(values * values, axis=-1, keepdims=True)) + EPSILON) * gain

def rotate(values, positions, sign):
    half = values.shape[-1] // 2
    freqs = ROPE_BASE ** (-(jnp.arange(half, dtype=jnp.float32) * 2.0) / values.shape[-1])
    angles = positions.astype(jnp.float32)[:, None] * freqs[None, :]
    cosine = jnp.cos(angles)[:, None, :]
    sine = sign * jnp.sin(angles)[:, None, :]
    first = values[..., :half]
    second = values[..., half:]
    return jnp.concatenate([first * cosine - second * sine, second * cosine + first * sine], axis=-1)

def matmul(left, right):
    return jnp.dot(left, right, preferred_element_type=jnp.float32, precision=lax.Precision.HIGHEST)

def project(inputs, weight, down, up):
    lowered = low_back(low(matmul(inputs, down)))
    return matmul(inputs, weight) + ADAPTER_SCALE * matmul(lowered, up)

def attention(queries, keys, values, segments, realness):
    seq_len = queries.shape[0]
    block = min(512, seq_len)
    scale = 1.0 / math.sqrt(queries.shape[-1])
    key_pad = jnp.concatenate([jnp.zeros((WINDOW,) + keys.shape[1:], keys.dtype), keys], axis=0)
    value_pad = jnp.concatenate([jnp.zeros((WINDOW,) + values.shape[1:], values.dtype), values], axis=0)
    segment_pad = jnp.concatenate([jnp.full((WINDOW,), -1, jnp.int32), segments.astype(jnp.int32)])
    real_pad = jnp.concatenate([jnp.zeros((WINDOW,), jnp.int32), realness.astype(jnp.int32)])

    def one_block(index):
        start = (index * block).astype(jnp.int32)
        query_part = lax.dynamic_slice_in_dim(queries, start, block, 0)
        key_part = lax.dynamic_slice_in_dim(key_pad, start, block + WINDOW, 0)
        value_part = lax.dynamic_slice_in_dim(value_pad, start, block + WINDOW, 0)
        key_segment = lax.dynamic_slice_in_dim(segment_pad, start, block + WINDOW, 0)
        key_real = lax.dynamic_slice_in_dim(real_pad, start, block + WINDOW, 0)
        query_segment = lax.dynamic_slice_in_dim(segments.astype(jnp.int32), start, block, 0)
        query_pos = start + jnp.arange(block, dtype=jnp.int32)
        key_pos = start - WINDOW + jnp.arange(block + WINDOW, dtype=jnp.int32)
        distance = query_pos[:, None] - key_pos[None, :]
        allowed = (key_pos[None, :] >= 0) & (distance >= 0) & (distance < WINDOW)
        allowed = allowed & (query_segment[:, None] == key_segment[None, :])
        allowed = allowed & ((key_real[None, :] == 1) | (distance == 0))
        raw = jnp.einsum('qhd,khd->hqk', query_part, key_part, precision=lax.Precision.HIGHEST) * scale
        raw = low_back(jnp.where(allowed[None], raw, MASKED))
        top = lax.optimization_barrier(jnp.max(raw, axis=-1, keepdims=True))
        shifted = jnp.exp(raw - top)
        probs = low(shifted / lax.optimization_barrier(jnp.sum(shifted, axis=-1, keepdims=True)))
        return jnp.einsum('hqk,khd->qhd', probs, value_part, precision=lax.Precision.HIGHEST)
    pieces = lax.map(jax.checkpoint(one_block), jnp.arange(seq_len // block, dtype=jnp.int32))
    return pieces.reshape((seq_len,) + queries.shape[1:])

def layer(flat, adapters, frozen, which, segments, realness):
    attn_gain, ffn_gain, w_query, w_keyval, w_output, w_gateup, w_down = frozen
    down_query, up_query, down_keyval, up_keyval, down_output, up_output, down_gateup, up_gateup, down_ffdown, up_ffdown = adapters
    seq_len = flat.shape[0]
    positions = jnp.arange(seq_len, dtype=jnp.int32)
    normed = low(rms_scale(flat, attn_gain))
    queries_pre = low_back(project(normed, w_query, down_query[which], up_query[which]))
    keys_pre = low_back(project(normed, w_keyval[0], down_keyval[which, 0], up_keyval[which, 0]))
    values_pre = low_back(project(normed, w_keyval[1], down_keyval[which, 1], up_keyval[which, 1]))
    queries = low(rotate(queries_pre.reshape(seq_len, HEADS, HEAD_DIM), positions, 1.0))
    keys = low(rotate(keys_pre.reshape(seq_len, KV_HEADS, HEAD_DIM), positions, 1.0))
    values = low(values_pre).reshape(seq_len, KV_HEADS, HEAD_DIM)
    keys_wide = jnp.repeat(keys, HEADS // KV_HEADS, axis=1)
    values_wide = jnp.repeat(values, HEADS // KV_HEADS, axis=1)
    attended = attention(queries, keys_wide, values_wide, segments, realness)
    mixed = low_back(low(attended.reshape(seq_len, D)))
    branch_attn = low_back(project(mixed, w_output, down_output[which], up_output[which]))
    middle = flat + branch_attn
    normed2 = low(rms_scale(middle, ffn_gain))
    gate = low_back(project(normed2, w_gateup[0], down_gateup[which, 0], up_gateup[which, 0]))
    upward = low_back(project(normed2, w_gateup[1], down_gateup[which, 1], up_gateup[which, 1]))
    activated = low(jax.nn.silu(gate) * upward)
    branch_ffn = low_back(project(activated, w_down, down_ffdown[which], up_ffdown[which]))
    return middle + branch_ffn

def reference(tokens, attn_gain, ffn_gain, query_weight, keyval_weight, output_weight, gateup_weight, down_weight, query_down, query_up, keyval_down, keyval_up, output_down, output_up, gateup_down, gateup_up, ffdown_down, ffdown_up, segment_ids, real_mask, adapter_index, out_grad):
    frozen = (attn_gain.astype(jnp.float32), ffn_gain.astype(jnp.float32), query_weight.astype(jnp.float32), keyval_weight.astype(jnp.float32), output_weight.astype(jnp.float32), gateup_weight.astype(jnp.float32), down_weight.astype(jnp.float32))
    adapters = (query_down.astype(jnp.float32), query_up.astype(jnp.float32), keyval_down.astype(jnp.float32), keyval_up.astype(jnp.float32), output_down.astype(jnp.float32), output_up.astype(jnp.float32), gateup_down.astype(jnp.float32), gateup_up.astype(jnp.float32), ffdown_down.astype(jnp.float32), ffdown_up.astype(jnp.float32))

    def one_sequence(carry, pieces):
        flat, segments, realness, which, cotangent = pieces

        def forward(flat_in, adapters_in):
            return layer(flat_in, adapters_in, frozen, which, segments, realness)
        result, pull = jax.vjp(forward, flat, adapters)
        grad_flat, grad_adapters = pull(cotangent)
        carry = jax.tree.map(lambda first, second: first + second, carry, grad_adapters)
        return (carry, (result.astype(jnp.bfloat16), grad_flat.astype(jnp.bfloat16)))
    zeros = jax.tree.map(jnp.zeros_like, adapters)
    totals, outputs = lax.scan(one_sequence, zeros, (tokens.astype(jnp.float32), segment_ids, real_mask, adapter_index, out_grad.astype(jnp.float32)))
    return (outputs[0], outputs[1], totals[0], totals[1], totals[2], totals[3], totals[4], totals[5], totals[6], totals[7], totals[8], totals[9])
```

```python
import functools
import math

import jax
import jax.numpy as jnp
import numpy as np
from jax import lax
from jax.experimental import pallas as pl
from jax.experimental.pallas import tpu as pltpu
from jax.sharding import PartitionSpec as P

HEADS = 20
KV_HEADS = 5
HEAD_DIM = 64
WINDOW = 1024


EPSILON = 1e-05
ROPE_BASE = 10000.0
ADAPTER_SCALE = 2.0
MASKED = -1e30


def passed_along(value, axis, steps):
    count = lax.axis_size(axis)
    initial, last = (max(0, -steps), min(count, count - steps))
    return lax.ppermute(value, axis, [(source, source + steps) for source in range(initial, last)])


def rms_scale(values, gain):
    return values * lax.rsqrt(jnp.mean(values * values, axis=-1, keepdims=True) + EPSILON) * gain


def rotate(values, positions, sign):
    half = values.shape[-1] // 2
    freqs = ROPE_BASE ** (-(jnp.arange(half, dtype=jnp.float32) * 2.0) / values.shape[-1])
    angles = positions.astype(jnp.float32)[:, None] * freqs[None, :]
    cosine = jnp.cos(angles)[:, None, :]
    sine = sign * jnp.sin(angles)[:, None, :]
    first = values[..., :half]
    second = values[..., half:]
    return jnp.concatenate(
        [first * cosine - second * sine, second * cosine + first * sine], axis=-1
    )


def gated(gate, upward):
    return jax.nn.silu(gate) * upward


def project(inputs, weight, down, up):
    lowered = jnp.einsum("sci,sir->scr", inputs, down, preferred_element_type=jnp.float32).astype(
        jnp.bfloat16
    )
    extra = ADAPTER_SCALE * jnp.einsum(
        "scr,sro->sco", lowered, up, preferred_element_type=jnp.float32
    )
    return (
        jnp.einsum("sci,io->sco", inputs, weight, preferred_element_type=jnp.float32) + extra,
        lowered,
    )


def project_back(inputs, lowered, grad_out, weight, down, up):
    grad_up = ADAPTER_SCALE * jnp.einsum(
        "scr,sco->sro", lowered, grad_out, preferred_element_type=jnp.float32
    )
    grad_low = (
        ADAPTER_SCALE * jnp.einsum("sco,sro->scr", grad_out, up, preferred_element_type=jnp.float32)
    ).astype(jnp.bfloat16)
    grad_down = jnp.einsum("sci,scr->sir", inputs, grad_low, preferred_element_type=jnp.float32)
    grad_in = jnp.einsum("sco,io->sci", grad_out, weight, preferred_element_type=jnp.float32)
    grad_in = grad_in + jnp.einsum(
        "scr,sir->sci", grad_low, down, preferred_element_type=jnp.float32
    )
    return (grad_in, grad_down, grad_up)


def on_device(
    tokens,
    attn_gain,
    ffn_gain,
    query_weight,
    keyval_weight,
    output_weight,
    gateup_weight,
    down_weight,
    query_down,
    query_up,
    keyval_down,
    keyval_up,
    output_down,
    output_up,
    gateup_down,
    gateup_up,
    ffdown_down,
    ffdown_up,
    segment_ids,
    real_mask,
    adapter_index,
    out_grad,
):
    seqs, per_device, width = tokens.shape
    groups = lax.axis_size("head")
    head_pos = lax.axis_index("head")
    blk_pos = lax.axis_index("blk")
    span = groups * per_device
    heads = HEADS
    head_dim = HEAD_DIM
    kv_heads = KV_HEADS
    local_heads = heads // groups
    share = heads // kv_heads
    reach = (WINDOW - 2) // span + 1
    scale = 1.0 / math.sqrt(head_dim)
    rows_a, rows_b, rows_c, rows_d, rows_e = (
        lax.all_gather(query_weight, "blk", axis=0, tiled=True),
        lax.all_gather(keyval_weight, "blk", axis=1, tiled=True),
        lax.all_gather(output_weight, "blk", axis=0, tiled=True),
        lax.all_gather(gateup_weight, "blk", axis=1, tiled=True),
        lax.all_gather(down_weight, "blk", axis=0, tiled=True),
    )
    w_query, w_keyval, w_output, w_gateup, w_down = (
        lax.all_gather(rows_a, "head", axis=1, tiled=True),
        lax.all_gather(rows_b, "head", axis=2, tiled=True),
        lax.all_gather(rows_c, "head", axis=1, tiled=True),
        lax.all_gather(rows_d, "head", axis=2, tiled=True),
        lax.all_gather(rows_e, "head", axis=1, tiled=True),
    )
    down_query = query_down[adapter_index]
    up_query = query_up[adapter_index]
    down_keyval = keyval_down[adapter_index]
    up_keyval = keyval_up[adapter_index]
    down_output = output_down[adapter_index]
    up_output = output_up[adapter_index]
    down_gateup = gateup_down[adapter_index]
    up_gateup = gateup_up[adapter_index]
    down_ffdown = ffdown_down[adapter_index]
    up_ffdown = ffdown_up[adapter_index]

    def first_norm(values):
        return rms_scale(values, attn_gain)

    def second_norm(values):
        return rms_scale(values, ffn_gain)

    flat = tokens.astype(jnp.float32)
    normed_full, first_norm_back = jax.vjp(first_norm, flat)
    normed = normed_full.astype(jnp.bfloat16)
    queries_pre, low_query = project(normed, w_query, down_query, up_query)
    keys_pre, low_key = project(normed, w_keyval[0], down_keyval[:, 0], up_keyval[:, 0])
    values_pre, low_value = project(normed, w_keyval[1], down_keyval[:, 1], up_keyval[:, 1])
    token_pos = (blk_pos * groups + head_pos) * per_device + jnp.arange(per_device, dtype=jnp.int32)
    queries = rotate(queries_pre.reshape(seqs, per_device, heads, head_dim), token_pos, 1.0).astype(
        jnp.bfloat16
    )
    keys = rotate(keys_pre.reshape(seqs, per_device, kv_heads, head_dim), token_pos, 1.0).astype(
        jnp.bfloat16
    )
    values = values_pre.reshape(seqs, per_device, kv_heads, head_dim).astype(jnp.bfloat16)
    owner = np.array(
        [
            [(group * local_heads + slot) // share for slot in range(local_heads)]
            for group in range(groups)
        ]
    )
    slot_of = jnp.arange(local_heads, dtype=jnp.int32)
    sender = jnp.asarray(
        (owner[:, :, None] == np.arange(kv_heads)[None, None, :]).astype(np.float32), jnp.bfloat16
    )
    spread = (slot_of[:, None] == jnp.arange(local_heads, dtype=jnp.int32)[None, :]).astype(
        jnp.bfloat16
    )
    pair = jnp.stack([keys, values], axis=3)
    outgoing = jnp.einsum(
        "sckxd,gmk->scgmxd", pair, sender, preferred_element_type=jnp.float32
    ).astype(jnp.bfloat16)
    outgoing = outgoing.reshape(seqs, per_device, groups, local_heads * 2 * head_dim)
    query_send = queries.reshape(seqs, per_device, groups, local_heads * head_dim)
    query_here, pair_here = (
        lax.all_to_all(query_send, "head", split_axis=2, concat_axis=1, tiled=True),
        lax.all_to_all(outgoing, "head", split_axis=2, concat_axis=1, tiled=True),
    )
    query_here = query_here.reshape(seqs, span, local_heads, head_dim)
    pair_here = pair_here.reshape(seqs, span, local_heads, 2, head_dim)
    received = [pair_here]
    moving = pair_here
    for hop in range(reach):
        moving = passed_along(moving, "blk", 1)
        received.append(moving)
    window_pairs = jnp.stack(received, axis=1)
    query_pos = blk_pos * span + jnp.arange(span, dtype=jnp.int32)
    key_pos = (blk_pos - jnp.arange(reach + 1, dtype=jnp.int32))[:, None] * span + jnp.arange(
        span, dtype=jnp.int32
    )[None, :]
    safe_pos = jnp.clip(key_pos, 0, segment_ids.shape[1] - 1)
    query_segment = lax.dynamic_slice_in_dim(segment_ids, blk_pos * span, span, 1)
    key_segment = segment_ids[:, safe_pos]
    key_real = real_mask[:, safe_pos]
    distance = query_pos[:, None, None] - key_pos[None]
    allowed = (key_pos[None] >= 0) & (distance >= 0) & (distance < WINDOW)
    allowed = allowed & (query_segment[:, :, None, None] == key_segment[:, None])
    allowed = allowed & ((key_real[:, None] == 1) | (distance[None] == 0))
    batch = 1
    target = max(1, 512 // span)
    for option in range(1, seqs + 1):
        if seqs % option == 0 and option <= target:
            batch = option
    count = seqs // batch

    def grouped(array):
        return array.reshape((count, batch) + array.shape[1:])

    def scores_of(query_part, pair_part, allowed_part):
        keys_wide = jnp.einsum(
            "gjlmd,hm->gjlhd", pair_part[:, :, :, :, 0], spread, preferred_element_type=jnp.float32
        ).astype(jnp.bfloat16)
        values_wide = jnp.einsum(
            "gjlmd,hm->gjlhd", pair_part[:, :, :, :, 1], spread, preferred_element_type=jnp.float32
        ).astype(jnp.bfloat16)
        raw = (
            jnp.einsum(
                "gqhd,gjlhd->ghqjl", query_part, keys_wide, preferred_element_type=jnp.float32
            )
            * scale
        )
        raw = jnp.where(allowed_part[:, None], raw, MASKED)
        return (raw, keys_wide, values_wide)

    def attend(pieces):
        query_part, pair_part, allowed_part = pieces
        raw, keys_wide, values_wide = scores_of(query_part, pair_part, allowed_part)
        top = jnp.max(raw, axis=(3, 4), keepdims=True)
        shifted = jnp.exp(raw - top)
        total = jnp.sum(shifted, axis=(3, 4), keepdims=True)
        probs_low = (shifted / total).astype(jnp.bfloat16)
        result = jnp.einsum(
            "ghqjl,gjlhd->gqhd", probs_low, values_wide, preferred_element_type=jnp.float32
        )
        return (result.astype(jnp.bfloat16), top + jnp.log(total))

    attended, logsum = lax.map(
        attend, (grouped(query_here), grouped(window_pairs), grouped(allowed))
    )
    mixed = lax.all_to_all(
        attended.reshape(seqs, span, local_heads * head_dim),
        "head",
        split_axis=1,
        concat_axis=2,
        tiled=True,
    )
    branch_attn, low_output = project(mixed, w_output, down_output, up_output)
    middle = flat + branch_attn
    normed2_full, second_norm_back = jax.vjp(second_norm, middle)
    normed2 = normed2_full.astype(jnp.bfloat16)
    gate, low_gate = project(normed2, w_gateup[0], down_gateup[:, 0], up_gateup[:, 0])
    upward, low_upward = project(normed2, w_gateup[1], down_gateup[:, 1], up_gateup[:, 1])
    activated_full, gated_back = jax.vjp(gated, gate, upward)
    activated = activated_full.astype(jnp.bfloat16)
    branch_ffn, low_ffdown = project(activated, w_down, down_ffdown, up_ffdown)
    output = (middle + branch_ffn).astype(jnp.bfloat16)
    grad_activated, gd_ffdown, gu_ffdown = project_back(
        activated, low_ffdown, out_grad, w_down, down_ffdown, up_ffdown
    )
    grad_gate, grad_upward = gated_back(grad_activated)
    grad_in_gate, gd_gate, gu_gate = project_back(
        normed2,
        low_gate,
        grad_gate.astype(jnp.bfloat16),
        w_gateup[0],
        down_gateup[:, 0],
        up_gateup[:, 0],
    )
    grad_in_up, gd_up, gu_up = project_back(
        normed2,
        low_upward,
        grad_upward.astype(jnp.bfloat16),
        w_gateup[1],
        down_gateup[:, 1],
        up_gateup[:, 1],
    )
    grad_middle = out_grad.astype(jnp.float32) + second_norm_back(grad_in_gate + grad_in_up)[0]
    grad_mixed, gd_output, gu_output = project_back(
        mixed, low_output, grad_middle.astype(jnp.bfloat16), w_output, down_output, up_output
    )
    grad_send = grad_mixed.astype(jnp.bfloat16).reshape(
        seqs, per_device, groups, local_heads * head_dim
    )
    grad_here = lax.all_to_all(grad_send, "head", split_axis=2, concat_axis=1, tiled=True).reshape(
        seqs, span, local_heads, head_dim
    )
    spread_full = spread.astype(jnp.float32)

    def attend_back(pieces):
        query_part, pair_part, allowed_part, logsum_part, grad_part = pieces
        raw, keys_wide, values_wide = scores_of(query_part, pair_part, allowed_part)
        probs = jnp.exp(raw - logsum_part)
        probs_low = probs.astype(jnp.bfloat16)
        grad_probs = jnp.einsum(
            "gqhd,gjlhd->ghqjl", grad_part, values_wide, preferred_element_type=jnp.float32
        )
        inner = jnp.sum(probs * grad_probs, axis=(3, 4), keepdims=True)
        grad_raw = (probs * (grad_probs - inner)).astype(jnp.bfloat16)
        grad_query = scale * jnp.einsum(
            "ghqjl,gjlhd->gqhd", grad_raw, keys_wide, preferred_element_type=jnp.float32
        )
        grad_keys = scale * jnp.einsum(
            "ghqjl,gqhd->gjlhd", grad_raw, query_part, preferred_element_type=jnp.float32
        )
        grad_values = jnp.einsum(
            "ghqjl,gqhd->gjlhd", probs_low, grad_part, preferred_element_type=jnp.float32
        )
        both = jnp.stack([grad_keys, grad_values], axis=4)
        folded = jnp.einsum("gjlhxd,hm->gjlmxd", both, spread_full, precision=lax.Precision.HIGHEST)
        return (grad_query, folded)

    grad_query, grad_pairs = lax.map(
        attend_back,
        (grouped(query_here), grouped(window_pairs), grouped(allowed), logsum, grouped(grad_here)),
    )
    grad_pairs = grad_pairs.reshape(seqs, reach + 1, span, local_heads, 2, head_dim)
    carried = grad_pairs[:, reach]
    for hop in range(reach - 1, -1, -1):
        carried = (
            passed_along(carried.astype(jnp.bfloat16), "blk", -1).astype(carried.dtype)
            + grad_pairs[:, hop]
        )
    grad_query = rotate(grad_query.reshape(seqs, span, local_heads, head_dim), query_pos, -1.0)
    grad_query = grad_query.astype(jnp.bfloat16).reshape(seqs, span, local_heads * head_dim)
    grad_queries_pre = lax.all_to_all(grad_query, "head", split_axis=1, concat_axis=2, tiled=True)
    grad_pair_tok = lax.all_to_all(
        carried.reshape(seqs, span, local_heads * 2 * head_dim).astype(jnp.bfloat16),
        "head",
        split_axis=1,
        concat_axis=2,
        tiled=True,
    ).astype(jnp.float32)
    grad_pair_tok = grad_pair_tok.reshape(seqs, per_device, groups, local_heads, 2, head_dim)
    grad_pair_heads = jnp.einsum(
        "scgmxd,gmk->sckxd",
        grad_pair_tok,
        sender.astype(jnp.float32),
        precision=lax.Precision.HIGHEST,
    )
    grad_keys_pre = (
        rotate(grad_pair_heads[:, :, :, 0], token_pos, -1.0)
        .astype(jnp.bfloat16)
        .reshape(seqs, per_device, kv_heads * head_dim)
    )
    grad_values_pre = (
        grad_pair_heads[:, :, :, 1]
        .astype(jnp.bfloat16)
        .reshape(seqs, per_device, kv_heads * head_dim)
    )
    grad_in_query, gd_query, gu_query = project_back(
        normed, low_query, grad_queries_pre, w_query, down_query, up_query
    )
    grad_in_key, gd_key, gu_key = project_back(
        normed, low_key, grad_keys_pre, w_keyval[0], down_keyval[:, 0], up_keyval[:, 0]
    )
    grad_in_value, gd_value, gu_value = project_back(
        normed, low_value, grad_values_pre, w_keyval[1], down_keyval[:, 1], up_keyval[:, 1]
    )
    grad_normed = grad_in_query + grad_in_key + grad_in_value
    input_grad = (grad_middle + first_norm_back(grad_normed)[0]).astype(jnp.bfloat16)
    chooser = (
        adapter_index[:, None] == jnp.arange(query_down.shape[0], dtype=jnp.int32)[None, :]
    ).astype(jnp.float32)

    def per_adapter(per_sequence):
        return jnp.einsum("sa,s...->a...", chooser, per_sequence, precision=lax.Precision.HIGHEST)

    sums = lax.psum(
        (
            per_adapter(gd_query),
            per_adapter(gu_query),
            per_adapter(jnp.stack([gd_key, gd_value], axis=1)),
            per_adapter(jnp.stack([gu_key, gu_value], axis=1)),
            per_adapter(gd_output),
            per_adapter(gu_output),
            per_adapter(jnp.stack([gd_gate, gd_up], axis=1)),
            per_adapter(jnp.stack([gu_gate, gu_up], axis=1)),
            per_adapter(gd_ffdown),
            per_adapter(gu_ffdown),
        ),
        ("blk", "head"),
    )
    return (
        output,
        input_grad,
        sums[0],
        sums[1],
        sums[2],
        sums[3],
        sums[4],
        sums[5],
        sums[6],
        sums[7],
        sums[8],
        sums[9],
    )


MESH = pl.DeviceIdType.MESH
F32 = jnp.float32
BF16 = jnp.bfloat16
TILE = 128
ANYWHERE = pl.BlockSpec(memory_space=pl.ANY)


def dot(left, right, left_dim=1, right_dim=0):
    return lax.dot_general(
        left, right, (((left_dim,), (right_dim,)), ((), ())), preferred_element_type=F32
    )


def place():
    blk, head = lax.axis_index("blk"), lax.axis_index("head")
    return blk // 2, blk % 2, head // 2, head % 2


def device(z, x, y, core):
    return (z * 2 + x, y * 2 + core)


def halves(count):
    first = (count // 2 + 15) // 16 * 16
    return ((0, first), (first, count - first))


class Spread:
    def __init__(self, sources, target, lines, sems):
        self.sources, self.target, self.lines = sources, target, lines
        self.z, self.x, self.y, self.core = place()
        self.z_in, self.x_in, self.y_in, self.d_in, self.c_in = sems[:5]
        self.z_out, self.x_out, self.y_out, self.d_out, self.c_out = sems[5:10]

    @staticmethod
    def semaphores(parts, lines):
        dma = pltpu.SemaphoreType.DMA
        return [
            dma((parts, lines)),
            dma((parts, lines)),
            dma((parts, lines)),
            dma((parts, lines, 2)),
            dma((parts, lines, 4)),
            dma((parts, 2, lines)),
            dma((parts, lines)),
            dma((parts, lines)),
            dma((parts, lines, 2)),
            dma((parts, lines, 4)),
        ]

    def inside(self, z):
        return (z >= 0) & (z < self.lines)

    def neighbours(self):
        z, x, y, core = self.z, self.x, self.y, self.core
        return (device(z, 1 - x, y, core), device(z, x, 1 - y, core), device(z, x, y, 1 - core))

    def greet(self):
        barrier = pltpu.get_barrier_semaphore()
        for side in (1, -1):

            @pl.when(self.inside(self.z + side))
            def _():
                other = device(self.z + side, self.x, self.y, self.core)
                pl.semaphore_signal(barrier, inc=1, device_id=other, device_id_type=MESH)

        for other in self.neighbours():
            pl.semaphore_signal(barrier, inc=1, device_id=other, device_id_type=MESH)
        ends = jnp.where(self.z > 0, 1, 0) + jnp.where(self.z < self.lines - 1, 1, 0)
        pl.semaphore_wait(barrier, 3 + ends)

    def copy(self, source, target, out, into, other):
        return pltpu.make_async_remote_copy(
            src_ref=source,
            dst_ref=target,
            send_sem=out,
            recv_sem=into,
            device_id=other,
            device_id_type=MESH,
        )

    def along_z(self, part, source, z, side):
        return self.copy(
            source,
            self.target(part, z, self.x, self.y, self.core),
            self.z_out.at[part, (side + 1) // 2, z],
            self.z_in.at[part, z],
            device(self.z + side, self.x, self.y, self.core),
        )

    def along_x(self, part, source, z):
        return self.copy(
            source,
            self.target(part, z, self.x, self.y, self.core),
            self.x_out.at[part, z],
            self.x_in.at[part, z],
            device(self.z, 1 - self.x, self.y, self.core),
        )

    def along_y(self, part, source, z):
        return self.copy(
            source,
            self.target(part, z, self.x, self.y, self.core),
            self.y_out.at[part, z],
            self.y_in.at[part, z],
            device(self.z, self.x, 1 - self.y, self.core),
        )

    def across(self, part, source, z, flip_x, flip_y):
        x, y = (self.x + flip_x) % 2, (self.y + flip_y) % 2
        return self.copy(
            source,
            self.target(part, z, x, y, self.core),
            self.c_out.at[part, z, flip_x * 2 + flip_y],
            self.c_in.at[part, z, flip_x * 2 + flip_y],
            device(self.z, self.x, self.y, 1 - self.core),
        )

    def piece(self, ref, which):
        begin, size = halves(ref.shape[0])[which]
        return ref.at[pl.ds(begin, size)]

    def diagonal(self, part, z, which):
        if which == 0:
            ref = self.target(part, z, self.x, 1 - self.y, self.core)
            other = device(self.z, 1 - self.x, self.y, self.core)
        else:
            ref = self.target(part, z, 1 - self.x, self.y, self.core)
            other = device(self.z, self.x, 1 - self.y, self.core)
        ref = self.piece(ref, which)
        return self.copy(
            ref, ref, self.d_out.at[part, z, which], self.d_in.at[part, z, which], other
        )

    def arrived(self, ref, out, into):
        self.copy(ref, ref, out, into, device(self.z, self.x, self.y, 1 - self.core)).wait_recv()

    def hand_on(self, part, source, z):
        self.along_x(part, source, z).start()
        self.along_y(part, source, z).start()
        self.across(part, source, z, 0, 0).start()

    def begin(self, part):
        for side in (1, -1):

            @pl.when(self.inside(self.z + side))
            def _():
                self.along_z(part, self.sources[part], self.z, side).start()

        self.hand_on(part, self.sources[part], self.z)

    def line_step(self, part, distance, side):
        z = self.z - side * distance

        @pl.when(self.inside(z))
        def _():
            ref = self.target(part, z, self.x, self.y, self.core)
            self.arrived(ref, self.z_out.at[part, 0, z], self.z_in.at[part, z])

            @pl.when(self.inside(self.z + side))
            def _():
                self.along_z(part, ref, z, side).start()

            self.hand_on(part, ref, z)

    def plane_step(self, part, z):
        ref = self.target(part, z, self.x, 1 - self.y, self.core)
        self.arrived(ref, self.y_out.at[part, z], self.y_in.at[part, z])
        self.diagonal(part, z, 0).start()
        self.across(part, ref, z, 0, 1).start()
        ref = self.target(part, z, 1 - self.x, self.y, self.core)
        self.arrived(ref, self.x_out.at[part, z], self.x_in.at[part, z])
        self.diagonal(part, z, 1).start()
        self.across(part, ref, z, 1, 0).start()

    def corner_step(self, part, z):
        ref = self.target(part, z, 1 - self.x, 1 - self.y, self.core)
        for which in (0, 1):
            self.arrived(
                self.piece(ref, which), self.d_out.at[part, z, which], self.d_in.at[part, z, which]
            )
        self.across(part, ref, z, 1, 1).start()

    def end(self, part, z):
        for flip_x in (0, 1):
            for flip_y in (0, 1):
                x, y = (self.x + flip_x) % 2, (self.y + flip_y) % 2
                which = flip_x * 2 + flip_y
                self.arrived(
                    self.target(part, z, x, y, 1 - self.core),
                    self.c_out.at[part, z, which],
                    self.c_in.at[part, z, which],
                )
                self.across(
                    part, self.target(part, z, x, y, self.core), z, flip_x, flip_y
                ).wait_send()
        mine = self.target(part, z, self.x, self.y, self.core)
        self.along_x(part, mine, z).wait_send()
        self.along_y(part, mine, z).wait_send()
        self.diagonal(part, z, 0).wait_send()
        self.diagonal(part, z, 1).wait_send()
        for side in (1, -1):

            @pl.when(self.inside(self.z + side) & ((self.z - z) * side >= 0))
            def _():
                self.along_z(part, mine, z, side).wait_send()

    def all_steps(self, parts):
        for part in parts:
            for distance in range(1, self.lines):
                for side in (1, -1):
                    self.line_step(part, distance, side)
        for part in parts:
            for z in range(self.lines):
                self.plane_step(part, z)
        for part in parts:
            for z in range(self.lines):
                self.corner_step(part, z)
        for part in parts:
            for z in range(self.lines):
                self.end(part, z)


def paired(own, other, core):
    own, other = own.astype(F32), other.astype(F32)
    return [jnp.where(core == 0, own, other), jnp.where(core == 0, other, own)]


def gather_kernel(lines, *refs):
    query, keyval, output, gateup, down, w_qkv, w_output, w_gateup, w_down = refs[:9]
    got_query, got_keyval, got_output, got_down, my_qkv, my_output, my_down = refs[9:16]
    pair_out, pair_in, local = refs[16:19]
    rows, deep = my_qkv.shape[0], my_down.shape[0]
    wide, mixed = my_output.shape[1], my_qkv.shape[1]
    span, hidden = gateup.shape[1:]

    def target(part, z, x, y, core):
        blk, head = z * 2 + x, y * 2 + core
        if part == 0:
            return w_qkv.at[pl.ds(blk * 2 * rows + core * rows, rows), pl.ds(y * mixed, mixed)]
        if part == 1:
            return w_output.at[pl.ds(blk * 2 * rows + core * rows, rows), pl.ds(y * wide, wide)]
        if part == 4:
            return w_down.at[pl.ds(blk * 2 * deep + core * deep, deep), pl.ds(y * wide, wide)]
        return w_gateup.at[part - 2, pl.ds(blk * span, span), pl.ds(head * hidden, hidden)]

    sources = [my_qkv, my_output, gateup.at[0], gateup.at[1], my_down]
    spread = Spread(sources, target, lines, refs[19:])
    core = spread.core
    spread.greet()
    sibling = device(spread.z, spread.x, spread.y, 1 - core)
    theirs = pl.ds((1 - core) * rows, rows)
    swaps = [
        spread.copy(query.at[theirs], got_query, pair_out.at[0], pair_in.at[0], sibling),
        spread.copy(keyval.at[:, theirs], got_keyval, pair_out.at[1], pair_in.at[1], sibling),
        spread.copy(output.at[theirs], got_output, pair_out.at[2], pair_in.at[2], sibling),
        spread.copy(
            down.at[pl.ds((1 - core) * deep, deep)], got_down, pair_out.at[3], pair_in.at[3], sibling
        ),
    ]
    for swap in swaps:
        swap.start()
    mine = pl.ds(core * rows, rows)
    swaps[0].wait_recv()
    swaps[1].wait_recv()
    pieces = paired(query[mine, :], got_query[...], core)
    pieces += paired(keyval[0, mine, :], got_keyval[0], core)
    pieces += paired(keyval[1, mine, :], got_keyval[1], core)
    filled = sum(p.shape[1] for p in pieces)
    pieces.append(jnp.zeros((rows, mixed - filled), F32))
    my_qkv[...] = jnp.concatenate(pieces, axis=1).astype(BF16)
    spread.begin(0)
    swaps[2].wait_recv()
    my_output[...] = jnp.concatenate(
        paired(output[mine, :], got_output[...], core), axis=1
    ).astype(BF16)
    spread.begin(1)
    spread.begin(2)
    spread.begin(3)
    swaps[3].wait_recv()
    my_down[...] = jnp.concatenate(
        paired(down[pl.ds(core * deep, deep), :], got_down[...], core), axis=1
    ).astype(BF16)
    spread.begin(4)
    own = [
        pltpu.make_async_copy(
            sources[part],
            target(part, spread.z, spread.x, spread.y, core),
            local.at[part],
        )
        for part in range(5)
    ]
    for copy in own:
        copy.start()
    spread.all_steps(range(5))
    for copy in own:
        copy.wait()
    for swap in swaps:
        swap.wait_send()


def gather_weights(query, keyval, output, gateup, down):
    rows, wide = query.shape
    deep = down.shape[0]
    blks, heads = lax.axis_size("blk"), lax.axis_size("head")
    narrow = keyval.shape[2]
    mixed = -(-2 * (wide + 2 * narrow) // TILE) * TILE
    dma = pltpu.SemaphoreType.DMA
    vmem = pl.BlockSpec(memory_space=pltpu.VMEM)
    shape = jax.ShapeDtypeStruct
    return pl.pallas_call(
        functools.partial(gather_kernel, blks // 2),
        out_shape=[
            shape((blks * rows, heads // 2 * mixed), BF16),
            shape((blks * rows, heads * wide), BF16),
            shape((2, blks * rows, heads * gateup.shape[2]), BF16),
            shape((blks * deep, heads * wide), BF16),
        ],
        in_specs=[vmem, vmem, vmem, ANYWHERE, vmem],
        out_specs=[ANYWHERE] * 4,
        scratch_shapes=[
            pltpu.VMEM((rows // 2, wide), BF16),
            pltpu.VMEM((2, rows // 2, narrow), BF16),
            pltpu.VMEM((rows // 2, wide), BF16),
            pltpu.VMEM((deep // 2, wide), BF16),
            pltpu.VMEM((rows // 2, mixed), BF16),
            pltpu.VMEM((rows // 2, 2 * wide), BF16),
            pltpu.VMEM((deep // 2, 2 * wide), BF16),
            dma((4,)),
            dma((4,)),
            dma((5,)),
            *Spread.semaphores(5, blks // 2),
        ],
        compiler_params=pltpu.CompilerParams(
            collective_id=0, has_side_effects=True, vmem_limit_bytes=24 << 20
        ),
    )(query, keyval, output, gateup, down)


def windows(blocks, span, low_part):
    reach = WINDOW + TILE
    fixed = [(0, (block + 1) * span) for block in range(WINDOW // span)]
    offset = TILE * (low_part // 2 + 1) - reach
    return fixed, reach, offset


def tiles_of(ref, flipped):
    lane = lax.broadcasted_iota(jnp.int32, (ref.shape[0], TILE), 1)
    result = []
    for slot in range(4):
        tile = ref[:, slot // 2 * TILE : (slot // 2 + 1) * TILE].astype(F32)
        if (slot % 2 == 0) == flipped:
            tile = pltpu.roll(tile, HEAD_DIM, 1)
        keep = lane >= HEAD_DIM if flipped else lane < HEAD_DIM
        result.append(jnp.where(keep, tile, 0.0).astype(BF16))
    return result


def joined(rows, flipped):
    span = rows.shape[0] // 4
    heads = [rows[slot * span : (slot + 1) * span] for slot in range(4)]
    lane = lax.broadcasted_iota(jnp.int32, (span, TILE), 1)
    result = []
    for first, second in ((heads[0], heads[1]), (heads[2], heads[3])):
        if flipped:
            first = pltpu.roll(first, HEAD_DIM, 1)
        else:
            second = pltpu.roll(second, HEAD_DIM, 1)
        result.append(jnp.where(lane < HEAD_DIM, first, second))
    return result


def bias_of(limits_ref, block, start, count):
    key = start + lax.broadcasted_iota(jnp.int32, (count, TILE), 0)
    least = limits_ref[0, pl.ds(block, 1), :]
    most = limits_ref[1, pl.ds(block, 1), :]
    self_pos = limits_ref[2, pl.ds(block, 1), :]
    allowed = ((key >= least) & (key <= most)) | (key == self_pos)
    bias = jnp.where(allowed, 0.0, MASKED)
    return jnp.concatenate([bias, bias], axis=1)


def each_block(blocks, body):
    span = 4 * HEAD_DIM
    fixed, reach, offset = windows(blocks, span, lax.axis_index("head"))
    for block, (start, count) in enumerate(fixed):
        body(block, start, count)

    @pl.loop(len(fixed), blocks)
    def _(block):
        body(block, pl.multiple_of(block * span + offset, TILE), reach)


def attend_kernel(limits_ref, q_ref, kv_ref, out_ref, lse_ref, q_rows, kv_turned):
    blocks, span = q_rows.shape[0], q_rows.shape[2]
    for slot, tile in enumerate(tiles_of(q_ref, False)):
        q_rows[:, slot] = (tile * BF16(HEAD_DIM**-0.5)).reshape(blocks, span, TILE)
    kv_turned[...] = kv_ref[...].astype(F32).T.astype(BF16)

    def body(block, start, count):
        queries = q_rows[block].reshape(4 * span, TILE)
        scores = dot(kv_ref[pl.ds(start, count), :], queries, 1, 1)
        scores = scores + bias_of(limits_ref, block, start, count)
        top = jnp.max(scores, axis=0, keepdims=True)
        shifted = jnp.exp(scores - top)
        total = jnp.sum(shifted, axis=0, keepdims=True)
        result = dot(kv_turned[:, pl.ds(start, count)], shifted.astype(BF16))
        lse_ref[0, pl.ds(block, 1), :] = top + jnp.log(total)
        result = (result / total).T
        for at, tile in enumerate(joined(result, True)):
            out_ref[pl.ds(block * span, span), at * TILE : (at + 1) * TILE] = tile.astype(BF16)

    each_block(blocks, body)


def attend(limits, queries, pairs):
    rows, width = queries.shape
    blocks = limits.shape[1]
    groups = width // (2 * TILE)
    return pl.pallas_call(
        attend_kernel,
        grid=(groups,),
        out_shape=[
            jax.ShapeDtypeStruct((rows, width), BF16),
            jax.ShapeDtypeStruct((groups, blocks, 2 * TILE), F32),
        ],
        in_specs=[
            pl.BlockSpec(limits.shape, lambda m: (0, 0, 0)),
            pl.BlockSpec((rows, 2 * TILE), lambda m: (0, m)),
            pl.BlockSpec((pairs.shape[0], TILE), lambda m: (0, m)),
        ],
        out_specs=[
            pl.BlockSpec((rows, 2 * TILE), lambda m: (0, m)),
            pl.BlockSpec((1, blocks, 2 * TILE), lambda m: (m, 0, 0)),
        ],
        scratch_shapes=[
            pltpu.VMEM((blocks, 4, rows // blocks, TILE), BF16),
            pltpu.VMEM((TILE, pairs.shape[0]), BF16),
        ],
        compiler_params=pltpu.CompilerParams(vmem_limit_bytes=48 << 20),
    )(limits, queries, pairs)


def attend_back_kernel(
    limits_ref, q_ref, kv_ref, lse_ref, grad_ref, dq_ref, dkv_ref, q_rows, g_rows, kv_turned, total
):
    blocks, span = q_rows.shape[0], q_rows.shape[2]
    scale = HEAD_DIM**-0.5
    for slot, tile in enumerate(tiles_of(q_ref, False)):
        q_rows[:, slot] = (tile * BF16(scale)).reshape(blocks, span, TILE)
    for slot, tile in enumerate(tiles_of(grad_ref, True)):
        g_rows[:, slot] = tile.reshape(blocks, span, TILE)
    kv_turned[...] = kv_ref[...].astype(F32).T.astype(BF16)
    total[...] = jnp.zeros_like(total)

    def body(block, start, count):
        keys = pl.ds(start, count)
        queries = q_rows[block].reshape(4 * span, TILE)
        grads = g_rows[block].reshape(4 * span, TILE)
        scores = dot(kv_ref[keys, :], queries, 1, 1)
        scores = scores + bias_of(limits_ref, block, start, count)
        probs = jnp.exp(scores - lse_ref[0, pl.ds(block, 1), :])
        grad_probs = dot(kv_ref[keys, :], grads, 1, 1)
        inner = jnp.sum(probs * grad_probs, axis=0, keepdims=True)
        grad_scores = (probs * (grad_probs - inner)).astype(BF16)
        total[keys, :] += dot(grad_scores, queries) + dot(probs.astype(BF16), grads)
        grad_q = (dot(kv_turned[:, keys], grad_scores) * scale).T
        for at, tile in enumerate(joined(grad_q, False)):
            dq_ref[pl.ds(block * span, span), at * TILE : (at + 1) * TILE] = tile

    each_block(blocks, body)
    dkv_ref[...] = total[...]


def attend_back(limits, queries, pairs, lse, grads):
    rows, width = queries.shape
    blocks = limits.shape[1]
    groups = width // (2 * TILE)
    wide = pl.BlockSpec((rows, 2 * TILE), lambda m: (0, m))
    long = pl.BlockSpec((pairs.shape[0], TILE), lambda m: (0, m))
    each = pltpu.VMEM((blocks, 4, rows // blocks, TILE), BF16)
    return pl.pallas_call(
        attend_back_kernel,
        grid=(groups,),
        out_shape=[
            jax.ShapeDtypeStruct((rows, width), F32),
            jax.ShapeDtypeStruct(pairs.shape, F32),
        ],
        in_specs=[
            pl.BlockSpec(limits.shape, lambda m: (0, 0, 0)),
            wide,
            long,
            pl.BlockSpec((1, blocks, 2 * TILE), lambda m: (m, 0, 0)),
            wide,
        ],
        out_specs=[wide, long],
        scratch_shapes=[
            each,
            each,
            pltpu.VMEM((TILE, pairs.shape[0]), BF16),
            pltpu.VMEM((pairs.shape[0], TILE), F32),
        ],
        compiler_params=pltpu.CompilerParams(vmem_limit_bytes=48 << 20),
    )(limits, queries, pairs, lse, grads)


def by_sequence(
    tokens,
    attn_gain,
    ffn_gain,
    query_weight,
    keyval_weight,
    output_weight,
    gateup_weight,
    down_weight,
    query_down,
    query_up,
    keyval_down,
    keyval_up,
    output_down,
    output_up,
    gateup_down,
    gateup_up,
    ffdown_down,
    ffdown_up,
    segment_ids,
    real_mask,
    adapter_index,
    out_grad,
):
    seqs, part, width = tokens.shape
    groups = lax.axis_size("head")
    seq, head_pos = lax.axis_index("blk"), lax.axis_index("head")
    rows = seqs * part
    span = groups * part
    adapter = adapter_index[seq]

    def moved(array):
        return lax.all_to_all(array, "blk", split_axis=0, concat_axis=0, tiled=True)

    flat = moved(tokens).reshape(rows, width).astype(F32)
    grad_flat = moved(out_grad).reshape(rows, width)
    w_qkv, w_output, w_gateup, w_down = gather_weights(
        query_weight, keyval_weight, output_weight, gateup_weight, down_weight
    )
    d_query = query_down.swapaxes(1, 2)[adapter]
    d_keyval = keyval_down.swapaxes(2, 3)[adapter]
    d_output = output_down.swapaxes(1, 2)[adapter]
    d_gateup = gateup_down.swapaxes(2, 3)[adapter]
    d_ffdown = ffdown_down.swapaxes(1, 2)[adapter]
    u_query, u_keyval, u_output = query_up[adapter], keyval_up[adapter], output_up[adapter]
    u_gateup, u_ffdown = gateup_up[adapter], ffdown_up[adapter]
    rank = d_query.shape[0]

    half, narrow = width // 2, u_keyval.shape[2] // 2
    mixed = w_qkv.shape[1] // 2
    fill = mixed - half - 2 * narrow

    def interleaved(query, key, value):
        empty = jnp.zeros(query.shape[:-1] + (fill,), query.dtype)
        pieces = []
        for y in (0, 1):
            pieces += [
                query[:, y * half : (y + 1) * half],
                key[:, y * narrow : (y + 1) * narrow],
                value[:, y * narrow : (y + 1) * narrow],
                empty,
            ]
        return jnp.concatenate(pieces, axis=1)

    def separated(array):
        def at(begin, size):
            return jnp.concatenate(
                [array[:, y * mixed + begin : y * mixed + begin + size] for y in (0, 1)], axis=1
            )

        return at(0, half), at(half, narrow), at(half + narrow, narrow)

    nil_q, nil_k = jnp.zeros_like(u_query), jnp.zeros_like(u_keyval[0])
    u_qkv = jnp.concatenate(
        [
            interleaved(u_query, nil_k, nil_k),
            interleaved(nil_q, u_keyval[0], nil_k),
            interleaved(nil_q, nil_k, u_keyval[1]),
        ],
        axis=0,
    )
    d_qkv = jnp.concatenate([d_query, d_keyval[0], d_keyval[1]], axis=0)

    def project(inputs, weight, down, up):
        lowered = dot(inputs, down, 1, 1).astype(BF16)
        return dot(inputs, weight) + ADAPTER_SCALE * dot(lowered, up), lowered

    def project_back(inputs, lowered, grad, weight, down, up):
        grad_up = ADAPTER_SCALE * dot(lowered, grad, 0, 0)
        grad_low = (ADAPTER_SCALE * dot(grad, up, 1, 1)).astype(BF16)
        grad_down = dot(grad_low, inputs, 0, 0)
        return dot(grad, weight, 1, 1) + dot(grad_low, down), grad_down, grad_up

    def norm(values, gain):
        inverse = lax.rsqrt(jnp.mean(values * values, axis=-1, keepdims=True) + EPSILON)
        return (values * inverse * gain).astype(BF16), inverse

    def norm_back(values, inverse, gain, grad):
        weighted = grad * gain
        mean = jnp.mean(values * weighted, axis=-1, keepdims=True)
        return inverse * weighted - values * (inverse * inverse * inverse * mean)

    position = (
        jnp.arange(seqs, dtype=jnp.int32)[:, None] * span
        + head_pos * part
        + jnp.arange(part, dtype=jnp.int32)[None, :]
    )
    length = jnp.sum(real_mask[seq])
    segment = segment_ids[seq]
    mine = jnp.take(segment, position)
    first = jnp.sum((segment[None, None, :] < mine[:, :, None]).astype(jnp.int32), axis=2)
    least = jnp.maximum(position - (WINDOW - 1), first)
    most = jnp.minimum(position, length - 1)
    limits = jnp.stack([least, most, position])
    limits = jnp.concatenate([limits, limits], axis=2)

    normed, inverse1 = norm(flat, attn_gain)
    qkv, low_qkv = project(normed, w_qkv, d_qkv, u_qkv)
    queries, keys, values = separated(qkv)
    flat_pos = position.reshape(rows)
    heads, kv_heads = HEADS, KV_HEADS
    queries = rotate(queries.reshape(rows, heads, HEAD_DIM), flat_pos, 1.0)
    queries = queries.astype(BF16).reshape(rows, width)
    keys = rotate(keys.reshape(rows, kv_heads, HEAD_DIM), flat_pos, 1.0).astype(BF16)
    values = values.reshape(rows, kv_heads, HEAD_DIM).astype(BF16)
    pairs = jnp.concatenate([keys, values], axis=2).reshape(seqs, part, 2 * kv_heads * HEAD_DIM)
    pairs = lax.all_gather(pairs, "head", axis=1, tiled=True)
    pairs = pairs.reshape(seqs * span, 2 * kv_heads * HEAD_DIM)
    attended, lse = attend(limits, queries, pairs)

    branch, low_output = project(attended, w_output, d_output, u_output)
    middle = flat + branch
    normed2, inverse2 = norm(middle, ffn_gain)
    gate, low_gate = project(normed2, w_gateup[0], d_gateup[0], u_gateup[0])
    upward, low_upward = project(normed2, w_gateup[1], d_gateup[1], u_gateup[1])
    sigma = jax.nn.sigmoid(gate)
    silu = gate * sigma
    activated = (silu * upward).astype(BF16)
    branch, low_ffdown = project(activated, w_down, d_ffdown, u_ffdown)
    output = (middle + branch).astype(BF16)

    grad_act, gd_ffdown, gu_ffdown = project_back(
        activated, low_ffdown, grad_flat, w_down, d_ffdown, u_ffdown
    )
    grad_gate = (grad_act * upward * (sigma * (1.0 + gate * (1.0 - sigma)))).astype(BF16)
    grad_upward = (grad_act * silu).astype(BF16)
    grad_in_gate, gd_gate, gu_gate = project_back(
        normed2, low_gate, grad_gate, w_gateup[0], d_gateup[0], u_gateup[0]
    )
    grad_in_up, gd_up, gu_up = project_back(
        normed2, low_upward, grad_upward, w_gateup[1], d_gateup[1], u_gateup[1]
    )
    grad_middle = grad_flat.astype(F32) + norm_back(
        middle, inverse2, ffn_gain, grad_in_gate + grad_in_up
    )
    grad_mixed, gd_output, gu_output = project_back(
        attended, low_output, grad_middle.astype(BF16), w_output, d_output, u_output
    )
    grad_query, grad_pairs = attend_back(limits, queries, pairs, lse, grad_mixed.astype(BF16))
    grad_pairs = lax.psum_scatter(
        grad_pairs.reshape(seqs, span, -1), "head", scatter_dimension=1, tiled=True
    ).reshape(rows, kv_heads, 2 * HEAD_DIM)
    grad_query = rotate(grad_query.reshape(rows, heads, HEAD_DIM), flat_pos, -1.0)
    grad_keys = rotate(grad_pairs[:, :, :HEAD_DIM], flat_pos, -1.0)
    grad_values = grad_pairs[:, :, HEAD_DIM:]
    grad_qkv = interleaved(
        grad_query.astype(BF16).reshape(rows, width),
        grad_keys.astype(BF16).reshape(rows, kv_heads * HEAD_DIM),
        grad_values.astype(BF16).reshape(rows, kv_heads * HEAD_DIM),
    )
    grad_normed, gd_qkv, gu_qkv = project_back(normed, low_qkv, grad_qkv, w_qkv, d_qkv, u_qkv)
    input_grad = grad_middle + norm_back(flat, inverse1, attn_gain, grad_normed)

    gu_query = separated(gu_qkv[:rank])[0]
    gu_key = separated(gu_qkv[rank : 2 * rank])[1]
    gu_value = separated(gu_qkv[2 * rank :])[2]
    terms = [
        gd_qkv[:rank],
        gu_query,
        gd_qkv[rank : 2 * rank],
        gd_qkv[2 * rank :],
        gu_key,
        gu_value,
        gd_output,
        gu_output,
        gd_gate,
        gd_up,
        gu_gate,
        gu_up,
        gd_ffdown,
        gu_ffdown,
    ]
    sizes = [term.shape[1] for term in terms]
    unit = groups * TILE
    extra = -sum(sizes) % unit
    terms.append(jnp.zeros((rank, extra), F32))
    shared = lax.psum_scatter(
        jnp.concatenate(terms, axis=1), "head", scatter_dimension=1, tiled=True
    )
    shared = lax.all_gather(shared.astype(BF16), ("blk", "head"), axis=0)
    shared = shared.reshape(seqs, groups, rank, -1).swapaxes(1, 2).reshape(seqs, rank, -1)
    adapters = jnp.arange(query_down.shape[0], dtype=jnp.int32)
    holder = jnp.argmax(adapter_index[None, :] == adapters[:, None], axis=1)
    shared = shared[holder]
    cuts = np.cumsum([0] + sizes)
    found = [shared[:, :, begin:end].astype(F32) for begin, end in zip(cuts[:-1], cuts[1:])]
    return (
        moved(output.reshape(seqs, part, width)),
        moved(input_grad.astype(BF16).reshape(seqs, part, width)),
        found[0].swapaxes(1, 2),
        found[1],
        jnp.stack([found[2], found[3]], axis=1).swapaxes(2, 3),
        jnp.stack([found[4], found[5]], axis=1),
        found[6].swapaxes(1, 2),
        found[7],
        jnp.stack([found[8], found[9]], axis=1).swapaxes(2, 3),
        jnp.stack([found[10], found[11]], axis=1),
        found[12].swapaxes(1, 2),
        found[13],
    )


def solution(mesh):
    in_specs = (
        P(None, ("blk", "head"), None),
        P(),
        P(),
        P("blk", "head"),
        P(None, "blk", "head"),
        P("blk", "head"),
        P(None, "blk", "head"),
        P("blk", "head"),
        P(),
        P(),
        P(),
        P(),
        P(),
        P(),
        P(),
        P(),
        P(),
        P(),
        P(),
        P(),
        P(),
        P(None, ("blk", "head"), None),
    )
    out_specs = (
        P(None, ("blk", "head"), None),
        P(None, ("blk", "head"), None),
        P(),
        P(),
        P(),
        P(),
        P(),
        P(),
        P(),
        P(),
        P(),
        P(),
    )

    def chosen(tokens, *rest):
        if mesh.shape["blk"] == tokens.shape[0] == 8 and mesh.shape["head"] == 4:
            return by_sequence(tokens, *rest)
        return on_device(tokens, *rest)

    return jax.shard_map(
        chosen, mesh=mesh, in_specs=in_specs, out_specs=out_specs, check_vma=False
    )
```

```python
import functools
import math

import jax
import jax.numpy as jnp
import numpy as np
from jax import lax
from jax.experimental import pallas as pl
from jax.experimental.pallas import tpu as pltpu
from jax.sharding import PartitionSpec as P

HEADS = 20
KV_HEADS = 5
HEAD_DIM = 64
WINDOW = 1024


EPSILON = 1e-05
ROPE_BASE = 10000.0
ADAPTER_SCALE = 2.0
MASKED = -1e30


def passed_along(value, axis, steps):
    count = lax.axis_size(axis)
    initial, last = (max(0, -steps), min(count, count - steps))
    return lax.ppermute(value, axis, [(source, source + steps) for source in range(initial, last)])


def rms_scale(values, gain):
    return values * lax.rsqrt(jnp.mean(values * values, axis=-1, keepdims=True) + EPSILON) * gain


def rotate(values, positions, sign):
    half = values.shape[-1] // 2
    freqs = ROPE_BASE ** (-(jnp.arange(half, dtype=jnp.float32) * 2.0) / values.shape[-1])
    angles = positions.astype(jnp.float32)[:, None] * freqs[None, :]
    cosine = jnp.cos(angles)[:, None, :]
    sine = sign * jnp.sin(angles)[:, None, :]
    first = values[..., :half]
    second = values[..., half:]
    return jnp.concatenate(
        [first * cosine - second * sine, second * cosine + first * sine], axis=-1
    )


def gated(gate, upward):
    return jax.nn.silu(gate) * upward


def project(inputs, weight, down, up):
    lowered = jnp.einsum("sci,sir->scr", inputs, down, preferred_element_type=jnp.float32).astype(
        jnp.bfloat16
    )
    extra = ADAPTER_SCALE * jnp.einsum(
        "scr,sro->sco", lowered, up, preferred_element_type=jnp.float32
    )
    return (
        jnp.einsum("sci,io->sco", inputs, weight, preferred_element_type=jnp.float32) + extra,
        lowered,
    )


def project_back(inputs, lowered, grad_out, weight, down, up):
    grad_up = ADAPTER_SCALE * jnp.einsum(
        "scr,sco->sro", lowered, grad_out, preferred_element_type=jnp.float32
    )
    grad_low = (
        ADAPTER_SCALE * jnp.einsum("sco,sro->scr", grad_out, up, preferred_element_type=jnp.float32)
    ).astype(jnp.bfloat16)
    grad_down = jnp.einsum("sci,scr->sir", inputs, grad_low, preferred_element_type=jnp.float32)
    grad_in = jnp.einsum("sco,io->sci", grad_out, weight, preferred_element_type=jnp.float32)
    grad_in = grad_in + jnp.einsum(
        "scr,sir->sci", grad_low, down, preferred_element_type=jnp.float32
    )
    return (grad_in, grad_down, grad_up)


def on_device(
    tokens,
    attn_gain,
    ffn_gain,
    query_weight,
    keyval_weight,
    output_weight,
    gateup_weight,
    down_weight,
    query_down,
    query_up,
    keyval_down,
    keyval_up,
    output_down,
    output_up,
    gateup_down,
    gateup_up,
    ffdown_down,
    ffdown_up,
    segment_ids,
    real_mask,
    adapter_index,
    out_grad,
):
    seqs, per_device, width = tokens.shape
    groups = lax.axis_size("head")
    head_pos = lax.axis_index("head")
    blk_pos = lax.axis_index("blk")
    span = groups * per_device
    heads = HEADS
    head_dim = HEAD_DIM
    kv_heads = KV_HEADS
    local_heads = heads // groups
    share = heads // kv_heads
    reach = (WINDOW - 2) // span + 1
    scale = 1.0 / math.sqrt(head_dim)
    rows_a, rows_b, rows_c, rows_d, rows_e = (
        lax.all_gather(query_weight, "blk", axis=0, tiled=True),
        lax.all_gather(keyval_weight, "blk", axis=1, tiled=True),
        lax.all_gather(output_weight, "blk", axis=0, tiled=True),
        lax.all_gather(gateup_weight, "blk", axis=1, tiled=True),
        lax.all_gather(down_weight, "blk", axis=0, tiled=True),
    )
    w_query, w_keyval, w_output, w_gateup, w_down = (
        lax.all_gather(rows_a, "head", axis=1, tiled=True),
        lax.all_gather(rows_b, "head", axis=2, tiled=True),
        lax.all_gather(rows_c, "head", axis=1, tiled=True),
        lax.all_gather(rows_d, "head", axis=2, tiled=True),
        lax.all_gather(rows_e, "head", axis=1, tiled=True),
    )
    down_query = query_down[adapter_index]
    up_query = query_up[adapter_index]
    down_keyval = keyval_down[adapter_index]
    up_keyval = keyval_up[adapter_index]
    down_output = output_down[adapter_index]
    up_output = output_up[adapter_index]
    down_gateup = gateup_down[adapter_index]
    up_gateup = gateup_up[adapter_index]
    down_ffdown = ffdown_down[adapter_index]
    up_ffdown = ffdown_up[adapter_index]

    def first_norm(values):
        return rms_scale(values, attn_gain)

    def second_norm(values):
        return rms_scale(values, ffn_gain)

    flat = tokens.astype(jnp.float32)
    normed_full, first_norm_back = jax.vjp(first_norm, flat)
    normed = normed_full.astype(jnp.bfloat16)
    queries_pre, low_query = project(normed, w_query, down_query, up_query)
    keys_pre, low_key = project(normed, w_keyval[0], down_keyval[:, 0], up_keyval[:, 0])
    values_pre, low_value = project(normed, w_keyval[1], down_keyval[:, 1], up_keyval[:, 1])
    token_pos = (blk_pos * groups + head_pos) * per_device + jnp.arange(per_device, dtype=jnp.int32)
    queries = rotate(queries_pre.reshape(seqs, per_device, heads, head_dim), token_pos, 1.0).astype(
        jnp.bfloat16
    )
    keys = rotate(keys_pre.reshape(seqs, per_device, kv_heads, head_dim), token_pos, 1.0).astype(
        jnp.bfloat16
    )
    values = values_pre.reshape(seqs, per_device, kv_heads, head_dim).astype(jnp.bfloat16)
    owner = np.array(
        [
            [(group * local_heads + slot) // share for slot in range(local_heads)]
            for group in range(groups)
        ]
    )
    slot_of = jnp.arange(local_heads, dtype=jnp.int32)
    sender = jnp.asarray(
        (owner[:, :, None] == np.arange(kv_heads)[None, None, :]).astype(np.float32), jnp.bfloat16
    )
    spread = (slot_of[:, None] == jnp.arange(local_heads, dtype=jnp.int32)[None, :]).astype(
        jnp.bfloat16
    )
    pair = jnp.stack([keys, values], axis=3)
    outgoing = jnp.einsum(
        "sckxd,gmk->scgmxd", pair, sender, preferred_element_type=jnp.float32
    ).astype(jnp.bfloat16)
    outgoing = outgoing.reshape(seqs, per_device, groups, local_heads * 2 * head_dim)
    query_send = queries.reshape(seqs, per_device, groups, local_heads * head_dim)
    query_here, pair_here = (
        lax.all_to_all(query_send, "head", split_axis=2, concat_axis=1, tiled=True),
        lax.all_to_all(outgoing, "head", split_axis=2, concat_axis=1, tiled=True),
    )
    query_here = query_here.reshape(seqs, span, local_heads, head_dim)
    pair_here = pair_here.reshape(seqs, span, local_heads, 2, head_dim)
    received = [pair_here]
    moving = pair_here
    for hop in range(reach):
        moving = passed_along(moving, "blk", 1)
        received.append(moving)
    window_pairs = jnp.stack(received, axis=1)
    query_pos = blk_pos * span + jnp.arange(span, dtype=jnp.int32)
    key_pos = (blk_pos - jnp.arange(reach + 1, dtype=jnp.int32))[:, None] * span + jnp.arange(
        span, dtype=jnp.int32
    )[None, :]
    safe_pos = jnp.clip(key_pos, 0, segment_ids.shape[1] - 1)
    query_segment = lax.dynamic_slice_in_dim(segment_ids, blk_pos * span, span, 1)
    key_segment = segment_ids[:, safe_pos]
    key_real = real_mask[:, safe_pos]
    distance = query_pos[:, None, None] - key_pos[None]
    allowed = (key_pos[None] >= 0) & (distance >= 0) & (distance < WINDOW)
    allowed = allowed & (query_segment[:, :, None, None] == key_segment[:, None])
    allowed = allowed & ((key_real[:, None] == 1) | (distance[None] == 0))
    batch = 1
    target = max(1, 512 // span)
    for option in range(1, seqs + 1):
        if seqs % option == 0 and option <= target:
            batch = option
    count = seqs // batch

    def grouped(array):
        return array.reshape((count, batch) + array.shape[1:])

    def scores_of(query_part, pair_part, allowed_part):
        keys_wide = jnp.einsum(
            "gjlmd,hm->gjlhd", pair_part[:, :, :, :, 0], spread, preferred_element_type=jnp.float32
        ).astype(jnp.bfloat16)
        values_wide = jnp.einsum(
            "gjlmd,hm->gjlhd", pair_part[:, :, :, :, 1], spread, preferred_element_type=jnp.float32
        ).astype(jnp.bfloat16)
        raw = (
            jnp.einsum(
                "gqhd,gjlhd->ghqjl", query_part, keys_wide, preferred_element_type=jnp.float32
            )
            * scale
        )
        raw = jnp.where(allowed_part[:, None], raw, MASKED)
        return (raw, keys_wide, values_wide)

    def attend(pieces):
        query_part, pair_part, allowed_part = pieces
        raw, keys_wide, values_wide = scores_of(query_part, pair_part, allowed_part)
        top = jnp.max(raw, axis=(3, 4), keepdims=True)
        shifted = jnp.exp(raw - top)
        total = jnp.sum(shifted, axis=(3, 4), keepdims=True)
        probs_low = (shifted / total).astype(jnp.bfloat16)
        result = jnp.einsum(
            "ghqjl,gjlhd->gqhd", probs_low, values_wide, preferred_element_type=jnp.float32
        )
        return (result.astype(jnp.bfloat16), top + jnp.log(total))

    attended, logsum = lax.map(
        attend, (grouped(query_here), grouped(window_pairs), grouped(allowed))
    )
    mixed = lax.all_to_all(
        attended.reshape(seqs, span, local_heads * head_dim),
        "head",
        split_axis=1,
        concat_axis=2,
        tiled=True,
    )
    branch_attn, low_output = project(mixed, w_output, down_output, up_output)
    middle = flat + branch_attn
    normed2_full, second_norm_back = jax.vjp(second_norm, middle)
    normed2 = normed2_full.astype(jnp.bfloat16)
    gate, low_gate = project(normed2, w_gateup[0], down_gateup[:, 0], up_gateup[:, 0])
    upward, low_upward = project(normed2, w_gateup[1], down_gateup[:, 1], up_gateup[:, 1])
    activated_full, gated_back = jax.vjp(gated, gate, upward)
    activated = activated_full.astype(jnp.bfloat16)
    branch_ffn, low_ffdown = project(activated, w_down, down_ffdown, up_ffdown)
    output = (middle + branch_ffn).astype(jnp.bfloat16)
    grad_activated, gd_ffdown, gu_ffdown = project_back(
        activated, low_ffdown, out_grad, w_down, down_ffdown, up_ffdown
    )
    grad_gate, grad_upward = gated_back(grad_activated)
    grad_in_gate, gd_gate, gu_gate = project_back(
        normed2,
        low_gate,
        grad_gate.astype(jnp.bfloat16),
        w_gateup[0],
        down_gateup[:, 0],
        up_gateup[:, 0],
    )
    grad_in_up, gd_up, gu_up = project_back(
        normed2,
        low_upward,
        grad_upward.astype(jnp.bfloat16),
        w_gateup[1],
        down_gateup[:, 1],
        up_gateup[:, 1],
    )
    grad_middle = out_grad.astype(jnp.float32) + second_norm_back(grad_in_gate + grad_in_up)[0]
    grad_mixed, gd_output, gu_output = project_back(
        mixed, low_output, grad_middle.astype(jnp.bfloat16), w_output, down_output, up_output
    )
    grad_send = grad_mixed.astype(jnp.bfloat16).reshape(
        seqs, per_device, groups, local_heads * head_dim
    )
    grad_here = lax.all_to_all(grad_send, "head", split_axis=2, concat_axis=1, tiled=True).reshape(
        seqs, span, local_heads, head_dim
    )
    spread_full = spread.astype(jnp.float32)

    def attend_back(pieces):
        query_part, pair_part, allowed_part, logsum_part, grad_part = pieces
        raw, keys_wide, values_wide = scores_of(query_part, pair_part, allowed_part)
        probs = jnp.exp(raw - logsum_part)
        probs_low = probs.astype(jnp.bfloat16)
        grad_probs = jnp.einsum(
            "gqhd,gjlhd->ghqjl", grad_part, values_wide, preferred_element_type=jnp.float32
        )
        inner = jnp.sum(probs * grad_probs, axis=(3, 4), keepdims=True)
        grad_raw = (probs * (grad_probs - inner)).astype(jnp.bfloat16)
        grad_query = scale * jnp.einsum(
            "ghqjl,gjlhd->gqhd", grad_raw, keys_wide, preferred_element_type=jnp.float32
        )
        grad_keys = scale * jnp.einsum(
            "ghqjl,gqhd->gjlhd", grad_raw, query_part, preferred_element_type=jnp.float32
        )
        grad_values = jnp.einsum(
            "ghqjl,gqhd->gjlhd", probs_low, grad_part, preferred_element_type=jnp.float32
        )
        both = jnp.stack([grad_keys, grad_values], axis=4)
        folded = jnp.einsum("gjlhxd,hm->gjlmxd", both, spread_full, precision=lax.Precision.HIGHEST)
        return (grad_query, folded)

    grad_query, grad_pairs = lax.map(
        attend_back,
        (grouped(query_here), grouped(window_pairs), grouped(allowed), logsum, grouped(grad_here)),
    )
    grad_pairs = grad_pairs.reshape(seqs, reach + 1, span, local_heads, 2, head_dim)
    carried = grad_pairs[:, reach]
    for hop in range(reach - 1, -1, -1):
        carried = (
            passed_along(carried.astype(jnp.bfloat16), "blk", -1).astype(carried.dtype)
            + grad_pairs[:, hop]
        )
    grad_query = rotate(grad_query.reshape(seqs, span, local_heads, head_dim), query_pos, -1.0)
    grad_query = grad_query.astype(jnp.bfloat16).reshape(seqs, span, local_heads * head_dim)
    grad_queries_pre = lax.all_to_all(grad_query, "head", split_axis=1, concat_axis=2, tiled=True)
    grad_pair_tok = lax.all_to_all(
        carried.reshape(seqs, span, local_heads * 2 * head_dim).astype(jnp.bfloat16),
        "head",
        split_axis=1,
        concat_axis=2,
        tiled=True,
    ).astype(jnp.float32)
    grad_pair_tok = grad_pair_tok.reshape(seqs, per_device, groups, local_heads, 2, head_dim)
    grad_pair_heads = jnp.einsum(
        "scgmxd,gmk->sckxd",
        grad_pair_tok,
        sender.astype(jnp.float32),
        precision=lax.Precision.HIGHEST,
    )
    grad_keys_pre = (
        rotate(grad_pair_heads[:, :, :, 0], token_pos, -1.0)
        .astype(jnp.bfloat16)
        .reshape(seqs, per_device, kv_heads * head_dim)
    )
    grad_values_pre = (
        grad_pair_heads[:, :, :, 1]
        .astype(jnp.bfloat16)
        .reshape(seqs, per_device, kv_heads * head_dim)
    )
    grad_in_query, gd_query, gu_query = project_back(
        normed, low_query, grad_queries_pre, w_query, down_query, up_query
    )
    grad_in_key, gd_key, gu_key = project_back(
        normed, low_key, grad_keys_pre, w_keyval[0], down_keyval[:, 0], up_keyval[:, 0]
    )
    grad_in_value, gd_value, gu_value = project_back(
        normed, low_value, grad_values_pre, w_keyval[1], down_keyval[:, 1], up_keyval[:, 1]
    )
    grad_normed = grad_in_query + grad_in_key + grad_in_value
    input_grad = (grad_middle + first_norm_back(grad_normed)[0]).astype(jnp.bfloat16)
    chooser = (
        adapter_index[:, None] == jnp.arange(query_down.shape[0], dtype=jnp.int32)[None, :]
    ).astype(jnp.float32)

    def per_adapter(per_sequence):
        return jnp.einsum("sa,s...->a...", chooser, per_sequence, precision=lax.Precision.HIGHEST)

    sums = lax.psum(
        (
            per_adapter(gd_query),
            per_adapter(gu_query),
            per_adapter(jnp.stack([gd_key, gd_value], axis=1)),
            per_adapter(jnp.stack([gu_key, gu_value], axis=1)),
            per_adapter(gd_output),
            per_adapter(gu_output),
            per_adapter(jnp.stack([gd_gate, gd_up], axis=1)),
            per_adapter(jnp.stack([gu_gate, gu_up], axis=1)),
            per_adapter(gd_ffdown),
            per_adapter(gu_ffdown),
        ),
        ("blk", "head"),
    )
    return (
        output,
        input_grad,
        sums[0],
        sums[1],
        sums[2],
        sums[3],
        sums[4],
        sums[5],
        sums[6],
        sums[7],
        sums[8],
        sums[9],
    )


MESH = pl.DeviceIdType.MESH
F32 = jnp.float32
BF16 = jnp.bfloat16
TILE = 128
ANYWHERE = pl.BlockSpec(memory_space=pl.ANY)


def dot(left, right, left_dim=1, right_dim=0):
    return lax.dot_general(
        left, right, (((left_dim,), (right_dim,)), ((), ())), preferred_element_type=F32
    )


def place():
    blk, head = lax.axis_index("blk"), lax.axis_index("head")
    return blk // 2, blk % 2, head // 2, head % 2


def device(z, x, y, core):
    return (z * 2 + x, y * 2 + core)


def halves(count):
    first = (count // 2 + 15) // 16 * 16
    return ((0, first), (first, count - first))


class Spread:
    def __init__(self, sources, target, lines, sems):
        self.sources, self.target, self.lines = sources, target, lines
        self.z, self.x, self.y, self.core = place()
        self.z_in, self.x_in, self.y_in, self.d_in, self.c_in = sems[:5]
        self.z_out, self.x_out, self.y_out, self.d_out, self.c_out = sems[5:10]

    @staticmethod
    def semaphores(parts, lines):
        dma = pltpu.SemaphoreType.DMA
        return [
            dma((parts, lines)),
            dma((parts, lines)),
            dma((parts, lines)),
            dma((parts, lines, 2)),
            dma((parts, lines, 4)),
            dma((parts, 2, lines)),
            dma((parts, lines)),
            dma((parts, lines)),
            dma((parts, lines, 2)),
            dma((parts, lines, 4)),
        ]

    def inside(self, z):
        return (z >= 0) & (z < self.lines)

    def neighbours(self):
        z, x, y, core = self.z, self.x, self.y, self.core
        return (device(z, 1 - x, y, core), device(z, x, 1 - y, core), device(z, x, y, 1 - core))

    def greet(self):
        barrier = pltpu.get_barrier_semaphore()
        for side in (1, -1):

            @pl.when(self.inside(self.z + side))
            def _():
                other = device(self.z + side, self.x, self.y, self.core)
                pl.semaphore_signal(barrier, inc=1, device_id=other, device_id_type=MESH)

        for other in self.neighbours():
            pl.semaphore_signal(barrier, inc=1, device_id=other, device_id_type=MESH)
        ends = jnp.where(self.z > 0, 1, 0) + jnp.where(self.z < self.lines - 1, 1, 0)
        pl.semaphore_wait(barrier, 3 + ends)

    def copy(self, source, target, out, into, other):
        return pltpu.make_async_remote_copy(
            src_ref=source,
            dst_ref=target,
            send_sem=out,
            recv_sem=into,
            device_id=other,
            device_id_type=MESH,
        )

    def along_z(self, part, source, z, side):
        return self.copy(
            source,
            self.target(part, z, self.x, self.y, self.core),
            self.z_out.at[part, (side + 1) // 2, z],
            self.z_in.at[part, z],
            device(self.z + side, self.x, self.y, self.core),
        )

    def along_x(self, part, source, z):
        return self.copy(
            source,
            self.target(part, z, self.x, self.y, self.core),
            self.x_out.at[part, z],
            self.x_in.at[part, z],
            device(self.z, 1 - self.x, self.y, self.core),
        )

    def along_y(self, part, source, z):
        return self.copy(
            source,
            self.target(part, z, self.x, self.y, self.core),
            self.y_out.at[part, z],
            self.y_in.at[part, z],
            device(self.z, self.x, 1 - self.y, self.core),
        )

    def across(self, part, source, z, flip_x, flip_y):
        x, y = (self.x + flip_x) % 2, (self.y + flip_y) % 2
        return self.copy(
            source,
            self.target(part, z, x, y, self.core),
            self.c_out.at[part, z, flip_x * 2 + flip_y],
            self.c_in.at[part, z, flip_x * 2 + flip_y],
            device(self.z, self.x, self.y, 1 - self.core),
        )

    def piece(self, ref, which):
        if ref.shape[0] < 32:
            size = ref.shape[1] // 2
            return ref.at[:, pl.ds(which * size, size)]
        begin, size = halves(ref.shape[0])[which]
        return ref.at[pl.ds(begin, size)]

    def diagonal(self, part, z, which):
        if which == 0:
            ref = self.target(part, z, self.x, 1 - self.y, self.core)
            other = device(self.z, 1 - self.x, self.y, self.core)
        else:
            ref = self.target(part, z, 1 - self.x, self.y, self.core)
            other = device(self.z, self.x, 1 - self.y, self.core)
        ref = self.piece(ref, which)
        return self.copy(
            ref, ref, self.d_out.at[part, z, which], self.d_in.at[part, z, which], other
        )

    def arrived(self, ref, out, into):
        self.copy(ref, ref, out, into, device(self.z, self.x, self.y, 1 - self.core)).wait_recv()

    def hand_on(self, part, source, z):
        self.along_x(part, source, z).start()
        self.along_y(part, source, z).start()
        self.across(part, source, z, 0, 0).start()

    def begin(self, part):
        for side in (1, -1):

            @pl.when(self.inside(self.z + side))
            def _():
                self.along_z(part, self.sources[part], self.z, side).start()

        self.hand_on(part, self.sources[part], self.z)

    def line_step(self, part, distance, side):
        z = self.z - side * distance

        @pl.when(self.inside(z))
        def _():
            ref = self.target(part, z, self.x, self.y, self.core)
            self.arrived(ref, self.z_out.at[part, 0, z], self.z_in.at[part, z])

            @pl.when(self.inside(self.z + side))
            def _():
                self.along_z(part, ref, z, side).start()

            self.hand_on(part, ref, z)

    def plane_step(self, part, z):
        ref = self.target(part, z, self.x, 1 - self.y, self.core)
        self.arrived(ref, self.y_out.at[part, z], self.y_in.at[part, z])
        self.diagonal(part, z, 0).start()
        self.across(part, ref, z, 0, 1).start()
        ref = self.target(part, z, 1 - self.x, self.y, self.core)
        self.arrived(ref, self.x_out.at[part, z], self.x_in.at[part, z])
        self.diagonal(part, z, 1).start()
        self.across(part, ref, z, 1, 0).start()

    def corner_step(self, part, z):
        ref = self.target(part, z, 1 - self.x, 1 - self.y, self.core)
        for which in (0, 1):
            self.arrived(
                self.piece(ref, which), self.d_out.at[part, z, which], self.d_in.at[part, z, which]
            )
        self.across(part, ref, z, 1, 1).start()

    def end(self, part, z):
        for flip_x in (0, 1):
            for flip_y in (0, 1):
                x, y = (self.x + flip_x) % 2, (self.y + flip_y) % 2
                which = flip_x * 2 + flip_y
                self.arrived(
                    self.target(part, z, x, y, 1 - self.core),
                    self.c_out.at[part, z, which],
                    self.c_in.at[part, z, which],
                )
                self.across(
                    part, self.target(part, z, x, y, self.core), z, flip_x, flip_y
                ).wait_send()
        mine = self.target(part, z, self.x, self.y, self.core)
        self.along_x(part, mine, z).wait_send()
        self.along_y(part, mine, z).wait_send()
        self.diagonal(part, z, 0).wait_send()
        self.diagonal(part, z, 1).wait_send()
        for side in (1, -1):

            @pl.when(self.inside(self.z + side) & ((self.z - z) * side >= 0))
            def _():
                self.along_z(part, mine, z, side).wait_send()

    def all_steps(self, parts):
        for part in parts:
            for distance in range(1, self.lines):
                for side in (1, -1):
                    self.line_step(part, distance, side)
        for part in parts:
            for z in range(self.lines):
                self.plane_step(part, z)
        for part in parts:
            for z in range(self.lines):
                self.corner_step(part, z)
        for part in parts:
            for z in range(self.lines):
                self.end(part, z)


def paired(own, other, core):
    own, other = own.astype(F32), other.astype(F32)
    return [jnp.where(core == 0, own, other), jnp.where(core == 0, other, own)]


def in_pairs(array):
    half = array.shape[1] // 2
    size = 2 * KV_HEADS * HEAD_DIM // 4
    keys = jnp.concatenate([array[:, :size], array[:, half : half + size]], axis=1)
    values = jnp.concatenate(
        [array[:, size : 2 * size], array[:, half + size : half + 2 * size]], axis=1
    )
    pieces = []
    for head in range(KV_HEADS):
        cut = slice(head * HEAD_DIM, (head + 1) * HEAD_DIM)
        pieces += [keys[:, cut], values[:, cut]]
    return jnp.concatenate(pieces, axis=1)


def gather_kernel(lines, *refs):
    query, keyval, output, gateup, down, w_qkv, w_output, w_gateup, w_down = refs[:9]
    got_query, got_keyval, got_output, got_down, my_query, my_keyval, my_output, my_down = refs[9:17]
    all_keyval, pairs, pair_out, pair_in, local = refs[17:22]
    rows, deep = my_query.shape[0], my_down.shape[0]
    wide, mixed = my_output.shape[1], my_keyval.shape[1]
    span, hidden = gateup.shape[1:]
    width = w_output.shape[1]

    def target(part, z, x, y, core):
        blk, head = z * 2 + x, y * 2 + core
        if part == 0:
            return all_keyval.at[pl.ds(blk * 2 * rows + core * rows, rows), pl.ds(y * mixed, mixed)]
        if part == 1:
            return w_qkv.at[pl.ds(blk * 2 * rows + core * rows, rows), pl.ds(y * wide, wide)]
        if part == 2:
            return w_output.at[pl.ds(blk * 2 * rows + core * rows, rows), pl.ds(y * wide, wide)]
        if part == 5:
            return w_down.at[pl.ds(blk * 2 * deep + core * deep, deep), pl.ds(y * wide, wide)]
        return w_gateup.at[part - 3, pl.ds(blk * span, span), pl.ds(head * hidden, hidden)]

    sources = [my_keyval, my_query, my_output, gateup.at[0], gateup.at[1], my_down]
    spread = Spread(sources, target, lines, refs[22:])
    core = spread.core
    spread.greet()
    sibling = device(spread.z, spread.x, spread.y, 1 - core)
    theirs = pl.ds((1 - core) * rows, rows)
    swaps = [
        spread.copy(keyval.at[:, theirs], got_keyval, pair_out.at[0], pair_in.at[0], sibling),
        spread.copy(query.at[theirs], got_query, pair_out.at[1], pair_in.at[1], sibling),
        spread.copy(output.at[theirs], got_output, pair_out.at[2], pair_in.at[2], sibling),
        spread.copy(
            down.at[pl.ds((1 - core) * deep, deep)], got_down, pair_out.at[3], pair_in.at[3], sibling
        ),
    ]
    for swap in swaps:
        swap.start()
    mine = pl.ds(core * rows, rows)
    swaps[0].wait_recv()
    pieces = paired(keyval[0, mine, :], got_keyval[0], core)
    pieces += paired(keyval[1, mine, :], got_keyval[1], core)
    filled = sum(p.shape[1] for p in pieces)
    pieces.append(jnp.zeros((rows, mixed - filled), F32))
    my_keyval[...] = jnp.concatenate(pieces, axis=1).astype(BF16)
    spread.begin(0)
    swaps[1].wait_recv()
    my_query[...] = jnp.concatenate(
        paired(query[mine, :], got_query[...], core), axis=1
    ).astype(BF16)
    spread.begin(1)
    swaps[2].wait_recv()
    my_output[...] = jnp.concatenate(
        paired(output[mine, :], got_output[...], core), axis=1
    ).astype(BF16)
    spread.begin(2)
    spread.begin(3)
    spread.begin(4)
    swaps[3].wait_recv()
    my_down[...] = jnp.concatenate(
        paired(down[pl.ds(core * deep, deep), :], got_down[...], core), axis=1
    ).astype(BF16)
    spread.begin(5)
    own = [
        pltpu.make_async_copy(
            sources[part],
            target(part, spread.z, spread.x, spread.y, core),
            local.at[part],
        )
        for part in range(6)
    ]
    for copy in own:
        copy.start()
    spread.all_steps(range(6))
    for copy in own:
        copy.wait()
    for swap in swaps:
        swap.wait_send()
    pairs[...] = in_pairs(all_keyval[...].astype(F32)).astype(BF16)
    last = pltpu.make_async_copy(
        pairs, w_qkv.at[:, pl.ds(width, pairs.shape[1])], local.at[6]
    )
    last.start()
    last.wait()


def gather_weights(query, keyval, output, gateup, down):
    rows, wide = query.shape
    deep = down.shape[0]
    blks, heads = lax.axis_size("blk"), lax.axis_size("head")
    narrow = keyval.shape[2]
    mixed = -(-4 * narrow // TILE) * TILE
    double = heads * narrow * 2
    dma = pltpu.SemaphoreType.DMA
    vmem = pl.BlockSpec(memory_space=pltpu.VMEM)
    shape = jax.ShapeDtypeStruct
    return pl.pallas_call(
        functools.partial(gather_kernel, blks // 2),
        out_shape=[
            shape((blks * rows, heads * wide + double), BF16),
            shape((blks * rows, heads * wide), BF16),
            shape((2, blks * rows, heads * gateup.shape[2]), BF16),
            shape((blks * deep, heads * wide), BF16),
        ],
        in_specs=[vmem, vmem, vmem, ANYWHERE, vmem],
        out_specs=[ANYWHERE] * 4,
        scratch_shapes=[
            pltpu.VMEM((rows // 2, wide), BF16),
            pltpu.VMEM((2, rows // 2, narrow), BF16),
            pltpu.VMEM((rows // 2, wide), BF16),
            pltpu.VMEM((deep // 2, wide), BF16),
            pltpu.VMEM((rows // 2, 2 * wide), BF16),
            pltpu.VMEM((rows // 2, mixed), BF16),
            pltpu.VMEM((rows // 2, 2 * wide), BF16),
            pltpu.VMEM((deep // 2, 2 * wide), BF16),
            pltpu.VMEM((blks * rows, heads // 2 * mixed), BF16),
            pltpu.VMEM((blks * rows, double), BF16),
            dma((4,)),
            dma((4,)),
            dma((7,)),
            *Spread.semaphores(6, blks // 2),
        ],
        compiler_params=pltpu.CompilerParams(
            collective_id=0, has_side_effects=True, vmem_limit_bytes=40 << 20
        ),
    )(query, keyval, output, gateup, down)


def windows(blocks, span, low_part):
    reach = WINDOW + TILE
    fixed = [(0, (block + 1) * span) for block in range(WINDOW // span)]
    offset = TILE * (low_part // 2 + 1) - reach
    return fixed, reach, offset


def tiles_of(ref, flipped):
    lane = lax.broadcasted_iota(jnp.int32, (ref.shape[0], TILE), 1)
    result = []
    for slot in range(4):
        tile = ref[:, slot // 2 * TILE : (slot // 2 + 1) * TILE].astype(F32)
        if (slot % 2 == 0) == flipped:
            tile = pltpu.roll(tile, HEAD_DIM, 1)
        keep = lane >= HEAD_DIM if flipped else lane < HEAD_DIM
        result.append(jnp.where(keep, tile, 0.0).astype(BF16))
    return result


def joined(rows, flipped):
    span = rows.shape[0] // 4
    heads = [rows[slot * span : (slot + 1) * span] for slot in range(4)]
    lane = lax.broadcasted_iota(jnp.int32, (span, TILE), 1)
    result = []
    for first, second in ((heads[0], heads[1]), (heads[2], heads[3])):
        if flipped:
            first = pltpu.roll(first, HEAD_DIM, 1)
        else:
            second = pltpu.roll(second, HEAD_DIM, 1)
        result.append(jnp.where(lane < HEAD_DIM, first, second))
    return result


def bias_of(limits_ref, block, start, count):
    key = start + lax.broadcasted_iota(jnp.int32, (count, TILE), 0)
    least = limits_ref[0, pl.ds(block, 1), :]
    most = limits_ref[1, pl.ds(block, 1), :]
    self_pos = limits_ref[2, pl.ds(block, 1), :]
    allowed = ((key >= least) & (key <= most)) | (key == self_pos)
    bias = jnp.where(allowed, 0.0, MASKED)
    return jnp.concatenate([bias, bias], axis=1)


def each_block(blocks, body, between=lambda: None):
    span = 4 * HEAD_DIM
    fixed, reach, offset = windows(blocks, span, lax.axis_index("head"))
    for block, (start, count) in enumerate(fixed):
        body(block, start, count)
        between()

    @pl.loop(len(fixed), blocks)
    def _(block):
        body(block, pl.multiple_of(block * span + offset, TILE), reach)


def attend_kernel(limits_ref, q_ref, kv_ref, out_ref, lse_ref, q_rows, kv_turned):
    blocks, span = q_rows.shape[0], q_rows.shape[2]
    for slot, tile in enumerate(tiles_of(q_ref, False)):
        q_rows[:, slot] = (tile * BF16(HEAD_DIM**-0.5)).reshape(blocks, span, TILE)
    kv_turned[...] = kv_ref[...].astype(F32).T.astype(BF16)

    def body(block, start, count):
        queries = q_rows[block].reshape(4 * span, TILE)
        scores = dot(kv_ref[pl.ds(start, count), :], queries, 1, 1)
        scores = scores + bias_of(limits_ref, block, start, count)
        top = jnp.max(scores, axis=0, keepdims=True)
        shifted = jnp.exp(scores - top)
        total = jnp.sum(shifted, axis=0, keepdims=True)
        result = dot(kv_turned[:, pl.ds(start, count)], shifted.astype(BF16))
        lse_ref[0, pl.ds(block, 1), :] = top + jnp.log(total)
        result = (result / total).T
        for at, tile in enumerate(joined(result, True)):
            out_ref[pl.ds(block * span, span), at * TILE : (at + 1) * TILE] = tile.astype(BF16)

    each_block(blocks, body)


def attend(limits, queries, pairs):
    rows, width = queries.shape
    blocks = limits.shape[1]
    groups = width // (2 * TILE)
    return pl.pallas_call(
        attend_kernel,
        grid=(groups,),
        out_shape=[
            jax.ShapeDtypeStruct((rows, width), BF16),
            jax.ShapeDtypeStruct((groups, blocks, 2 * TILE), F32),
        ],
        in_specs=[
            pl.BlockSpec(limits.shape, lambda m: (0, 0, 0)),
            pl.BlockSpec((rows, 2 * TILE), lambda m: (0, m)),
            pl.BlockSpec((pairs.shape[0], TILE), lambda m: (0, m)),
        ],
        out_specs=[
            pl.BlockSpec((rows, 2 * TILE), lambda m: (0, m)),
            pl.BlockSpec((1, blocks, 2 * TILE), lambda m: (m, 0, 0)),
        ],
        scratch_shapes=[
            pltpu.VMEM((blocks, 4, rows // blocks, TILE), BF16),
            pltpu.VMEM((TILE, pairs.shape[0]), BF16),
        ],
        compiler_params=pltpu.CompilerParams(vmem_limit_bytes=48 << 20),
    )(limits, queries, pairs)


def meet(others):
    barrier = pltpu.get_barrier_semaphore()
    for other in others:
        pl.semaphore_signal(barrier, inc=1, device_id=other, device_id_type=MESH)
    pl.semaphore_wait(barrier, len(others))


def remote(source, target, out, into, other):
    return pltpu.make_async_remote_copy(
        src_ref=source,
        dst_ref=target,
        send_sem=out,
        recv_sem=into,
        device_id=other,
        device_id_type=MESH,
    )


def along(count):
    blk, head = lax.axis_index("blk"), lax.axis_index("head")
    return [((blk + ahead) % count, head) for ahead in range(1, count)]


def beside():
    z, x, y, core = place()
    return [
        device(z, x, y, 1 - core),
        device(z, x, 1 - y, core),
        device(z, x, 1 - y, 1 - core),
    ]


class Exchange:
    def __init__(self, source, target, size, out, into, local):
        count = target.shape[0]
        blk, head = lax.axis_index("blk"), lax.axis_index("head")
        self.own = pltpu.make_async_copy(source.at[pl.ds(blk * size, size)], target.at[blk], local)
        self.copies, self.arrivals = [], []
        for at, (other, _) in enumerate(along(count)):
            self.copies.append(
                remote(
                    source.at[pl.ds(other * size, size)],
                    target.at[blk],
                    out.at[at],
                    into.at[at],
                    (other, head),
                )
            )
            giver = (blk + count - 1 - at) % count
            self.arrivals.append(
                remote(target.at[giver], target.at[giver], out.at[at], into.at[at], (other, head))
            )

    def start(self):
        self.own.start()
        for copy in self.copies:
            copy.start()

    def wait(self):
        for copy in self.arrivals:
            copy.wait_recv()
        for copy in self.copies:
            copy.wait_send()
        self.own.wait()


class Quarters:
    def __init__(self, terms, low, got, out, into):
        z, x, y, core = place()
        self.size = low.shape[1] // 4
        self.terms, self.low, self.got = terms, low, got
        self.mine = pl.ds((y * 2 + core) * self.size, self.size)
        self.copies = []
        for at, (flip_y, flip_core) in enumerate(((0, 1), (1, 0), (1, 1))):
            other_y, other_core = (y + flip_y) % 2, (core + flip_core) % 2
            theirs = pl.ds((other_y * 2 + other_core) * self.size, self.size)
            self.copies.append(
                remote(
                    low.at[:, theirs],
                    got.at[at],
                    out.at[at],
                    into.at[at],
                    device(z, x, other_y, other_core),
                )
            )

    def start(self):
        self.low[...] = self.terms[...].astype(BF16)
        for copy in self.copies:
            copy.start()

    def total(self):
        for copy in self.copies:
            copy.wait_recv()
        total = self.terms[:, self.mine]
        for at in range(3):
            total = total + self.got[at].astype(F32)
        return total.astype(BF16)

    def end(self):
        for copy in self.copies:
            copy.wait_send()


def turned(tile, cosine, sine, only_low=False):
    lane = lax.broadcasted_iota(jnp.int32, tile.shape, 1)
    half = HEAD_DIM // 2
    partner = jnp.where(
        lane % HEAD_DIM < half, pltpu.roll(tile, TILE - half, 1), pltpu.roll(tile, half, 1)
    )
    result = tile * cosine + partner * sine
    return jnp.where(lane < HEAD_DIM, result, tile) if only_low else result


def attend_back_kernel(
    lines,
    limits_ref,
    q_ref,
    kv_ref,
    lse_ref,
    grad_ref,
    turn_ref,
    output_ref,
    terms_ref,
    dqkv_ref,
    moved_ref,
    shared_ref,
    q_rows,
    g_rows,
    kv_turned,
    total,
    pair_low,
    pair_got,
    kept,
    y_low,
    y_got,
    low,
    got,
    shard,
    pair_out,
    pair_in,
    y_out,
    y_in,
    move_out,
    move_in,
    four_out,
    four_in,
    local,
    *sems,
):
    blocks, span = q_rows.shape[0], q_rows.shape[2]
    width = q_ref.shape[1]
    groups = width // (2 * TILE)
    scale = HEAD_DIM**-0.5
    z, x, y, core = place()
    size = shard.shape[1]

    def target(part, z, x, y, core):
        return shared_ref.at[z * 2 + x, :, pl.ds((y * 2 + core) * size, size)]

    spread = Spread([shard], target, lines, sems)
    meet(along(blocks) + beside())
    exchange = Exchange(output_ref, moved_ref, span, move_out, move_in, local.at[0])
    exchange.start()
    quarters = Quarters(terms_ref, low, got, four_out, four_in)
    quarters.start()
    own = pltpu.make_async_copy(shard, target(0, z, x, y, core), local.at[1])

    def gather_start():
        shard[...] = quarters.total()
        own.start()
        spread.begin(0)

    def line(distance):
        def run():
            spread.line_step(0, distance, 1)
            spread.line_step(0, distance, -1)

        return run

    def planes(first):
        def run():
            spread.plane_step(0, first)
            spread.plane_step(0, first + 1)

        return run

    def corners(first):
        def run():
            spread.corner_step(0, first)
            spread.corner_step(0, first + 1)

        return run

    later = [None, None, None, gather_start, None]
    later += [line(1), None, line(2), None, line(3), None, planes(0), None, planes(2), None]
    later += [corners(0), None, corners(2)]

    def pump():
        if later:
            step = later.pop(0)
            if step is not None:
                step()

    def pair_copy(m):
        return remote(
            pair_low.at[m, 1 - core],
            pair_got.at[m],
            pair_out.at[m],
            pair_in.at[m],
            device(z, x, y, 1 - core),
        )

    def y_copy(m):
        return remote(
            y_low.at[m], y_got.at[m], y_out.at[m], y_in.at[m], device(z, x, 1 - y, core)
        )

    def give(m):
        whole = total[...].reshape(blocks, 4, span, TILE)
        for at in range(4):
            pair_low[m, at % 2, at // 2] = whole[:, at].astype(BF16)
        spot = total.reshape(blocks, 4, span, TILE)
        for at in range(2):
            kept[m, at] = spot[:, at * 2 + core]
        pair_copy(m).start()

    def add_pair(m):
        pair_copy(m).wait_recv()
        y_low[m] = (kept[m, 1 - y] + pair_got[m, 1 - y].astype(F32)).astype(BF16)
        y_copy(m).start()

    def add_y(m):
        y_copy(m).wait_recv()
        tile = kept[m, y] + pair_got[m, y].astype(F32) + y_got[m].astype(F32)
        tile = turned(tile.reshape(blocks * span, TILE), turn_ref[0], -turn_ref[1], True)
        at = width + m * TILE
        dqkv_ref[:, at : at + TILE] = tile.astype(BF16)

    for m in range(groups):
        columns = slice(m * 2 * TILE, (m + 1) * 2 * TILE)
        tile = slice(m * TILE, (m + 1) * TILE)
        for slot, rows in enumerate(tiles_of(q_ref[:, columns], False)):
            q_rows[:, slot] = (rows * BF16(scale)).reshape(blocks, span, TILE)
        for slot, rows in enumerate(tiles_of(grad_ref[:, columns], True)):
            g_rows[:, slot] = rows.reshape(blocks, span, TILE)
        kv_turned[...] = kv_ref[:, tile].astype(F32).T.astype(BF16)
        total[...] = jnp.zeros_like(total)

        def body(block, start, count):
            keys = pl.ds(start, count)
            queries = q_rows[block].reshape(4 * span, TILE)
            grads = g_rows[block].reshape(4 * span, TILE)
            scores = dot(kv_ref[keys, tile], queries, 1, 1)
            scores = scores + bias_of(limits_ref, block, start, count)
            probs = jnp.exp(scores - lse_ref[m, pl.ds(block, 1), :])
            grad_probs = dot(kv_ref[keys, tile], grads, 1, 1)
            inner = jnp.sum(probs * grad_probs, axis=0, keepdims=True)
            grad_scores = (probs * (grad_probs - inner)).astype(BF16)
            total[keys, :] += dot(grad_scores, queries) + dot(probs.astype(BF16), grads)
            grad_q = (dot(kv_turned[:, keys], grad_scores) * scale).T
            rows = pl.ds(block * span, span)
            cosine, sine = turn_ref[0, rows, :], -turn_ref[1, rows, :]
            for at, part in enumerate(joined(grad_q, False)):
                at = m * 2 * TILE + at * TILE
                dqkv_ref[rows, at : at + TILE] = turned(part, cosine, sine).astype(BF16)

        each_block(blocks, body, pump)
        give(m)
        if m >= 1:
            add_pair(m - 1)
        if m >= 2:
            add_y(m - 2)
    while later:
        pump()
    add_pair(groups - 1)
    add_y(groups - 2)
    for z_at in range(lines):
        spread.end(0, z_at)
    own.wait()
    exchange.wait()
    quarters.end()
    add_y(groups - 1)
    for m in range(groups):
        pair_copy(m).wait_send()
        y_copy(m).wait_send()


def attend_back(limits, queries, pairs, lse, grads, turn, output, terms):
    rows, width = queries.shape
    blocks = limits.shape[1]
    span = rows // blocks
    groups = width // (2 * TILE)
    rank, total = terms.shape
    seqs = lax.axis_size("blk")
    each = pltpu.VMEM((blocks, 4, span, TILE), BF16)
    dma = pltpu.SemaphoreType.DMA
    vmem = pl.BlockSpec(memory_space=pltpu.VMEM)
    shape = jax.ShapeDtypeStruct
    return pl.pallas_call(
        functools.partial(attend_back_kernel, seqs // 2),
        out_shape=[
            shape((rows, width + pairs.shape[1]), BF16),
            shape((seqs, span, width), BF16),
            shape((seqs, rank, total), BF16),
        ],
        in_specs=[vmem] * 8,
        out_specs=[vmem, ANYWHERE, ANYWHERE],
        scratch_shapes=[
            each,
            each,
            pltpu.VMEM((TILE, pairs.shape[0]), BF16),
            pltpu.VMEM((pairs.shape[0], TILE), F32),
            pltpu.VMEM((groups, 2, 2, blocks, span, TILE), BF16),
            pltpu.VMEM((groups, 2, blocks, span, TILE), BF16),
            pltpu.VMEM((groups, 2, blocks, span, TILE), F32),
            pltpu.VMEM((groups, blocks, span, TILE), BF16),
            pltpu.VMEM((groups, blocks, span, TILE), BF16),
            pltpu.VMEM((rank, total), BF16),
            pltpu.VMEM((3, rank, total // 4), BF16),
            pltpu.VMEM((rank, total // 4), BF16),
            dma((groups,)),
            dma((groups,)),
            dma((groups,)),
            dma((groups,)),
            dma((seqs - 1,)),
            dma((seqs - 1,)),
            dma((3,)),
            dma((3,)),
            dma((2,)),
            *Spread.semaphores(1, seqs // 2),
        ],
        compiler_params=pltpu.CompilerParams(
            collective_id=1, has_side_effects=True, vmem_limit_bytes=56 << 20
        ),
    )(limits, queries, pairs, lse, grads, turn, output, terms)


def first_back_kernel(
    lines,
    dqkv_ref,
    weight_ref,
    down_ref,
    up_ref,
    normed_ref,
    low_ref,
    middle_ref,
    flat_ref,
    inverse_ref,
    gain_ref,
    moved_ref,
    shared_ref,
    result,
    terms,
    low,
    got,
    shard,
    move_out,
    move_in,
    four_out,
    four_in,
    local,
    *sems,
):
    blocks, span = moved_ref.shape[:2]
    z, x, y, core = place()
    size = shard.shape[1]
    rank = down_ref.shape[0] // 3
    width = flat_ref.shape[1]

    def target(part, z, x, y, core):
        return shared_ref.at[z * 2 + x, :, pl.ds((y * 2 + core) * size, size)]

    spread = Spread([shard], target, lines, sems)
    meet(along(blocks) + beside())
    grad_low = (ADAPTER_SCALE * dot(dqkv_ref[...], up_ref[...], 1, 1)).astype(BF16)
    grad = dot(dqkv_ref[...], weight_ref[...], 1, 1) + dot(grad_low, down_ref[...])
    weighted = grad * gain_ref[...]
    flat, inverse = flat_ref[...].astype(F32), inverse_ref[...]
    mean = jnp.mean(flat * weighted, axis=1, keepdims=True)
    grad = middle_ref[...] + inverse * weighted - flat * (inverse * inverse * inverse * mean)
    result[...] = grad.astype(BF16)
    exchange = Exchange(result, moved_ref, span, move_out, move_in, local.at[0])
    exchange.start()
    grad_up = ADAPTER_SCALE * dot(low_ref[...], dqkv_ref[...], 0, 0)
    grad_down = dot(grad_low, normed_ref[...], 0, 0)
    terms[:, :width] = grad_up[:rank, :width]
    at = width
    while at < dqkv_ref.shape[1]:
        lane = lax.broadcasted_iota(jnp.int32, (rank, TILE), 1)
        terms[:, at : at + TILE] = jnp.where(
            lane < HEAD_DIM,
            grad_up[rank : 2 * rank, at : at + TILE],
            grad_up[2 * rank :, at : at + TILE],
        )
        at += TILE
    for which in range(3):
        terms[:, at : at + width] = grad_down[which * rank : (which + 1) * rank]
        at += width
    if at < terms.shape[1]:
        terms[:, at:] = jnp.zeros((rank, terms.shape[1] - at), F32)
    quarters = Quarters(terms, low, got, four_out, four_in)
    quarters.start()
    shard[...] = quarters.total()
    own = pltpu.make_async_copy(shard, target(0, z, x, y, core), local.at[1])
    own.start()
    spread.begin(0)
    spread.all_steps([0])
    own.wait()
    quarters.end()
    exchange.wait()


def first_back(grad_qkv, weight, down, up, normed, low, middle, flat, inverse, gain):
    rows, width = flat.shape
    rank = down.shape[0] // 3
    seqs, heads = lax.axis_size("blk"), lax.axis_size("head")
    total = 3 * width + weight.shape[1]
    total += -total % (2 * heads * TILE)
    dma = pltpu.SemaphoreType.DMA
    vmem = pl.BlockSpec(memory_space=pltpu.VMEM)
    shape = jax.ShapeDtypeStruct
    return pl.pallas_call(
        functools.partial(first_back_kernel, seqs // 2),
        out_shape=[
            shape((seqs, rows // seqs, width), BF16),
            shape((seqs, rank, total), BF16),
        ],
        in_specs=[vmem] * 10,
        out_specs=[ANYWHERE, ANYWHERE],
        scratch_shapes=[
            pltpu.VMEM((rows, width), BF16),
            pltpu.VMEM((rank, total), F32),
            pltpu.VMEM((rank, total), BF16),
            pltpu.VMEM((3, rank, total // 4), BF16),
            pltpu.VMEM((rank, total // 4), BF16),
            dma((seqs - 1,)),
            dma((seqs - 1,)),
            dma((3,)),
            dma((3,)),
            dma((2,)),
            *Spread.semaphores(1, seqs // 2),
        ],
        compiler_params=pltpu.CompilerParams(
            collective_id=2, has_side_effects=True, vmem_limit_bytes=56 << 20
        ),
    )(grad_qkv, weight, down, up, normed, low, middle, flat, inverse, gain.reshape(1, -1))


def placed_kernel(sizes, width, holder_ref, early_ref, late_ref, *outs):
    q_down, q_up, kv_down, kv_up, o_down, o_up, gu_down, gu_up, ff_down, ff_up = outs
    cuts = np.cumsum([0] + sizes)
    early = [slice(int(begin), int(end)) for begin, end in zip(cuts[:-1], cuts[1:])]
    for out, cut in zip((o_down, o_up), early[:2]):
        out[0] = early_ref[0, :, cut].astype(F32)
    for which in range(2):
        gu_down[0, which] = early_ref[0, :, early[2 + which]].astype(F32)
        gu_up[0, which] = early_ref[0, :, early[4 + which]].astype(F32)
    for out, cut in zip((ff_down, ff_up), early[6:]):
        out[0] = early_ref[0, :, cut].astype(F32)
    q_up[0] = late_ref[0, :, :width].astype(F32)
    narrow = KV_HEADS * HEAD_DIM
    pairs = late_ref[0, :, width : width + 2 * narrow].astype(F32)
    for which in range(2):
        pieces = [
            pairs[:, (2 * head + which) * HEAD_DIM : (2 * head + which + 1) * HEAD_DIM]
            for head in range(KV_HEADS)
        ]
        kv_up[0, which] = jnp.concatenate(pieces, axis=1)
    at = width + 2 * narrow
    q_down[0] = late_ref[0, :, at : at + width].astype(F32)
    for which in range(2):
        at += width
        kv_down[0, which] = late_ref[0, :, at : at + width].astype(F32)


def placed(holder, early, late, sizes, width):
    adapters, rank = early.shape[:2]
    hidden = sizes[4]
    narrow = KV_HEADS * HEAD_DIM
    shapes = [
        (rank, width),
        (rank, width),
        (2, rank, width),
        (2, rank, narrow),
        (rank, width),
        (rank, width),
        (2, rank, width),
        (2, rank, hidden),
        (rank, hidden),
        (rank, width),
    ]

    def whole(shape):
        return pl.BlockSpec((1,) + shape, lambda a, held: (a,) + (0,) * len(shape))

    return pl.pallas_call(
        functools.partial(placed_kernel, sizes, width),
        grid_spec=pltpu.PrefetchScalarGridSpec(
            num_scalar_prefetch=1,
            grid=(adapters,),
            in_specs=[
                pl.BlockSpec((1, rank, early.shape[2]), lambda a, held: (held[a], 0, 0)),
                pl.BlockSpec((1, rank, late.shape[2]), lambda a, held: (held[a], 0, 0)),
            ],
            out_specs=[whole(shape) for shape in shapes],
        ),
        out_shape=[jax.ShapeDtypeStruct((adapters,) + shape, F32) for shape in shapes],
    )(holder, early, late)


def by_sequence(
    tokens,
    attn_gain,
    ffn_gain,
    query_weight,
    keyval_weight,
    output_weight,
    gateup_weight,
    down_weight,
    query_down,
    query_up,
    keyval_down,
    keyval_up,
    output_down,
    output_up,
    gateup_down,
    gateup_up,
    ffdown_down,
    ffdown_up,
    segment_ids,
    real_mask,
    adapter_index,
    out_grad,
):
    seqs, part, width = tokens.shape
    groups = lax.axis_size("head")
    seq, head_pos = lax.axis_index("blk"), lax.axis_index("head")
    rows = seqs * part
    span = groups * part
    adapter = adapter_index[seq]

    def moved(array):
        return lax.all_to_all(array, "blk", split_axis=0, concat_axis=0, tiled=True)

    flat = moved(tokens).reshape(rows, width).astype(F32)
    grad_flat = moved(out_grad).reshape(rows, width)
    w_qkv, w_output, w_gateup, w_down = gather_weights(
        query_weight, keyval_weight, output_weight, gateup_weight, down_weight
    )
    d_query = query_down.swapaxes(1, 2)[adapter]
    d_keyval = keyval_down.swapaxes(2, 3)[adapter]
    d_output = output_down.swapaxes(1, 2)[adapter]
    d_gateup = gateup_down.swapaxes(2, 3)[adapter]
    d_ffdown = ffdown_down.swapaxes(1, 2)[adapter]
    u_query, u_keyval, u_output = query_up[adapter], keyval_up[adapter], output_up[adapter]
    u_gateup, u_ffdown = gateup_up[adapter], ffdown_up[adapter]
    rank = d_query.shape[0]

    def in_turn(first, second):
        cut = (first.shape[0], KV_HEADS, HEAD_DIM)
        both = jnp.concatenate([first.reshape(cut), second.reshape(cut)], axis=2)
        return both.reshape(first.shape[0], 2 * first.shape[1])

    nil = jnp.zeros_like(u_keyval[0])
    u_keys, u_values = in_turn(u_keyval[0], nil), in_turn(nil, u_keyval[1])
    u_qkv = jnp.concatenate(
        [
            jnp.pad(u_query, ((0, 0), (0, u_keys.shape[1]))),
            jnp.pad(jnp.concatenate([u_keys, u_values], axis=0), ((0, 0), (width, 0))),
        ],
        axis=0,
    )
    d_qkv = jnp.concatenate([d_query, d_keyval[0], d_keyval[1]], axis=0)

    def project(inputs, weight, down, up):
        lowered = dot(inputs, down, 1, 1).astype(BF16)
        return dot(inputs, weight) + ADAPTER_SCALE * dot(lowered, up), lowered

    def project_back(inputs, lowered, grad, weight, down, up):
        grad_up = ADAPTER_SCALE * dot(lowered, grad, 0, 0)
        grad_low = (ADAPTER_SCALE * dot(grad, up, 1, 1)).astype(BF16)
        grad_down = dot(grad_low, inputs, 0, 0)
        return dot(grad, weight, 1, 1) + dot(grad_low, down), grad_down, grad_up

    def norm(values, gain):
        inverse = lax.rsqrt(jnp.mean(values * values, axis=-1, keepdims=True) + EPSILON)
        return (values * inverse * gain).astype(BF16), inverse

    def norm_back(values, inverse, gain, grad):
        weighted = grad * gain
        mean = jnp.mean(values * weighted, axis=-1, keepdims=True)
        return inverse * weighted - values * (inverse * inverse * inverse * mean)

    position = (
        jnp.arange(seqs, dtype=jnp.int32)[:, None] * span
        + head_pos * part
        + jnp.arange(part, dtype=jnp.int32)[None, :]
    )
    length = jnp.sum(real_mask[seq])
    segment = segment_ids[seq]
    mine = jnp.take(segment, position)
    first = jnp.sum((segment[None, None, :] < mine[:, :, None]).astype(jnp.int32), axis=2)
    least = jnp.maximum(position - (WINDOW - 1), first)
    most = jnp.minimum(position, length - 1)
    limits = jnp.stack([least, most, position])
    limits = jnp.concatenate([limits, limits], axis=2)

    flat_pos = position.reshape(rows)
    freqs = ROPE_BASE ** (
        -(jnp.arange(HEAD_DIM // 2, dtype=F32) * 2.0) / HEAD_DIM
    )
    angles = flat_pos.astype(F32)[:, None] * freqs[None, :]
    cosine, sine = jnp.cos(angles), jnp.sin(angles)
    turn = jnp.stack(
        [jnp.tile(cosine, (1, 4)), jnp.tile(jnp.concatenate([-sine, sine], axis=1), (1, 2))]
    )

    normed, inverse1 = norm(flat, attn_gain)
    qkv, low_qkv = project(normed, w_qkv, d_qkv, u_qkv)
    queries, pairs = qkv[:, :width], qkv[:, width:]
    heads, kv_heads = HEADS, KV_HEADS
    queries = rotate(queries.reshape(rows, heads, HEAD_DIM), flat_pos, 1.0)
    queries = queries.astype(BF16).reshape(rows, width)
    pairs = pairs.reshape(rows, kv_heads, 2 * HEAD_DIM)
    keys = rotate(pairs[:, :, :HEAD_DIM], flat_pos, 1.0)
    pairs = jnp.concatenate([keys, pairs[:, :, HEAD_DIM:]], axis=2).astype(BF16)
    pairs = pairs.reshape(seqs, part, 2 * kv_heads * HEAD_DIM)
    pairs = lax.all_gather(pairs, "head", axis=1, tiled=True)
    pairs = pairs.reshape(seqs * span, 2 * kv_heads * HEAD_DIM)
    attended, lse = attend(limits, queries, pairs)

    branch, low_output = project(attended, w_output, d_output, u_output)
    middle = flat + branch
    normed2, inverse2 = norm(middle, ffn_gain)
    gate, low_gate = project(normed2, w_gateup[0], d_gateup[0], u_gateup[0])
    upward, low_upward = project(normed2, w_gateup[1], d_gateup[1], u_gateup[1])
    sigma = jax.nn.sigmoid(gate)
    silu = gate * sigma
    activated = (silu * upward).astype(BF16)
    branch, low_ffdown = project(activated, w_down, d_ffdown, u_ffdown)
    output = (middle + branch).astype(BF16)

    grad_act, gd_ffdown, gu_ffdown = project_back(
        activated, low_ffdown, grad_flat, w_down, d_ffdown, u_ffdown
    )
    grad_gate = (grad_act * upward * (sigma * (1.0 + gate * (1.0 - sigma)))).astype(BF16)
    grad_upward = (grad_act * silu).astype(BF16)
    grad_in_gate, gd_gate, gu_gate = project_back(
        normed2, low_gate, grad_gate, w_gateup[0], d_gateup[0], u_gateup[0]
    )
    grad_in_up, gd_up, gu_up = project_back(
        normed2, low_upward, grad_upward, w_gateup[1], d_gateup[1], u_gateup[1]
    )
    grad_middle = grad_flat.astype(F32) + norm_back(
        middle, inverse2, ffn_gain, grad_in_gate + grad_in_up
    )
    grad_mixed, gd_output, gu_output = project_back(
        attended, low_output, grad_middle.astype(BF16), w_output, d_output, u_output
    )
    early = [gd_output, gu_output, gd_gate, gd_up, gu_gate, gu_up, gd_ffdown, gu_ffdown]
    sizes = [term.shape[1] for term in early]
    fill = -sum(sizes) % (2 * groups * TILE)
    early = jnp.concatenate(early + [jnp.zeros((rank, fill), F32)], axis=1)
    grad_qkv, output, early = attend_back(
        limits, queries, pairs, lse, grad_mixed.astype(BF16), turn, output, early
    )
    input_grad, late = first_back(
        grad_qkv, w_qkv, d_qkv, u_qkv, normed, low_qkv, grad_middle, flat, inverse1, attn_gain
    )
    adapters = jnp.arange(query_down.shape[0], dtype=jnp.int32)
    holder = jnp.argmax(adapter_index[None, :] == adapters[:, None], axis=1).astype(jnp.int32)
    found = placed(holder, early, late, sizes, width)
    return (
        output,
        input_grad,
        found[0].swapaxes(1, 2),
        found[1],
        found[2].swapaxes(2, 3),
        found[3],
        found[4].swapaxes(1, 2),
        found[5],
        found[6].swapaxes(2, 3),
        found[7],
        found[8].swapaxes(1, 2),
        found[9],
    )


def solution(mesh):
    in_specs = (
        P(None, ("blk", "head"), None),
        P(),
        P(),
        P("blk", "head"),
        P(None, "blk", "head"),
        P("blk", "head"),
        P(None, "blk", "head"),
        P("blk", "head"),
        P(),
        P(),
        P(),
        P(),
        P(),
        P(),
        P(),
        P(),
        P(),
        P(),
        P(),
        P(),
        P(),
        P(None, ("blk", "head"), None),
    )
    out_specs = (
        P(None, ("blk", "head"), None),
        P(None, ("blk", "head"), None),
        P(),
        P(),
        P(),
        P(),
        P(),
        P(),
        P(),
        P(),
        P(),
        P(),
    )

    def chosen(tokens, *rest):
        if mesh.shape["blk"] == tokens.shape[0] == 8 and mesh.shape["head"] == 4:
            return by_sequence(tokens, *rest)
        return on_device(tokens, *rest)

    return jax.shard_map(
        chosen, mesh=mesh, in_specs=in_specs, out_specs=out_specs, check_vma=False
    )
```

```python
import functools
import math

import jax
import jax.numpy as jnp
import numpy as np
from jax import lax
from jax.experimental import pallas as pl
from jax.experimental.pallas import tpu as pltpu
from jax.sharding import PartitionSpec as P

HEADS = 20
KV_HEADS = 5
HEAD_DIM = 64
WINDOW = 1024


EPSILON = 1e-05
ROPE_BASE = 10000.0
ADAPTER_SCALE = 2.0
MASKED = -1e30


def passed_along(value, axis, steps):
    count = lax.axis_size(axis)
    initial, last = (max(0, -steps), min(count, count - steps))
    return lax.ppermute(value, axis, [(source, source + steps) for source in range(initial, last)])


def rms_scale(values, gain):
    return values * lax.rsqrt(jnp.mean(values * values, axis=-1, keepdims=True) + EPSILON) * gain


def rotate(values, positions, sign):
    half = values.shape[-1] // 2
    freqs = ROPE_BASE ** (-(jnp.arange(half, dtype=jnp.float32) * 2.0) / values.shape[-1])
    angles = positions.astype(jnp.float32)[:, None] * freqs[None, :]
    cosine = jnp.cos(angles)[:, None, :]
    sine = sign * jnp.sin(angles)[:, None, :]
    first = values[..., :half]
    second = values[..., half:]
    return jnp.concatenate(
        [first * cosine - second * sine, second * cosine + first * sine], axis=-1
    )


def gated(gate, upward):
    return jax.nn.silu(gate) * upward


def project(inputs, weight, down, up):
    lowered = jnp.einsum("sci,sir->scr", inputs, down, preferred_element_type=jnp.float32).astype(
        jnp.bfloat16
    )
    extra = ADAPTER_SCALE * jnp.einsum(
        "scr,sro->sco", lowered, up, preferred_element_type=jnp.float32
    )
    return (
        jnp.einsum("sci,io->sco", inputs, weight, preferred_element_type=jnp.float32) + extra,
        lowered,
    )


def project_back(inputs, lowered, grad_out, weight, down, up):
    grad_up = ADAPTER_SCALE * jnp.einsum(
        "scr,sco->sro", lowered, grad_out, preferred_element_type=jnp.float32
    )
    grad_low = (
        ADAPTER_SCALE * jnp.einsum("sco,sro->scr", grad_out, up, preferred_element_type=jnp.float32)
    ).astype(jnp.bfloat16)
    grad_down = jnp.einsum("sci,scr->sir", inputs, grad_low, preferred_element_type=jnp.float32)
    grad_in = jnp.einsum("sco,io->sci", grad_out, weight, preferred_element_type=jnp.float32)
    grad_in = grad_in + jnp.einsum(
        "scr,sir->sci", grad_low, down, preferred_element_type=jnp.float32
    )
    return (grad_in, grad_down, grad_up)


def on_device(
    tokens,
    attn_gain,
    ffn_gain,
    query_weight,
    keyval_weight,
    output_weight,
    gateup_weight,
    down_weight,
    query_down,
    query_up,
    keyval_down,
    keyval_up,
    output_down,
    output_up,
    gateup_down,
    gateup_up,
    ffdown_down,
    ffdown_up,
    segment_ids,
    real_mask,
    adapter_index,
    out_grad,
):
    seqs, per_device, width = tokens.shape
    groups = lax.axis_size("head")
    head_pos = lax.axis_index("head")
    blk_pos = lax.axis_index("blk")
    span = groups * per_device
    heads = HEADS
    head_dim = HEAD_DIM
    kv_heads = KV_HEADS
    local_heads = heads // groups
    share = heads // kv_heads
    reach = (WINDOW - 2) // span + 1
    scale = 1.0 / math.sqrt(head_dim)
    rows_a, rows_b, rows_c, rows_d, rows_e = (
        lax.all_gather(query_weight, "blk", axis=0, tiled=True),
        lax.all_gather(keyval_weight, "blk", axis=1, tiled=True),
        lax.all_gather(output_weight, "blk", axis=0, tiled=True),
        lax.all_gather(gateup_weight, "blk", axis=1, tiled=True),
        lax.all_gather(down_weight, "blk", axis=0, tiled=True),
    )
    w_query, w_keyval, w_output, w_gateup, w_down = (
        lax.all_gather(rows_a, "head", axis=1, tiled=True),
        lax.all_gather(rows_b, "head", axis=2, tiled=True),
        lax.all_gather(rows_c, "head", axis=1, tiled=True),
        lax.all_gather(rows_d, "head", axis=2, tiled=True),
        lax.all_gather(rows_e, "head", axis=1, tiled=True),
    )
    down_query = query_down[adapter_index]
    up_query = query_up[adapter_index]
    down_keyval = keyval_down[adapter_index]
    up_keyval = keyval_up[adapter_index]
    down_output = output_down[adapter_index]
    up_output = output_up[adapter_index]
    down_gateup = gateup_down[adapter_index]
    up_gateup = gateup_up[adapter_index]
    down_ffdown = ffdown_down[adapter_index]
    up_ffdown = ffdown_up[adapter_index]

    def first_norm(values):
        return rms_scale(values, attn_gain)

    def second_norm(values):
        return rms_scale(values, ffn_gain)

    flat = tokens.astype(jnp.float32)
    normed_full, first_norm_back = jax.vjp(first_norm, flat)
    normed = normed_full.astype(jnp.bfloat16)
    queries_pre, low_query = project(normed, w_query, down_query, up_query)
    keys_pre, low_key = project(normed, w_keyval[0], down_keyval[:, 0], up_keyval[:, 0])
    values_pre, low_value = project(normed, w_keyval[1], down_keyval[:, 1], up_keyval[:, 1])
    token_pos = (blk_pos * groups + head_pos) * per_device + jnp.arange(per_device, dtype=jnp.int32)
    queries = rotate(queries_pre.reshape(seqs, per_device, heads, head_dim), token_pos, 1.0).astype(
        jnp.bfloat16
    )
    keys = rotate(keys_pre.reshape(seqs, per_device, kv_heads, head_dim), token_pos, 1.0).astype(
        jnp.bfloat16
    )
    values = values_pre.reshape(seqs, per_device, kv_heads, head_dim).astype(jnp.bfloat16)
    owner = np.array(
        [
            [(group * local_heads + slot) // share for slot in range(local_heads)]
            for group in range(groups)
        ]
    )
    slot_of = jnp.arange(local_heads, dtype=jnp.int32)
    sender = jnp.asarray(
        (owner[:, :, None] == np.arange(kv_heads)[None, None, :]).astype(np.float32), jnp.bfloat16
    )
    spread = (slot_of[:, None] == jnp.arange(local_heads, dtype=jnp.int32)[None, :]).astype(
        jnp.bfloat16
    )
    pair = jnp.stack([keys, values], axis=3)
    outgoing = jnp.einsum(
        "sckxd,gmk->scgmxd", pair, sender, preferred_element_type=jnp.float32
    ).astype(jnp.bfloat16)
    outgoing = outgoing.reshape(seqs, per_device, groups, local_heads * 2 * head_dim)
    query_send = queries.reshape(seqs, per_device, groups, local_heads * head_dim)
    query_here, pair_here = (
        lax.all_to_all(query_send, "head", split_axis=2, concat_axis=1, tiled=True),
        lax.all_to_all(outgoing, "head", split_axis=2, concat_axis=1, tiled=True),
    )
    query_here = query_here.reshape(seqs, span, local_heads, head_dim)
    pair_here = pair_here.reshape(seqs, span, local_heads, 2, head_dim)
    received = [pair_here]
    moving = pair_here
    for hop in range(reach):
        moving = passed_along(moving, "blk", 1)
        received.append(moving)
    window_pairs = jnp.stack(received, axis=1)
    query_pos = blk_pos * span + jnp.arange(span, dtype=jnp.int32)
    key_pos = (blk_pos - jnp.arange(reach + 1, dtype=jnp.int32))[:, None] * span + jnp.arange(
        span, dtype=jnp.int32
    )[None, :]
    safe_pos = jnp.clip(key_pos, 0, segment_ids.shape[1] - 1)
    query_segment = lax.dynamic_slice_in_dim(segment_ids, blk_pos * span, span, 1)
    key_segment = segment_ids[:, safe_pos]
    key_real = real_mask[:, safe_pos]
    distance = query_pos[:, None, None] - key_pos[None]
    allowed = (key_pos[None] >= 0) & (distance >= 0) & (distance < WINDOW)
    allowed = allowed & (query_segment[:, :, None, None] == key_segment[:, None])
    allowed = allowed & ((key_real[:, None] == 1) | (distance[None] == 0))
    batch = 1
    target = max(1, 512 // span)
    for option in range(1, seqs + 1):
        if seqs % option == 0 and option <= target:
            batch = option
    count = seqs // batch

    def grouped(array):
        return array.reshape((count, batch) + array.shape[1:])

    def scores_of(query_part, pair_part, allowed_part):
        keys_wide = jnp.einsum(
            "gjlmd,hm->gjlhd", pair_part[:, :, :, :, 0], spread, preferred_element_type=jnp.float32
        ).astype(jnp.bfloat16)
        values_wide = jnp.einsum(
            "gjlmd,hm->gjlhd", pair_part[:, :, :, :, 1], spread, preferred_element_type=jnp.float32
        ).astype(jnp.bfloat16)
        raw = (
            jnp.einsum(
                "gqhd,gjlhd->ghqjl", query_part, keys_wide, preferred_element_type=jnp.float32
            )
            * scale
        )
        raw = jnp.where(allowed_part[:, None], raw, MASKED)
        return (raw, keys_wide, values_wide)

    def attend(pieces):
        query_part, pair_part, allowed_part = pieces
        raw, keys_wide, values_wide = scores_of(query_part, pair_part, allowed_part)
        top = jnp.max(raw, axis=(3, 4), keepdims=True)
        shifted = jnp.exp(raw - top)
        total = jnp.sum(shifted, axis=(3, 4), keepdims=True)
        probs_low = (shifted / total).astype(jnp.bfloat16)
        result = jnp.einsum(
            "ghqjl,gjlhd->gqhd", probs_low, values_wide, preferred_element_type=jnp.float32
        )
        return (result.astype(jnp.bfloat16), top + jnp.log(total))

    attended, logsum = lax.map(
        attend, (grouped(query_here), grouped(window_pairs), grouped(allowed))
    )
    mixed = lax.all_to_all(
        attended.reshape(seqs, span, local_heads * head_dim),
        "head",
        split_axis=1,
        concat_axis=2,
        tiled=True,
    )
    branch_attn, low_output = project(mixed, w_output, down_output, up_output)
    middle = flat + branch_attn
    normed2_full, second_norm_back = jax.vjp(second_norm, middle)
    normed2 = normed2_full.astype(jnp.bfloat16)
    gate, low_gate = project(normed2, w_gateup[0], down_gateup[:, 0], up_gateup[:, 0])
    upward, low_upward = project(normed2, w_gateup[1], down_gateup[:, 1], up_gateup[:, 1])
    activated_full, gated_back = jax.vjp(gated, gate, upward)
    activated = activated_full.astype(jnp.bfloat16)
    branch_ffn, low_ffdown = project(activated, w_down, down_ffdown, up_ffdown)
    output = (middle + branch_ffn).astype(jnp.bfloat16)
    grad_activated, gd_ffdown, gu_ffdown = project_back(
        activated, low_ffdown, out_grad, w_down, down_ffdown, up_ffdown
    )
    grad_gate, grad_upward = gated_back(grad_activated)
    grad_in_gate, gd_gate, gu_gate = project_back(
        normed2,
        low_gate,
        grad_gate.astype(jnp.bfloat16),
        w_gateup[0],
        down_gateup[:, 0],
        up_gateup[:, 0],
    )
    grad_in_up, gd_up, gu_up = project_back(
        normed2,
        low_upward,
        grad_upward.astype(jnp.bfloat16),
        w_gateup[1],
        down_gateup[:, 1],
        up_gateup[:, 1],
    )
    grad_middle = out_grad.astype(jnp.float32) + second_norm_back(grad_in_gate + grad_in_up)[0]
    grad_mixed, gd_output, gu_output = project_back(
        mixed, low_output, grad_middle.astype(jnp.bfloat16), w_output, down_output, up_output
    )
    grad_send = grad_mixed.astype(jnp.bfloat16).reshape(
        seqs, per_device, groups, local_heads * head_dim
    )
    grad_here = lax.all_to_all(grad_send, "head", split_axis=2, concat_axis=1, tiled=True).reshape(
        seqs, span, local_heads, head_dim
    )
    spread_full = spread.astype(jnp.float32)

    def attend_back(pieces):
        query_part, pair_part, allowed_part, logsum_part, grad_part = pieces
        raw, keys_wide, values_wide = scores_of(query_part, pair_part, allowed_part)
        probs = jnp.exp(raw - logsum_part)
        probs_low = probs.astype(jnp.bfloat16)
        grad_probs = jnp.einsum(
            "gqhd,gjlhd->ghqjl", grad_part, values_wide, preferred_element_type=jnp.float32
        )
        inner = jnp.sum(probs * grad_probs, axis=(3, 4), keepdims=True)
        grad_raw = (probs * (grad_probs - inner)).astype(jnp.bfloat16)
        grad_query = scale * jnp.einsum(
            "ghqjl,gjlhd->gqhd", grad_raw, keys_wide, preferred_element_type=jnp.float32
        )
        grad_keys = scale * jnp.einsum(
            "ghqjl,gqhd->gjlhd", grad_raw, query_part, preferred_element_type=jnp.float32
        )
        grad_values = jnp.einsum(
            "ghqjl,gqhd->gjlhd", probs_low, grad_part, preferred_element_type=jnp.float32
        )
        both = jnp.stack([grad_keys, grad_values], axis=4)
        folded = jnp.einsum("gjlhxd,hm->gjlmxd", both, spread_full, precision=lax.Precision.HIGHEST)
        return (grad_query, folded)

    grad_query, grad_pairs = lax.map(
        attend_back,
        (grouped(query_here), grouped(window_pairs), grouped(allowed), logsum, grouped(grad_here)),
    )
    grad_pairs = grad_pairs.reshape(seqs, reach + 1, span, local_heads, 2, head_dim)
    carried = grad_pairs[:, reach]
    for hop in range(reach - 1, -1, -1):
        carried = (
            passed_along(carried.astype(jnp.bfloat16), "blk", -1).astype(carried.dtype)
            + grad_pairs[:, hop]
        )
    grad_query = rotate(grad_query.reshape(seqs, span, local_heads, head_dim), query_pos, -1.0)
    grad_query = grad_query.astype(jnp.bfloat16).reshape(seqs, span, local_heads * head_dim)
    grad_queries_pre = lax.all_to_all(grad_query, "head", split_axis=1, concat_axis=2, tiled=True)
    grad_pair_tok = lax.all_to_all(
        carried.reshape(seqs, span, local_heads * 2 * head_dim).astype(jnp.bfloat16),
        "head",
        split_axis=1,
        concat_axis=2,
        tiled=True,
    ).astype(jnp.float32)
    grad_pair_tok = grad_pair_tok.reshape(seqs, per_device, groups, local_heads, 2, head_dim)
    grad_pair_heads = jnp.einsum(
        "scgmxd,gmk->sckxd",
        grad_pair_tok,
        sender.astype(jnp.float32),
        precision=lax.Precision.HIGHEST,
    )
    grad_keys_pre = (
        rotate(grad_pair_heads[:, :, :, 0], token_pos, -1.0)
        .astype(jnp.bfloat16)
        .reshape(seqs, per_device, kv_heads * head_dim)
    )
    grad_values_pre = (
        grad_pair_heads[:, :, :, 1]
        .astype(jnp.bfloat16)
        .reshape(seqs, per_device, kv_heads * head_dim)
    )
    grad_in_query, gd_query, gu_query = project_back(
        normed, low_query, grad_queries_pre, w_query, down_query, up_query
    )
    grad_in_key, gd_key, gu_key = project_back(
        normed, low_key, grad_keys_pre, w_keyval[0], down_keyval[:, 0], up_keyval[:, 0]
    )
    grad_in_value, gd_value, gu_value = project_back(
        normed, low_value, grad_values_pre, w_keyval[1], down_keyval[:, 1], up_keyval[:, 1]
    )
    grad_normed = grad_in_query + grad_in_key + grad_in_value
    input_grad = (grad_middle + first_norm_back(grad_normed)[0]).astype(jnp.bfloat16)
    chooser = (
        adapter_index[:, None] == jnp.arange(query_down.shape[0], dtype=jnp.int32)[None, :]
    ).astype(jnp.float32)

    def per_adapter(per_sequence):
        return jnp.einsum("sa,s...->a...", chooser, per_sequence, precision=lax.Precision.HIGHEST)

    sums = lax.psum(
        (
            per_adapter(gd_query),
            per_adapter(gu_query),
            per_adapter(jnp.stack([gd_key, gd_value], axis=1)),
            per_adapter(jnp.stack([gu_key, gu_value], axis=1)),
            per_adapter(gd_output),
            per_adapter(gu_output),
            per_adapter(jnp.stack([gd_gate, gd_up], axis=1)),
            per_adapter(jnp.stack([gu_gate, gu_up], axis=1)),
            per_adapter(gd_ffdown),
            per_adapter(gu_ffdown),
        ),
        ("blk", "head"),
    )
    return (
        output,
        input_grad,
        sums[0],
        sums[1],
        sums[2],
        sums[3],
        sums[4],
        sums[5],
        sums[6],
        sums[7],
        sums[8],
        sums[9],
    )


MESH = pl.DeviceIdType.MESH
F32 = jnp.float32
BF16 = jnp.bfloat16
TILE = 128
ANYWHERE = pl.BlockSpec(memory_space=pl.ANY)


def dot(left, right, left_dim=1, right_dim=0):
    return lax.dot_general(
        left, right, (((left_dim,), (right_dim,)), ((), ())), preferred_element_type=F32
    )


def place():
    blk, head = lax.axis_index("blk"), lax.axis_index("head")
    return blk // 2, blk % 2, head // 2, head % 2


def device(z, x, y, core):
    return (z * 2 + x, y * 2 + core)


def halves(count):
    first = (count // 2 + 15) // 16 * 16
    return ((0, first), (first, count - first))


class Spread:
    def __init__(self, sources, target, lines, sems):
        self.sources, self.target, self.lines = sources, target, lines
        self.z, self.x, self.y, self.core = place()
        self.z_in, self.x_in, self.y_in, self.d_in, self.c_in = sems[:5]
        self.z_out, self.x_out, self.y_out, self.d_out, self.c_out = sems[5:10]

    @staticmethod
    def semaphores(parts, lines):
        dma = pltpu.SemaphoreType.DMA
        return [
            dma((parts, lines)),
            dma((parts, lines)),
            dma((parts, lines)),
            dma((parts, lines, 2)),
            dma((parts, lines, 4)),
            dma((parts, 2, lines)),
            dma((parts, lines)),
            dma((parts, lines)),
            dma((parts, lines, 2)),
            dma((parts, lines, 4)),
        ]

    def inside(self, z):
        return (z >= 0) & (z < self.lines)

    def neighbours(self):
        z, x, y, core = self.z, self.x, self.y, self.core
        return (device(z, 1 - x, y, core), device(z, x, 1 - y, core), device(z, x, y, 1 - core))

    def copy(self, source, target, out, into, other):
        return pltpu.make_async_remote_copy(
            src_ref=source,
            dst_ref=target,
            send_sem=out,
            recv_sem=into,
            device_id=other,
            device_id_type=MESH,
        )

    def along_z(self, part, source, z, side):
        return self.copy(
            source,
            self.target(part, z, self.x, self.y, self.core),
            self.z_out.at[part, (side + 1) // 2, z],
            self.z_in.at[part, z],
            device(self.z + side, self.x, self.y, self.core),
        )

    def along_x(self, part, source, z):
        return self.copy(
            source,
            self.target(part, z, self.x, self.y, self.core),
            self.x_out.at[part, z],
            self.x_in.at[part, z],
            device(self.z, 1 - self.x, self.y, self.core),
        )

    def along_y(self, part, source, z):
        return self.copy(
            source,
            self.target(part, z, self.x, self.y, self.core),
            self.y_out.at[part, z],
            self.y_in.at[part, z],
            device(self.z, self.x, 1 - self.y, self.core),
        )

    def across(self, part, source, z, flip_x, flip_y):
        x, y = (self.x + flip_x) % 2, (self.y + flip_y) % 2
        return self.copy(
            source,
            self.target(part, z, x, y, self.core),
            self.c_out.at[part, z, flip_x * 2 + flip_y],
            self.c_in.at[part, z, flip_x * 2 + flip_y],
            device(self.z, self.x, self.y, 1 - self.core),
        )

    def piece(self, ref, which):
        if ref.shape[0] < 32:
            size = ref.shape[1] // 2
            return ref.at[:, pl.ds(which * size, size)]
        begin, size = halves(ref.shape[0])[which]
        return ref.at[pl.ds(begin, size)]

    def diagonal(self, part, z, which):
        if which == 0:
            ref = self.target(part, z, self.x, 1 - self.y, self.core)
            other = device(self.z, 1 - self.x, self.y, self.core)
        else:
            ref = self.target(part, z, 1 - self.x, self.y, self.core)
            other = device(self.z, self.x, 1 - self.y, self.core)
        ref = self.piece(ref, which)
        return self.copy(
            ref, ref, self.d_out.at[part, z, which], self.d_in.at[part, z, which], other
        )

    def arrived(self, ref, out, into):
        self.copy(ref, ref, out, into, device(self.z, self.x, self.y, 1 - self.core)).wait_recv()

    def hand_on(self, part, source, z):
        self.along_x(part, source, z).start()
        self.along_y(part, source, z).start()
        self.across(part, source, z, 0, 0).start()

    def begin(self, part):
        for side in (1, -1):

            @pl.when(self.inside(self.z + side))
            def _():
                self.along_z(part, self.sources[part], self.z, side).start()

        self.hand_on(part, self.sources[part], self.z)

    def line_step(self, part, distance, side):
        z = self.z - side * distance

        @pl.when(self.inside(z))
        def _():
            ref = self.target(part, z, self.x, self.y, self.core)
            self.arrived(ref, self.z_out.at[part, 0, z], self.z_in.at[part, z])

            @pl.when(self.inside(self.z + side))
            def _():
                self.along_z(part, ref, z, side).start()

            self.hand_on(part, ref, z)

    def plane_step(self, part, z):
        ref = self.target(part, z, self.x, 1 - self.y, self.core)
        self.arrived(ref, self.y_out.at[part, z], self.y_in.at[part, z])
        self.diagonal(part, z, 0).start()
        self.across(part, ref, z, 0, 1).start()
        ref = self.target(part, z, 1 - self.x, self.y, self.core)
        self.arrived(ref, self.x_out.at[part, z], self.x_in.at[part, z])
        self.diagonal(part, z, 1).start()
        self.across(part, ref, z, 1, 0).start()

    def corner_step(self, part, z):
        ref = self.target(part, z, 1 - self.x, 1 - self.y, self.core)
        for which in (0, 1):
            self.arrived(
                self.piece(ref, which), self.d_out.at[part, z, which], self.d_in.at[part, z, which]
            )
        self.across(part, ref, z, 1, 1).start()

    def end(self, part, z):
        for flip_x in (0, 1):
            for flip_y in (0, 1):
                x, y = (self.x + flip_x) % 2, (self.y + flip_y) % 2
                which = flip_x * 2 + flip_y
                self.arrived(
                    self.target(part, z, x, y, 1 - self.core),
                    self.c_out.at[part, z, which],
                    self.c_in.at[part, z, which],
                )
                self.across(
                    part, self.target(part, z, x, y, self.core), z, flip_x, flip_y
                ).wait_send()
        mine = self.target(part, z, self.x, self.y, self.core)
        self.along_x(part, mine, z).wait_send()
        self.along_y(part, mine, z).wait_send()
        self.diagonal(part, z, 0).wait_send()
        self.diagonal(part, z, 1).wait_send()
        for side in (1, -1):

            @pl.when(self.inside(self.z + side) & ((self.z - z) * side >= 0))
            def _():
                self.along_z(part, mine, z, side).wait_send()

    def all_steps(self, parts):
        for part in parts:
            for distance in range(1, self.lines):
                for side in (1, -1):
                    self.line_step(part, distance, side)
        for part in parts:
            for z in range(self.lines):
                self.plane_step(part, z)
        for part in parts:
            for z in range(self.lines):
                self.corner_step(part, z)
        for part in parts:
            for z in range(self.lines):
                self.end(part, z)


def paired(own, other, core):
    own, other = own.astype(F32), other.astype(F32)
    return [jnp.where(core == 0, own, other), jnp.where(core == 0, other, own)]


def in_pairs(array):
    half = array.shape[1] // 2
    size = 2 * KV_HEADS * HEAD_DIM // 4
    keys = jnp.concatenate([array[:, :size], array[:, half : half + size]], axis=1)
    values = jnp.concatenate(
        [array[:, size : 2 * size], array[:, half + size : half + 2 * size]], axis=1
    )
    pieces = []
    for head in range(KV_HEADS):
        cut = slice(head * HEAD_DIM, (head + 1) * HEAD_DIM)
        pieces += [keys[:, cut], values[:, cut]]
    return jnp.concatenate(pieces, axis=1)


def windows(blocks, span, low_part):
    reach = WINDOW + TILE
    fixed = [(0, (block + 1) * span) for block in range(WINDOW // span)]
    offset = TILE * (low_part // 2 + 1) - reach
    return fixed, reach, offset


def tiles_of(ref, flipped):
    lane = lax.broadcasted_iota(jnp.int32, (ref.shape[0], TILE), 1)
    result = []
    for slot in range(4):
        tile = ref[:, slot // 2 * TILE : (slot // 2 + 1) * TILE].astype(F32)
        if (slot % 2 == 0) == flipped:
            tile = pltpu.roll(tile, HEAD_DIM, 1)
        keep = lane >= HEAD_DIM if flipped else lane < HEAD_DIM
        result.append(jnp.where(keep, tile, 0.0).astype(BF16))
    return result


def joined(rows, flipped):
    span = rows.shape[0] // 4
    heads = [rows[slot * span : (slot + 1) * span] for slot in range(4)]
    lane = lax.broadcasted_iota(jnp.int32, (span, TILE), 1)
    result = []
    for first, second in ((heads[0], heads[1]), (heads[2], heads[3])):
        if flipped:
            first = pltpu.roll(first, HEAD_DIM, 1)
        else:
            second = pltpu.roll(second, HEAD_DIM, 1)
        result.append(jnp.where(lane < HEAD_DIM, first, second))
    return result


def bias_of(limits_ref, block, start, count):
    key = start + lax.broadcasted_iota(jnp.int32, (count, TILE), 0)
    least = limits_ref[0, pl.ds(block, 1), :]
    most = limits_ref[1, pl.ds(block, 1), :]
    self_pos = limits_ref[2, pl.ds(block, 1), :]
    allowed = ((key >= least) & (key <= most)) | (key == self_pos)
    bias = jnp.where(allowed, 0.0, MASKED)
    return jnp.concatenate([bias, bias], axis=1)


def each_block(blocks, body, between=lambda: None):
    span = 4 * HEAD_DIM
    fixed, reach, offset = windows(blocks, span, lax.axis_index("head"))
    for block, (start, count) in enumerate(fixed):
        body(block, start, count)
    between()

    @pl.loop(len(fixed), blocks)
    def _(block):
        body(block, pl.multiple_of(block * span + offset, TILE), reach)


def meet(others):
    barrier = pltpu.get_barrier_semaphore()
    for other in others:
        pl.semaphore_signal(barrier, inc=1, device_id=other, device_id_type=MESH)
    pl.semaphore_wait(barrier, len(others))


def remote(source, target, out, into, other):
    return pltpu.make_async_remote_copy(
        src_ref=source,
        dst_ref=target,
        send_sem=out,
        recv_sem=into,
        device_id=other,
        device_id_type=MESH,
    )


def along(count):
    blk, head = lax.axis_index("blk"), lax.axis_index("head")
    return [((blk + ahead) % count, head) for ahead in range(1, count)]


def beside():
    z, x, y, core = place()
    return [
        device(z, x, y, 1 - core),
        device(z, x, 1 - y, core),
        device(z, x, 1 - y, 1 - core),
    ]


class Exchange:
    def __init__(self, source, target, size, out, into, local):
        count = target.shape[0]
        blk, head = lax.axis_index("blk"), lax.axis_index("head")
        self.own = pltpu.make_async_copy(source.at[pl.ds(blk * size, size)], target.at[blk], local)
        self.copies, self.arrivals = [], []
        for at, (other, _) in enumerate(along(count)):
            self.copies.append(
                remote(
                    source.at[pl.ds(other * size, size)],
                    target.at[blk],
                    out.at[at],
                    into.at[at],
                    (other, head),
                )
            )
            giver = (blk + count - 1 - at) % count
            self.arrivals.append(
                remote(target.at[giver], target.at[giver], out.at[at], into.at[at], (other, head))
            )

    def start(self):
        self.own.start()
        for copy in self.copies:
            copy.start()

    def wait(self):
        for copy in self.arrivals:
            copy.wait_recv()
        for copy in self.copies:
            copy.wait_send()
        self.own.wait()


class Quarters:
    def __init__(self, terms, low, got, out, into):
        z, x, y, core = place()
        self.size = low.shape[1] // 4
        self.terms, self.low, self.got = terms, low, got
        self.mine = pl.ds((y * 2 + core) * self.size, self.size)
        self.copies = []
        for at, (flip_y, flip_core) in enumerate(((0, 1), (1, 0), (1, 1))):
            other_y, other_core = (y + flip_y) % 2, (core + flip_core) % 2
            theirs = pl.ds((other_y * 2 + other_core) * self.size, self.size)
            self.copies.append(
                remote(
                    low.at[:, theirs],
                    got.at[at],
                    out.at[at],
                    into.at[at],
                    device(z, x, other_y, other_core),
                )
            )

    def start(self):
        self.low[...] = self.terms[...].astype(BF16)
        for copy in self.copies:
            copy.start()

    def total(self):
        for copy in self.copies:
            copy.wait_recv()
        total = self.terms[:, self.mine]
        for at in range(3):
            total = total + self.got[at].astype(F32)
        return total.astype(BF16)

    def end(self):
        for copy in self.copies:
            copy.wait_send()


def turned(tile, cosine, sine, only_low=False):
    lane = lax.broadcasted_iota(jnp.int32, tile.shape, 1)
    half = HEAD_DIM // 2
    partner = jnp.where(
        lane % HEAD_DIM < half, pltpu.roll(tile, TILE - half, 1), pltpu.roll(tile, half, 1)
    )
    result = tile * cosine + partner * sine
    return jnp.where(lane < HEAD_DIM, result, tile) if only_low else result


def attend_back_kernel(
    lines,
    limits_ref,
    q_ref,
    kv_ref,
    lse_ref,
    grad_ref,
    turn_ref,
    output_ref,
    terms_ref,
    dqkv_ref,
    moved_ref,
    shared_ref,
    q_rows,
    g_rows,
    kv_turned,
    total,
    pair_low,
    pair_got,
    kept,
    y_low,
    y_got,
    low,
    got,
    shard,
    pair_out,
    pair_in,
    y_out,
    y_in,
    move_out,
    move_in,
    four_out,
    four_in,
    local,
    *sems,
):
    blocks, span = q_rows.shape[0], q_rows.shape[2]
    width = q_ref.shape[1]
    groups = width // (2 * TILE)
    scale = HEAD_DIM**-0.5
    z, x, y, core = place()
    size = shard.shape[1]

    def target(part, z, x, y, core):
        return shared_ref.at[z * 2 + x, :, pl.ds((y * 2 + core) * size, size)]

    spread = Spread([shard], target, lines, sems)
    meet(along(blocks) + beside())
    exchange = Exchange(output_ref, moved_ref, span, move_out, move_in, local.at[0])
    quarters = Quarters(terms_ref, low, got, four_out, four_in)
    quarters.start()
    own = pltpu.make_async_copy(shard, target(0, z, x, y, core), local.at[1])

    def gather_start():
        shard[...] = quarters.total()
        own.start()
        spread.begin(0)

    def line(distance):
        def run():
            spread.line_step(0, distance, 1)
            spread.line_step(0, distance, -1)

        return run

    def planes(first):
        def run():
            spread.plane_step(0, first)
            spread.plane_step(0, first + 1)

        return run

    def corners(first):
        def run():
            spread.corner_step(0, first)
            spread.corner_step(0, first + 1)

        return run

    later = [None, gather_start, line(1), line(2), line(3), exchange.start]
    later += [planes(0), planes(2), corners(0), corners(2)]

    def pump():
        if later:
            step = later.pop(0)
            if step is not None:
                step()

    def pair_copy(m):
        return remote(
            pair_low.at[m, 1 - core],
            pair_got.at[m],
            pair_out.at[m],
            pair_in.at[m],
            device(z, x, y, 1 - core),
        )

    def y_copy(m):
        return remote(
            y_low.at[m], y_got.at[m], y_out.at[m], y_in.at[m], device(z, x, 1 - y, core)
        )

    def give(m):
        whole = total[...].reshape(blocks, 4, span, TILE)
        for at in range(4):
            pair_low[m, at % 2, at // 2] = whole[:, at].astype(BF16)
        spot = total.reshape(blocks, 4, span, TILE)
        for at in range(2):
            kept[m, at] = spot[:, at * 2 + core]
        pair_copy(m).start()

    def add_pair(m):
        pair_copy(m).wait_recv()
        y_low[m] = (kept[m, 1 - y] + pair_got[m, 1 - y].astype(F32)).astype(BF16)
        y_copy(m).start()

    def add_y(m):
        y_copy(m).wait_recv()
        tile = kept[m, y] + pair_got[m, y].astype(F32) + y_got[m].astype(F32)
        tile = turned(tile.reshape(blocks * span, TILE), turn_ref[0], -turn_ref[1], True)
        at = width + m * TILE
        dqkv_ref[:, at : at + TILE] = tile.astype(BF16)

    for m in range(groups):
        columns = slice(m * 2 * TILE, (m + 1) * 2 * TILE)
        tile = slice(m * TILE, (m + 1) * TILE)
        for slot, rows in enumerate(tiles_of(q_ref[:, columns], False)):
            q_rows[:, slot] = (rows * BF16(scale)).reshape(blocks, span, TILE)
        for slot, rows in enumerate(tiles_of(grad_ref[:, columns], True)):
            g_rows[:, slot] = rows.reshape(blocks, span, TILE)
        kv_turned[...] = kv_ref[:, tile].astype(F32).T.astype(BF16)
        total[...] = jnp.zeros_like(total)

        def body(block, start, count):
            keys = pl.ds(start, count)
            queries = q_rows[block].reshape(4 * span, TILE)
            grads = g_rows[block].reshape(4 * span, TILE)
            scores = dot(kv_ref[keys, tile], queries, 1, 1)
            scores = scores + bias_of(limits_ref, block, start, count)
            probs = jnp.exp(scores - lse_ref[m, pl.ds(block, 1), :])
            grad_probs = dot(kv_ref[keys, tile], grads, 1, 1)
            inner = jnp.sum(probs * grad_probs, axis=0, keepdims=True)
            grad_scores = (probs * (grad_probs - inner)).astype(BF16)
            total[keys, :] += dot(grad_scores, queries) + dot(probs.astype(BF16), grads)
            grad_q = (dot(kv_turned[:, keys], grad_scores) * scale).T
            rows = pl.ds(block * span, span)
            cosine, sine = turn_ref[0, rows, :], -turn_ref[1, rows, :]
            for at, part in enumerate(joined(grad_q, False)):
                at = m * 2 * TILE + at * TILE
                dqkv_ref[rows, at : at + TILE] = turned(part, cosine, sine).astype(BF16)

        each_block(blocks, body, pump)
        pump()
        give(m)
        if m >= 1:
            add_pair(m - 1)
        if m >= 2:
            add_y(m - 2)
    while later:
        pump()
    add_pair(groups - 1)
    add_y(groups - 2)
    for z_at in range(lines):
        spread.end(0, z_at)
    own.wait()
    exchange.wait()
    quarters.end()
    add_y(groups - 1)
    for m in range(groups):
        pair_copy(m).wait_send()
        y_copy(m).wait_send()


def attend_back(limits, queries, pairs, lse, grads, turn, output, terms):
    rows, width = queries.shape
    blocks = limits.shape[1]
    span = rows // blocks
    groups = width // (2 * TILE)
    rank, total = terms.shape
    seqs = lax.axis_size("blk")
    each = pltpu.VMEM((blocks, 4, span, TILE), BF16)
    dma = pltpu.SemaphoreType.DMA
    vmem = pl.BlockSpec(memory_space=pltpu.VMEM)
    shape = jax.ShapeDtypeStruct
    return pl.pallas_call(
        functools.partial(attend_back_kernel, seqs // 2),
        out_shape=[
            shape((rows, width + pairs.shape[1]), BF16),
            shape((seqs, span, width), BF16),
            shape((seqs, rank, total), BF16),
        ],
        in_specs=[vmem] * 8,
        out_specs=[vmem, ANYWHERE, ANYWHERE],
        scratch_shapes=[
            each,
            each,
            pltpu.VMEM((TILE, pairs.shape[0]), BF16),
            pltpu.VMEM((pairs.shape[0], TILE), F32),
            pltpu.VMEM((groups, 2, 2, blocks, span, TILE), BF16),
            pltpu.VMEM((groups, 2, blocks, span, TILE), BF16),
            pltpu.VMEM((groups, 2, blocks, span, TILE), F32),
            pltpu.VMEM((groups, blocks, span, TILE), BF16),
            pltpu.VMEM((groups, blocks, span, TILE), BF16),
            pltpu.VMEM((rank, total), BF16),
            pltpu.VMEM((3, rank, total // 4), BF16),
            pltpu.VMEM((rank, total // 4), BF16),
            dma((groups,)),
            dma((groups,)),
            dma((groups,)),
            dma((groups,)),
            dma((seqs - 1,)),
            dma((seqs - 1,)),
            dma((3,)),
            dma((3,)),
            dma((2,)),
            *Spread.semaphores(1, seqs // 2),
        ],
        compiler_params=pltpu.CompilerParams(
            collective_id=1, has_side_effects=True, vmem_limit_bytes=56 << 20
        ),
    )(limits, queries, pairs, lse, grads, turn, output, terms)


def first_back_kernel(
    lines,
    dqkv_ref,
    weight_ref,
    down_ref,
    up_ref,
    normed_ref,
    low_ref,
    middle_ref,
    flat_ref,
    inverse_ref,
    gain_ref,
    moved_ref,
    shared_ref,
    result,
    terms,
    low,
    got,
    shard,
    move_out,
    move_in,
    four_out,
    four_in,
    local,
    *sems,
):
    blocks, span = moved_ref.shape[:2]
    z, x, y, core = place()
    size = shard.shape[1]
    rank = down_ref.shape[0] // 3
    width = flat_ref.shape[1]

    def target(part, z, x, y, core):
        return shared_ref.at[z * 2 + x, :, pl.ds((y * 2 + core) * size, size)]

    spread = Spread([shard], target, lines, sems)
    meet(along(blocks) + beside())
    grad_low = (ADAPTER_SCALE * dot(dqkv_ref[...], up_ref[...], 1, 1)).astype(BF16)
    grad_up = ADAPTER_SCALE * dot(low_ref[...], dqkv_ref[...], 0, 0)
    grad_down = dot(grad_low, normed_ref[...], 0, 0)
    terms[:, :width] = grad_up[:rank, :width]
    at = width
    while at < dqkv_ref.shape[1]:
        lane = lax.broadcasted_iota(jnp.int32, (rank, TILE), 1)
        terms[:, at : at + TILE] = jnp.where(
            lane < HEAD_DIM,
            grad_up[rank : 2 * rank, at : at + TILE],
            grad_up[2 * rank :, at : at + TILE],
        )
        at += TILE
    for which in range(3):
        terms[:, at : at + width] = grad_down[which * rank : (which + 1) * rank]
        at += width
    if at < terms.shape[1]:
        terms[:, at:] = jnp.zeros((rank, terms.shape[1] - at), F32)
    quarters = Quarters(terms, low, got, four_out, four_in)
    quarters.start()
    own = pltpu.make_async_copy(shard, target(0, z, x, y, core), local.at[1])
    exchange = Exchange(result, moved_ref, span, move_out, move_in, local.at[0])
    grad = dot(dqkv_ref[...], weight_ref[...], 1, 1) + dot(grad_low, down_ref[...])
    shard[...] = quarters.total()
    own.start()
    spread.begin(0)
    weighted = grad * gain_ref[...]
    flat, inverse = flat_ref[...].astype(F32), inverse_ref[...]
    mean = jnp.mean(flat * weighted, axis=1, keepdims=True)
    grad = middle_ref[...] + inverse * weighted - flat * (inverse * inverse * inverse * mean)
    result[...] = grad.astype(BF16)
    spread.line_step(0, 1, 1)
    spread.line_step(0, 1, -1)
    spread.line_step(0, 2, 1)
    spread.line_step(0, 2, -1)
    spread.line_step(0, 3, 1)
    spread.line_step(0, 3, -1)
    exchange.start()
    for z_at in range(lines):
        spread.plane_step(0, z_at)
    for z_at in range(lines):
        spread.corner_step(0, z_at)
    for z_at in range(lines):
        spread.end(0, z_at)
    own.wait()
    quarters.end()
    exchange.wait()


def first_back(grad_qkv, weight, down, up, normed, low, middle, flat, inverse, gain):
    rows, width = flat.shape
    rank = down.shape[0] // 3
    seqs, heads = lax.axis_size("blk"), lax.axis_size("head")
    total = 3 * width + weight.shape[1]
    total += -total % (2 * heads * TILE)
    dma = pltpu.SemaphoreType.DMA
    vmem = pl.BlockSpec(memory_space=pltpu.VMEM)
    shape = jax.ShapeDtypeStruct
    return pl.pallas_call(
        functools.partial(first_back_kernel, seqs // 2),
        out_shape=[
            shape((seqs, rows // seqs, width), BF16),
            shape((seqs, rank, total), BF16),
        ],
        in_specs=[vmem] * 10,
        out_specs=[ANYWHERE, ANYWHERE],
        scratch_shapes=[
            pltpu.VMEM((rows, width), BF16),
            pltpu.VMEM((rank, total), F32),
            pltpu.VMEM((rank, total), BF16),
            pltpu.VMEM((3, rank, total // 4), BF16),
            pltpu.VMEM((rank, total // 4), BF16),
            dma((seqs - 1,)),
            dma((seqs - 1,)),
            dma((3,)),
            dma((3,)),
            dma((2,)),
            *Spread.semaphores(1, seqs // 2),
        ],
        compiler_params=pltpu.CompilerParams(
            collective_id=2, has_side_effects=True, vmem_limit_bytes=56 << 20
        ),
    )(grad_qkv, weight, down, up, normed, low, middle, flat, inverse, gain.reshape(1, -1))


def placed_kernel(sizes, width, holder_ref, early_ref, late_ref, *outs):
    q_down, q_up, kv_down, kv_up, o_down, o_up, gu_down, gu_up, ff_down, ff_up = outs
    cuts = np.cumsum([0] + sizes)
    early = [slice(int(begin), int(end)) for begin, end in zip(cuts[:-1], cuts[1:])]
    for out, cut in zip((o_down, o_up), early[:2]):
        out[0] = early_ref[0, :, cut].astype(F32)
    for which in range(2):
        gu_down[0, which] = early_ref[0, :, early[2 + which]].astype(F32)
        gu_up[0, which] = early_ref[0, :, early[4 + which]].astype(F32)
    for out, cut in zip((ff_down, ff_up), early[6:]):
        out[0] = early_ref[0, :, cut].astype(F32)
    q_up[0] = late_ref[0, :, :width].astype(F32)
    narrow = KV_HEADS * HEAD_DIM
    pairs = late_ref[0, :, width : width + 2 * narrow].astype(F32)
    for which in range(2):
        pieces = [
            pairs[:, (2 * head + which) * HEAD_DIM : (2 * head + which + 1) * HEAD_DIM]
            for head in range(KV_HEADS)
        ]
        kv_up[0, which] = jnp.concatenate(pieces, axis=1)
    at = width + 2 * narrow
    q_down[0] = late_ref[0, :, at : at + width].astype(F32)
    for which in range(2):
        at += width
        kv_down[0, which] = late_ref[0, :, at : at + width].astype(F32)


def placed(holder, early, late, sizes, width):
    adapters, rank = early.shape[:2]
    hidden = sizes[4]
    narrow = KV_HEADS * HEAD_DIM
    shapes = [
        (rank, width),
        (rank, width),
        (2, rank, width),
        (2, rank, narrow),
        (rank, width),
        (rank, width),
        (2, rank, width),
        (2, rank, hidden),
        (rank, hidden),
        (rank, width),
    ]

    def whole(shape):
        return pl.BlockSpec((1,) + shape, lambda a, held: (a,) + (0,) * len(shape))

    return pl.pallas_call(
        functools.partial(placed_kernel, sizes, width),
        grid_spec=pltpu.PrefetchScalarGridSpec(
            num_scalar_prefetch=1,
            grid=(adapters,),
            in_specs=[
                pl.BlockSpec((1, rank, early.shape[2]), lambda a, held: (held[a], 0, 0)),
                pl.BlockSpec((1, rank, late.shape[2]), lambda a, held: (held[a], 0, 0)),
            ],
            out_specs=[whole(shape) for shape in shapes],
        ),
        out_shape=[jax.ShapeDtypeStruct((adapters,) + shape, F32) for shape in shapes],
    )(holder, early, late)


def norm_of(values, gain):
    inverse = lax.rsqrt(jnp.mean(values * values, axis=-1, keepdims=True) + EPSILON)
    return (values * inverse * gain).astype(BF16), inverse


def norm_back(values, inverse, gain, grad):
    weighted = grad * gain
    mean = jnp.mean(values * weighted, axis=-1, keepdims=True)
    return inverse * weighted - values * (inverse * inverse * inverse * mean)


def lowered(inputs, down):
    return dot(inputs, down, 1, 1).astype(BF16)


def front_kernel(lines, *refs):
    (
        tokens,
        out_grad,
        query,
        keyval,
        output,
        gateup,
        down,
        limits_ref,
        turn_ref,
        d_qkv_ref,
        u_qkv_ref,
        gain_ref,
        w_qkv,
        w_output,
        w_gateup,
        w_down,
        flat_ref,
        grad_ref,
        normed_ref,
        inverse_ref,
        low_ref,
        q_ref,
        pairs_ref,
        out_ref,
        lse_ref,
    ) = refs[:25]
    got_query, got_keyval, got_output, got_down, my_query, my_keyval, my_output, my_down = refs[25:33]
    all_keyval, first_weights, q_rows, kv_turned = refs[33:37]
    pair_out, pair_in, local, move_out, move_in, share_out, share_in = refs[37:44]
    rows, deep = my_query.shape[0], my_down.shape[0]
    wide, mixed = my_output.shape[1], my_keyval.shape[1]
    span, hidden = gateup.shape[1:]
    width = w_output.shape[1]
    blocks, part_rows = flat_ref.shape[:2]
    groups = width // (2 * TILE)

    def target(part, z, x, y, core):
        blk, head = z * 2 + x, y * 2 + core
        if part == 0:
            return all_keyval.at[pl.ds(blk * 2 * rows + core * rows, rows), pl.ds(y * mixed, mixed)]
        if part == 1:
            return first_weights.at[
                pl.ds(blk * 2 * rows + core * rows, rows), pl.ds(y * wide, wide)
            ]
        if part == 2:
            return w_output.at[pl.ds(blk * 2 * rows + core * rows, rows), pl.ds(y * wide, wide)]
        if part == 5:
            return w_down.at[pl.ds(blk * 2 * deep + core * deep, deep), pl.ds(y * wide, wide)]
        return w_gateup.at[part - 3, pl.ds(blk * span, span), pl.ds(head * hidden, hidden)]

    sources = [my_keyval, my_query, my_output, gateup.at[0], gateup.at[1], my_down]
    spread = Spread(sources, target, lines, refs[44:])
    z, x, y, core = place()
    head = y * 2 + core
    meet(along(blocks) + beside())
    sibling = device(z, x, y, 1 - core)
    theirs = pl.ds((1 - core) * rows, rows)
    swaps = [
        remote(keyval.at[:, theirs], got_keyval, pair_out.at[0], pair_in.at[0], sibling),
        remote(query.at[theirs], got_query, pair_out.at[1], pair_in.at[1], sibling),
        remote(output.at[theirs], got_output, pair_out.at[2], pair_in.at[2], sibling),
        remote(
            down.at[pl.ds((1 - core) * deep, deep)], got_down, pair_out.at[3], pair_in.at[3], sibling
        ),
    ]
    for swap in swaps:
        swap.start()
    arrive = Exchange(tokens, flat_ref, part_rows, move_out.at[0], move_in.at[0], local.at[7])
    arrive.start()
    later_grad = Exchange(out_grad, grad_ref, part_rows, move_out.at[1], move_in.at[1], local.at[8])
    own = [
        pltpu.make_async_copy(sources[part], target(part, z, x, y, core), local.at[part])
        for part in range(6)
    ]

    def begin(part):
        spread.begin(part)
        own[part].start()

    mine = pl.ds(core * rows, rows)
    swaps[0].wait_recv()
    pieces = paired(keyval[0, mine, :], got_keyval[0], core)
    pieces += paired(keyval[1, mine, :], got_keyval[1], core)
    filled = sum(p.shape[1] for p in pieces)
    pieces.append(jnp.zeros((rows, mixed - filled), F32))
    my_keyval[...] = jnp.concatenate(pieces, axis=1).astype(BF16)
    begin(0)
    swaps[1].wait_recv()
    my_query[...] = jnp.concatenate(
        paired(query[mine, :], got_query[...], core), axis=1
    ).astype(BF16)
    begin(1)
    swaps[2].wait_recv()
    my_output[...] = jnp.concatenate(
        paired(output[mine, :], got_output[...], core), axis=1
    ).astype(BF16)
    swaps[3].wait_recv()
    my_down[...] = jnp.concatenate(
        paired(down[pl.ds(core * deep, deep), :], got_down[...], core), axis=1
    ).astype(BF16)

    def line(part, distance):
        spread.line_step(part, distance, 1)
        spread.line_step(part, distance, -1)

    for distance in range(1, lines):
        line(0, distance)
        line(1, distance)
    for part in (2, 3):
        begin(part)
    for part in (0, 1):
        for z_at in range(lines):
            spread.plane_step(part, z_at)
    for part in (4, 5):
        begin(part)
    line(2, 1)
    line(3, 1)
    for part in (0, 1):
        for z_at in range(lines):
            spread.corner_step(part, z_at)
    line(2, 2)
    line(3, 2)
    events = []
    for step in FRONT_ORDER:
        kind, part, at = step
        if kind == "grad":
            events.append(later_grad.start)
        else:
            run = {"line": line, "plane": spread.plane_step, "corner": spread.corner_step}[kind]
            events.append(functools.partial(run, part, at))

    def pump(count=1):
        for _ in range(min(count, len(events))):
            events.pop(0)()

    arrive.wait()
    flat = flat_ref[...].reshape(blocks * part_rows, width).astype(F32)
    normed, inverse = norm_of(flat, gain_ref[...])
    normed_ref[...] = normed
    inverse_ref[...] = inverse
    low_ref[...] = lowered(normed, d_qkv_ref[...])
    pump()
    for z_at in range(lines):
        spread.end(0, z_at)
    own[0].wait()
    first_weights[:, width:] = in_pairs(all_keyval[...].astype(F32)).astype(BF16)
    pump()

    def first(columns):
        return dot(normed_ref[...], first_weights[:, columns]) + ADAPTER_SCALE * dot(
            low_ref[...], u_qkv_ref[:, columns]
        )

    cosine, sine = turn_ref[0], turn_ref[1]
    here = pl.ds(head * part_rows, part_rows)
    for m in range(groups):
        at = width + m * TILE
        tile = turned(first(slice(at, at + TILE)), cosine, sine, True).astype(BF16)
        pairs_ref[:, here, m * TILE : (m + 1) * TILE] = tile.reshape(blocks, part_rows, TILE)
    shares = []
    for at, (flip_y, flip_core, other) in enumerate(
        (
            (0, 0, device(z, x, 1 - y, core)),
            (0, 0, sibling),
            (1, 0, sibling),
        )
    ):
        source_head = ((y + flip_y) % 2) * 2 + core
        ref = pairs_ref.at[:, pl.ds(source_head * part_rows, part_rows)]
        shares.append(remote(ref, ref, share_out.at[at], share_in.at[at], other))

    def share_arrived(at, from_y, from_core):
        ref = pairs_ref.at[:, pl.ds((from_y * 2 + from_core) * part_rows, part_rows)]
        remote(ref, ref, share_out.at[at], share_in.at[at], sibling).wait_recv()

    shares[0].start()
    shares[1].start()
    pump()
    for z_at in range(lines):
        spread.end(1, z_at)
    own[1].wait()
    weights_out = pltpu.make_async_copy(first_weights, w_qkv, local.at[6])
    weights_out.start()
    for m in range(groups):
        columns = slice(m * 2 * TILE, (m + 1) * 2 * TILE)
        both = first(columns)
        for at in range(2):
            tile = turned(both[:, at * TILE : (at + 1) * TILE], cosine, sine).astype(BF16)
            q_ref[:, (2 * m + at) * TILE : (2 * m + at + 1) * TILE] = tile
        pump()
    share_arrived(0, 1 - y, core)
    shares[2].start()
    share_arrived(1, y, 1 - core)
    pump()
    share_arrived(2, 1 - y, 1 - core)
    kv_ref = pairs_ref.reshape(blocks * pairs_ref.shape[1], pairs_ref.shape[2])

    for m in range(groups):
        columns = slice(m * 2 * TILE, (m + 1) * 2 * TILE)
        tile = slice(m * TILE, (m + 1) * TILE)
        for slot, part in enumerate(tiles_of(q_ref[:, columns], False)):
            q_rows[:, slot] = (part * BF16(HEAD_DIM**-0.5)).reshape(blocks, part_rows, TILE)
        kv_turned[...] = kv_ref[:, tile].astype(F32).T.astype(BF16)

        def body(block, start, count):
            queries = q_rows[block].reshape(4 * part_rows, TILE)
            scores = dot(kv_ref[pl.ds(start, count), tile], queries, 1, 1)
            scores = scores + bias_of(limits_ref, block, start, count)
            top = jnp.max(scores, axis=0, keepdims=True)
            shifted = jnp.exp(scores - top)
            total = jnp.sum(shifted, axis=0, keepdims=True)
            result = dot(kv_turned[:, pl.ds(start, count)], shifted.astype(BF16))
            lse_ref[m, pl.ds(block, 1), :] = top + jnp.log(total)
            result = (result / total).T
            for at, part in enumerate(joined(result, True)):
                at = m * 2 * TILE + at * TILE
                out_ref[pl.ds(block * part_rows, part_rows), at : at + TILE] = part.astype(BF16)

        each_block(blocks, body, pump)
        pump(2)
    pump(len(events))
    for part in range(2, 6):
        for z_at in range(lines):
            spread.end(part, z_at)
        own[part].wait()
    weights_out.wait()
    for copy in swaps + shares:
        copy.wait_send()
    later_grad.wait()


def front_order(lines):
    order = [("line", 4, 1), ("line", 5, 1), ("line", 2, 3), ("line", 3, 3)]
    order += [("line", 4, 2), ("line", 5, 2), ("line", 4, 3), ("line", 5, 3)]
    order += [("grad", 0, 0)]
    for part in range(2, 6):
        order += [("plane", part, z) for z in range(lines)]
        if part > 2:
            order += [("corner", part - 1, z) for z in range(lines)]
    return order + [("corner", 5, z) for z in range(lines)]


FRONT_ORDER = front_order(4)


def front(tokens, out_grad, weights, limits, turn, down, up, gain):
    query, keyval, output, gateup, w_down = weights
    seqs, part, width = tokens.shape
    rows, wide = query.shape
    deep = w_down.shape[0]
    blks, heads = lax.axis_size("blk"), lax.axis_size("head")
    narrow = keyval.shape[2]
    mixed = -(-4 * narrow // TILE) * TILE
    double = heads * narrow * 2
    groups = width // (2 * TILE)
    dma = pltpu.SemaphoreType.DMA
    vmem = pl.BlockSpec(memory_space=pltpu.VMEM)
    shape = jax.ShapeDtypeStruct
    return pl.pallas_call(
        functools.partial(front_kernel, blks // 2),
        out_shape=[
            shape((blks * rows, heads * wide + double), BF16),
            shape((blks * rows, heads * wide), BF16),
            shape((2, blks * rows, heads * gateup.shape[2]), BF16),
            shape((blks * deep, heads * wide), BF16),
            shape((seqs, part, width), BF16),
            shape((seqs, part, width), BF16),
            shape((seqs * part, width), BF16),
            shape((seqs * part, 1), F32),
            shape((seqs * part, down.shape[0]), BF16),
            shape((seqs * part, width), BF16),
            shape((seqs, heads * part, double), BF16),
            shape((seqs * part, width), BF16),
            shape((groups, seqs, 2 * TILE), F32),
        ],
        in_specs=[ANYWHERE, ANYWHERE, vmem, vmem, vmem, ANYWHERE] + [vmem] * 6,
        out_specs=[ANYWHERE] * 4 + [vmem, ANYWHERE] + [vmem] * 7,
        scratch_shapes=[
            pltpu.VMEM((rows // 2, wide), BF16),
            pltpu.VMEM((2, rows // 2, narrow), BF16),
            pltpu.VMEM((rows // 2, wide), BF16),
            pltpu.VMEM((deep // 2, wide), BF16),
            pltpu.VMEM((rows // 2, 2 * wide), BF16),
            pltpu.VMEM((rows // 2, mixed), BF16),
            pltpu.VMEM((rows // 2, 2 * wide), BF16),
            pltpu.VMEM((deep // 2, 2 * wide), BF16),
            pltpu.VMEM((blks * rows, heads // 2 * mixed), BF16),
            pltpu.VMEM((blks * rows, heads * wide + double), BF16),
            pltpu.VMEM((seqs, 4, part, TILE), BF16),
            pltpu.VMEM((TILE, seqs * heads * part), BF16),
            dma((4,)),
            dma((4,)),
            dma((9,)),
            dma((2, seqs - 1)),
            dma((2, seqs - 1)),
            dma((3,)),
            dma((3,)),
            *Spread.semaphores(6, blks // 2),
        ],
        compiler_params=pltpu.CompilerParams(
            collective_id=0, has_side_effects=True, vmem_limit_bytes=56 << 20
        ),
    )(
        tokens.reshape(seqs * part, width),
        out_grad.reshape(seqs * part, width),
        query,
        keyval,
        output,
        gateup,
        w_down,
        limits,
        turn,
        down,
        up,
        gain.reshape(1, -1),
    )


def feed_kernel(
    attended_ref,
    flat_ref,
    grad_ref,
    w_output_ref,
    w_gateup_ref,
    w_down_ref,
    d_output_ref,
    u_output_ref,
    d_gateup_ref,
    u_gateup_ref,
    d_ffdown_ref,
    u_ffdown_ref,
    gain_ref,
    output_ref,
    grad_middle_ref,
    grad_mixed_ref,
    terms_ref,
    middle,
    normed,
    result,
    grad_normed,
    low_output,
    low_gate,
    low_up,
    low_down,
    grad_low_down,
    grad_low_gate,
    grad_low_up,
):
    step = pl.program_id(0)
    rows, width = attended_ref.shape
    chunk = w_down_ref.shape[0]
    hidden = chunk * pl.num_programs(0)

    @pl.when(step == 0)
    def _():
        attended = attended_ref[...]
        low_output[...] = lowered(attended, d_output_ref[...])
        branch = dot(attended, w_output_ref[...])
        branch = branch + ADAPTER_SCALE * dot(low_output[...], u_output_ref[...])
        middle[...] = flat_ref[...].astype(F32) + branch
        normed[...] = norm_of(middle[...], gain_ref[...])[0]
        low_gate[...] = lowered(normed[...], d_gateup_ref[0])
        low_up[...] = lowered(normed[...], d_gateup_ref[1])
        grad_low_down[...] = (ADAPTER_SCALE * dot(grad_ref[...], u_ffdown_ref[...], 1, 1)).astype(
            BF16
        )
        for ref in (result, grad_normed, low_down, grad_low_gate, grad_low_up):
            ref[...] = jnp.zeros_like(ref)

    inputs = normed[...]
    w_gate, w_up = w_gateup_ref[0], w_gateup_ref[1]
    u_gate, u_up = u_gateup_ref[0], u_gateup_ref[1]
    gate = dot(inputs, w_gate) + ADAPTER_SCALE * dot(low_gate[...], u_gate)
    upward = dot(inputs, w_up) + ADAPTER_SCALE * dot(low_up[...], u_up)
    grad_act = dot(grad_ref[...], w_down_ref[...], 1, 1) + dot(grad_low_down[...], d_ffdown_ref[...])
    sigma = 1.0 / (1.0 + jnp.exp(-gate))
    silu = gate * sigma
    activated = (silu * upward).astype(BF16)
    grad_gate = (grad_act * upward * (sigma * (1.0 + gate * (1.0 - sigma)))).astype(BF16)
    grad_up = (grad_act * silu).astype(BF16)
    result[...] += dot(activated, w_down_ref[...])
    grad_normed[...] += dot(grad_gate, w_gate, 1, 1) + dot(grad_up, w_up, 1, 1)
    low_down[...] += dot(activated, d_ffdown_ref[...], 1, 1)
    grad_low_gate[...] += dot(grad_gate, u_gate, 1, 1)
    grad_low_up[...] += dot(grad_up, u_up, 1, 1)
    at = 4 * width + step * chunk
    spot = pl.ds(pl.multiple_of(at, TILE), chunk)
    terms_ref[:, spot] = ADAPTER_SCALE * dot(low_gate[...], grad_gate, 0, 0)
    spot = pl.ds(pl.multiple_of(at + hidden, TILE), chunk)
    terms_ref[:, spot] = ADAPTER_SCALE * dot(low_up[...], grad_up, 0, 0)
    spot = pl.ds(pl.multiple_of(at + 2 * hidden, TILE), chunk)
    terms_ref[:, spot] = dot(grad_low_down[...], activated, 0, 0)

    @pl.when(step == pl.num_programs(0) - 1)
    def _():
        low = low_down[...].astype(BF16)
        branch = result[...] + ADAPTER_SCALE * dot(low, u_ffdown_ref[...])
        output_ref[...] = (middle[...] + branch).astype(BF16)
        at = 4 * width + 3 * hidden
        terms_ref[:, at : at + width] = ADAPTER_SCALE * dot(low, grad_ref[...], 0, 0)
        if at + width < terms_ref.shape[1]:
            terms_ref[:, at + width :] = jnp.zeros(
                (terms_ref.shape[0], terms_ref.shape[1] - at - width), F32
            )
        low_g = (ADAPTER_SCALE * grad_low_gate[...]).astype(BF16)
        low_u = (ADAPTER_SCALE * grad_low_up[...]).astype(BF16)
        terms_ref[:, 2 * width : 3 * width] = dot(low_g, normed[...], 0, 0)
        terms_ref[:, 3 * width : 4 * width] = dot(low_u, normed[...], 0, 0)
        grad = grad_normed[...] + dot(low_g, d_gateup_ref[0]) + dot(low_u, d_gateup_ref[1])
        inverse = norm_of(middle[...], gain_ref[...])[1]
        grad = grad_ref[...].astype(F32) + norm_back(middle[...], inverse, gain_ref[...], grad)
        grad_middle_ref[...] = grad
        grad = grad.astype(BF16)
        low = (ADAPTER_SCALE * dot(grad, u_output_ref[...], 1, 1)).astype(BF16)
        mixed = dot(grad, w_output_ref[...], 1, 1) + dot(low, d_output_ref[...])
        grad_mixed_ref[...] = mixed.astype(BF16)
        terms_ref[:, :width] = dot(low, attended_ref[...], 0, 0)
        terms_ref[:, width : 2 * width] = ADAPTER_SCALE * dot(low_output[...], grad, 0, 0)


def feed(attended, flat, grad, w_output, w_gateup, w_down, factors, gain):
    rows, width = flat.shape
    hidden = w_down.shape[0]
    chunk = 4 * TILE
    rank = factors[0].shape[0]
    total = 5 * width + 3 * hidden
    total += -total % (2 * 4 * TILE)
    d_output, u_output, d_gateup, u_gateup, d_ffdown, u_ffdown = factors
    shape = jax.ShapeDtypeStruct

    def whole(array):
        return pl.BlockSpec(array.shape, lambda f: (0,) * len(array.shape))

    gain = gain.reshape(1, -1)
    outs = [
        shape((rows, width), BF16),
        shape((rows, width), F32),
        shape((rows, width), BF16),
        shape((rank, total), F32),
    ]
    return pl.pallas_call(
        feed_kernel,
        grid=(hidden // chunk,),
        out_shape=outs,
        in_specs=[
            whole(attended),
            whole(flat),
            whole(grad),
            whole(w_output),
            pl.BlockSpec((2, width, chunk), lambda f: (0, 0, f)),
            pl.BlockSpec((chunk, width), lambda f: (f, 0)),
            whole(d_output),
            whole(u_output),
            whole(d_gateup),
            pl.BlockSpec((2, rank, chunk), lambda f: (0, 0, f)),
            pl.BlockSpec((rank, chunk), lambda f: (0, f)),
            whole(u_ffdown),
            whole(gain),
        ],
        out_specs=[whole(out) for out in outs],
        scratch_shapes=[
            pltpu.VMEM((rows, width), F32),
            pltpu.VMEM((rows, width), BF16),
            pltpu.VMEM((rows, width), F32),
            pltpu.VMEM((rows, width), F32),
            pltpu.VMEM((rows, rank), BF16),
            pltpu.VMEM((rows, rank), BF16),
            pltpu.VMEM((rows, rank), BF16),
            pltpu.VMEM((rows, rank), F32),
            pltpu.VMEM((rows, rank), BF16),
            pltpu.VMEM((rows, rank), F32),
            pltpu.VMEM((rows, rank), F32),
        ],
        compiler_params=pltpu.CompilerParams(vmem_limit_bytes=56 << 20),
    )(
        attended,
        flat,
        grad,
        w_output,
        w_gateup,
        w_down,
        d_output,
        u_output,
        d_gateup,
        u_gateup,
        d_ffdown,
        u_ffdown,
        gain,
    )


def by_sequence(
    tokens,
    attn_gain,
    ffn_gain,
    query_weight,
    keyval_weight,
    output_weight,
    gateup_weight,
    down_weight,
    query_down,
    query_up,
    keyval_down,
    keyval_up,
    output_down,
    output_up,
    gateup_down,
    gateup_up,
    ffdown_down,
    ffdown_up,
    segment_ids,
    real_mask,
    adapter_index,
    out_grad,
):
    seqs, part, width = tokens.shape
    groups = lax.axis_size("head")
    seq, head_pos = lax.axis_index("blk"), lax.axis_index("head")
    rows = seqs * part
    span = groups * part
    adapter = adapter_index[seq]

    d_query = query_down.swapaxes(1, 2)[adapter]
    d_keyval = keyval_down.swapaxes(2, 3)[adapter]
    d_output = output_down.swapaxes(1, 2)[adapter]
    d_gateup = gateup_down.swapaxes(2, 3)[adapter]
    d_ffdown = ffdown_down.swapaxes(1, 2)[adapter]
    u_query, u_keyval, u_output = query_up[adapter], keyval_up[adapter], output_up[adapter]
    u_gateup, u_ffdown = gateup_up[adapter], ffdown_up[adapter]
    rank = d_query.shape[0]

    def in_turn(first, second):
        cut = (first.shape[0], KV_HEADS, HEAD_DIM)
        both = jnp.concatenate([first.reshape(cut), second.reshape(cut)], axis=2)
        return both.reshape(first.shape[0], 2 * first.shape[1])

    nil = jnp.zeros_like(u_keyval[0])
    u_keys, u_values = in_turn(u_keyval[0], nil), in_turn(nil, u_keyval[1])
    u_qkv = jnp.concatenate(
        [
            jnp.pad(u_query, ((0, 0), (0, u_keys.shape[1]))),
            jnp.pad(jnp.concatenate([u_keys, u_values], axis=0), ((0, 0), (width, 0))),
        ],
        axis=0,
    )
    d_qkv = jnp.concatenate([d_query, d_keyval[0], d_keyval[1]], axis=0)

    position = (
        jnp.arange(seqs, dtype=jnp.int32)[:, None] * span
        + head_pos * part
        + jnp.arange(part, dtype=jnp.int32)[None, :]
    )
    length = jnp.sum(real_mask[seq])
    segment = segment_ids[seq]
    mine = jnp.take(segment, position)
    first = jnp.sum((segment[None, None, :] < mine[:, :, None]).astype(jnp.int32), axis=2)
    least = jnp.maximum(position - (WINDOW - 1), first)
    most = jnp.minimum(position, length - 1)
    limits = jnp.stack([least, most, position])
    limits = jnp.concatenate([limits, limits], axis=2)

    flat_pos = position.reshape(rows)
    freqs = ROPE_BASE ** (
        -(jnp.arange(HEAD_DIM // 2, dtype=F32) * 2.0) / HEAD_DIM
    )
    angles = flat_pos.astype(F32)[:, None] * freqs[None, :]
    cosine, sine = jnp.cos(angles), jnp.sin(angles)
    turn = jnp.stack(
        [jnp.tile(cosine, (1, 4)), jnp.tile(jnp.concatenate([-sine, sine], axis=1), (1, 2))]
    )

    (
        w_qkv,
        w_output,
        w_gateup,
        w_down,
        flat,
        grad_flat,
        normed,
        inverse1,
        low_qkv,
        queries,
        pairs,
        attended,
        lse,
    ) = front(
        tokens,
        out_grad,
        (query_weight, keyval_weight, output_weight, gateup_weight, down_weight),
        limits,
        turn,
        d_qkv,
        u_qkv,
        attn_gain,
    )
    flat, grad_flat = flat.reshape(rows, width), grad_flat.reshape(rows, width)
    pairs = pairs.reshape(seqs * span, pairs.shape[2])
    output, grad_middle, grad_mixed, early = feed(
        attended,
        flat,
        grad_flat,
        w_output,
        w_gateup,
        w_down,
        (d_output, u_output, d_gateup, u_gateup, d_ffdown, u_ffdown),
        ffn_gain,
    )
    hidden = w_down.shape[0]
    sizes = [width] * 4 + [hidden] * 3 + [width]
    grad_qkv, output, early = attend_back(
        limits, queries, pairs, lse, grad_mixed, turn, output, early
    )
    input_grad, late = first_back(
        grad_qkv, w_qkv, d_qkv, u_qkv, normed, low_qkv, grad_middle, flat, inverse1, attn_gain
    )
    adapters = jnp.arange(query_down.shape[0], dtype=jnp.int32)
    holder = jnp.argmax(adapter_index[None, :] == adapters[:, None], axis=1).astype(jnp.int32)
    found = placed(holder, early, late, sizes, width)
    return (
        output,
        input_grad,
        found[0].swapaxes(1, 2),
        found[1],
        found[2].swapaxes(2, 3),
        found[3],
        found[4].swapaxes(1, 2),
        found[5],
        found[6].swapaxes(2, 3),
        found[7],
        found[8].swapaxes(1, 2),
        found[9],
    )


def solution(mesh):
    in_specs = (
        P(None, ("blk", "head"), None),
        P(),
        P(),
        P("blk", "head"),
        P(None, "blk", "head"),
        P("blk", "head"),
        P(None, "blk", "head"),
        P("blk", "head"),
        P(),
        P(),
        P(),
        P(),
        P(),
        P(),
        P(),
        P(),
        P(),
        P(),
        P(),
        P(),
        P(),
        P(None, ("blk", "head"), None),
    )
    out_specs = (
        P(None, ("blk", "head"), None),
        P(None, ("blk", "head"), None),
        P(),
        P(),
        P(),
        P(),
        P(),
        P(),
        P(),
        P(),
        P(),
        P(),
    )

    def chosen(tokens, *rest):
        if mesh.shape["blk"] == tokens.shape[0] == 8 and mesh.shape["head"] == 4:
            return by_sequence(tokens, *rest)
        return on_device(tokens, *rest)

    return jax.shard_map(
        chosen, mesh=mesh, in_specs=in_specs, out_specs=out_specs, check_vma=False
    )
```

```python
import functools
import math

import jax
import jax.numpy as jnp
import numpy as np
from jax import lax
from jax.experimental import pallas as pl
from jax.experimental.pallas import tpu as pltpu
from jax.sharding import PartitionSpec as P

HEADS = 20
KV_HEADS = 5
HEAD_DIM = 64
WINDOW = 1024


EPSILON = 1e-05
ROPE_BASE = 10000.0
ADAPTER_SCALE = 2.0
MASKED = -1e30


def passed_along(value, axis, steps):
    count = lax.axis_size(axis)
    initial, last = (max(0, -steps), min(count, count - steps))
    return lax.ppermute(value, axis, [(source, source + steps) for source in range(initial, last)])


def rms_scale(values, gain):
    return values * lax.rsqrt(jnp.mean(values * values, axis=-1, keepdims=True) + EPSILON) * gain


def rotate(values, positions, sign):
    half = values.shape[-1] // 2
    freqs = ROPE_BASE ** (-(jnp.arange(half, dtype=jnp.float32) * 2.0) / values.shape[-1])
    angles = positions.astype(jnp.float32)[:, None] * freqs[None, :]
    cosine = jnp.cos(angles)[:, None, :]
    sine = sign * jnp.sin(angles)[:, None, :]
    first = values[..., :half]
    second = values[..., half:]
    return jnp.concatenate(
        [first * cosine - second * sine, second * cosine + first * sine], axis=-1
    )


def gated(gate, upward):
    return jax.nn.silu(gate) * upward


def project(inputs, weight, down, up):
    lowered = jnp.einsum("sci,sir->scr", inputs, down, preferred_element_type=jnp.float32).astype(
        jnp.bfloat16
    )
    extra = ADAPTER_SCALE * jnp.einsum(
        "scr,sro->sco", lowered, up, preferred_element_type=jnp.float32
    )
    return (
        jnp.einsum("sci,io->sco", inputs, weight, preferred_element_type=jnp.float32) + extra,
        lowered,
    )


def project_back(inputs, lowered, grad_out, weight, down, up):
    grad_up = ADAPTER_SCALE * jnp.einsum(
        "scr,sco->sro", lowered, grad_out, preferred_element_type=jnp.float32
    )
    grad_low = (
        ADAPTER_SCALE * jnp.einsum("sco,sro->scr", grad_out, up, preferred_element_type=jnp.float32)
    ).astype(jnp.bfloat16)
    grad_down = jnp.einsum("sci,scr->sir", inputs, grad_low, preferred_element_type=jnp.float32)
    grad_in = jnp.einsum("sco,io->sci", grad_out, weight, preferred_element_type=jnp.float32)
    grad_in = grad_in + jnp.einsum(
        "scr,sir->sci", grad_low, down, preferred_element_type=jnp.float32
    )
    return (grad_in, grad_down, grad_up)


def on_device(
    tokens,
    attn_gain,
    ffn_gain,
    query_weight,
    keyval_weight,
    output_weight,
    gateup_weight,
    down_weight,
    query_down,
    query_up,
    keyval_down,
    keyval_up,
    output_down,
    output_up,
    gateup_down,
    gateup_up,
    ffdown_down,
    ffdown_up,
    segment_ids,
    real_mask,
    adapter_index,
    out_grad,
):
    seqs, per_device, width = tokens.shape
    groups = lax.axis_size("head")
    head_pos = lax.axis_index("head")
    blk_pos = lax.axis_index("blk")
    span = groups * per_device
    heads = HEADS
    head_dim = HEAD_DIM
    kv_heads = KV_HEADS
    local_heads = heads // groups
    share = heads // kv_heads
    reach = (WINDOW - 2) // span + 1
    scale = 1.0 / math.sqrt(head_dim)
    rows_a, rows_b, rows_c, rows_d, rows_e = (
        lax.all_gather(query_weight, "blk", axis=0, tiled=True),
        lax.all_gather(keyval_weight, "blk", axis=1, tiled=True),
        lax.all_gather(output_weight, "blk", axis=0, tiled=True),
        lax.all_gather(gateup_weight, "blk", axis=1, tiled=True),
        lax.all_gather(down_weight, "blk", axis=0, tiled=True),
    )
    w_query, w_keyval, w_output, w_gateup, w_down = (
        lax.all_gather(rows_a, "head", axis=1, tiled=True),
        lax.all_gather(rows_b, "head", axis=2, tiled=True),
        lax.all_gather(rows_c, "head", axis=1, tiled=True),
        lax.all_gather(rows_d, "head", axis=2, tiled=True),
        lax.all_gather(rows_e, "head", axis=1, tiled=True),
    )
    down_query = query_down[adapter_index]
    up_query = query_up[adapter_index]
    down_keyval = keyval_down[adapter_index]
    up_keyval = keyval_up[adapter_index]
    down_output = output_down[adapter_index]
    up_output = output_up[adapter_index]
    down_gateup = gateup_down[adapter_index]
    up_gateup = gateup_up[adapter_index]
    down_ffdown = ffdown_down[adapter_index]
    up_ffdown = ffdown_up[adapter_index]

    def first_norm(values):
        return rms_scale(values, attn_gain)

    def second_norm(values):
        return rms_scale(values, ffn_gain)

    flat = tokens.astype(jnp.float32)
    normed_full, first_norm_back = jax.vjp(first_norm, flat)
    normed = normed_full.astype(jnp.bfloat16)
    queries_pre, low_query = project(normed, w_query, down_query, up_query)
    keys_pre, low_key = project(normed, w_keyval[0], down_keyval[:, 0], up_keyval[:, 0])
    values_pre, low_value = project(normed, w_keyval[1], down_keyval[:, 1], up_keyval[:, 1])
    token_pos = (blk_pos * groups + head_pos) * per_device + jnp.arange(per_device, dtype=jnp.int32)
    queries = rotate(queries_pre.reshape(seqs, per_device, heads, head_dim), token_pos, 1.0).astype(
        jnp.bfloat16
    )
    keys = rotate(keys_pre.reshape(seqs, per_device, kv_heads, head_dim), token_pos, 1.0).astype(
        jnp.bfloat16
    )
    values = values_pre.reshape(seqs, per_device, kv_heads, head_dim).astype(jnp.bfloat16)
    owner = np.array(
        [
            [(group * local_heads + slot) // share for slot in range(local_heads)]
            for group in range(groups)
        ]
    )
    slot_of = jnp.arange(local_heads, dtype=jnp.int32)
    sender = jnp.asarray(
        (owner[:, :, None] == np.arange(kv_heads)[None, None, :]).astype(np.float32), jnp.bfloat16
    )
    spread = (slot_of[:, None] == jnp.arange(local_heads, dtype=jnp.int32)[None, :]).astype(
        jnp.bfloat16
    )
    pair = jnp.stack([keys, values], axis=3)
    outgoing = jnp.einsum(
        "sckxd,gmk->scgmxd", pair, sender, preferred_element_type=jnp.float32
    ).astype(jnp.bfloat16)
    outgoing = outgoing.reshape(seqs, per_device, groups, local_heads * 2 * head_dim)
    query_send = queries.reshape(seqs, per_device, groups, local_heads * head_dim)
    query_here, pair_here = (
        lax.all_to_all(query_send, "head", split_axis=2, concat_axis=1, tiled=True),
        lax.all_to_all(outgoing, "head", split_axis=2, concat_axis=1, tiled=True),
    )
    query_here = query_here.reshape(seqs, span, local_heads, head_dim)
    pair_here = pair_here.reshape(seqs, span, local_heads, 2, head_dim)
    received = [pair_here]
    moving = pair_here
    for hop in range(reach):
        moving = passed_along(moving, "blk", 1)
        received.append(moving)
    window_pairs = jnp.stack(received, axis=1)
    query_pos = blk_pos * span + jnp.arange(span, dtype=jnp.int32)
    key_pos = (blk_pos - jnp.arange(reach + 1, dtype=jnp.int32))[:, None] * span + jnp.arange(
        span, dtype=jnp.int32
    )[None, :]
    safe_pos = jnp.clip(key_pos, 0, segment_ids.shape[1] - 1)
    query_segment = lax.dynamic_slice_in_dim(segment_ids, blk_pos * span, span, 1)
    key_segment = segment_ids[:, safe_pos]
    key_real = real_mask[:, safe_pos]
    distance = query_pos[:, None, None] - key_pos[None]
    allowed = (key_pos[None] >= 0) & (distance >= 0) & (distance < WINDOW)
    allowed = allowed & (query_segment[:, :, None, None] == key_segment[:, None])
    allowed = allowed & ((key_real[:, None] == 1) | (distance[None] == 0))
    batch = 1
    target = max(1, 512 // span)
    for option in range(1, seqs + 1):
        if seqs % option == 0 and option <= target:
            batch = option
    count = seqs // batch

    def grouped(array):
        return array.reshape((count, batch) + array.shape[1:])

    def scores_of(query_part, pair_part, allowed_part):
        keys_wide = jnp.einsum(
            "gjlmd,hm->gjlhd", pair_part[:, :, :, :, 0], spread, preferred_element_type=jnp.float32
        ).astype(jnp.bfloat16)
        values_wide = jnp.einsum(
            "gjlmd,hm->gjlhd", pair_part[:, :, :, :, 1], spread, preferred_element_type=jnp.float32
        ).astype(jnp.bfloat16)
        raw = (
            jnp.einsum(
                "gqhd,gjlhd->ghqjl", query_part, keys_wide, preferred_element_type=jnp.float32
            )
            * scale
        )
        raw = jnp.where(allowed_part[:, None], raw, MASKED)
        return (raw, keys_wide, values_wide)

    def attend(pieces):
        query_part, pair_part, allowed_part = pieces
        raw, keys_wide, values_wide = scores_of(query_part, pair_part, allowed_part)
        top = jnp.max(raw, axis=(3, 4), keepdims=True)
        shifted = jnp.exp(raw - top)
        total = jnp.sum(shifted, axis=(3, 4), keepdims=True)
        probs_low = (shifted / total).astype(jnp.bfloat16)
        result = jnp.einsum(
            "ghqjl,gjlhd->gqhd", probs_low, values_wide, preferred_element_type=jnp.float32
        )
        return (result.astype(jnp.bfloat16), top + jnp.log(total))

    attended, logsum = lax.map(
        attend, (grouped(query_here), grouped(window_pairs), grouped(allowed))
    )
    mixed = lax.all_to_all(
        attended.reshape(seqs, span, local_heads * head_dim),
        "head",
        split_axis=1,
        concat_axis=2,
        tiled=True,
    )
    branch_attn, low_output = project(mixed, w_output, down_output, up_output)
    middle = flat + branch_attn
    normed2_full, second_norm_back = jax.vjp(second_norm, middle)
    normed2 = normed2_full.astype(jnp.bfloat16)
    gate, low_gate = project(normed2, w_gateup[0], down_gateup[:, 0], up_gateup[:, 0])
    upward, low_upward = project(normed2, w_gateup[1], down_gateup[:, 1], up_gateup[:, 1])
    activated_full, gated_back = jax.vjp(gated, gate, upward)
    activated = activated_full.astype(jnp.bfloat16)
    branch_ffn, low_ffdown = project(activated, w_down, down_ffdown, up_ffdown)
    output = (middle + branch_ffn).astype(jnp.bfloat16)
    grad_activated, gd_ffdown, gu_ffdown = project_back(
        activated, low_ffdown, out_grad, w_down, down_ffdown, up_ffdown
    )
    grad_gate, grad_upward = gated_back(grad_activated)
    grad_in_gate, gd_gate, gu_gate = project_back(
        normed2,
        low_gate,
        grad_gate.astype(jnp.bfloat16),
        w_gateup[0],
        down_gateup[:, 0],
        up_gateup[:, 0],
    )
    grad_in_up, gd_up, gu_up = project_back(
        normed2,
        low_upward,
        grad_upward.astype(jnp.bfloat16),
        w_gateup[1],
        down_gateup[:, 1],
        up_gateup[:, 1],
    )
    grad_middle = out_grad.astype(jnp.float32) + second_norm_back(grad_in_gate + grad_in_up)[0]
    grad_mixed, gd_output, gu_output = project_back(
        mixed, low_output, grad_middle.astype(jnp.bfloat16), w_output, down_output, up_output
    )
    grad_send = grad_mixed.astype(jnp.bfloat16).reshape(
        seqs, per_device, groups, local_heads * head_dim
    )
    grad_here = lax.all_to_all(grad_send, "head", split_axis=2, concat_axis=1, tiled=True).reshape(
        seqs, span, local_heads, head_dim
    )
    spread_full = spread.astype(jnp.float32)

    def attend_back(pieces):
        query_part, pair_part, allowed_part, logsum_part, grad_part = pieces
        raw, keys_wide, values_wide = scores_of(query_part, pair_part, allowed_part)
        probs = jnp.exp(raw - logsum_part)
        probs_low = probs.astype(jnp.bfloat16)
        grad_probs = jnp.einsum(
            "gqhd,gjlhd->ghqjl", grad_part, values_wide, preferred_element_type=jnp.float32
        )
        inner = jnp.sum(probs * grad_probs, axis=(3, 4), keepdims=True)
        grad_raw = (probs * (grad_probs - inner)).astype(jnp.bfloat16)
        grad_query = scale * jnp.einsum(
            "ghqjl,gjlhd->gqhd", grad_raw, keys_wide, preferred_element_type=jnp.float32
        )
        grad_keys = scale * jnp.einsum(
            "ghqjl,gqhd->gjlhd", grad_raw, query_part, preferred_element_type=jnp.float32
        )
        grad_values = jnp.einsum(
            "ghqjl,gqhd->gjlhd", probs_low, grad_part, preferred_element_type=jnp.float32
        )
        both = jnp.stack([grad_keys, grad_values], axis=4)
        folded = jnp.einsum("gjlhxd,hm->gjlmxd", both, spread_full, precision=lax.Precision.HIGHEST)
        return (grad_query, folded)

    grad_query, grad_pairs = lax.map(
        attend_back,
        (grouped(query_here), grouped(window_pairs), grouped(allowed), logsum, grouped(grad_here)),
    )
    grad_pairs = grad_pairs.reshape(seqs, reach + 1, span, local_heads, 2, head_dim)
    carried = grad_pairs[:, reach]
    for hop in range(reach - 1, -1, -1):
        carried = (
            passed_along(carried.astype(jnp.bfloat16), "blk", -1).astype(carried.dtype)
            + grad_pairs[:, hop]
        )
    grad_query = rotate(grad_query.reshape(seqs, span, local_heads, head_dim), query_pos, -1.0)
    grad_query = grad_query.astype(jnp.bfloat16).reshape(seqs, span, local_heads * head_dim)
    grad_queries_pre = lax.all_to_all(grad_query, "head", split_axis=1, concat_axis=2, tiled=True)
    grad_pair_tok = lax.all_to_all(
        carried.reshape(seqs, span, local_heads * 2 * head_dim).astype(jnp.bfloat16),
        "head",
        split_axis=1,
        concat_axis=2,
        tiled=True,
    ).astype(jnp.float32)
    grad_pair_tok = grad_pair_tok.reshape(seqs, per_device, groups, local_heads, 2, head_dim)
    grad_pair_heads = jnp.einsum(
        "scgmxd,gmk->sckxd",
        grad_pair_tok,
        sender.astype(jnp.float32),
        precision=lax.Precision.HIGHEST,
    )
    grad_keys_pre = (
        rotate(grad_pair_heads[:, :, :, 0], token_pos, -1.0)
        .astype(jnp.bfloat16)
        .reshape(seqs, per_device, kv_heads * head_dim)
    )
    grad_values_pre = (
        grad_pair_heads[:, :, :, 1]
        .astype(jnp.bfloat16)
        .reshape(seqs, per_device, kv_heads * head_dim)
    )
    grad_in_query, gd_query, gu_query = project_back(
        normed, low_query, grad_queries_pre, w_query, down_query, up_query
    )
    grad_in_key, gd_key, gu_key = project_back(
        normed, low_key, grad_keys_pre, w_keyval[0], down_keyval[:, 0], up_keyval[:, 0]
    )
    grad_in_value, gd_value, gu_value = project_back(
        normed, low_value, grad_values_pre, w_keyval[1], down_keyval[:, 1], up_keyval[:, 1]
    )
    grad_normed = grad_in_query + grad_in_key + grad_in_value
    input_grad = (grad_middle + first_norm_back(grad_normed)[0]).astype(jnp.bfloat16)
    chooser = (
        adapter_index[:, None] == jnp.arange(query_down.shape[0], dtype=jnp.int32)[None, :]
    ).astype(jnp.float32)

    def per_adapter(per_sequence):
        return jnp.einsum("sa,s...->a...", chooser, per_sequence, precision=lax.Precision.HIGHEST)

    sums = lax.psum(
        (
            per_adapter(gd_query),
            per_adapter(gu_query),
            per_adapter(jnp.stack([gd_key, gd_value], axis=1)),
            per_adapter(jnp.stack([gu_key, gu_value], axis=1)),
            per_adapter(gd_output),
            per_adapter(gu_output),
            per_adapter(jnp.stack([gd_gate, gd_up], axis=1)),
            per_adapter(jnp.stack([gu_gate, gu_up], axis=1)),
            per_adapter(gd_ffdown),
            per_adapter(gu_ffdown),
        ),
        ("blk", "head"),
    )
    return (
        output,
        input_grad,
        sums[0],
        sums[1],
        sums[2],
        sums[3],
        sums[4],
        sums[5],
        sums[6],
        sums[7],
        sums[8],
        sums[9],
    )


MESH = pl.DeviceIdType.MESH
F32 = jnp.float32
BF16 = jnp.bfloat16
TILE = 128
ANYWHERE = pl.BlockSpec(memory_space=pl.ANY)


def dot(left, right, left_dim=1, right_dim=0):
    return lax.dot_general(
        left, right, (((left_dim,), (right_dim,)), ((), ())), preferred_element_type=F32
    )


def place():
    blk, head = lax.axis_index("blk"), lax.axis_index("head")
    return blk // 2, blk % 2, head // 2, head % 2


def device(z, x, y, core):
    return (z * 2 + x, y * 2 + core)


FLIPS = ((0, 0), (0, 1), (1, 0), (1, 1))


def remote(source, target, out, into, other):
    return pltpu.make_async_remote_copy(
        src_ref=source,
        dst_ref=target,
        send_sem=out,
        recv_sem=into,
        device_id=other,
        device_id_type=MESH,
    )


class Spread:
    def __init__(self, sources, target, lines, sems, planes=(), shares=None):
        self.sources, self.target, self.lines = sources, target, lines
        self.planes, self.shares = planes, shares or {}
        self.z, self.x, self.y, self.core = place()
        self.z_in, self.x_in, self.y_in, self.d_in, self.c_in = sems[:5]
        self.z_out, self.x_out, self.y_out, self.d_out, self.c_out = sems[5:10]

    @staticmethod
    def semaphores(parts, lines):
        dma = pltpu.SemaphoreType.DMA
        return [
            dma((parts, lines, 4)),
            dma((parts, lines)),
            dma((parts, lines)),
            dma((parts, lines, 2)),
            dma((parts, lines, 4)),
            dma((parts, 2, lines, 4)),
            dma((parts, lines)),
            dma((parts, lines)),
            dma((parts, lines, 2)),
            dma((parts, lines, 4)),
        ]

    def inside(self, z):
        return (z >= 0) & (z < self.lines)

    def slot(self, part, z, flip_x=0, flip_y=0):
        return self.target(part, z, (self.x + flip_x) % 2, (self.y + flip_y) % 2, self.core)

    def along_z(self, part, source, z, side, flip_x=0, flip_y=0):
        which = flip_x * 2 + flip_y
        return remote(
            source,
            self.slot(part, z, flip_x, flip_y),
            self.z_out.at[part, (side + 1) // 2, z, which],
            self.z_in.at[part, z, which],
            device(self.z + side, self.x, self.y, self.core),
        )

    def along_x(self, part, source, z):
        return remote(
            source,
            self.slot(part, z),
            self.x_out.at[part, z],
            self.x_in.at[part, z],
            device(self.z, 1 - self.x, self.y, self.core),
        )

    def along_y(self, part, source, z):
        return remote(
            source,
            self.slot(part, z),
            self.y_out.at[part, z],
            self.y_in.at[part, z],
            device(self.z, self.x, 1 - self.y, self.core),
        )

    def across(self, part, source, z, flip_x, flip_y):
        which = flip_x * 2 + flip_y
        return remote(
            source,
            self.slot(part, z, flip_x, flip_y),
            self.c_out.at[part, z, which],
            self.c_in.at[part, z, which],
            device(self.z, self.x, self.y, 1 - self.core),
        )

    def piece(self, part, ref, which):
        if ref.shape[0] < 32:
            size = ref.shape[1] // 2
            return ref.at[:, pl.ds(which * size, size)]
        count = ref.shape[0]
        first = int(count * self.shares.get(part, 0.5) + 15) // 16 * 16
        return ref.at[pl.ds(0, first)] if which == 0 else ref.at[pl.ds(first, count - first)]

    def diagonal(self, part, z, which):
        if which == 0:
            ref = self.slot(part, z, 0, 1)
            other = device(self.z, 1 - self.x, self.y, self.core)
        else:
            ref = self.slot(part, z, 1, 0)
            other = device(self.z, self.x, 1 - self.y, self.core)
        ref = self.piece(part, ref, which)
        return remote(ref, ref, self.d_out.at[part, z, which], self.d_in.at[part, z, which], other)

    def arrived(self, ref, out, into):
        remote(ref, ref, out, into, device(self.z, self.x, self.y, 1 - self.core)).wait_recv()

    def toward(self, part, source, z, flip_x, flip_y, sides=(1, -1)):
        for side in sides:

            @pl.when(self.inside(self.z + side))
            def _():
                self.along_z(part, source, z, side, flip_x, flip_y).start()

    def hand_on(self, part, source, z):
        self.along_x(part, source, z).start()
        self.along_y(part, source, z).start()
        self.across(part, source, z, 0, 0).start()

    def begin_line(self, part):
        self.toward(part, self.sources[part], self.z, 0, 0)

    def begin_plane(self, part):
        self.hand_on(part, self.sources[part], self.z)

    def line_step(self, part, distance, side):
        z = self.z - side * distance

        @pl.when(self.inside(z))
        def _():
            for flip_x, flip_y in FLIPS if part in self.planes else FLIPS[:1]:
                ref = self.slot(part, z, flip_x, flip_y)
                which = flip_x * 2 + flip_y
                self.arrived(ref, self.z_out.at[part, 0, z, which], self.z_in.at[part, z, which])
                self.toward(part, ref, z, flip_x, flip_y, (side,))
                if part in self.planes:
                    self.across(part, ref, z, flip_x, flip_y).start()
            if part not in self.planes:
                self.hand_on(part, ref, z)

    def y_step(self, part, z):
        ref = self.slot(part, z, 0, 1)
        self.arrived(ref, self.y_out.at[part, z], self.y_in.at[part, z])
        self.diagonal(part, z, 0).start()
        self.across(part, ref, z, 0, 1).start()
        if part in self.planes:
            self.toward(part, ref, z, 0, 1)

    def x_step(self, part, z):
        ref = self.slot(part, z, 1, 0)
        self.arrived(ref, self.x_out.at[part, z], self.x_in.at[part, z])
        self.diagonal(part, z, 1).start()
        self.across(part, ref, z, 1, 0).start()
        if part in self.planes:
            self.toward(part, ref, z, 1, 0)

    def corner_step(self, part, z):
        ref = self.slot(part, z, 1, 1)
        for which in (0, 1):
            self.arrived(
                self.piece(part, ref, which),
                self.d_out.at[part, z, which],
                self.d_in.at[part, z, which],
            )
        self.across(part, ref, z, 1, 1).start()
        if part in self.planes:
            self.toward(part, ref, z, 1, 1)

    def sent(self, part, z):
        mine = self.slot(part, z)
        self.along_x(part, mine, z).wait_send()
        self.along_y(part, mine, z).wait_send()
        self.diagonal(part, z, 0).wait_send()
        self.diagonal(part, z, 1).wait_send()

    def end(self, part):
        for z in range(self.lines):
            for flip_x, flip_y in FLIPS:
                which = flip_x * 2 + flip_y
                x, y = (self.x + flip_x) % 2, (self.y + flip_y) % 2
                self.arrived(
                    self.target(part, z, x, y, 1 - self.core),
                    self.c_out.at[part, z, which],
                    self.c_in.at[part, z, which],
                )
                mine = self.slot(part, z, flip_x, flip_y)
                self.across(part, mine, z, flip_x, flip_y).wait_send()
                if part not in self.planes and which > 0:
                    continue
                for side in (1, -1):

                    @pl.when(self.inside(self.z + side) & ((self.z - z) * side >= 0))
                    def _():
                        self.along_z(part, mine, z, side, flip_x, flip_y).wait_send()

            if part not in self.planes:
                self.sent(part, z)
        if part in self.planes:
            self.sent(part, self.z)

    def at(self, distance, run):
        if distance == 0:
            run(self.z)
            return
        for side in (1, -1):
            pl.when(self.inside(self.z - side * distance))(
                functools.partial(run, self.z - side * distance)
            )

    def do(self, kind, part, distance=0, side=0):
        if kind == "bz":
            self.begin_line(part)
        elif kind == "bh":
            self.begin_plane(part)
        elif kind == "line":
            self.line_step(part, distance, side)
        else:
            run = {"pY": self.y_step, "pX": self.x_step, "co": self.corner_step}[kind]
            self.at(distance, functools.partial(run, part))

    def all_steps(self, part):
        result = []
        for stage in range(1, self.lines + 2):
            steps = []
            if stage < self.lines:
                steps += [("line", part, stage, 1), ("line", part, stage, -1)]
            if stage >= 2:
                steps += [("co", part, stage - 2)]
            if stage <= self.lines:
                steps += [("pY", part, stage - 1), ("pX", part, stage - 1)]
            result += [functools.partial(self.do, *step) for step in steps]
        return result


def paired(own, other, core):
    own, other = own.astype(F32), other.astype(F32)
    return [jnp.where(core == 0, own, other), jnp.where(core == 0, other, own)]


def in_pairs(array):
    half = array.shape[1] // 2
    size = 2 * KV_HEADS * HEAD_DIM // 4
    keys = jnp.concatenate([array[:, :size], array[:, half : half + size]], axis=1)
    values = jnp.concatenate(
        [array[:, size : 2 * size], array[:, half + size : half + 2 * size]], axis=1
    )
    pieces = []
    for head in range(KV_HEADS):
        cut = slice(head * HEAD_DIM, (head + 1) * HEAD_DIM)
        pieces += [keys[:, cut], values[:, cut]]
    return jnp.concatenate(pieces, axis=1)


def windows(blocks, span, low_part):
    reach = WINDOW + TILE
    fixed = [(0, (block + 1) * span) for block in range(WINDOW // span)]
    offset = TILE * (low_part // 2 + 1) - reach
    return fixed, reach, offset


def tiles_of(ref, flipped):
    lane = lax.broadcasted_iota(jnp.int32, (ref.shape[0], TILE), 1)
    result = []
    for slot in range(4):
        tile = ref[:, slot // 2 * TILE : (slot // 2 + 1) * TILE].astype(F32)
        if (slot % 2 == 0) == flipped:
            tile = pltpu.roll(tile, HEAD_DIM, 1)
        keep = lane >= HEAD_DIM if flipped else lane < HEAD_DIM
        result.append(jnp.where(keep, tile, 0.0).astype(BF16))
    return result


def joined(rows, flipped):
    span = rows.shape[0] // 4
    heads = [rows[slot * span : (slot + 1) * span] for slot in range(4)]
    lane = lax.broadcasted_iota(jnp.int32, (span, TILE), 1)
    result = []
    for first, second in ((heads[0], heads[1]), (heads[2], heads[3])):
        if flipped:
            first = pltpu.roll(first, HEAD_DIM, 1)
        else:
            second = pltpu.roll(second, HEAD_DIM, 1)
        result.append(jnp.where(lane < HEAD_DIM, first, second))
    return result


def bias_of(limits_ref, block, start, count):
    key = start + lax.broadcasted_iota(jnp.int32, (count, TILE), 0)
    least = limits_ref[0, pl.ds(block, 1), :]
    most = limits_ref[1, pl.ds(block, 1), :]
    self_pos = limits_ref[2, pl.ds(block, 1), :]
    allowed = ((key >= least) & (key <= most)) | (key == self_pos)
    bias = jnp.where(allowed, 0.0, MASKED)
    return jnp.concatenate([bias, bias], axis=1)


def each_block(blocks, body, between=lambda: None):
    span = 4 * HEAD_DIM
    fixed, reach, offset = windows(blocks, span, lax.axis_index("head"))
    for block, (start, count) in enumerate(fixed):
        body(block, start, count)
    between()

    @pl.loop(len(fixed), blocks)
    def _(block):
        body(block, pl.multiple_of(block * span + offset, TILE), reach)


def meet(others):
    barrier = pltpu.get_barrier_semaphore()
    for other in others:
        pl.semaphore_signal(barrier, inc=1, device_id=other, device_id_type=MESH)
    pl.semaphore_wait(barrier, len(others))


def along(count):
    blk, head = lax.axis_index("blk"), lax.axis_index("head")
    return [((blk + ahead) % count, head) for ahead in range(1, count)]


def beside():
    z, x, y, core = place()
    return [
        device(z, x, y, 1 - core),
        device(z, x, 1 - y, core),
        device(z, x, 1 - y, 1 - core),
    ]


class Exchange:
    def __init__(self, source, target, size, out, into, local):
        count = target.shape[0]
        blk, head = lax.axis_index("blk"), lax.axis_index("head")
        self.own = pltpu.make_async_copy(source.at[pl.ds(blk * size, size)], target.at[blk], local)
        self.copies, self.arrivals = [], []
        for at, (other, _) in enumerate(along(count)):
            self.copies.append(
                remote(
                    source.at[pl.ds(other * size, size)],
                    target.at[blk],
                    out.at[at],
                    into.at[at],
                    (other, head),
                )
            )
            giver = (blk + count - 1 - at) % count
            self.arrivals.append(
                remote(target.at[giver], target.at[giver], out.at[at], into.at[at], (other, head))
            )

    def start(self):
        self.own.start()
        for copy in self.copies:
            copy.start()

    def wait(self):
        for copy in self.arrivals:
            copy.wait_recv()
        for copy in self.copies:
            copy.wait_send()
        self.own.wait()


class Quarters:
    def __init__(self, terms, low, got, out, into):
        z, x, y, core = place()
        self.size = low.shape[1] // 4
        self.terms, self.low, self.got = terms, low, got
        self.mine = pl.ds((y * 2 + core) * self.size, self.size)
        self.copies = []
        for at, (flip_y, flip_core) in enumerate(((0, 1), (1, 0), (1, 1))):
            other_y, other_core = (y + flip_y) % 2, (core + flip_core) % 2
            theirs = pl.ds((other_y * 2 + other_core) * self.size, self.size)
            self.copies.append(
                remote(
                    low.at[:, theirs],
                    got.at[at],
                    out.at[at],
                    into.at[at],
                    device(z, x, other_y, other_core),
                )
            )

    def start(self):
        self.low[...] = self.terms[...].astype(BF16)
        for copy in self.copies:
            copy.start()

    def total(self):
        for copy in self.copies:
            copy.wait_recv()
        total = self.terms[:, self.mine]
        for at in range(3):
            total = total + self.got[at].astype(F32)
        return total.astype(BF16)

    def end(self):
        for copy in self.copies:
            copy.wait_send()


def turned(tile, cosine, sine, only_low=False):
    lane = lax.broadcasted_iota(jnp.int32, tile.shape, 1)
    half = HEAD_DIM // 2
    partner = jnp.where(
        lane % HEAD_DIM < half, pltpu.roll(tile, TILE - half, 1), pltpu.roll(tile, half, 1)
    )
    result = tile * cosine + partner * sine
    return jnp.where(lane < HEAD_DIM, result, tile) if only_low else result


def attend_back_kernel(
    lines,
    limits_ref,
    q_ref,
    kv_ref,
    lse_ref,
    grad_ref,
    turn_ref,
    output_ref,
    terms_ref,
    dqkv_ref,
    moved_ref,
    shared_ref,
    q_rows,
    g_rows,
    kv_turned,
    total,
    pair_low,
    pair_got,
    kept,
    y_low,
    y_got,
    low,
    got,
    shard,
    pair_out,
    pair_in,
    y_out,
    y_in,
    move_out,
    move_in,
    four_out,
    four_in,
    local,
    *sems,
):
    blocks, span = q_rows.shape[0], q_rows.shape[2]
    width = q_ref.shape[1]
    groups = width // (2 * TILE)
    scale = HEAD_DIM**-0.5
    z, x, y, core = place()
    size = shard.shape[1]

    def target(part, z, x, y, core):
        return shared_ref.at[z * 2 + x, :, pl.ds((y * 2 + core) * size, size)]

    spread = Spread([shard], target, lines, sems)
    meet(along(blocks) + beside())
    exchange = Exchange(output_ref, moved_ref, span, move_out, move_in, local.at[0])
    quarters = Quarters(terms_ref, low, got, four_out, four_in)
    quarters.start()
    own = pltpu.make_async_copy(shard, target(0, z, x, y, core), local.at[1])

    def gather_start():
        shard[...] = quarters.total()
        own.start()
        spread.begin_line(0)
        spread.begin_plane(0)

    steps = spread.all_steps(0)

    def some(count):
        def run():
            for _ in range(count):
                steps.pop(0)()

        return run

    later = [None, gather_start, some(4), some(3), some(4), exchange.start]
    later += [some(3), some(3), some(1)]

    def pump():
        if later:
            step = later.pop(0)
            if step is not None:
                step()

    def pair_copy(m):
        return remote(
            pair_low.at[m, 1 - core],
            pair_got.at[m],
            pair_out.at[m],
            pair_in.at[m],
            device(z, x, y, 1 - core),
        )

    def y_copy(m):
        return remote(
            y_low.at[m], y_got.at[m], y_out.at[m], y_in.at[m], device(z, x, 1 - y, core)
        )

    def give(m):
        whole = total[...].reshape(blocks, 4, span, TILE)
        for at in range(4):
            pair_low[m, at % 2, at // 2] = whole[:, at].astype(BF16)
        spot = total.reshape(blocks, 4, span, TILE)
        for at in range(2):
            kept[m, at] = spot[:, at * 2 + core]
        pair_copy(m).start()

    def add_pair(m):
        pair_copy(m).wait_recv()
        y_low[m] = (kept[m, 1 - y] + pair_got[m, 1 - y].astype(F32)).astype(BF16)
        y_copy(m).start()

    def add_y(m):
        y_copy(m).wait_recv()
        tile = kept[m, y] + pair_got[m, y].astype(F32) + y_got[m].astype(F32)
        tile = turned(tile.reshape(blocks * span, TILE), turn_ref[0], -turn_ref[1], True)
        at = width + m * TILE
        dqkv_ref[:, at : at + TILE] = tile.astype(BF16)

    for m in range(groups):
        columns = slice(m * 2 * TILE, (m + 1) * 2 * TILE)
        tile = slice(m * TILE, (m + 1) * TILE)
        for slot, rows in enumerate(tiles_of(q_ref[:, columns], False)):
            q_rows[:, slot] = (rows * BF16(scale)).reshape(blocks, span, TILE)
        for slot, rows in enumerate(tiles_of(grad_ref[:, columns], True)):
            g_rows[:, slot] = rows.reshape(blocks, span, TILE)
        kv_turned[...] = kv_ref[:, tile].astype(F32).T.astype(BF16)
        total[...] = jnp.zeros_like(total)

        def body(block, start, count):
            keys = pl.ds(start, count)
            queries = q_rows[block].reshape(4 * span, TILE)
            grads = g_rows[block].reshape(4 * span, TILE)
            scores = dot(kv_ref[keys, tile], queries, 1, 1)
            scores = scores + bias_of(limits_ref, block, start, count)
            probs = jnp.exp(scores - lse_ref[m, pl.ds(block, 1), :])
            grad_probs = dot(kv_ref[keys, tile], grads, 1, 1)
            inner = jnp.sum(probs * grad_probs, axis=0, keepdims=True)
            grad_scores = (probs * (grad_probs - inner)).astype(BF16)
            total[keys, :] += dot(grad_scores, queries) + dot(probs.astype(BF16), grads)
            grad_q = (dot(kv_turned[:, keys], grad_scores) * scale).T
            rows = pl.ds(block * span, span)
            cosine, sine = turn_ref[0, rows, :], -turn_ref[1, rows, :]
            for at, part in enumerate(joined(grad_q, False)):
                at = m * 2 * TILE + at * TILE
                dqkv_ref[rows, at : at + TILE] = turned(part, cosine, sine).astype(BF16)

        each_block(blocks, body, pump)
        pump()
        give(m)
        if m >= 1:
            add_pair(m - 1)
        if m >= 2:
            add_y(m - 2)
    while later:
        pump()
    add_pair(groups - 1)
    add_y(groups - 2)
    spread.end(0)
    own.wait()
    exchange.wait()
    quarters.end()
    add_y(groups - 1)
    for m in range(groups):
        pair_copy(m).wait_send()
        y_copy(m).wait_send()


def attend_back(limits, queries, pairs, lse, grads, turn, output, terms):
    rows, width = queries.shape
    blocks = limits.shape[1]
    span = rows // blocks
    groups = width // (2 * TILE)
    rank, total = terms.shape
    seqs = lax.axis_size("blk")
    each = pltpu.VMEM((blocks, 4, span, TILE), BF16)
    dma = pltpu.SemaphoreType.DMA
    vmem = pl.BlockSpec(memory_space=pltpu.VMEM)
    shape = jax.ShapeDtypeStruct
    return pl.pallas_call(
        functools.partial(attend_back_kernel, seqs // 2),
        out_shape=[
            shape((rows, width + pairs.shape[1]), BF16),
            shape((seqs, span, width), BF16),
            shape((seqs, rank, total), BF16),
        ],
        in_specs=[vmem] * 8,
        out_specs=[vmem, ANYWHERE, ANYWHERE],
        scratch_shapes=[
            each,
            each,
            pltpu.VMEM((TILE, pairs.shape[0]), BF16),
            pltpu.VMEM((pairs.shape[0], TILE), F32),
            pltpu.VMEM((groups, 2, 2, blocks, span, TILE), BF16),
            pltpu.VMEM((groups, 2, blocks, span, TILE), BF16),
            pltpu.VMEM((groups, 2, blocks, span, TILE), F32),
            pltpu.VMEM((groups, blocks, span, TILE), BF16),
            pltpu.VMEM((groups, blocks, span, TILE), BF16),
            pltpu.VMEM((rank, total), BF16),
            pltpu.VMEM((3, rank, total // 4), BF16),
            pltpu.VMEM((rank, total // 4), BF16),
            dma((groups,)),
            dma((groups,)),
            dma((groups,)),
            dma((groups,)),
            dma((seqs - 1,)),
            dma((seqs - 1,)),
            dma((3,)),
            dma((3,)),
            dma((2,)),
            *Spread.semaphores(1, seqs // 2),
        ],
        compiler_params=pltpu.CompilerParams(
            collective_id=1, has_side_effects=True, vmem_limit_bytes=56 << 20
        ),
    )(limits, queries, pairs, lse, grads, turn, output, terms)


def first_back_kernel(
    lines,
    dqkv_ref,
    weight_ref,
    down_ref,
    up_ref,
    normed_ref,
    low_ref,
    middle_ref,
    flat_ref,
    inverse_ref,
    gain_ref,
    moved_ref,
    shared_ref,
    result,
    terms,
    low,
    got,
    shard,
    move_out,
    move_in,
    four_out,
    four_in,
    local,
    *sems,
):
    blocks, span = moved_ref.shape[:2]
    z, x, y, core = place()
    size = shard.shape[1]
    rank = down_ref.shape[0] // 3
    width = flat_ref.shape[1]

    def target(part, z, x, y, core):
        return shared_ref.at[z * 2 + x, :, pl.ds((y * 2 + core) * size, size)]

    spread = Spread([shard], target, lines, sems)
    meet(along(blocks) + beside())
    grad_low = (ADAPTER_SCALE * dot(dqkv_ref[...], up_ref[...], 1, 1)).astype(BF16)
    grad_up = ADAPTER_SCALE * dot(low_ref[...], dqkv_ref[...], 0, 0)
    grad_down = dot(grad_low, normed_ref[...], 0, 0)
    terms[:, :width] = grad_up[:rank, :width]
    at = width
    while at < dqkv_ref.shape[1]:
        lane = lax.broadcasted_iota(jnp.int32, (rank, TILE), 1)
        terms[:, at : at + TILE] = jnp.where(
            lane < HEAD_DIM,
            grad_up[rank : 2 * rank, at : at + TILE],
            grad_up[2 * rank :, at : at + TILE],
        )
        at += TILE
    for which in range(3):
        terms[:, at : at + width] = grad_down[which * rank : (which + 1) * rank]
        at += width
    if at < terms.shape[1]:
        terms[:, at:] = jnp.zeros((rank, terms.shape[1] - at), F32)
    quarters = Quarters(terms, low, got, four_out, four_in)
    quarters.start()
    own = pltpu.make_async_copy(shard, target(0, z, x, y, core), local.at[1])
    exchange = Exchange(result, moved_ref, span, move_out, move_in, local.at[0])
    grad = dot(dqkv_ref[...], weight_ref[...], 1, 1) + dot(grad_low, down_ref[...])
    shard[...] = quarters.total()
    own.start()
    spread.begin_line(0)
    spread.begin_plane(0)
    weighted = grad * gain_ref[...]
    flat, inverse = flat_ref[...].astype(F32), inverse_ref[...]
    mean = jnp.mean(flat * weighted, axis=1, keepdims=True)
    grad = middle_ref[...] + inverse * weighted - flat * (inverse * inverse * inverse * mean)
    result[...] = grad.astype(BF16)
    steps = spread.all_steps(0)
    for step in steps[:11]:
        step()
    exchange.start()
    for step in steps[11:]:
        step()
    spread.end(0)
    own.wait()
    quarters.end()
    exchange.wait()


def first_back(grad_qkv, weight, down, up, normed, low, middle, flat, inverse, gain):
    rows, width = flat.shape
    rank = down.shape[0] // 3
    seqs, heads = lax.axis_size("blk"), lax.axis_size("head")
    total = 3 * width + weight.shape[1]
    total += -total % (2 * heads * TILE)
    dma = pltpu.SemaphoreType.DMA
    vmem = pl.BlockSpec(memory_space=pltpu.VMEM)
    shape = jax.ShapeDtypeStruct
    return pl.pallas_call(
        functools.partial(first_back_kernel, seqs // 2),
        out_shape=[
            shape((seqs, rows // seqs, width), BF16),
            shape((seqs, rank, total), BF16),
        ],
        in_specs=[vmem] * 10,
        out_specs=[ANYWHERE, ANYWHERE],
        scratch_shapes=[
            pltpu.VMEM((rows, width), BF16),
            pltpu.VMEM((rank, total), F32),
            pltpu.VMEM((rank, total), BF16),
            pltpu.VMEM((3, rank, total // 4), BF16),
            pltpu.VMEM((rank, total // 4), BF16),
            dma((seqs - 1,)),
            dma((seqs - 1,)),
            dma((3,)),
            dma((3,)),
            dma((2,)),
            *Spread.semaphores(1, seqs // 2),
        ],
        compiler_params=pltpu.CompilerParams(
            collective_id=2, has_side_effects=True, vmem_limit_bytes=56 << 20
        ),
    )(grad_qkv, weight, down, up, normed, low, middle, flat, inverse, gain.reshape(1, -1))


def placed_kernel(sizes, width, holder_ref, early_ref, late_ref, *outs):
    q_down, q_up, kv_down, kv_up, o_down, o_up, gu_down, gu_up, ff_down, ff_up = outs
    cuts = np.cumsum([0] + sizes)
    early = [slice(int(begin), int(end)) for begin, end in zip(cuts[:-1], cuts[1:])]
    for out, cut in zip((o_down, o_up), early[:2]):
        out[0] = early_ref[0, :, cut].astype(F32)
    for which in range(2):
        gu_down[0, which] = early_ref[0, :, early[2 + which]].astype(F32)
        gu_up[0, which] = early_ref[0, :, early[4 + which]].astype(F32)
    for out, cut in zip((ff_down, ff_up), early[6:]):
        out[0] = early_ref[0, :, cut].astype(F32)
    q_up[0] = late_ref[0, :, :width].astype(F32)
    narrow = KV_HEADS * HEAD_DIM
    pairs = late_ref[0, :, width : width + 2 * narrow].astype(F32)
    for which in range(2):
        pieces = [
            pairs[:, (2 * head + which) * HEAD_DIM : (2 * head + which + 1) * HEAD_DIM]
            for head in range(KV_HEADS)
        ]
        kv_up[0, which] = jnp.concatenate(pieces, axis=1)
    at = width + 2 * narrow
    q_down[0] = late_ref[0, :, at : at + width].astype(F32)
    for which in range(2):
        at += width
        kv_down[0, which] = late_ref[0, :, at : at + width].astype(F32)


def placed(holder, early, late, sizes, width):
    adapters, rank = early.shape[:2]
    hidden = sizes[4]
    narrow = KV_HEADS * HEAD_DIM
    shapes = [
        (rank, width),
        (rank, width),
        (2, rank, width),
        (2, rank, narrow),
        (rank, width),
        (rank, width),
        (2, rank, width),
        (2, rank, hidden),
        (rank, hidden),
        (rank, width),
    ]

    def whole(shape):
        return pl.BlockSpec((1,) + shape, lambda a, held: (a,) + (0,) * len(shape))

    return pl.pallas_call(
        functools.partial(placed_kernel, sizes, width),
        grid_spec=pltpu.PrefetchScalarGridSpec(
            num_scalar_prefetch=1,
            grid=(adapters,),
            in_specs=[
                pl.BlockSpec((1, rank, early.shape[2]), lambda a, held: (held[a], 0, 0)),
                pl.BlockSpec((1, rank, late.shape[2]), lambda a, held: (held[a], 0, 0)),
            ],
            out_specs=[whole(shape) for shape in shapes],
        ),
        out_shape=[jax.ShapeDtypeStruct((adapters,) + shape, F32) for shape in shapes],
    )(holder, early, late)


def norm_of(values, gain):
    inverse = lax.rsqrt(jnp.mean(values * values, axis=-1, keepdims=True) + EPSILON)
    return (values * inverse * gain).astype(BF16), inverse


def norm_back(values, inverse, gain, grad):
    weighted = grad * gain
    mean = jnp.mean(values * weighted, axis=-1, keepdims=True)
    return inverse * weighted - values * (inverse * inverse * inverse * mean)


def lowered(inputs, down):
    return dot(inputs, down, 1, 1).astype(BF16)


def front_kernel(lines, *refs):
    (
        tokens,
        out_grad,
        query,
        keyval,
        output,
        gateup,
        down,
        limits_ref,
        turn_ref,
        d_qkv_ref,
        u_qkv_ref,
        gain_ref,
        w_qkv,
        w_output,
        w_gateup,
        w_down,
        flat_ref,
        grad_ref,
        normed_ref,
        inverse_ref,
        low_ref,
        q_ref,
        pairs_ref,
        out_ref,
        lse_ref,
    ) = refs[:25]
    got_query, got_keyval, got_output, got_down, my_query, my_keyval, my_output, my_down = refs[25:33]
    all_keyval, first_weights, q_rows, kv_turned = refs[33:37]
    pair_out, pair_in, local, move_out, move_in, share_out, share_in = refs[37:44]
    rows, deep = my_query.shape[0], my_down.shape[0]
    wide, mixed = my_output.shape[1], my_keyval.shape[1]
    span, hidden = gateup.shape[1:]
    width = w_output.shape[1]
    blocks, part_rows = flat_ref.shape[:2]
    groups = width // (2 * TILE)

    def target(part, z, x, y, core):
        blk, head = z * 2 + x, y * 2 + core
        if part == 0:
            return all_keyval.at[pl.ds(blk * 2 * rows + core * rows, rows), pl.ds(y * mixed, mixed)]
        if part == 1:
            return first_weights.at[
                pl.ds(blk * 2 * rows + core * rows, rows), pl.ds(y * wide, wide)
            ]
        if part == 2:
            return w_output.at[pl.ds(blk * 2 * rows + core * rows, rows), pl.ds(y * wide, wide)]
        if part == 5:
            return w_down.at[pl.ds(blk * 2 * deep + core * deep, deep), pl.ds(y * wide, wide)]
        return w_gateup.at[part - 3, pl.ds(blk * span, span), pl.ds(head * hidden, hidden)]

    sources = [my_keyval, my_query, my_output, gateup.at[0], gateup.at[1], my_down]
    spread = Spread(sources, target, lines, refs[44:], FRONT_PLANES, FRONT_SHARES)
    z, x, y, core = place()
    head = y * 2 + core
    meet(along(blocks) + beside())
    sibling = device(z, x, y, 1 - core)
    theirs = pl.ds((1 - core) * rows, rows)
    swaps = [
        remote(keyval.at[:, theirs], got_keyval, pair_out.at[0], pair_in.at[0], sibling),
        remote(query.at[theirs], got_query, pair_out.at[1], pair_in.at[1], sibling),
        remote(output.at[theirs], got_output, pair_out.at[2], pair_in.at[2], sibling),
        remote(
            down.at[pl.ds((1 - core) * deep, deep)], got_down, pair_out.at[3], pair_in.at[3], sibling
        ),
    ]
    for swap in swaps:
        swap.start()
    arrive = Exchange(tokens, flat_ref, part_rows, move_out.at[0], move_in.at[0], local.at[7])
    later_grad = Exchange(out_grad, grad_ref, part_rows, move_out.at[1], move_in.at[1], local.at[8])
    own = [
        pltpu.make_async_copy(sources[part], target(part, z, x, y, core), local.at[part])
        for part in range(6)
    ]

    mine = pl.ds(core * rows, rows)
    kv_ref = pairs_ref.reshape(blocks * pairs_ref.shape[1], pairs_ref.shape[2])
    cosine, sine = turn_ref[0], turn_ref[1]
    here = pl.ds(head * part_rows, part_rows)
    weights_out = pltpu.make_async_copy(first_weights, w_qkv, local.at[6])
    shares = []
    for at, (flip_y, other) in enumerate(((0, device(z, x, 1 - y, core)), (0, sibling), (1, sibling))):
        source_head = ((y + flip_y) % 2) * 2 + core
        ref = pairs_ref.at[:, pl.ds(source_head * part_rows, part_rows)]
        shares.append(remote(ref, ref, share_out.at[at], share_in.at[at], other))

    def share_arrived(at, from_y, from_core):
        ref = pairs_ref.at[:, pl.ds((from_y * 2 + from_core) * part_rows, part_rows)]
        remote(ref, ref, share_out.at[at], share_in.at[at], sibling).wait_recv()

    def first(columns):
        return dot(normed_ref[...], first_weights[:, columns]) + ADAPTER_SCALE * dot(
            low_ref[...], u_qkv_ref[:, columns]
        )

    def pack_first():
        swaps[0].wait_recv()
        pieces = paired(keyval[0, mine, :], got_keyval[0], core)
        pieces += paired(keyval[1, mine, :], got_keyval[1], core)
        filled = sum(p.shape[1] for p in pieces)
        pieces.append(jnp.zeros((rows, mixed - filled), F32))
        my_keyval[...] = jnp.concatenate(pieces, axis=1).astype(BF16)
        swaps[1].wait_recv()
        my_query[...] = jnp.concatenate(
            paired(query[mine, :], got_query[...], core), axis=1
        ).astype(BF16)

    def pack_others():
        swaps[2].wait_recv()
        my_output[...] = jnp.concatenate(
            paired(output[mine, :], got_output[...], core), axis=1
        ).astype(BF16)
        swaps[3].wait_recv()
        my_down[...] = jnp.concatenate(
            paired(down[pl.ds(core * deep, deep), :], got_down[...], core), axis=1
        ).astype(BF16)

    def norm_first():
        flat = flat_ref[...].reshape(blocks * part_rows, width).astype(F32)
        normed, inverse = norm_of(flat, gain_ref[...])
        normed_ref[...] = normed
        inverse_ref[...] = inverse
        low_ref[...] = lowered(normed, d_qkv_ref[...])

    def pair_weights():
        own[0].wait()
        first_weights[:, width:] = in_pairs(all_keyval[...].astype(F32)).astype(BF16)

    def make_pairs():
        for m in range(groups):
            at = width + m * TILE
            tile = turned(first(slice(at, at + TILE)), cosine, sine, True).astype(BF16)
            pairs_ref[:, here, m * TILE : (m + 1) * TILE] = tile.reshape(blocks, part_rows, TILE)

    def give_pairs():
        shares[0].start()
        shares[1].start()

    def get_pairs():
        share_arrived(0, 1 - y, core)
        shares[2].start()
        share_arrived(1, y, 1 - core)
        share_arrived(2, 1 - y, 1 - core)

    def make_queries(m):
        if m == 0:
            own[1].wait()
            weights_out.start()
        both = first(slice(m * 2 * TILE, (m + 1) * 2 * TILE))
        for at in range(2):
            tile = turned(both[:, at * TILE : (at + 1) * TILE], cosine, sine).astype(BF16)
            q_ref[:, (2 * m + at) * TILE : (2 * m + at + 1) * TILE] = tile

    def body(m, block, start, count):
        tile = slice(m * TILE, (m + 1) * TILE)
        queries = q_rows[block].reshape(4 * part_rows, TILE)
        scores = dot(kv_ref[pl.ds(start, count), tile], queries, 1, 1)
        scores = scores + bias_of(limits_ref, block, start, count)
        top = jnp.max(scores, axis=0, keepdims=True)
        shifted = jnp.exp(scores - top)
        total = jnp.sum(shifted, axis=0, keepdims=True)
        result = dot(kv_turned[:, pl.ds(start, count)], shifted.astype(BF16))
        lse_ref[m, pl.ds(block, 1), :] = top + jnp.log(total)
        result = (result / total).T
        for at, part in enumerate(joined(result, True)):
            at = m * 2 * TILE + at * TILE
            out_ref[pl.ds(block * part_rows, part_rows), at : at + TILE] = part.astype(BF16)

    fixed, reach, offset = windows(blocks, 4 * part_rows, head)

    def attend_start(m):
        columns = slice(m * 2 * TILE, (m + 1) * 2 * TILE)
        for slot, part in enumerate(tiles_of(q_ref[:, columns], False)):
            q_rows[:, slot] = (part * BF16(HEAD_DIM**-0.5)).reshape(blocks, part_rows, TILE)
        kv_turned[...] = kv_ref[:, m * TILE : (m + 1) * TILE].astype(F32).T.astype(BF16)
        for block in range(2):
            body(m, block, *fixed[block])

    def attend_middle(m):
        for block in range(2, len(fixed)):
            body(m, block, *fixed[block])

    def attend_end(m):
        @pl.loop(len(fixed), blocks)
        def _(block):
            body(m, block, pl.multiple_of(block * 4 * part_rows + offset, TILE), reach)

    others = {
        "pack": (pack_first, pack_others),
        "norm": norm_first,
        "pairs": pair_weights,
        "keys": make_pairs,
        "kv": give_pairs,
        "kvw": get_pairs,
        "query": make_queries,
        "att0": attend_start,
        "att1": attend_middle,
        "att2": attend_end,
    }
    exchanges = {"tok": arrive, "grad": later_grad}
    for kind, *rest in FRONT_ORDER:
        if kind == "ex":
            exchanges[rest[0]].start()
        elif kind == "exw":
            exchanges[rest[0]].wait()
        elif kind == "end":
            spread.end(rest[0])
        elif kind == "pack":
            others[kind][rest[0]]()
        elif kind in others:
            others[kind](*rest)
        else:
            spread.do(kind, *rest)
            if kind == "bh":
                own[rest[0]].start()
    for part in range(2, 6):
        own[part].wait()
    weights_out.wait()
    for copy in swaps + shares:
        copy.wait_send()


FRONT_PLANES = (2,)
FRONT_SHARES = {3: 0.4, 4: 0.4}
FRONT_ORDER = (
    ("bh", 3), ("bz", 4), ("bh", 4), ("pack", 0), ("bz", 0), ("bz", 1), ("line", 0, 1, 1),
    ("line", 0, 1, -1), ("line", 0, 2, 1), ("bh", 0), ("line", 1, 1, 1), ("pX", 3, 0),
    ("bz", 3), ("line", 1, 1, -1), ("pY", 0, 1), ("line", 0, 2, -1), ("line", 0, 3, 1),
    ("pX", 0, 1), ("ex", "tok"), ("line", 1, 2, 1), ("pX", 4, 0), ("line", 0, 3, -1),
    ("pack", 1), ("bh", 5), ("bh", 2), ("pY", 0, 3), ("pY", 1, 1), ("line", 1, 3, -1),
    ("bh", 1), ("line", 1, 2, -1), ("pX", 1, 1), ("pY", 0, 2), ("pY", 1, 0), ("bz", 5),
    ("pX", 0, 0), ("pY", 0, 0), ("line", 3, 1, -1), ("line", 1, 3, 1), ("pX", 0, 2),
    ("line", 3, 1, 1), ("pX", 5, 0), ("pY", 1, 2), ("co", 0, 1), ("pX", 1, 2), ("co", 0, 0),
    ("pX", 0, 3), ("pX", 1, 0), ("co", 1, 1), ("co", 0, 2), ("pY", 5, 0), ("exw", "tok"),
    ("pY", 4, 0), ("pY", 2, 0), ("norm",), ("co", 0, 3), ("pX", 2, 0), ("pX", 1, 3),
    ("pY", 1, 3), ("line", 3, 2, -1), ("end", 0), ("line", 3, 2, 1), ("pairs",), ("keys",),
    ("kv",), ("co", 1, 0), ("co", 1, 2), ("line", 4, 1, -1), ("co", 1, 3), ("end", 1),
    ("bz", 2), ("co", 4, 0), ("line", 3, 3, -1), ("line", 5, 1, -1), ("query", 0), ("co", 2, 0),
    ("line", 4, 1, 1), ("query", 1), ("query", 2), ("query", 3), ("pY", 3, 1), ("query", 4),
    ("line", 3, 3, 1), ("line", 5, 1, 1), ("line", 4, 2, -1), ("kvw",), ("line", 4, 2, 1),
    ("att0", 0), ("ex", "grad"), ("att1", 0), ("att2", 0), ("att0", 1), ("line", 4, 3, -1),
    ("pX", 3, 3), ("att1", 1), ("line", 5, 2, 1), ("att2", 1), ("att0", 2), ("line", 4, 3, 1),
    ("line", 5, 2, -1), ("att1", 2), ("pX", 3, 2), ("pY", 4, 1), ("att2", 2), ("att0", 3),
    ("att1", 3), ("att2", 3), ("att0", 4), ("att1", 4), ("att2", 4), ("line", 5, 3, -1),
    ("line", 2, 1, -1), ("pY", 5, 1), ("co", 5, 0), ("pX", 3, 1), ("line", 2, 1, 1),
    ("pX", 4, 1), ("pY", 3, 0), ("pY", 3, 2), ("pX", 5, 2), ("pY", 3, 3), ("line", 5, 3, 1),
    ("pX", 4, 3), ("pX", 4, 2), ("pX", 5, 1), ("co", 4, 1), ("pY", 4, 2), ("line", 2, 2, -1),
    ("line", 2, 2, 1), ("pY", 5, 3), ("pY", 4, 3), ("line", 2, 3, 1), ("pX", 5, 3),
    ("pY", 5, 2), ("line", 2, 3, -1), ("co", 3, 0), ("co", 5, 1), ("co", 4, 2), ("co", 3, 1),
    ("co", 4, 3), ("end", 2), ("co", 3, 3), ("co", 3, 2), ("end", 3), ("co", 5, 3),
    ("co", 5, 2), ("end", 4), ("end", 5), ("exw", "grad"),
)


def front(tokens, out_grad, weights, limits, turn, down, up, gain):
    query, keyval, output, gateup, w_down = weights
    seqs, part, width = tokens.shape
    rows, wide = query.shape
    deep = w_down.shape[0]
    blks, heads = lax.axis_size("blk"), lax.axis_size("head")
    narrow = keyval.shape[2]
    mixed = -(-4 * narrow // TILE) * TILE
    double = heads * narrow * 2
    groups = width // (2 * TILE)
    dma = pltpu.SemaphoreType.DMA
    vmem = pl.BlockSpec(memory_space=pltpu.VMEM)
    shape = jax.ShapeDtypeStruct
    return pl.pallas_call(
        functools.partial(front_kernel, blks // 2),
        out_shape=[
            shape((blks * rows, heads * wide + double), BF16),
            shape((blks * rows, heads * wide), BF16),
            shape((2, blks * rows, heads * gateup.shape[2]), BF16),
            shape((blks * deep, heads * wide), BF16),
            shape((seqs, part, width), BF16),
            shape((seqs, part, width), BF16),
            shape((seqs * part, width), BF16),
            shape((seqs * part, 1), F32),
            shape((seqs * part, down.shape[0]), BF16),
            shape((seqs * part, width), BF16),
            shape((seqs, heads * part, double), BF16),
            shape((seqs * part, width), BF16),
            shape((groups, seqs, 2 * TILE), F32),
        ],
        in_specs=[ANYWHERE, ANYWHERE, vmem, vmem, vmem, ANYWHERE] + [vmem] * 6,
        out_specs=[ANYWHERE] * 4 + [vmem, ANYWHERE] + [vmem] * 7,
        scratch_shapes=[
            pltpu.VMEM((rows // 2, wide), BF16),
            pltpu.VMEM((2, rows // 2, narrow), BF16),
            pltpu.VMEM((rows // 2, wide), BF16),
            pltpu.VMEM((deep // 2, wide), BF16),
            pltpu.VMEM((rows // 2, 2 * wide), BF16),
            pltpu.VMEM((rows // 2, mixed), BF16),
            pltpu.VMEM((rows // 2, 2 * wide), BF16),
            pltpu.VMEM((deep // 2, 2 * wide), BF16),
            pltpu.VMEM((blks * rows, heads // 2 * mixed), BF16),
            pltpu.VMEM((blks * rows, heads * wide + double), BF16),
            pltpu.VMEM((seqs, 4, part, TILE), BF16),
            pltpu.VMEM((TILE, seqs * heads * part), BF16),
            dma((4,)),
            dma((4,)),
            dma((9,)),
            dma((2, seqs - 1)),
            dma((2, seqs - 1)),
            dma((3,)),
            dma((3,)),
            *Spread.semaphores(6, blks // 2),
        ],
        compiler_params=pltpu.CompilerParams(
            collective_id=0, has_side_effects=True, vmem_limit_bytes=56 << 20
        ),
    )(
        tokens.reshape(seqs * part, width),
        out_grad.reshape(seqs * part, width),
        query,
        keyval,
        output,
        gateup,
        w_down,
        limits,
        turn,
        down,
        up,
        gain.reshape(1, -1),
    )


def feed_kernel(
    attended_ref,
    flat_ref,
    grad_ref,
    w_output_ref,
    w_gateup_ref,
    w_down_ref,
    d_output_ref,
    u_output_ref,
    d_gateup_ref,
    u_gateup_ref,
    d_ffdown_ref,
    u_ffdown_ref,
    gain_ref,
    output_ref,
    grad_middle_ref,
    grad_mixed_ref,
    terms_ref,
    middle,
    normed,
    result,
    grad_normed,
    low_output,
    low_gate,
    low_up,
    low_down,
    grad_low_down,
    grad_low_gate,
    grad_low_up,
):
    step = pl.program_id(0)
    rows, width = attended_ref.shape
    chunk = w_down_ref.shape[0]
    hidden = chunk * pl.num_programs(0)

    @pl.when(step == 0)
    def _():
        attended = attended_ref[...]
        low_output[...] = lowered(attended, d_output_ref[...])
        branch = dot(attended, w_output_ref[...])
        branch = branch + ADAPTER_SCALE * dot(low_output[...], u_output_ref[...])
        middle[...] = flat_ref[...].astype(F32) + branch
        normed[...] = norm_of(middle[...], gain_ref[...])[0]
        low_gate[...] = lowered(normed[...], d_gateup_ref[0])
        low_up[...] = lowered(normed[...], d_gateup_ref[1])
        grad_low_down[...] = (ADAPTER_SCALE * dot(grad_ref[...], u_ffdown_ref[...], 1, 1)).astype(
            BF16
        )
        for ref in (result, grad_normed, low_down, grad_low_gate, grad_low_up):
            ref[...] = jnp.zeros_like(ref)

    inputs = normed[...]
    w_gate, w_up = w_gateup_ref[0], w_gateup_ref[1]
    u_gate, u_up = u_gateup_ref[0], u_gateup_ref[1]
    gate = dot(inputs, w_gate) + ADAPTER_SCALE * dot(low_gate[...], u_gate)
    upward = dot(inputs, w_up) + ADAPTER_SCALE * dot(low_up[...], u_up)
    grad_act = dot(grad_ref[...], w_down_ref[...], 1, 1) + dot(grad_low_down[...], d_ffdown_ref[...])
    sigma = 1.0 / (1.0 + jnp.exp(-gate))
    silu = gate * sigma
    activated = (silu * upward).astype(BF16)
    grad_gate = (grad_act * upward * (sigma * (1.0 + gate * (1.0 - sigma)))).astype(BF16)
    grad_up = (grad_act * silu).astype(BF16)
    result[...] += dot(activated, w_down_ref[...])
    grad_normed[...] += dot(grad_gate, w_gate, 1, 1) + dot(grad_up, w_up, 1, 1)
    low_down[...] += dot(activated, d_ffdown_ref[...], 1, 1)
    grad_low_gate[...] += dot(grad_gate, u_gate, 1, 1)
    grad_low_up[...] += dot(grad_up, u_up, 1, 1)
    at = 4 * width + step * chunk
    spot = pl.ds(pl.multiple_of(at, TILE), chunk)
    terms_ref[:, spot] = ADAPTER_SCALE * dot(low_gate[...], grad_gate, 0, 0)
    spot = pl.ds(pl.multiple_of(at + hidden, TILE), chunk)
    terms_ref[:, spot] = ADAPTER_SCALE * dot(low_up[...], grad_up, 0, 0)
    spot = pl.ds(pl.multiple_of(at + 2 * hidden, TILE), chunk)
    terms_ref[:, spot] = dot(grad_low_down[...], activated, 0, 0)

    @pl.when(step == pl.num_programs(0) - 1)
    def _():
        low = low_down[...].astype(BF16)
        branch = result[...] + ADAPTER_SCALE * dot(low, u_ffdown_ref[...])
        output_ref[...] = (middle[...] + branch).astype(BF16)
        at = 4 * width + 3 * hidden
        terms_ref[:, at : at + width] = ADAPTER_SCALE * dot(low, grad_ref[...], 0, 0)
        if at + width < terms_ref.shape[1]:
            terms_ref[:, at + width :] = jnp.zeros(
                (terms_ref.shape[0], terms_ref.shape[1] - at - width), F32
            )
        low_g = (ADAPTER_SCALE * grad_low_gate[...]).astype(BF16)
        low_u = (ADAPTER_SCALE * grad_low_up[...]).astype(BF16)
        terms_ref[:, 2 * width : 3 * width] = dot(low_g, normed[...], 0, 0)
        terms_ref[:, 3 * width : 4 * width] = dot(low_u, normed[...], 0, 0)
        grad = grad_normed[...] + dot(low_g, d_gateup_ref[0]) + dot(low_u, d_gateup_ref[1])
        inverse = norm_of(middle[...], gain_ref[...])[1]
        grad = grad_ref[...].astype(F32) + norm_back(middle[...], inverse, gain_ref[...], grad)
        grad_middle_ref[...] = grad
        grad = grad.astype(BF16)
        low = (ADAPTER_SCALE * dot(grad, u_output_ref[...], 1, 1)).astype(BF16)
        mixed = dot(grad, w_output_ref[...], 1, 1) + dot(low, d_output_ref[...])
        grad_mixed_ref[...] = mixed.astype(BF16)
        terms_ref[:, :width] = dot(low, attended_ref[...], 0, 0)
        terms_ref[:, width : 2 * width] = ADAPTER_SCALE * dot(low_output[...], grad, 0, 0)


def feed(attended, flat, grad, w_output, w_gateup, w_down, factors, gain):
    rows, width = flat.shape
    hidden = w_down.shape[0]
    chunk = 4 * TILE
    rank = factors[0].shape[0]
    total = 5 * width + 3 * hidden
    total += -total % (2 * 4 * TILE)
    d_output, u_output, d_gateup, u_gateup, d_ffdown, u_ffdown = factors
    shape = jax.ShapeDtypeStruct

    def whole(array):
        return pl.BlockSpec(array.shape, lambda f: (0,) * len(array.shape))

    gain = gain.reshape(1, -1)
    outs = [
        shape((rows, width), BF16),
        shape((rows, width), F32),
        shape((rows, width), BF16),
        shape((rank, total), F32),
    ]
    return pl.pallas_call(
        feed_kernel,
        grid=(hidden // chunk,),
        out_shape=outs,
        in_specs=[
            whole(attended),
            whole(flat),
            whole(grad),
            whole(w_output),
            pl.BlockSpec((2, width, chunk), lambda f: (0, 0, f)),
            pl.BlockSpec((chunk, width), lambda f: (f, 0)),
            whole(d_output),
            whole(u_output),
            whole(d_gateup),
            pl.BlockSpec((2, rank, chunk), lambda f: (0, 0, f)),
            pl.BlockSpec((rank, chunk), lambda f: (0, f)),
            whole(u_ffdown),
            whole(gain),
        ],
        out_specs=[whole(out) for out in outs],
        scratch_shapes=[
            pltpu.VMEM((rows, width), F32),
            pltpu.VMEM((rows, width), BF16),
            pltpu.VMEM((rows, width), F32),
            pltpu.VMEM((rows, width), F32),
            pltpu.VMEM((rows, rank), BF16),
            pltpu.VMEM((rows, rank), BF16),
            pltpu.VMEM((rows, rank), BF16),
            pltpu.VMEM((rows, rank), F32),
            pltpu.VMEM((rows, rank), BF16),
            pltpu.VMEM((rows, rank), F32),
            pltpu.VMEM((rows, rank), F32),
        ],
        compiler_params=pltpu.CompilerParams(vmem_limit_bytes=56 << 20),
    )(
        attended,
        flat,
        grad,
        w_output,
        w_gateup,
        w_down,
        d_output,
        u_output,
        d_gateup,
        u_gateup,
        d_ffdown,
        u_ffdown,
        gain,
    )


def by_sequence(
    tokens,
    attn_gain,
    ffn_gain,
    query_weight,
    keyval_weight,
    output_weight,
    gateup_weight,
    down_weight,
    query_down,
    query_up,
    keyval_down,
    keyval_up,
    output_down,
    output_up,
    gateup_down,
    gateup_up,
    ffdown_down,
    ffdown_up,
    segment_ids,
    real_mask,
    adapter_index,
    out_grad,
):
    seqs, part, width = tokens.shape
    groups = lax.axis_size("head")
    seq, head_pos = lax.axis_index("blk"), lax.axis_index("head")
    rows = seqs * part
    span = groups * part
    adapter = adapter_index[seq]

    d_query = query_down.swapaxes(1, 2)[adapter]
    d_keyval = keyval_down.swapaxes(2, 3)[adapter]
    d_output = output_down.swapaxes(1, 2)[adapter]
    d_gateup = gateup_down.swapaxes(2, 3)[adapter]
    d_ffdown = ffdown_down.swapaxes(1, 2)[adapter]
    u_query, u_keyval, u_output = query_up[adapter], keyval_up[adapter], output_up[adapter]
    u_gateup, u_ffdown = gateup_up[adapter], ffdown_up[adapter]
    rank = d_query.shape[0]

    def in_turn(first, second):
        cut = (first.shape[0], KV_HEADS, HEAD_DIM)
        both = jnp.concatenate([first.reshape(cut), second.reshape(cut)], axis=2)
        return both.reshape(first.shape[0], 2 * first.shape[1])

    nil = jnp.zeros_like(u_keyval[0])
    u_keys, u_values = in_turn(u_keyval[0], nil), in_turn(nil, u_keyval[1])
    u_qkv = jnp.concatenate(
        [
            jnp.pad(u_query, ((0, 0), (0, u_keys.shape[1]))),
            jnp.pad(jnp.concatenate([u_keys, u_values], axis=0), ((0, 0), (width, 0))),
        ],
        axis=0,
    )
    d_qkv = jnp.concatenate([d_query, d_keyval[0], d_keyval[1]], axis=0)

    position = (
        jnp.arange(seqs, dtype=jnp.int32)[:, None] * span
        + head_pos * part
        + jnp.arange(part, dtype=jnp.int32)[None, :]
    )
    length = jnp.sum(real_mask[seq])
    segment = segment_ids[seq]
    mine = jnp.take(segment, position)
    first = jnp.sum((segment[None, None, :] < mine[:, :, None]).astype(jnp.int32), axis=2)
    least = jnp.maximum(position - (WINDOW - 1), first)
    most = jnp.minimum(position, length - 1)
    limits = jnp.stack([least, most, position])
    limits = jnp.concatenate([limits, limits], axis=2)

    flat_pos = position.reshape(rows)
    freqs = ROPE_BASE ** (
        -(jnp.arange(HEAD_DIM // 2, dtype=F32) * 2.0) / HEAD_DIM
    )
    angles = flat_pos.astype(F32)[:, None] * freqs[None, :]
    cosine, sine = jnp.cos(angles), jnp.sin(angles)
    turn = jnp.stack(
        [jnp.tile(cosine, (1, 4)), jnp.tile(jnp.concatenate([-sine, sine], axis=1), (1, 2))]
    )

    (
        w_qkv,
        w_output,
        w_gateup,
        w_down,
        flat,
        grad_flat,
        normed,
        inverse1,
        low_qkv,
        queries,
        pairs,
        attended,
        lse,
    ) = front(
        tokens,
        out_grad,
        (query_weight, keyval_weight, output_weight, gateup_weight, down_weight),
        limits,
        turn,
        d_qkv,
        u_qkv,
        attn_gain,
    )
    flat, grad_flat = flat.reshape(rows, width), grad_flat.reshape(rows, width)
    pairs = pairs.reshape(seqs * span, pairs.shape[2])
    output, grad_middle, grad_mixed, early = feed(
        attended,
        flat,
        grad_flat,
        w_output,
        w_gateup,
        w_down,
        (d_output, u_output, d_gateup, u_gateup, d_ffdown, u_ffdown),
        ffn_gain,
    )
    hidden = w_down.shape[0]
    sizes = [width] * 4 + [hidden] * 3 + [width]
    grad_qkv, output, early = attend_back(
        limits, queries, pairs, lse, grad_mixed, turn, output, early
    )
    input_grad, late = first_back(
        grad_qkv, w_qkv, d_qkv, u_qkv, normed, low_qkv, grad_middle, flat, inverse1, attn_gain
    )
    adapters = jnp.arange(query_down.shape[0], dtype=jnp.int32)
    holder = jnp.argmax(adapter_index[None, :] == adapters[:, None], axis=1).astype(jnp.int32)
    found = placed(holder, early, late, sizes, width)
    return (
        output,
        input_grad,
        found[0].swapaxes(1, 2),
        found[1],
        found[2].swapaxes(2, 3),
        found[3],
        found[4].swapaxes(1, 2),
        found[5],
        found[6].swapaxes(2, 3),
        found[7],
        found[8].swapaxes(1, 2),
        found[9],
    )


def solution(mesh):
    in_specs = (
        P(None, ("blk", "head"), None),
        P(),
        P(),
        P("blk", "head"),
        P(None, "blk", "head"),
        P("blk", "head"),
        P(None, "blk", "head"),
        P("blk", "head"),
        P(),
        P(),
        P(),
        P(),
        P(),
        P(),
        P(),
        P(),
        P(),
        P(),
        P(),
        P(),
        P(),
        P(None, ("blk", "head"), None),
    )
    out_specs = (
        P(None, ("blk", "head"), None),
        P(None, ("blk", "head"), None),
        P(),
        P(),
        P(),
        P(),
        P(),
        P(),
        P(),
        P(),
        P(),
        P(),
    )

    def chosen(tokens, *rest):
        if mesh.shape["blk"] == tokens.shape[0] == 8 and mesh.shape["head"] == 4:
            return by_sequence(tokens, *rest)
        return on_device(tokens, *rest)

    return jax.shard_map(
        chosen, mesh=mesh, in_specs=in_specs, out_specs=out_specs, check_vma=False
    )
```

```python
import functools
import math

import jax
import jax.numpy as jnp
import numpy as np
from jax import lax
from jax.experimental import pallas as pl
from jax.experimental.pallas import tpu as pltpu
from jax.sharding import PartitionSpec as P

HEADS = 20
KV_HEADS = 5
HEAD_DIM = 64
WINDOW = 1024


EPSILON = 1e-05
ROPE_BASE = 10000.0
ADAPTER_SCALE = 2.0
MASKED = -1e30


def passed_along(value, axis, steps):
    count = lax.axis_size(axis)
    initial, last = (max(0, -steps), min(count, count - steps))
    return lax.ppermute(value, axis, [(source, source + steps) for source in range(initial, last)])


def rms_scale(values, gain):
    return values * lax.rsqrt(jnp.mean(values * values, axis=-1, keepdims=True) + EPSILON) * gain


def rotate(values, positions, sign):
    half = values.shape[-1] // 2
    freqs = ROPE_BASE ** (-(jnp.arange(half, dtype=jnp.float32) * 2.0) / values.shape[-1])
    angles = positions.astype(jnp.float32)[:, None] * freqs[None, :]
    cosine = jnp.cos(angles)[:, None, :]
    sine = sign * jnp.sin(angles)[:, None, :]
    first = values[..., :half]
    second = values[..., half:]
    return jnp.concatenate(
        [first * cosine - second * sine, second * cosine + first * sine], axis=-1
    )


def gated(gate, upward):
    return jax.nn.silu(gate) * upward


def project(inputs, weight, down, up):
    lowered = jnp.einsum("sci,sir->scr", inputs, down, preferred_element_type=jnp.float32).astype(
        jnp.bfloat16
    )
    extra = ADAPTER_SCALE * jnp.einsum(
        "scr,sro->sco", lowered, up, preferred_element_type=jnp.float32
    )
    return (
        jnp.einsum("sci,io->sco", inputs, weight, preferred_element_type=jnp.float32) + extra,
        lowered,
    )


def project_back(inputs, lowered, grad_out, weight, down, up):
    grad_up = ADAPTER_SCALE * jnp.einsum(
        "scr,sco->sro", lowered, grad_out, preferred_element_type=jnp.float32
    )
    grad_low = (
        ADAPTER_SCALE * jnp.einsum("sco,sro->scr", grad_out, up, preferred_element_type=jnp.float32)
    ).astype(jnp.bfloat16)
    grad_down = jnp.einsum("sci,scr->sir", inputs, grad_low, preferred_element_type=jnp.float32)
    grad_in = jnp.einsum("sco,io->sci", grad_out, weight, preferred_element_type=jnp.float32)
    grad_in = grad_in + jnp.einsum(
        "scr,sir->sci", grad_low, down, preferred_element_type=jnp.float32
    )
    return (grad_in, grad_down, grad_up)


def on_device(
    tokens,
    attn_gain,
    ffn_gain,
    query_weight,
    keyval_weight,
    output_weight,
    gateup_weight,
    down_weight,
    query_down,
    query_up,
    keyval_down,
    keyval_up,
    output_down,
    output_up,
    gateup_down,
    gateup_up,
    ffdown_down,
    ffdown_up,
    segment_ids,
    real_mask,
    adapter_index,
    out_grad,
):
    seqs, per_device, width = tokens.shape
    groups = lax.axis_size("head")
    head_pos = lax.axis_index("head")
    blk_pos = lax.axis_index("blk")
    span = groups * per_device
    heads = HEADS
    head_dim = HEAD_DIM
    kv_heads = KV_HEADS
    local_heads = heads // groups
    share = heads // kv_heads
    reach = (WINDOW - 2) // span + 1
    scale = 1.0 / math.sqrt(head_dim)
    rows_a, rows_b, rows_c, rows_d, rows_e = (
        lax.all_gather(query_weight, "blk", axis=0, tiled=True),
        lax.all_gather(keyval_weight, "blk", axis=1, tiled=True),
        lax.all_gather(output_weight, "blk", axis=0, tiled=True),
        lax.all_gather(gateup_weight, "blk", axis=1, tiled=True),
        lax.all_gather(down_weight, "blk", axis=0, tiled=True),
    )
    w_query, w_keyval, w_output, w_gateup, w_down = (
        lax.all_gather(rows_a, "head", axis=1, tiled=True),
        lax.all_gather(rows_b, "head", axis=2, tiled=True),
        lax.all_gather(rows_c, "head", axis=1, tiled=True),
        lax.all_gather(rows_d, "head", axis=2, tiled=True),
        lax.all_gather(rows_e, "head", axis=1, tiled=True),
    )
    down_query = query_down[adapter_index]
    up_query = query_up[adapter_index]
    down_keyval = keyval_down[adapter_index]
    up_keyval = keyval_up[adapter_index]
    down_output = output_down[adapter_index]
    up_output = output_up[adapter_index]
    down_gateup = gateup_down[adapter_index]
    up_gateup = gateup_up[adapter_index]
    down_ffdown = ffdown_down[adapter_index]
    up_ffdown = ffdown_up[adapter_index]

    def first_norm(values):
        return rms_scale(values, attn_gain)

    def second_norm(values):
        return rms_scale(values, ffn_gain)

    flat = tokens.astype(jnp.float32)
    normed_full, first_norm_back = jax.vjp(first_norm, flat)
    normed = normed_full.astype(jnp.bfloat16)
    queries_pre, low_query = project(normed, w_query, down_query, up_query)
    keys_pre, low_key = project(normed, w_keyval[0], down_keyval[:, 0], up_keyval[:, 0])
    values_pre, low_value = project(normed, w_keyval[1], down_keyval[:, 1], up_keyval[:, 1])
    token_pos = (blk_pos * groups + head_pos) * per_device + jnp.arange(per_device, dtype=jnp.int32)
    queries = rotate(queries_pre.reshape(seqs, per_device, heads, head_dim), token_pos, 1.0).astype(
        jnp.bfloat16
    )
    keys = rotate(keys_pre.reshape(seqs, per_device, kv_heads, head_dim), token_pos, 1.0).astype(
        jnp.bfloat16
    )
    values = values_pre.reshape(seqs, per_device, kv_heads, head_dim).astype(jnp.bfloat16)
    owner = np.array(
        [
            [(group * local_heads + slot) // share for slot in range(local_heads)]
            for group in range(groups)
        ]
    )
    slot_of = jnp.arange(local_heads, dtype=jnp.int32)
    sender = jnp.asarray(
        (owner[:, :, None] == np.arange(kv_heads)[None, None, :]).astype(np.float32), jnp.bfloat16
    )
    spread = (slot_of[:, None] == jnp.arange(local_heads, dtype=jnp.int32)[None, :]).astype(
        jnp.bfloat16
    )
    pair = jnp.stack([keys, values], axis=3)
    outgoing = jnp.einsum(
        "sckxd,gmk->scgmxd", pair, sender, preferred_element_type=jnp.float32
    ).astype(jnp.bfloat16)
    outgoing = outgoing.reshape(seqs, per_device, groups, local_heads * 2 * head_dim)
    query_send = queries.reshape(seqs, per_device, groups, local_heads * head_dim)
    query_here, pair_here = (
        lax.all_to_all(query_send, "head", split_axis=2, concat_axis=1, tiled=True),
        lax.all_to_all(outgoing, "head", split_axis=2, concat_axis=1, tiled=True),
    )
    query_here = query_here.reshape(seqs, span, local_heads, head_dim)
    pair_here = pair_here.reshape(seqs, span, local_heads, 2, head_dim)
    received = [pair_here]
    moving = pair_here
    for hop in range(reach):
        moving = passed_along(moving, "blk", 1)
        received.append(moving)
    window_pairs = jnp.stack(received, axis=1)
    query_pos = blk_pos * span + jnp.arange(span, dtype=jnp.int32)
    key_pos = (blk_pos - jnp.arange(reach + 1, dtype=jnp.int32))[:, None] * span + jnp.arange(
        span, dtype=jnp.int32
    )[None, :]
    safe_pos = jnp.clip(key_pos, 0, segment_ids.shape[1] - 1)
    query_segment = lax.dynamic_slice_in_dim(segment_ids, blk_pos * span, span, 1)
    key_segment = segment_ids[:, safe_pos]
    key_real = real_mask[:, safe_pos]
    distance = query_pos[:, None, None] - key_pos[None]
    allowed = (key_pos[None] >= 0) & (distance >= 0) & (distance < WINDOW)
    allowed = allowed & (query_segment[:, :, None, None] == key_segment[:, None])
    allowed = allowed & ((key_real[:, None] == 1) | (distance[None] == 0))
    batch = 1
    target = max(1, 512 // span)
    for option in range(1, seqs + 1):
        if seqs % option == 0 and option <= target:
            batch = option
    count = seqs // batch

    def grouped(array):
        return array.reshape((count, batch) + array.shape[1:])

    def scores_of(query_part, pair_part, allowed_part):
        keys_wide = jnp.einsum(
            "gjlmd,hm->gjlhd", pair_part[:, :, :, :, 0], spread, preferred_element_type=jnp.float32
        ).astype(jnp.bfloat16)
        values_wide = jnp.einsum(
            "gjlmd,hm->gjlhd", pair_part[:, :, :, :, 1], spread, preferred_element_type=jnp.float32
        ).astype(jnp.bfloat16)
        raw = (
            jnp.einsum(
                "gqhd,gjlhd->ghqjl", query_part, keys_wide, preferred_element_type=jnp.float32
            )
            * scale
        )
        raw = jnp.where(allowed_part[:, None], raw, MASKED)
        return (raw, keys_wide, values_wide)

    def attend(pieces):
        query_part, pair_part, allowed_part = pieces
        raw, keys_wide, values_wide = scores_of(query_part, pair_part, allowed_part)
        top = jnp.max(raw, axis=(3, 4), keepdims=True)
        shifted = jnp.exp(raw - top)
        total = jnp.sum(shifted, axis=(3, 4), keepdims=True)
        probs_low = (shifted / total).astype(jnp.bfloat16)
        result = jnp.einsum(
            "ghqjl,gjlhd->gqhd", probs_low, values_wide, preferred_element_type=jnp.float32
        )
        return (result.astype(jnp.bfloat16), top + jnp.log(total))

    attended, logsum = lax.map(
        attend, (grouped(query_here), grouped(window_pairs), grouped(allowed))
    )
    mixed = lax.all_to_all(
        attended.reshape(seqs, span, local_heads * head_dim),
        "head",
        split_axis=1,
        concat_axis=2,
        tiled=True,
    )
    branch_attn, low_output = project(mixed, w_output, down_output, up_output)
    middle = flat + branch_attn
    normed2_full, second_norm_back = jax.vjp(second_norm, middle)
    normed2 = normed2_full.astype(jnp.bfloat16)
    gate, low_gate = project(normed2, w_gateup[0], down_gateup[:, 0], up_gateup[:, 0])
    upward, low_upward = project(normed2, w_gateup[1], down_gateup[:, 1], up_gateup[:, 1])
    activated_full, gated_back = jax.vjp(gated, gate, upward)
    activated = activated_full.astype(jnp.bfloat16)
    branch_ffn, low_ffdown = project(activated, w_down, down_ffdown, up_ffdown)
    output = (middle + branch_ffn).astype(jnp.bfloat16)
    grad_activated, gd_ffdown, gu_ffdown = project_back(
        activated, low_ffdown, out_grad, w_down, down_ffdown, up_ffdown
    )
    grad_gate, grad_upward = gated_back(grad_activated)
    grad_in_gate, gd_gate, gu_gate = project_back(
        normed2,
        low_gate,
        grad_gate.astype(jnp.bfloat16),
        w_gateup[0],
        down_gateup[:, 0],
        up_gateup[:, 0],
    )
    grad_in_up, gd_up, gu_up = project_back(
        normed2,
        low_upward,
        grad_upward.astype(jnp.bfloat16),
        w_gateup[1],
        down_gateup[:, 1],
        up_gateup[:, 1],
    )
    grad_middle = out_grad.astype(jnp.float32) + second_norm_back(grad_in_gate + grad_in_up)[0]
    grad_mixed, gd_output, gu_output = project_back(
        mixed, low_output, grad_middle.astype(jnp.bfloat16), w_output, down_output, up_output
    )
    grad_send = grad_mixed.astype(jnp.bfloat16).reshape(
        seqs, per_device, groups, local_heads * head_dim
    )
    grad_here = lax.all_to_all(grad_send, "head", split_axis=2, concat_axis=1, tiled=True).reshape(
        seqs, span, local_heads, head_dim
    )
    spread_full = spread.astype(jnp.float32)

    def attend_back(pieces):
        query_part, pair_part, allowed_part, logsum_part, grad_part = pieces
        raw, keys_wide, values_wide = scores_of(query_part, pair_part, allowed_part)
        probs = jnp.exp(raw - logsum_part)
        probs_low = probs.astype(jnp.bfloat16)
        grad_probs = jnp.einsum(
            "gqhd,gjlhd->ghqjl", grad_part, values_wide, preferred_element_type=jnp.float32
        )
        inner = jnp.sum(probs * grad_probs, axis=(3, 4), keepdims=True)
        grad_raw = (probs * (grad_probs - inner)).astype(jnp.bfloat16)
        grad_query = scale * jnp.einsum(
            "ghqjl,gjlhd->gqhd", grad_raw, keys_wide, preferred_element_type=jnp.float32
        )
        grad_keys = scale * jnp.einsum(
            "ghqjl,gqhd->gjlhd", grad_raw, query_part, preferred_element_type=jnp.float32
        )
        grad_values = jnp.einsum(
            "ghqjl,gqhd->gjlhd", probs_low, grad_part, preferred_element_type=jnp.float32
        )
        both = jnp.stack([grad_keys, grad_values], axis=4)
        folded = jnp.einsum("gjlhxd,hm->gjlmxd", both, spread_full, precision=lax.Precision.HIGHEST)
        return (grad_query, folded)

    grad_query, grad_pairs = lax.map(
        attend_back,
        (grouped(query_here), grouped(window_pairs), grouped(allowed), logsum, grouped(grad_here)),
    )
    grad_pairs = grad_pairs.reshape(seqs, reach + 1, span, local_heads, 2, head_dim)
    carried = grad_pairs[:, reach]
    for hop in range(reach - 1, -1, -1):
        carried = (
            passed_along(carried.astype(jnp.bfloat16), "blk", -1).astype(carried.dtype)
            + grad_pairs[:, hop]
        )
    grad_query = rotate(grad_query.reshape(seqs, span, local_heads, head_dim), query_pos, -1.0)
    grad_query = grad_query.astype(jnp.bfloat16).reshape(seqs, span, local_heads * head_dim)
    grad_queries_pre = lax.all_to_all(grad_query, "head", split_axis=1, concat_axis=2, tiled=True)
    grad_pair_tok = lax.all_to_all(
        carried.reshape(seqs, span, local_heads * 2 * head_dim).astype(jnp.bfloat16),
        "head",
        split_axis=1,
        concat_axis=2,
        tiled=True,
    ).astype(jnp.float32)
    grad_pair_tok = grad_pair_tok.reshape(seqs, per_device, groups, local_heads, 2, head_dim)
    grad_pair_heads = jnp.einsum(
        "scgmxd,gmk->sckxd",
        grad_pair_tok,
        sender.astype(jnp.float32),
        precision=lax.Precision.HIGHEST,
    )
    grad_keys_pre = (
        rotate(grad_pair_heads[:, :, :, 0], token_pos, -1.0)
        .astype(jnp.bfloat16)
        .reshape(seqs, per_device, kv_heads * head_dim)
    )
    grad_values_pre = (
        grad_pair_heads[:, :, :, 1]
        .astype(jnp.bfloat16)
        .reshape(seqs, per_device, kv_heads * head_dim)
    )
    grad_in_query, gd_query, gu_query = project_back(
        normed, low_query, grad_queries_pre, w_query, down_query, up_query
    )
    grad_in_key, gd_key, gu_key = project_back(
        normed, low_key, grad_keys_pre, w_keyval[0], down_keyval[:, 0], up_keyval[:, 0]
    )
    grad_in_value, gd_value, gu_value = project_back(
        normed, low_value, grad_values_pre, w_keyval[1], down_keyval[:, 1], up_keyval[:, 1]
    )
    grad_normed = grad_in_query + grad_in_key + grad_in_value
    input_grad = (grad_middle + first_norm_back(grad_normed)[0]).astype(jnp.bfloat16)
    chooser = (
        adapter_index[:, None] == jnp.arange(query_down.shape[0], dtype=jnp.int32)[None, :]
    ).astype(jnp.float32)

    def per_adapter(per_sequence):
        return jnp.einsum("sa,s...->a...", chooser, per_sequence, precision=lax.Precision.HIGHEST)

    sums = lax.psum(
        (
            per_adapter(gd_query),
            per_adapter(gu_query),
            per_adapter(jnp.stack([gd_key, gd_value], axis=1)),
            per_adapter(jnp.stack([gu_key, gu_value], axis=1)),
            per_adapter(gd_output),
            per_adapter(gu_output),
            per_adapter(jnp.stack([gd_gate, gd_up], axis=1)),
            per_adapter(jnp.stack([gu_gate, gu_up], axis=1)),
            per_adapter(gd_ffdown),
            per_adapter(gu_ffdown),
        ),
        ("blk", "head"),
    )
    return (
        output,
        input_grad,
        sums[0],
        sums[1],
        sums[2],
        sums[3],
        sums[4],
        sums[5],
        sums[6],
        sums[7],
        sums[8],
        sums[9],
    )


MESH = pl.DeviceIdType.MESH
F32 = jnp.float32
BF16 = jnp.bfloat16
TILE = 128
ANYWHERE = pl.BlockSpec(memory_space=pl.ANY)


def dot(left, right, left_dim=1, right_dim=0):
    return lax.dot_general(
        left, right, (((left_dim,), (right_dim,)), ((), ())), preferred_element_type=F32
    )


def place():
    blk, head = lax.axis_index("blk"), lax.axis_index("head")
    return blk // 2, blk % 2, head // 2, head % 2


def device(z, x, y, core):
    return (z * 2 + x, y * 2 + core)


FLIPS = ((0, 0), (0, 1), (1, 0), (1, 1))
BZ, BH, LINE, PY, PX, CO = range(6)
END, EX, EXW, PACK, NORM, PAIRS, KEYS, GIVE, GET, QUERY, ATT0, ATT1, ATT2, OUT, FEED, LAST = range(6, 22)
TOKENS, GRADS = range(2)


def remote(source, target, out, into, other):
    return pltpu.make_async_remote_copy(
        src_ref=source,
        dst_ref=target,
        send_sem=out,
        recv_sem=into,
        device_id=other,
        device_id_type=MESH,
    )


class Spread:
    def __init__(self, sources, target, lines, sems, planes=(), shares=None):
        self.sources, self.target, self.lines = sources, target, lines
        self.planes, self.shares = planes, shares or {}
        self.z, self.x, self.y, self.core = place()
        self.z_in, self.x_in, self.y_in, self.d_in, self.c_in = sems[:5]
        self.z_out, self.x_out, self.y_out, self.d_out, self.c_out = sems[5:10]

    @staticmethod
    def semaphores(parts, lines):
        dma = pltpu.SemaphoreType.DMA
        return [
            dma((parts, lines, 4)),
            dma((parts, lines)),
            dma((parts, lines)),
            dma((parts, lines, 2)),
            dma((parts, lines, 4)),
            dma((parts, 2, lines, 4)),
            dma((parts, lines)),
            dma((parts, lines)),
            dma((parts, lines, 2)),
            dma((parts, lines, 4)),
        ]

    def inside(self, z):
        return (z >= 0) & (z < self.lines)

    def slot(self, part, z, flip_x=0, flip_y=0):
        return self.target(part, z, (self.x + flip_x) % 2, (self.y + flip_y) % 2, self.core)

    def along_z(self, part, source, z, side, flip_x=0, flip_y=0):
        which = flip_x * 2 + flip_y
        return remote(
            source,
            self.slot(part, z, flip_x, flip_y),
            self.z_out.at[part, (side + 1) // 2, z, which],
            self.z_in.at[part, z, which],
            device(self.z + side, self.x, self.y, self.core),
        )

    def along_x(self, part, source, z):
        return remote(
            source,
            self.slot(part, z),
            self.x_out.at[part, z],
            self.x_in.at[part, z],
            device(self.z, 1 - self.x, self.y, self.core),
        )

    def along_y(self, part, source, z):
        return remote(
            source,
            self.slot(part, z),
            self.y_out.at[part, z],
            self.y_in.at[part, z],
            device(self.z, self.x, 1 - self.y, self.core),
        )

    def across(self, part, source, z, flip_x, flip_y):
        which = flip_x * 2 + flip_y
        return remote(
            source,
            self.slot(part, z, flip_x, flip_y),
            self.c_out.at[part, z, which],
            self.c_in.at[part, z, which],
            device(self.z, self.x, self.y, 1 - self.core),
        )

    def piece(self, part, ref, which):
        if len(ref.shape) == 3:
            return ref.at[pl.ds(which, 1)]
        if ref.shape[0] < 32:
            size = ref.shape[1] // 2
            return ref.at[:, pl.ds(which * size, size)]
        count = ref.shape[0]
        first = int(count * self.shares.get(part, 0.5) + 15) // 16 * 16
        return ref.at[pl.ds(0, first)] if which == 0 else ref.at[pl.ds(first, count - first)]

    def diagonal(self, part, z, which):
        if which == 0:
            ref = self.slot(part, z, 0, 1)
            other = device(self.z, 1 - self.x, self.y, self.core)
        else:
            ref = self.slot(part, z, 1, 0)
            other = device(self.z, self.x, 1 - self.y, self.core)
        ref = self.piece(part, ref, which)
        return remote(ref, ref, self.d_out.at[part, z, which], self.d_in.at[part, z, which], other)

    def arrived(self, ref, out, into):
        remote(ref, ref, out, into, device(self.z, self.x, self.y, 1 - self.core)).wait_recv()

    def toward(self, part, source, z, flip_x, flip_y, sides=(1, -1)):
        for side in sides:

            @pl.when(self.inside(self.z + side))
            def _():
                self.along_z(part, source, z, side, flip_x, flip_y).start()

    def hand_on(self, part, source, z):
        self.along_x(part, source, z).start()
        self.along_y(part, source, z).start()
        self.across(part, source, z, 0, 0).start()

    def begin_line(self, part):
        self.toward(part, self.sources[part], self.z, 0, 0)

    def begin_plane(self, part):
        self.hand_on(part, self.sources[part], self.z)

    def line_step(self, part, distance, side):
        z = self.z - side * distance

        @pl.when(self.inside(z))
        def _():
            for flip_x, flip_y in FLIPS if part in self.planes else FLIPS[:1]:
                ref = self.slot(part, z, flip_x, flip_y)
                which = flip_x * 2 + flip_y
                self.arrived(ref, self.z_out.at[part, 0, z, which], self.z_in.at[part, z, which])
                self.toward(part, ref, z, flip_x, flip_y, (side,))
                if part in self.planes:
                    self.across(part, ref, z, flip_x, flip_y).start()
            if part not in self.planes:
                self.hand_on(part, ref, z)

    def y_step(self, part, z):
        ref = self.slot(part, z, 0, 1)
        self.arrived(ref, self.y_out.at[part, z], self.y_in.at[part, z])
        self.diagonal(part, z, 0).start()
        self.across(part, ref, z, 0, 1).start()
        if part in self.planes:
            self.toward(part, ref, z, 0, 1)

    def x_step(self, part, z):
        ref = self.slot(part, z, 1, 0)
        self.arrived(ref, self.x_out.at[part, z], self.x_in.at[part, z])
        self.diagonal(part, z, 1).start()
        self.across(part, ref, z, 1, 0).start()
        if part in self.planes:
            self.toward(part, ref, z, 1, 0)

    def corner_step(self, part, z):
        ref = self.slot(part, z, 1, 1)
        for which in (0, 1):
            self.arrived(
                self.piece(part, ref, which),
                self.d_out.at[part, z, which],
                self.d_in.at[part, z, which],
            )
        self.across(part, ref, z, 1, 1).start()
        if part in self.planes:
            self.toward(part, ref, z, 1, 1)

    def sent(self, part, z):
        mine = self.slot(part, z)
        self.along_x(part, mine, z).wait_send()
        self.along_y(part, mine, z).wait_send()
        self.diagonal(part, z, 0).wait_send()
        self.diagonal(part, z, 1).wait_send()

    def end(self, part):
        for z in range(self.lines):
            for flip_x, flip_y in FLIPS:
                which = flip_x * 2 + flip_y
                x, y = (self.x + flip_x) % 2, (self.y + flip_y) % 2
                self.arrived(
                    self.target(part, z, x, y, 1 - self.core),
                    self.c_out.at[part, z, which],
                    self.c_in.at[part, z, which],
                )
                mine = self.slot(part, z, flip_x, flip_y)
                self.across(part, mine, z, flip_x, flip_y).wait_send()
                if part not in self.planes and which > 0:
                    continue
                for side in (1, -1):

                    @pl.when(self.inside(self.z + side) & ((self.z - z) * side >= 0))
                    def _():
                        self.along_z(part, mine, z, side, flip_x, flip_y).wait_send()

            if part not in self.planes:
                self.sent(part, z)
        if part in self.planes:
            self.sent(part, self.z)

    def at(self, distance, run):
        if distance == 0:
            run(self.z)
            return
        for side in (1, -1):
            pl.when(self.inside(self.z - side * distance))(
                functools.partial(run, self.z - side * distance)
            )

    def do(self, kind, part, distance=0, side=0):
        if kind == BZ:
            self.begin_line(part)
        elif kind == BH:
            self.begin_plane(part)
        elif kind == LINE:
            self.line_step(part, distance, side)
        else:
            run = {PY: self.y_step, PX: self.x_step, CO: self.corner_step}[kind]
            self.at(distance, functools.partial(run, part))

    def all_steps(self, part):
        result = []
        for stage in range(1, self.lines + 2):
            steps = []
            if stage < self.lines:
                steps += [(LINE, part, stage, 1), (LINE, part, stage, -1)]
            if stage >= 2:
                steps += [(CO, part, stage - 2)]
            if stage <= self.lines:
                steps += [(PY, part, stage - 1), (PX, part, stage - 1)]
            result += [functools.partial(self.do, *step) for step in steps]
        return result


def paired(own, other, core):
    own, other = own.astype(F32), other.astype(F32)
    return [jnp.where(core == 0, own, other), jnp.where(core == 0, other, own)]


def in_pairs(array):
    half = array.shape[1] // 2
    size = 2 * KV_HEADS * HEAD_DIM // 4
    keys = jnp.concatenate([array[:, :size], array[:, half : half + size]], axis=1)
    values = jnp.concatenate(
        [array[:, size : 2 * size], array[:, half + size : half + 2 * size]], axis=1
    )
    pieces = []
    for head in range(KV_HEADS):
        cut = slice(head * HEAD_DIM, (head + 1) * HEAD_DIM)
        pieces += [keys[:, cut], values[:, cut]]
    return jnp.concatenate(pieces, axis=1)


def windows(blocks, span, low_part):
    reach = WINDOW + TILE
    fixed = [(0, (block + 1) * span) for block in range(WINDOW // span)]
    offset = TILE * (low_part // 2 + 1) - reach
    return fixed, reach, offset


def tiles_of(ref, flipped):
    lane = lax.broadcasted_iota(jnp.int32, (ref.shape[0], TILE), 1)
    result = []
    for slot in range(4):
        tile = ref[:, slot // 2 * TILE : (slot // 2 + 1) * TILE].astype(F32)
        if (slot % 2 == 0) == flipped:
            tile = pltpu.roll(tile, HEAD_DIM, 1)
        keep = lane >= HEAD_DIM if flipped else lane < HEAD_DIM
        result.append(jnp.where(keep, tile, 0.0).astype(BF16))
    return result


def joined(rows, flipped):
    span = rows.shape[0] // 4
    heads = [rows[slot * span : (slot + 1) * span] for slot in range(4)]
    lane = lax.broadcasted_iota(jnp.int32, (span, TILE), 1)
    result = []
    for first, second in ((heads[0], heads[1]), (heads[2], heads[3])):
        if flipped:
            first = pltpu.roll(first, HEAD_DIM, 1)
        else:
            second = pltpu.roll(second, HEAD_DIM, 1)
        result.append(jnp.where(lane < HEAD_DIM, first, second))
    return result


def bias_of(limits_ref, block, start, count):
    key = start + lax.broadcasted_iota(jnp.int32, (count, TILE), 0)
    least = limits_ref[0, pl.ds(block, 1), :]
    most = limits_ref[1, pl.ds(block, 1), :]
    self_pos = limits_ref[2, pl.ds(block, 1), :]
    allowed = ((key >= least) & (key <= most)) | (key == self_pos)
    bias = jnp.where(allowed, 0.0, MASKED)
    return jnp.concatenate([bias, bias], axis=1)


def each_block(blocks, body, between=lambda: None):
    span = 4 * HEAD_DIM
    fixed, reach, offset = windows(blocks, span, lax.axis_index("head"))
    for block, (start, count) in enumerate(fixed):
        body(block, start, count)
    between()

    @pl.loop(len(fixed), blocks)
    def _(block):
        body(block, pl.multiple_of(block * span + offset, TILE), reach)


def meet(others):
    barrier = pltpu.get_barrier_semaphore()
    for other in others:
        pl.semaphore_signal(barrier, inc=1, device_id=other, device_id_type=MESH)
    pl.semaphore_wait(barrier, len(others))


def along(count):
    blk, head = lax.axis_index("blk"), lax.axis_index("head")
    return [((blk + ahead) % count, head) for ahead in range(1, count)]


def beside():
    z, x, y, core = place()
    return [
        device(z, x, y, 1 - core),
        device(z, x, 1 - y, core),
        device(z, x, 1 - y, 1 - core),
    ]


class Exchange:
    def __init__(self, source, target, size, out, into, local):
        count = target.shape[0]
        blk, head = lax.axis_index("blk"), lax.axis_index("head")
        self.own = pltpu.make_async_copy(source.at[pl.ds(blk * size, size)], target.at[blk], local)
        self.copies, self.arrivals = [], []
        for at, (other, _) in enumerate(along(count)):
            self.copies.append(
                remote(
                    source.at[pl.ds(other * size, size)],
                    target.at[blk],
                    out.at[at],
                    into.at[at],
                    (other, head),
                )
            )
            giver = (blk + count - 1 - at) % count
            self.arrivals.append(
                remote(target.at[giver], target.at[giver], out.at[at], into.at[at], (other, head))
            )

    def start(self):
        self.own.start()
        for copy in self.copies:
            copy.start()

    def wait(self):
        for copy in self.arrivals:
            copy.wait_recv()
        for copy in self.copies:
            copy.wait_send()
        self.own.wait()


class Quarters:
    def __init__(self, terms, low, got, out, into):
        z, x, y, core = place()
        self.size = low.shape[1] // 4
        self.terms, self.low, self.got = terms, low, got
        self.mine = pl.ds((y * 2 + core) * self.size, self.size)
        self.copies = []
        for at, (flip_y, flip_core) in enumerate(((0, 1), (1, 0), (1, 1))):
            other_y, other_core = (y + flip_y) % 2, (core + flip_core) % 2
            theirs = pl.ds((other_y * 2 + other_core) * self.size, self.size)
            self.copies.append(
                remote(
                    low.at[:, theirs],
                    got.at[at],
                    out.at[at],
                    into.at[at],
                    device(z, x, other_y, other_core),
                )
            )

    def start(self):
        self.low[...] = self.terms[...].astype(BF16)
        for copy in self.copies:
            copy.start()

    def total(self):
        for copy in self.copies:
            copy.wait_recv()
        total = self.terms[:, self.mine]
        for at in range(3):
            total = total + self.got[at].astype(F32)
        return total.astype(BF16)

    def end(self):
        for copy in self.copies:
            copy.wait_send()


def turned(tile, cosine, sine, only_low=False):
    lane = lax.broadcasted_iota(jnp.int32, tile.shape, 1)
    half = HEAD_DIM // 2
    partner = jnp.where(
        lane % HEAD_DIM < half, pltpu.roll(tile, TILE - half, 1), pltpu.roll(tile, half, 1)
    )
    result = tile * cosine + partner * sine
    return jnp.where(lane < HEAD_DIM, result, tile) if only_low else result


def attend_back_kernel(
    lines,
    limits_ref,
    q_ref,
    kv_ref,
    lse_ref,
    grad_ref,
    turn_ref,
    output_ref,
    terms_ref,
    dqkv_ref,
    moved_ref,
    shared_ref,
    q_rows,
    g_rows,
    kv_turned,
    total,
    pair_low,
    pair_got,
    kept,
    y_low,
    y_got,
    low,
    got,
    shard,
    pair_out,
    pair_in,
    y_out,
    y_in,
    move_out,
    move_in,
    four_out,
    four_in,
    local,
    *sems,
):
    blocks, span = q_rows.shape[0], q_rows.shape[2]
    width = q_ref.shape[1]
    groups = width // (2 * TILE)
    scale = HEAD_DIM**-0.5
    z, x, y, core = place()
    size = shard.shape[1]

    def target(part, z, x, y, core):
        return shared_ref.at[z * 2 + x, :, pl.ds((y * 2 + core) * size, size)]

    spread = Spread([shard], target, lines, sems)
    meet(along(blocks) + beside())
    exchange = Exchange(output_ref, moved_ref, span, move_out, move_in, local.at[0])
    quarters = Quarters(terms_ref, low, got, four_out, four_in)
    quarters.start()
    own = pltpu.make_async_copy(shard, target(0, z, x, y, core), local.at[1])

    def gather_start():
        shard[...] = quarters.total()
        own.start()
        spread.begin_line(0)
        spread.begin_plane(0)

    steps = spread.all_steps(0)

    def some(count):
        def run():
            for _ in range(count):
                steps.pop(0)()

        return run

    later = [None, gather_start, some(4), some(3), some(4), exchange.start]
    later += [some(3), some(3), some(1)]

    def pump():
        if later:
            step = later.pop(0)
            if step is not None:
                step()

    def pair_copy(m):
        return remote(
            pair_low.at[m, 1 - core],
            pair_got.at[m],
            pair_out.at[m],
            pair_in.at[m],
            device(z, x, y, 1 - core),
        )

    def y_copy(m):
        return remote(
            y_low.at[m], y_got.at[m], y_out.at[m], y_in.at[m], device(z, x, 1 - y, core)
        )

    def give(m):
        whole = total[...].reshape(blocks, 4, span, TILE)
        for at in range(4):
            pair_low[m, at % 2, at // 2] = whole[:, at].astype(BF16)
        spot = total.reshape(blocks, 4, span, TILE)
        for at in range(2):
            kept[m, at] = spot[:, at * 2 + core]
        pair_copy(m).start()

    def add_pair(m):
        pair_copy(m).wait_recv()
        y_low[m] = (kept[m, 1 - y] + pair_got[m, 1 - y].astype(F32)).astype(BF16)
        y_copy(m).start()

    def add_y(m):
        y_copy(m).wait_recv()
        tile = kept[m, y] + pair_got[m, y].astype(F32) + y_got[m].astype(F32)
        tile = turned(tile.reshape(blocks * span, TILE), turn_ref[0], -turn_ref[1], True)
        at = width + m * TILE
        dqkv_ref[:, at : at + TILE] = tile.astype(BF16)

    for m in range(groups):
        columns = slice(m * 2 * TILE, (m + 1) * 2 * TILE)
        tile = slice(m * TILE, (m + 1) * TILE)
        for slot, rows in enumerate(tiles_of(q_ref[:, columns], False)):
            q_rows[:, slot] = (rows * BF16(scale)).reshape(blocks, span, TILE)
        for slot, rows in enumerate(tiles_of(grad_ref[:, columns], True)):
            g_rows[:, slot] = rows.reshape(blocks, span, TILE)
        kv_turned[...] = kv_ref[:, tile].astype(F32).T.astype(BF16)
        total[...] = jnp.zeros_like(total)

        def body(block, start, count):
            keys = pl.ds(start, count)
            queries = q_rows[block].reshape(4 * span, TILE)
            grads = g_rows[block].reshape(4 * span, TILE)
            scores = dot(kv_ref[keys, tile], queries, 1, 1)
            scores = scores + bias_of(limits_ref, block, start, count)
            probs = jnp.exp(scores - lse_ref[m, pl.ds(block, 1), :])
            grad_probs = dot(kv_ref[keys, tile], grads, 1, 1)
            inner = jnp.sum(probs * grad_probs, axis=0, keepdims=True)
            grad_scores = (probs * (grad_probs - inner)).astype(BF16)
            total[keys, :] += dot(grad_scores, queries) + dot(probs.astype(BF16), grads)
            grad_q = (dot(kv_turned[:, keys], grad_scores) * scale).T
            rows = pl.ds(block * span, span)
            cosine, sine = turn_ref[0, rows, :], -turn_ref[1, rows, :]
            for at, part in enumerate(joined(grad_q, False)):
                at = m * 2 * TILE + at * TILE
                dqkv_ref[rows, at : at + TILE] = turned(part, cosine, sine).astype(BF16)

        each_block(blocks, body, pump)
        pump()
        give(m)
        if m >= 1:
            add_pair(m - 1)
        if m >= 2:
            add_y(m - 2)
    while later:
        pump()
    add_pair(groups - 1)
    add_y(groups - 2)
    spread.end(0)
    own.wait()
    exchange.wait()
    quarters.end()
    add_y(groups - 1)
    for m in range(groups):
        pair_copy(m).wait_send()
        y_copy(m).wait_send()


def attend_back(limits, queries, pairs, lse, grads, turn, output, terms):
    rows, width = queries.shape
    blocks = limits.shape[1]
    span = rows // blocks
    groups = width // (2 * TILE)
    rank, total = terms.shape
    seqs = lax.axis_size("blk")
    each = pltpu.VMEM((blocks, 4, span, TILE), BF16)
    dma = pltpu.SemaphoreType.DMA
    vmem = pl.BlockSpec(memory_space=pltpu.VMEM)
    shape = jax.ShapeDtypeStruct
    return pl.pallas_call(
        functools.partial(attend_back_kernel, seqs // 2),
        out_shape=[
            shape((rows, width + pairs.shape[1]), BF16),
            shape((seqs, span, width), BF16),
            shape((seqs, rank, total), BF16),
        ],
        in_specs=[vmem] * 8,
        out_specs=[vmem, ANYWHERE, ANYWHERE],
        scratch_shapes=[
            each,
            each,
            pltpu.VMEM((TILE, pairs.shape[0]), BF16),
            pltpu.VMEM((pairs.shape[0], TILE), F32),
            pltpu.VMEM((groups, 2, 2, blocks, span, TILE), BF16),
            pltpu.VMEM((groups, 2, blocks, span, TILE), BF16),
            pltpu.VMEM((groups, 2, blocks, span, TILE), F32),
            pltpu.VMEM((groups, blocks, span, TILE), BF16),
            pltpu.VMEM((groups, blocks, span, TILE), BF16),
            pltpu.VMEM((rank, total), BF16),
            pltpu.VMEM((3, rank, total // 4), BF16),
            pltpu.VMEM((rank, total // 4), BF16),
            dma((groups,)),
            dma((groups,)),
            dma((groups,)),
            dma((groups,)),
            dma((seqs - 1,)),
            dma((seqs - 1,)),
            dma((3,)),
            dma((3,)),
            dma((2,)),
            *Spread.semaphores(1, seqs // 2),
        ],
        compiler_params=pltpu.CompilerParams(
            collective_id=1, has_side_effects=True, vmem_limit_bytes=56 << 20
        ),
    )(limits, queries, pairs, lse, grads, turn, output, terms)


def first_back_kernel(
    lines,
    dqkv_ref,
    weight_ref,
    down_ref,
    up_ref,
    normed_ref,
    low_ref,
    middle_ref,
    flat_ref,
    inverse_ref,
    gain_ref,
    moved_ref,
    shared_ref,
    result,
    terms,
    low,
    got,
    shard,
    move_out,
    move_in,
    four_out,
    four_in,
    local,
    *sems,
):
    blocks, span = moved_ref.shape[:2]
    z, x, y, core = place()
    size = shard.shape[1]
    rank = down_ref.shape[0] // 3
    width = flat_ref.shape[1]

    def target(part, z, x, y, core):
        return shared_ref.at[z * 2 + x, :, pl.ds((y * 2 + core) * size, size)]

    spread = Spread([shard], target, lines, sems)
    meet(along(blocks) + beside())
    grad_low = (ADAPTER_SCALE * dot(dqkv_ref[...], up_ref[...], 1, 1)).astype(BF16)
    grad_up = ADAPTER_SCALE * dot(low_ref[...], dqkv_ref[...], 0, 0)
    grad_down = dot(grad_low, normed_ref[...], 0, 0)
    terms[:, :width] = grad_up[:rank, :width]
    at = width
    while at < dqkv_ref.shape[1]:
        lane = lax.broadcasted_iota(jnp.int32, (rank, TILE), 1)
        terms[:, at : at + TILE] = jnp.where(
            lane < HEAD_DIM,
            grad_up[rank : 2 * rank, at : at + TILE],
            grad_up[2 * rank :, at : at + TILE],
        )
        at += TILE
    for which in range(3):
        terms[:, at : at + width] = grad_down[which * rank : (which + 1) * rank]
        at += width
    if at < terms.shape[1]:
        terms[:, at:] = jnp.zeros((rank, terms.shape[1] - at), F32)
    quarters = Quarters(terms, low, got, four_out, four_in)
    quarters.start()
    own = pltpu.make_async_copy(shard, target(0, z, x, y, core), local.at[1])
    exchange = Exchange(result, moved_ref, span, move_out, move_in, local.at[0])
    grad = dot(dqkv_ref[...], weight_ref[...], 1, 1) + dot(grad_low, down_ref[...])
    shard[...] = quarters.total()
    own.start()
    spread.begin_line(0)
    spread.begin_plane(0)
    weighted = grad * gain_ref[...]
    flat, inverse = flat_ref[...].astype(F32), inverse_ref[...]
    mean = jnp.mean(flat * weighted, axis=1, keepdims=True)
    grad = middle_ref[...] + inverse * weighted - flat * (inverse * inverse * inverse * mean)
    result[...] = grad.astype(BF16)
    steps = spread.all_steps(0)
    for step in steps[:11]:
        step()
    exchange.start()
    for step in steps[11:]:
        step()
    spread.end(0)
    own.wait()
    quarters.end()
    exchange.wait()


def first_back(grad_qkv, weight, down, up, normed, low, middle, flat, inverse, gain):
    rows, width = flat.shape
    rank = down.shape[0] // 3
    seqs, heads = lax.axis_size("blk"), lax.axis_size("head")
    total = 3 * width + weight.shape[1]
    total += -total % (2 * heads * TILE)
    dma = pltpu.SemaphoreType.DMA
    vmem = pl.BlockSpec(memory_space=pltpu.VMEM)
    shape = jax.ShapeDtypeStruct
    return pl.pallas_call(
        functools.partial(first_back_kernel, seqs // 2),
        out_shape=[
            shape((seqs, rows // seqs, width), BF16),
            shape((seqs, rank, total), BF16),
        ],
        in_specs=[vmem] * 10,
        out_specs=[ANYWHERE, ANYWHERE],
        scratch_shapes=[
            pltpu.VMEM((rows, width), BF16),
            pltpu.VMEM((rank, total), F32),
            pltpu.VMEM((rank, total), BF16),
            pltpu.VMEM((3, rank, total // 4), BF16),
            pltpu.VMEM((rank, total // 4), BF16),
            dma((seqs - 1,)),
            dma((seqs - 1,)),
            dma((3,)),
            dma((3,)),
            dma((2,)),
            *Spread.semaphores(1, seqs // 2),
        ],
        compiler_params=pltpu.CompilerParams(
            collective_id=2, has_side_effects=True, vmem_limit_bytes=56 << 20
        ),
    )(grad_qkv, weight, down, up, normed, low, middle, flat, inverse, gain.reshape(1, -1))


def placed_kernel(sizes, width, holder_ref, early_ref, late_ref, *outs):
    q_down, q_up, kv_down, kv_up, o_down, o_up, gu_down, gu_up, ff_down, ff_up = outs
    cuts = np.cumsum([0] + sizes)
    early = [slice(int(begin), int(end)) for begin, end in zip(cuts[:-1], cuts[1:])]
    for out, cut in zip((o_down, o_up), early[:2]):
        out[0] = early_ref[0, :, cut].astype(F32)
    for which in range(2):
        gu_down[0, which] = early_ref[0, :, early[2 + which]].astype(F32)
        gu_up[0, which] = early_ref[0, :, early[4 + which]].astype(F32)
    for out, cut in zip((ff_down, ff_up), early[6:]):
        out[0] = early_ref[0, :, cut].astype(F32)
    q_up[0] = late_ref[0, :, :width].astype(F32)
    narrow = KV_HEADS * HEAD_DIM
    pairs = late_ref[0, :, width : width + 2 * narrow].astype(F32)
    for which in range(2):
        pieces = [
            pairs[:, (2 * head + which) * HEAD_DIM : (2 * head + which + 1) * HEAD_DIM]
            for head in range(KV_HEADS)
        ]
        kv_up[0, which] = jnp.concatenate(pieces, axis=1)
    at = width + 2 * narrow
    q_down[0] = late_ref[0, :, at : at + width].astype(F32)
    for which in range(2):
        at += width
        kv_down[0, which] = late_ref[0, :, at : at + width].astype(F32)


def placed(holder, early, late, sizes, width):
    adapters, rank = early.shape[:2]
    hidden = sizes[4]
    narrow = KV_HEADS * HEAD_DIM
    shapes = [
        (rank, width),
        (rank, width),
        (2, rank, width),
        (2, rank, narrow),
        (rank, width),
        (rank, width),
        (2, rank, width),
        (2, rank, hidden),
        (rank, hidden),
        (rank, width),
    ]

    def whole(shape):
        return pl.BlockSpec((1,) + shape, lambda a, held: (a,) + (0,) * len(shape))

    return pl.pallas_call(
        functools.partial(placed_kernel, sizes, width),
        grid_spec=pltpu.PrefetchScalarGridSpec(
            num_scalar_prefetch=1,
            grid=(adapters,),
            in_specs=[
                pl.BlockSpec((1, rank, early.shape[2]), lambda a, held: (held[a], 0, 0)),
                pl.BlockSpec((1, rank, late.shape[2]), lambda a, held: (held[a], 0, 0)),
            ],
            out_specs=[whole(shape) for shape in shapes],
        ),
        out_shape=[jax.ShapeDtypeStruct((adapters,) + shape, F32) for shape in shapes],
    )(holder, early, late)


def norm_of(values, gain):
    inverse = lax.rsqrt(jnp.mean(values * values, axis=-1, keepdims=True) + EPSILON)
    return (values * inverse * gain).astype(BF16), inverse


def norm_back(values, inverse, gain, grad):
    weighted = grad * gain
    mean = jnp.mean(values * weighted, axis=-1, keepdims=True)
    return inverse * weighted - values * (inverse * inverse * inverse * mean)


def lowered(inputs, down):
    return dot(inputs, down, 1, 1).astype(BF16)


def front_kernel(lines, *refs):
    tokens, out_grad, query, keyval, output, gateup, down = refs[:7]
    limits_ref, turn_ref, d_qkv_ref, u_qkv_ref, gain_ref = refs[7:12]
    d_output, u_output, d_gateup, u_gateup, d_ffdown, u_ffdown, gain2_ref = refs[12:19]
    w_qkv, w_output, w_gateup, w_down, flat_ref, normed_ref, inverse_ref, low_ref = refs[19:27]
    q_ref, pairs_ref, lse_ref, output_ref, middle, grad_mixed_ref, terms_ref = refs[27:34]
    got_query, got_keyval, got_output, got_down, my_query, my_keyval, my_output, my_down = refs[34:42]
    all_keyval, first_weights, q_rows, kv_turned, out_ref, grad_ref = refs[42:48]
    normed2, result, grad_normed, two_gateup, two_down = refs[48:53]
    low_output, low_gate, low_up, low_down, grad_low_down, grad_low_gate, grad_low_up = refs[53:60]
    pair_out, pair_in, local, move_out, move_in, share_out, share_in, feed_in = refs[60:68]
    rows, deep = my_query.shape[0], my_down.shape[0]
    wide, mixed = my_output.shape[1], my_keyval.shape[1]
    span, hidden = gateup.shape[1:]
    width = w_output.shape[1]
    units = w_down.shape[0]
    blocks, part_rows = flat_ref.shape[:2]
    groups = width // (2 * TILE)

    def target(part, z, x, y, core):
        blk, head = z * 2 + x, y * 2 + core
        if part == 0:
            return all_keyval.at[pl.ds(blk * 2 * rows + core * rows, rows), pl.ds(y * mixed, mixed)]
        if part == 1:
            return first_weights.at[
                pl.ds(blk * 2 * rows + core * rows, rows), pl.ds(y * wide, wide)
            ]
        if part == 2:
            return w_output.at[pl.ds(blk * 2 * rows + core * rows, rows), pl.ds(y * wide, wide)]
        if part == 3:
            return w_down.at[pl.ds(blk * 2 * deep + core * deep, deep), pl.ds(y * wide, wide)]
        begin, size = FRONT_CHUNKS[part]
        return w_gateup.at[:, pl.ds(blk * span, span), pl.ds(head * hidden + begin, size)]

    sources = [my_keyval, my_query, my_output, my_down]
    sources += [gateup.at[:, :, pl.ds(*FRONT_CHUNKS[part])] for part in range(4, FRONT_PARTS)]
    spread = Spread(sources, target, lines, refs[68:], FRONT_PLANES, FRONT_SHARES)
    z, x, y, core = place()
    head = y * 2 + core
    meet(along(blocks) + beside())
    sibling = device(z, x, y, 1 - core)
    theirs = pl.ds((1 - core) * rows, rows)
    swaps = [
        remote(keyval.at[:, theirs], got_keyval, pair_out.at[0], pair_in.at[0], sibling),
        remote(query.at[theirs], got_query, pair_out.at[1], pair_in.at[1], sibling),
        remote(output.at[theirs], got_output, pair_out.at[2], pair_in.at[2], sibling),
        remote(
            down.at[pl.ds((1 - core) * deep, deep)], got_down, pair_out.at[3], pair_in.at[3], sibling
        ),
    ]
    for swap in swaps:
        swap.start()
    exchanges = [
        Exchange(source, target_ref, part_rows, move_out.at[at], move_in.at[at], local.at[at])
        for at, (source, target_ref) in enumerate(((tokens, flat_ref), (out_grad, grad_ref)))
    ]
    own = [
        pltpu.make_async_copy(sources[part], target(part, z, x, y, core), local.at[4 + part])
        for part in range(FRONT_PARTS)
    ]
    mine = pl.ds(core * rows, rows)
    kv_ref = pairs_ref.reshape(blocks * pairs_ref.shape[1], pairs_ref.shape[2])
    cosine, sine = turn_ref[0], turn_ref[1]
    here = pl.ds(head * part_rows, part_rows)
    weights_out = pltpu.make_async_copy(first_weights, w_qkv, local.at[2])
    w_output_here = first_weights.at[:, pl.ds(0, width)]
    output_in = pltpu.make_async_copy(w_output, w_output_here, local.at[3])
    shares = []
    for at, (flip_y, other) in enumerate(((0, device(z, x, 1 - y, core)), (0, sibling), (1, sibling))):
        source_head = ((y + flip_y) % 2) * 2 + core
        ref = pairs_ref.at[:, pl.ds(source_head * part_rows, part_rows)]
        shares.append(remote(ref, ref, share_out.at[at], share_in.at[at], other))

    def share_arrived(at, from_y, from_core):
        ref = pairs_ref.at[:, pl.ds((from_y * 2 + from_core) * part_rows, part_rows)]
        remote(ref, ref, share_out.at[at], share_in.at[at], sibling).wait_recv()

    def first(columns):
        return dot(normed_ref[...], first_weights[:, columns]) + ADAPTER_SCALE * dot(
            low_ref[...], u_qkv_ref[:, columns]
        )

    def pack(which):
        if which == 0:
            swaps[0].wait_recv()
            pieces = paired(keyval[0, mine, :], got_keyval[0], core)
            pieces += paired(keyval[1, mine, :], got_keyval[1], core)
            filled = sum(p.shape[1] for p in pieces)
            pieces.append(jnp.zeros((rows, mixed - filled), F32))
            my_keyval[...] = jnp.concatenate(pieces, axis=1).astype(BF16)
            swaps[1].wait_recv()
            pieces = paired(query[mine, :], got_query[...], core)
            my_query[...] = jnp.concatenate(pieces, axis=1).astype(BF16)
        else:
            swaps[2].wait_recv()
            pieces = paired(output[mine, :], got_output[...], core)
            my_output[...] = jnp.concatenate(pieces, axis=1).astype(BF16)
            swaps[3].wait_recv()
            pieces = paired(down[pl.ds(core * deep, deep), :], got_down[...], core)
            my_down[...] = jnp.concatenate(pieces, axis=1).astype(BF16)

    def norm_first():
        @pl.loop(0, blocks)
        def _(block):
            spot = pl.ds(block * part_rows, part_rows)
            normed, inverse = norm_of(flat_ref[block].astype(F32), gain_ref[...])
            normed_ref[spot, :] = normed
            inverse_ref[spot, :] = inverse

        low_ref[...] = lowered(normed_ref[...], d_qkv_ref[...])

    def pair_weights():
        @pl.loop(0, first_weights.shape[0] // (2 * rows))
        def _(at):
            spot = pl.ds(at * 2 * rows, 2 * rows)
            first_weights[spot, width:] = in_pairs(all_keyval[spot, :].astype(F32)).astype(BF16)

    def make_pairs():
        for m in range(groups):
            at = width + m * TILE
            tile = turned(first(slice(at, at + TILE)), cosine, sine, True).astype(BF16)
            pairs_ref[:, here, m * TILE : (m + 1) * TILE] = tile.reshape(blocks, part_rows, TILE)

    def give_pairs():
        shares[0].start()
        shares[1].start()

    def get_pairs():
        share_arrived(0, 1 - y, core)
        shares[2].start()
        share_arrived(1, y, 1 - core)
        share_arrived(2, 1 - y, 1 - core)

    def make_queries(m):
        if m == 0:
            weights_out.start()
        both = first(slice(m * 2 * TILE, (m + 1) * 2 * TILE))
        for at in range(2):
            tile = turned(both[:, at * TILE : (at + 1) * TILE], cosine, sine).astype(BF16)
            q_ref[:, (2 * m + at) * TILE : (2 * m + at + 1) * TILE] = tile

    def body(m, block, start, count):
        tile = slice(m * TILE, (m + 1) * TILE)
        queries = q_rows[block].reshape(4 * part_rows, TILE)
        scores = dot(kv_ref[pl.ds(start, count), tile], queries, 1, 1)
        scores = scores + bias_of(limits_ref, block, start, count)
        top = jnp.max(scores, axis=0, keepdims=True)
        shifted = jnp.exp(scores - top)
        total = jnp.sum(shifted, axis=0, keepdims=True)
        attended = dot(kv_turned[:, pl.ds(start, count)], shifted.astype(BF16))
        lse_ref[m, pl.ds(block, 1), :] = top + jnp.log(total)
        attended = (attended / total).T
        for at, part in enumerate(joined(attended, True)):
            at = m * 2 * TILE + at * TILE
            out_ref[pl.ds(block * part_rows, part_rows), at : at + TILE] = part.astype(BF16)

    fixed, reach, offset = windows(blocks, 4 * part_rows, head)

    def attend_start(m):
        columns = slice(m * 2 * TILE, (m + 1) * 2 * TILE)
        for slot, part in enumerate(tiles_of(q_ref[:, columns], False)):
            q_rows[:, slot] = (part * BF16(HEAD_DIM**-0.5)).reshape(blocks, part_rows, TILE)
        kv_turned[...] = kv_ref[:, m * TILE : (m + 1) * TILE].astype(F32).T.astype(BF16)
        for block in range(2):
            body(m, block, *fixed[block])

    def attend_middle(m):
        for block in range(2, len(fixed)):
            body(m, block, *fixed[block])

    def attend_end(m):
        @pl.loop(len(fixed), blocks)
        def _(block):
            body(m, block, pl.multiple_of(block * 4 * part_rows + offset, TILE), reach)

    def grads():
        return grad_ref[...].reshape(blocks * part_rows, width)

    def out_step():
        weights_out.wait()
        output_in.start()
        attended = out_ref[...]
        low_output[...] = lowered(attended, d_output[...])
        grad_low_down[...] = (ADAPTER_SCALE * dot(grads(), u_ffdown[...], 1, 1)).astype(BF16)
        for ref in (result, grad_normed, low_down, grad_low_gate, grad_low_up):
            ref[...] = jnp.zeros_like(ref)
        output_in.wait()
        branch = dot(attended, w_output_here[...])
        middle[...] = branch + ADAPTER_SCALE * dot(low_output[...], u_output[...])

        @pl.loop(0, blocks)
        def _(block):
            spot = pl.ds(block * part_rows, part_rows)
            values = flat_ref[block].astype(F32) + middle[spot, :]
            middle[spot, :] = values
            normed2[spot, :] = norm_of(values, gain2_ref[...])[0]

        low_gate[...] = lowered(normed2[...], d_gateup[0])
        low_up[...] = lowered(normed2[...], d_gateup[1])

    def chunk_in(part, which):
        begin, size = FRONT_CHUNKS[part]
        at = pl.ds(which * hidden + begin, size)
        slot = which % 2
        return (
            pltpu.make_async_copy(
                w_gateup.at[:, :, at],
                two_gateup.at[slot, :, :, pl.ds(0, size)],
                feed_in.at[slot, 0],
            ),
            pltpu.make_async_copy(
                w_down.at[at], two_down.at[slot, pl.ds(0, size)], feed_in.at[slot, 1]
            ),
        )

    def feed(part, which):
        if which == 0:
            for copy in chunk_in(part, which):
                copy.start()
        if which < 3:
            for copy in chunk_in(part, which + 1):
                copy.start()
        for copy in chunk_in(part, which):
            copy.wait()
        begin, size = FRONT_CHUNKS[part]
        at, slot = which * hidden + begin, which % 2
        columns = slice(at, at + size)
        w_gate, w_up = two_gateup[slot, 0, :, :size], two_gateup[slot, 1, :, :size]
        w_deep = two_down[slot, :size, :]
        u_gate, u_up, d_deep = u_gateup[0, :, columns], u_gateup[1, :, columns], d_ffdown[:, columns]
        inputs, grad = normed2[...], grads()
        gate = dot(inputs, w_gate) + ADAPTER_SCALE * dot(low_gate[...], u_gate)
        upward = dot(inputs, w_up) + ADAPTER_SCALE * dot(low_up[...], u_up)
        grad_act = dot(grad, w_deep, 1, 1) + dot(grad_low_down[...], d_deep)
        sigma = 1.0 / (1.0 + jnp.exp(-gate))
        silu = gate * sigma
        activated = (silu * upward).astype(BF16)
        grad_gate = (grad_act * upward * (sigma * (1.0 + gate * (1.0 - sigma)))).astype(BF16)
        grad_up = (grad_act * silu).astype(BF16)
        result[...] += dot(activated, w_deep)
        grad_normed[...] += dot(grad_gate, w_gate, 1, 1) + dot(grad_up, w_up, 1, 1)
        low_down[...] += dot(activated, d_deep, 1, 1)
        grad_low_gate[...] += dot(grad_gate, u_gate, 1, 1)
        grad_low_up[...] += dot(grad_up, u_up, 1, 1)
        at += 4 * width
        terms_ref[:, at : at + size] = ADAPTER_SCALE * dot(low_gate[...], grad_gate, 0, 0)
        at += units
        terms_ref[:, at : at + size] = ADAPTER_SCALE * dot(low_up[...], grad_up, 0, 0)
        at += units
        terms_ref[:, at : at + size] = dot(grad_low_down[...], activated, 0, 0)

    def last():
        low = low_down[...].astype(BF16)
        result[...] += ADAPTER_SCALE * dot(low, u_ffdown[...])
        at = 4 * width + 3 * units
        terms_ref[:, at : at + width] = ADAPTER_SCALE * dot(low, grads(), 0, 0)
        if at + width < terms_ref.shape[1]:
            terms_ref[:, at + width :] = jnp.zeros(
                (terms_ref.shape[0], terms_ref.shape[1] - at - width), F32
            )
        low_g = (ADAPTER_SCALE * grad_low_gate[...]).astype(BF16)
        low_u = (ADAPTER_SCALE * grad_low_up[...]).astype(BF16)
        terms_ref[:, 2 * width : 3 * width] = dot(low_g, normed2[...], 0, 0)
        terms_ref[:, 3 * width : 4 * width] = dot(low_u, normed2[...], 0, 0)
        grad_normed[...] += dot(low_g, d_gateup[0]) + dot(low_u, d_gateup[1])

        @pl.loop(0, blocks)
        def _(block):
            spot = pl.ds(block * part_rows, part_rows)
            values = middle[spot, :]
            output_ref[spot, :] = (values + result[spot, :]).astype(BF16)
            inverse = norm_of(values, gain2_ref[...])[1]
            back = norm_back(values, inverse, gain2_ref[...], grad_normed[spot, :])
            grad = grad_ref[block].astype(F32) + back
            middle[spot, :] = grad
            normed2[spot, :] = grad.astype(BF16)

        grad = normed2[...]
        low = (ADAPTER_SCALE * dot(grad, u_output[...], 1, 1)).astype(BF16)
        grad_mixed = dot(grad, w_output_here[...], 1, 1) + dot(low, d_output[...])
        grad_mixed_ref[...] = grad_mixed.astype(BF16)
        terms_ref[:, :width] = dot(low, out_ref[...], 0, 0)
        terms_ref[:, width : 2 * width] = ADAPTER_SCALE * dot(low_output[...], grad, 0, 0)

    def end(part):
        spread.end(part)
        own[part].wait()

    run = {
        END: end,
        EX: lambda which: exchanges[which].start(),
        EXW: lambda which: exchanges[which].wait(),
        PACK: pack,
        NORM: norm_first,
        PAIRS: pair_weights,
        KEYS: make_pairs,
        GIVE: give_pairs,
        GET: get_pairs,
        QUERY: make_queries,
        ATT0: attend_start,
        ATT1: attend_middle,
        ATT2: attend_end,
        OUT: out_step,
        FEED: feed,
        LAST: last,
    }
    for kind, *rest in FRONT_ORDER:
        if kind in run:
            run[kind](*rest)
        else:
            spread.do(kind, *rest)
            if kind == BH:
                own[rest[0]].start()
    for copy in swaps + shares:
        copy.wait_send()


FRONT_PARTS = 7
FRONT_CHUNKS = {4: (0, 384), 5: (384, 256), 6: (640, 256)}
FRONT_PLANES = (2,)
FRONT_SHARES = {3: 0.35}
FRONT_ORDER = (
    (BH, 6), (BH, 4), (BH, 5), (EX, TOKENS), (PACK, 0), (BZ, 1), (PACK, 1), (BZ, 0), (BH, 3),
    (BH, 1), (LINE, 1, 1, -1), (LINE, 1, 1, 1), (LINE, 1, 2, 1), (LINE, 1, 2, -1),
    (LINE, 0, 1, -1), (LINE, 0, 1, 1), (BH, 0), (BH, 2), (PX, 3, 0), (BZ, 3), (PX, 4, 0), (BZ, 4),
    (PX, 1, 1), (PY, 0, 0), (EXW, TOKENS), (LINE, 1, 3, -1), (PY, 1, 2), (NORM,), (PX, 0, 0),
    (PX, 1, 0), (LINE, 1, 3, 1), (LINE, 0, 3, -1), (PY, 1, 1), (LINE, 0, 2, 1), (PY, 1, 0),
    (LINE, 0, 2, -1), (PY, 4, 0), (LINE, 4, 1, 1), (PY, 1, 3), (BZ, 2), (LINE, 0, 3, 1),
    (PX, 5, 0), (CO, 1, 1), (PY, 0, 2), (PX, 2, 0), (PY, 0, 1), (LINE, 4, 2, 1), (PX, 0, 1),
    (PX, 0, 2), (PX, 1, 2), (LINE, 4, 1, -1), (PY, 2, 0), (LINE, 4, 2, -1), (CO, 0, 0),
    (PX, 0, 3), (LINE, 3, 1, -1), (PY, 0, 3), (BZ, 5), (PX, 1, 3), (PY, 3, 0), (CO, 0, 1),
    (LINE, 3, 1, 1), (PX, 6, 0), (LINE, 3, 2, 1), (LINE, 4, 3, 1), (CO, 0, 2), (CO, 2, 0),
    (PY, 6, 0), (CO, 1, 3), (PY, 4, 1), (LINE, 3, 2, -1), (LINE, 4, 3, -1), (PY, 5, 0),
    (LINE, 2, 1, -1), (CO, 0, 3), (END, 0), (LINE, 2, 1, 1), (PAIRS,), (PX, 4, 2), (KEYS,),
    (CO, 1, 2), (CO, 1, 0), (GIVE,), (PX, 4, 1), (LINE, 3, 3, 1), (BZ, 6), (LINE, 5, 1, -1),
    (END, 1), (LINE, 2, 2, -1), (LINE, 5, 1, 1), (QUERY, 0), (LINE, 5, 2, 1), (LINE, 6, 1, 1),
    (PY, 4, 2), (QUERY, 1), (QUERY, 2), (PY, 4, 3), (LINE, 3, 3, -1), (PX, 4, 3), (EX, GRADS),
    (QUERY, 3), (QUERY, 4), (GET,), (CO, 4, 0), (LINE, 2, 2, 1), (PY, 3, 2), (PX, 3, 1),
    (PX, 3, 2), (PY, 3, 1), (ATT0, 0), (ATT1, 0), (LINE, 5, 2, -1), (CO, 6, 0), (ATT2, 0),
    (ATT0, 1), (ATT1, 1), (ATT2, 1), (PX, 5, 1), (ATT0, 2), (ATT1, 2), (ATT2, 2), (PY, 3, 3),
    (PX, 3, 3), (LINE, 6, 1, -1), (LINE, 6, 2, 1), (ATT0, 3), (ATT1, 3), (CO, 5, 0),
    (LINE, 2, 3, 1), (ATT2, 3), (ATT0, 4), (LINE, 2, 3, -1), (ATT1, 4), (ATT2, 4), (PY, 5, 2),
    (END, 2), (CO, 3, 2), (LINE, 6, 3, 1), (EXW, GRADS), (LINE, 5, 3, -1), (CO, 4, 1),
    (LINE, 5, 3, 1), (CO, 4, 2), (CO, 3, 0), (PY, 5, 1), (CO, 3, 3), (CO, 3, 1), (CO, 4, 3),
    (LINE, 6, 2, -1), (PX, 5, 2), (OUT,), (END, 3), (END, 4), (FEED, 4, 0), (FEED, 4, 1),
    (PX, 5, 3), (PX, 6, 1), (CO, 5, 1), (PX, 6, 2), (PY, 5, 3), (PY, 6, 1), (FEED, 4, 2),
    (CO, 5, 2), (PY, 6, 2), (CO, 5, 3), (FEED, 4, 3), (LINE, 6, 3, -1), (END, 5), (FEED, 5, 0),
    (PY, 6, 3), (CO, 6, 2), (PX, 6, 3), (CO, 6, 1), (FEED, 5, 1), (FEED, 5, 2), (CO, 6, 3),
    (FEED, 5, 3), (END, 6), (FEED, 6, 0), (FEED, 6, 1), (FEED, 6, 2), (FEED, 6, 3), (LAST,),
)


def front(tokens, out_grad, weights, limits, turn, down, up, gain, factors, gain2):
    query, keyval, output, gateup, w_down = weights
    seqs, part, width = tokens.shape
    rows, wide = query.shape
    deep = w_down.shape[0]
    blks, heads = lax.axis_size("blk"), lax.axis_size("head")
    narrow = keyval.shape[2]
    mixed = -(-4 * narrow // TILE) * TILE
    double = heads * narrow * 2
    groups = width // (2 * TILE)
    count, units = seqs * part, blks * deep
    rank = factors[0].shape[0]
    total = 5 * width + 3 * units
    total += -total % (2 * heads * TILE)
    most = max(size for _, size in FRONT_CHUNKS.values())
    dma = pltpu.SemaphoreType.DMA
    vmem = pl.BlockSpec(memory_space=pltpu.VMEM)
    shape = jax.ShapeDtypeStruct
    held = pltpu.VMEM
    return pl.pallas_call(
        functools.partial(front_kernel, blks // 2),
        out_shape=[
            shape((blks * rows, heads * wide + double), BF16),
            shape((blks * rows, heads * wide), BF16),
            shape((2, blks * rows, heads * gateup.shape[2]), BF16),
            shape((units, heads * wide), BF16),
            shape((seqs, part, width), BF16),
            shape((count, width), BF16),
            shape((count, 1), F32),
            shape((count, down.shape[0]), BF16),
            shape((count, width), BF16),
            shape((seqs, heads * part, double), BF16),
            shape((groups, seqs, 2 * TILE), F32),
            shape((count, width), BF16),
            shape((count, width), F32),
            shape((count, width), BF16),
            shape((rank, total), F32),
        ],
        in_specs=[ANYWHERE, ANYWHERE, vmem, vmem, vmem, ANYWHERE] + [vmem] * 13,
        out_specs=[ANYWHERE] * 4 + [vmem] * 11,
        scratch_shapes=[
            held((rows // 2, wide), BF16),
            held((2, rows // 2, narrow), BF16),
            held((rows // 2, wide), BF16),
            held((deep // 2, wide), BF16),
            held((rows // 2, 2 * wide), BF16),
            held((rows // 2, mixed), BF16),
            held((rows // 2, 2 * wide), BF16),
            held((deep // 2, 2 * wide), BF16),
            held((blks * rows, heads // 2 * mixed), BF16),
            held((blks * rows, heads * wide + double), BF16),
            held((seqs, 4, part, TILE), BF16),
            held((TILE, seqs * heads * part), BF16),
            held((count, width), BF16),
            held((seqs, part, width), BF16),
            held((count, width), BF16),
            held((count, width), F32),
            held((count, width), F32),
            held((2, 2, width, most), BF16),
            held((2, most, width), BF16),
            held((count, rank), BF16),
            held((count, rank), BF16),
            held((count, rank), BF16),
            held((count, rank), F32),
            held((count, rank), BF16),
            held((count, rank), F32),
            held((count, rank), F32),
            dma((4,)),
            dma((4,)),
            dma((4 + FRONT_PARTS,)),
            dma((2, seqs - 1)),
            dma((2, seqs - 1)),
            dma((3,)),
            dma((3,)),
            dma((2, 2)),
            *Spread.semaphores(FRONT_PARTS, blks // 2),
        ],
        compiler_params=pltpu.CompilerParams(
            collective_id=0, has_side_effects=True, vmem_limit_bytes=60 << 20
        ),
    )(
        tokens.reshape(count, width),
        out_grad.reshape(count, width),
        query,
        keyval,
        output,
        gateup,
        w_down,
        limits,
        turn,
        down,
        up,
        gain.reshape(1, -1),
        *factors,
        gain2.reshape(1, -1),
    )


def prepare_kernel(
    adapters_ref,
    where_ref,
    freqs_ref,
    segment_ref,
    real_ref,
    query_down,
    query_up,
    keyval_down,
    keyval_up,
    output_down,
    output_up,
    gateup_down,
    gateup_up,
    ffdown_down,
    ffdown_up,
    limits_ref,
    turn_ref,
    d_qkv,
    u_qkv,
    d_output,
    u_output,
    d_gateup,
    u_gateup,
    d_ffdown,
    u_ffdown,
):
    seq, head = where_ref[0], where_ref[1]
    blocks, part = limits_ref.shape[1], limits_ref.shape[2] // 2
    span = segment_ref.shape[1] // blocks
    rank, width = query_up.shape[1:]
    for out, ref in ((d_output, output_down), (u_output, output_up), (d_gateup, gateup_down)):
        out[...] = ref[0]
    for out, ref in ((u_gateup, gateup_up), (d_ffdown, ffdown_down), (u_ffdown, ffdown_up)):
        out[...] = ref[0]
    d_qkv[:rank] = query_down[0]
    d_qkv[rank : 2 * rank] = keyval_down[0, 0]
    d_qkv[2 * rank :] = keyval_down[0, 1]
    u_qkv[...] = jnp.zeros_like(u_qkv)
    u_qkv[:rank, :width] = query_up[0]
    nil = jnp.zeros((rank, HEAD_DIM), F32)
    for which in range(2):
        ups, pieces = keyval_up[0, which].astype(F32), []
        for m in range(KV_HEADS):
            piece = ups[:, m * HEAD_DIM : (m + 1) * HEAD_DIM]
            pieces += [piece, nil] if which == 0 else [nil, piece]
        u_qkv[(1 + which) * rank : (2 + which) * rank, width:] = jnp.concatenate(
            pieces, axis=1
        ).astype(BF16)
    segment = segment_ref[pl.ds(seq, 1), :].astype(F32)
    length = jnp.sum(real_ref[pl.ds(seq, 1), :], axis=1, keepdims=True)
    column = jnp.broadcast_to(segment, (TILE, segment.shape[1])).T
    lane = lax.broadcasted_iota(jnp.int32, (1, TILE), 1)
    for block in range(blocks):
        mine = segment[:, block * span : (block + 1) * span]
        mine = pltpu.roll(jnp.broadcast_to(mine, (8, span)), span - head * part, 1)[:1, :TILE]
        twin = pltpu.roll(jnp.broadcast_to(mine, (8, TILE)), part, 1)[:1]
        mine = jnp.where(lane < part, mine, twin)
        before = jnp.sum((column < mine).astype(F32), axis=0, keepdims=True).astype(jnp.int32)
        position = block * span + head * part + lane % part
        limits_ref[0, block : block + 1, :] = jnp.maximum(position - (WINDOW - 1), before)
        limits_ref[1, block : block + 1, :] = jnp.minimum(position, length - 1)
        limits_ref[2, block : block + 1, :] = position
    shape = (part, TILE)
    row = lax.broadcasted_iota(jnp.int32, shape, 0)
    lanes = lax.broadcasted_iota(jnp.int32, shape, 1)
    sign = jnp.where(lanes % HEAD_DIM < HEAD_DIM // 2, -1.0, 1.0)
    for block in range(blocks):
        angle = (block * span + head * part + row).astype(F32) * freqs_ref[...]
        turn_ref[0, block * part : (block + 1) * part, :] = jnp.cos(angle)
        turn_ref[1, block * part : (block + 1) * part, :] = sign * jnp.sin(angle)


def prepare(adapter_index, seq, head, segment_ids, real_mask, factors, part):
    seqs = adapter_index.shape[0]
    rank, width = factors[1].shape[1:]
    freqs = ROPE_BASE ** (-(jnp.arange(HEAD_DIM // 2, dtype=F32) * 2.0) / HEAD_DIM)
    freqs = jnp.tile(freqs, 2 * TILE // HEAD_DIM)[None, :]
    double = 2 * factors[3].shape[3]
    shapes = [
        ((3, seqs, 2 * part), jnp.int32),
        ((2, seqs * part, TILE), F32),
        ((3 * rank, width), BF16),
        ((3 * rank, width + double), BF16),
    ] + [(factor.shape[1:], BF16) for factor in factors[4:]]

    def whole(shape):
        return pl.BlockSpec(shape, lambda i, adapters, where: (0,) * len(shape))

    def one(shape):
        return pl.BlockSpec(
            (1,) + shape, lambda i, adapters, where: (adapters[where[0]],) + (0,) * len(shape)
        )

    return pl.pallas_call(
        prepare_kernel,
        grid_spec=pltpu.PrefetchScalarGridSpec(
            num_scalar_prefetch=2,
            grid=(1,),
            in_specs=[whole(freqs.shape), whole(segment_ids.shape), whole(real_mask.shape)]
            + [one(factor.shape[1:]) for factor in factors],
            out_specs=[whole(shape) for shape, _ in shapes],
        ),
        out_shape=[jax.ShapeDtypeStruct(shape, dtype) for shape, dtype in shapes],
    )(adapter_index, jnp.stack([seq, head]).astype(jnp.int32), freqs, segment_ids, real_mask, *factors)


def by_sequence(
    tokens,
    attn_gain,
    ffn_gain,
    query_weight,
    keyval_weight,
    output_weight,
    gateup_weight,
    down_weight,
    query_down,
    query_up,
    keyval_down,
    keyval_up,
    output_down,
    output_up,
    gateup_down,
    gateup_up,
    ffdown_down,
    ffdown_up,
    segment_ids,
    real_mask,
    adapter_index,
    out_grad,
):
    seqs, part, width = tokens.shape
    groups = lax.axis_size("head")
    seq, head_pos = lax.axis_index("blk"), lax.axis_index("head")
    rows = seqs * part
    span = groups * part
    rank = query_up.shape[1]
    limits, turn, d_qkv, u_qkv, *factors = prepare(
        adapter_index,
        seq,
        head_pos,
        segment_ids,
        real_mask,
        (
            query_down.swapaxes(1, 2),
            query_up,
            keyval_down.swapaxes(2, 3),
            keyval_up,
            output_down.swapaxes(1, 2),
            output_up,
            gateup_down.swapaxes(2, 3),
            gateup_up,
            ffdown_down.swapaxes(1, 2),
            ffdown_up,
        ),
        part,
    )
    (
        w_qkv,
        _,
        _,
        _,
        flat,
        normed,
        inverse1,
        low_qkv,
        queries,
        pairs,
        lse,
        output,
        grad_middle,
        grad_mixed,
        early,
    ) = front(
        tokens,
        out_grad,
        (query_weight, keyval_weight, output_weight, gateup_weight, down_weight),
        limits,
        turn,
        d_qkv,
        u_qkv,
        attn_gain,
        factors,
        ffn_gain,
    )
    flat = flat.reshape(rows, width)
    pairs = pairs.reshape(seqs * span, pairs.shape[2])
    hidden = ffdown_down.shape[1]
    sizes = [width] * 4 + [hidden] * 3 + [width]
    grad_qkv, output, early = attend_back(
        limits, queries, pairs, lse, grad_mixed, turn, output, early
    )
    input_grad, late = first_back(
        grad_qkv, w_qkv, d_qkv, u_qkv, normed, low_qkv, grad_middle, flat, inverse1, attn_gain
    )
    adapters = jnp.arange(query_down.shape[0], dtype=jnp.int32)
    holder = jnp.argmax(adapter_index[None, :] == adapters[:, None], axis=1).astype(jnp.int32)
    found = placed(holder, early, late, sizes, width)
    return (
        output,
        input_grad,
        found[0].swapaxes(1, 2),
        found[1],
        found[2].swapaxes(2, 3),
        found[3],
        found[4].swapaxes(1, 2),
        found[5],
        found[6].swapaxes(2, 3),
        found[7],
        found[8].swapaxes(1, 2),
        found[9],
    )


def solution(mesh):
    in_specs = (
        P(None, ("blk", "head"), None),
        P(),
        P(),
        P("blk", "head"),
        P(None, "blk", "head"),
        P("blk", "head"),
        P(None, "blk", "head"),
        P("blk", "head"),
        P(),
        P(),
        P(),
        P(),
        P(),
        P(),
        P(),
        P(),
        P(),
        P(),
        P(),
        P(),
        P(),
        P(None, ("blk", "head"), None),
    )
    out_specs = (
        P(None, ("blk", "head"), None),
        P(None, ("blk", "head"), None),
        P(),
        P(),
        P(),
        P(),
        P(),
        P(),
        P(),
        P(),
        P(),
        P(),
    )

    def chosen(tokens, *rest):
        if mesh.shape["blk"] == tokens.shape[0] == 8 and mesh.shape["head"] == 4:
            return by_sequence(tokens, *rest)
        return on_device(tokens, *rest)

    return jax.shard_map(
        chosen, mesh=mesh, in_specs=in_specs, out_specs=out_specs, check_vma=False
    )
```

```python
import functools
import math

import jax
import jax.numpy as jnp
import numpy as np
from jax import lax
from jax.experimental import pallas as pl
from jax.experimental.pallas import tpu as pltpu
from jax.sharding import PartitionSpec as P

HEADS = 20
KV_HEADS = 5
HEAD_DIM = 64
WINDOW = 1024


EPSILON = 1e-05
ROPE_BASE = 10000.0
ADAPTER_SCALE = 2.0
MASKED = -1e30


def passed_along(value, axis, steps):
    count = lax.axis_size(axis)
    initial, last = (max(0, -steps), min(count, count - steps))
    return lax.ppermute(value, axis, [(source, source + steps) for source in range(initial, last)])


def rms_scale(values, gain):
    return values * lax.rsqrt(jnp.mean(values * values, axis=-1, keepdims=True) + EPSILON) * gain


def rotate(values, positions, sign):
    half = values.shape[-1] // 2
    freqs = ROPE_BASE ** (-(jnp.arange(half, dtype=jnp.float32) * 2.0) / values.shape[-1])
    angles = positions.astype(jnp.float32)[:, None] * freqs[None, :]
    cosine = jnp.cos(angles)[:, None, :]
    sine = sign * jnp.sin(angles)[:, None, :]
    first = values[..., :half]
    second = values[..., half:]
    return jnp.concatenate(
        [first * cosine - second * sine, second * cosine + first * sine], axis=-1
    )


def gated(gate, upward):
    return jax.nn.silu(gate) * upward


def project(inputs, weight, down, up):
    lowered = jnp.einsum("sci,sir->scr", inputs, down, preferred_element_type=jnp.float32).astype(
        jnp.bfloat16
    )
    extra = ADAPTER_SCALE * jnp.einsum(
        "scr,sro->sco", lowered, up, preferred_element_type=jnp.float32
    )
    return (
        jnp.einsum("sci,io->sco", inputs, weight, preferred_element_type=jnp.float32) + extra,
        lowered,
    )


def project_back(inputs, lowered, grad_out, weight, down, up):
    grad_up = ADAPTER_SCALE * jnp.einsum(
        "scr,sco->sro", lowered, grad_out, preferred_element_type=jnp.float32
    )
    grad_low = (
        ADAPTER_SCALE * jnp.einsum("sco,sro->scr", grad_out, up, preferred_element_type=jnp.float32)
    ).astype(jnp.bfloat16)
    grad_down = jnp.einsum("sci,scr->sir", inputs, grad_low, preferred_element_type=jnp.float32)
    grad_in = jnp.einsum("sco,io->sci", grad_out, weight, preferred_element_type=jnp.float32)
    grad_in = grad_in + jnp.einsum(
        "scr,sir->sci", grad_low, down, preferred_element_type=jnp.float32
    )
    return (grad_in, grad_down, grad_up)


def on_device(
    tokens,
    attn_gain,
    ffn_gain,
    query_weight,
    keyval_weight,
    output_weight,
    gateup_weight,
    down_weight,
    query_down,
    query_up,
    keyval_down,
    keyval_up,
    output_down,
    output_up,
    gateup_down,
    gateup_up,
    ffdown_down,
    ffdown_up,
    segment_ids,
    real_mask,
    adapter_index,
    out_grad,
):
    seqs, per_device, width = tokens.shape
    groups = lax.axis_size("head")
    head_pos = lax.axis_index("head")
    blk_pos = lax.axis_index("blk")
    span = groups * per_device
    heads = HEADS
    head_dim = HEAD_DIM
    kv_heads = KV_HEADS
    local_heads = heads // groups
    share = heads // kv_heads
    reach = (WINDOW - 2) // span + 1
    scale = 1.0 / math.sqrt(head_dim)
    rows_a, rows_b, rows_c, rows_d, rows_e = (
        lax.all_gather(query_weight, "blk", axis=0, tiled=True),
        lax.all_gather(keyval_weight, "blk", axis=1, tiled=True),
        lax.all_gather(output_weight, "blk", axis=0, tiled=True),
        lax.all_gather(gateup_weight, "blk", axis=1, tiled=True),
        lax.all_gather(down_weight, "blk", axis=0, tiled=True),
    )
    w_query, w_keyval, w_output, w_gateup, w_down = (
        lax.all_gather(rows_a, "head", axis=1, tiled=True),
        lax.all_gather(rows_b, "head", axis=2, tiled=True),
        lax.all_gather(rows_c, "head", axis=1, tiled=True),
        lax.all_gather(rows_d, "head", axis=2, tiled=True),
        lax.all_gather(rows_e, "head", axis=1, tiled=True),
    )
    down_query = query_down[adapter_index]
    up_query = query_up[adapter_index]
    down_keyval = keyval_down[adapter_index]
    up_keyval = keyval_up[adapter_index]
    down_output = output_down[adapter_index]
    up_output = output_up[adapter_index]
    down_gateup = gateup_down[adapter_index]
    up_gateup = gateup_up[adapter_index]
    down_ffdown = ffdown_down[adapter_index]
    up_ffdown = ffdown_up[adapter_index]

    def first_norm(values):
        return rms_scale(values, attn_gain)

    def second_norm(values):
        return rms_scale(values, ffn_gain)

    flat = tokens.astype(jnp.float32)
    normed_full, first_norm_back = jax.vjp(first_norm, flat)
    normed = normed_full.astype(jnp.bfloat16)
    queries_pre, low_query = project(normed, w_query, down_query, up_query)
    keys_pre, low_key = project(normed, w_keyval[0], down_keyval[:, 0], up_keyval[:, 0])
    values_pre, low_value = project(normed, w_keyval[1], down_keyval[:, 1], up_keyval[:, 1])
    token_pos = (blk_pos * groups + head_pos) * per_device + jnp.arange(per_device, dtype=jnp.int32)
    queries = rotate(queries_pre.reshape(seqs, per_device, heads, head_dim), token_pos, 1.0).astype(
        jnp.bfloat16
    )
    keys = rotate(keys_pre.reshape(seqs, per_device, kv_heads, head_dim), token_pos, 1.0).astype(
        jnp.bfloat16
    )
    values = values_pre.reshape(seqs, per_device, kv_heads, head_dim).astype(jnp.bfloat16)
    owner = np.array(
        [
            [(group * local_heads + slot) // share for slot in range(local_heads)]
            for group in range(groups)
        ]
    )
    slot_of = jnp.arange(local_heads, dtype=jnp.int32)
    sender = jnp.asarray(
        (owner[:, :, None] == np.arange(kv_heads)[None, None, :]).astype(np.float32), jnp.bfloat16
    )
    spread = (slot_of[:, None] == jnp.arange(local_heads, dtype=jnp.int32)[None, :]).astype(
        jnp.bfloat16
    )
    pair = jnp.stack([keys, values], axis=3)
    outgoing = jnp.einsum(
        "sckxd,gmk->scgmxd", pair, sender, preferred_element_type=jnp.float32
    ).astype(jnp.bfloat16)
    outgoing = outgoing.reshape(seqs, per_device, groups, local_heads * 2 * head_dim)
    query_send = queries.reshape(seqs, per_device, groups, local_heads * head_dim)
    query_here, pair_here = (
        lax.all_to_all(query_send, "head", split_axis=2, concat_axis=1, tiled=True),
        lax.all_to_all(outgoing, "head", split_axis=2, concat_axis=1, tiled=True),
    )
    query_here = query_here.reshape(seqs, span, local_heads, head_dim)
    pair_here = pair_here.reshape(seqs, span, local_heads, 2, head_dim)
    received = [pair_here]
    moving = pair_here
    for hop in range(reach):
        moving = passed_along(moving, "blk", 1)
        received.append(moving)
    window_pairs = jnp.stack(received, axis=1)
    query_pos = blk_pos * span + jnp.arange(span, dtype=jnp.int32)
    key_pos = (blk_pos - jnp.arange(reach + 1, dtype=jnp.int32))[:, None] * span + jnp.arange(
        span, dtype=jnp.int32
    )[None, :]
    safe_pos = jnp.clip(key_pos, 0, segment_ids.shape[1] - 1)
    query_segment = lax.dynamic_slice_in_dim(segment_ids, blk_pos * span, span, 1)
    key_segment = segment_ids[:, safe_pos]
    key_real = real_mask[:, safe_pos]
    distance = query_pos[:, None, None] - key_pos[None]
    allowed = (key_pos[None] >= 0) & (distance >= 0) & (distance < WINDOW)
    allowed = allowed & (query_segment[:, :, None, None] == key_segment[:, None])
    allowed = allowed & ((key_real[:, None] == 1) | (distance[None] == 0))
    batch = 1
    target = max(1, 512 // span)
    for option in range(1, seqs + 1):
        if seqs % option == 0 and option <= target:
            batch = option
    count = seqs // batch

    def grouped(array):
        return array.reshape((count, batch) + array.shape[1:])

    def scores_of(query_part, pair_part, allowed_part):
        keys_wide = jnp.einsum(
            "gjlmd,hm->gjlhd", pair_part[:, :, :, :, 0], spread, preferred_element_type=jnp.float32
        ).astype(jnp.bfloat16)
        values_wide = jnp.einsum(
            "gjlmd,hm->gjlhd", pair_part[:, :, :, :, 1], spread, preferred_element_type=jnp.float32
        ).astype(jnp.bfloat16)
        raw = (
            jnp.einsum(
                "gqhd,gjlhd->ghqjl", query_part, keys_wide, preferred_element_type=jnp.float32
            )
            * scale
        )
        raw = jnp.where(allowed_part[:, None], raw, MASKED)
        return (raw, keys_wide, values_wide)

    def attend(pieces):
        query_part, pair_part, allowed_part = pieces
        raw, keys_wide, values_wide = scores_of(query_part, pair_part, allowed_part)
        top = jnp.max(raw, axis=(3, 4), keepdims=True)
        shifted = jnp.exp(raw - top)
        total = jnp.sum(shifted, axis=(3, 4), keepdims=True)
        probs_low = (shifted / total).astype(jnp.bfloat16)
        result = jnp.einsum(
            "ghqjl,gjlhd->gqhd", probs_low, values_wide, preferred_element_type=jnp.float32
        )
        return (result.astype(jnp.bfloat16), top + jnp.log(total))

    attended, logsum = lax.map(
        attend, (grouped(query_here), grouped(window_pairs), grouped(allowed))
    )
    mixed = lax.all_to_all(
        attended.reshape(seqs, span, local_heads * head_dim),
        "head",
        split_axis=1,
        concat_axis=2,
        tiled=True,
    )
    branch_attn, low_output = project(mixed, w_output, down_output, up_output)
    middle = flat + branch_attn
    normed2_full, second_norm_back = jax.vjp(second_norm, middle)
    normed2 = normed2_full.astype(jnp.bfloat16)
    gate, low_gate = project(normed2, w_gateup[0], down_gateup[:, 0], up_gateup[:, 0])
    upward, low_upward = project(normed2, w_gateup[1], down_gateup[:, 1], up_gateup[:, 1])
    activated_full, gated_back = jax.vjp(gated, gate, upward)
    activated = activated_full.astype(jnp.bfloat16)
    branch_ffn, low_ffdown = project(activated, w_down, down_ffdown, up_ffdown)
    output = (middle + branch_ffn).astype(jnp.bfloat16)
    grad_activated, gd_ffdown, gu_ffdown = project_back(
        activated, low_ffdown, out_grad, w_down, down_ffdown, up_ffdown
    )
    grad_gate, grad_upward = gated_back(grad_activated)
    grad_in_gate, gd_gate, gu_gate = project_back(
        normed2,
        low_gate,
        grad_gate.astype(jnp.bfloat16),
        w_gateup[0],
        down_gateup[:, 0],
        up_gateup[:, 0],
    )
    grad_in_up, gd_up, gu_up = project_back(
        normed2,
        low_upward,
        grad_upward.astype(jnp.bfloat16),
        w_gateup[1],
        down_gateup[:, 1],
        up_gateup[:, 1],
    )
    grad_middle = out_grad.astype(jnp.float32) + second_norm_back(grad_in_gate + grad_in_up)[0]
    grad_mixed, gd_output, gu_output = project_back(
        mixed, low_output, grad_middle.astype(jnp.bfloat16), w_output, down_output, up_output
    )
    grad_send = grad_mixed.astype(jnp.bfloat16).reshape(
        seqs, per_device, groups, local_heads * head_dim
    )
    grad_here = lax.all_to_all(grad_send, "head", split_axis=2, concat_axis=1, tiled=True).reshape(
        seqs, span, local_heads, head_dim
    )
    spread_full = spread.astype(jnp.float32)

    def attend_back(pieces):
        query_part, pair_part, allowed_part, logsum_part, grad_part = pieces
        raw, keys_wide, values_wide = scores_of(query_part, pair_part, allowed_part)
        probs = jnp.exp(raw - logsum_part)
        probs_low = probs.astype(jnp.bfloat16)
        grad_probs = jnp.einsum(
            "gqhd,gjlhd->ghqjl", grad_part, values_wide, preferred_element_type=jnp.float32
        )
        inner = jnp.sum(probs * grad_probs, axis=(3, 4), keepdims=True)
        grad_raw = (probs * (grad_probs - inner)).astype(jnp.bfloat16)
        grad_query = scale * jnp.einsum(
            "ghqjl,gjlhd->gqhd", grad_raw, keys_wide, preferred_element_type=jnp.float32
        )
        grad_keys = scale * jnp.einsum(
            "ghqjl,gqhd->gjlhd", grad_raw, query_part, preferred_element_type=jnp.float32
        )
        grad_values = jnp.einsum(
            "ghqjl,gqhd->gjlhd", probs_low, grad_part, preferred_element_type=jnp.float32
        )
        both = jnp.stack([grad_keys, grad_values], axis=4)
        folded = jnp.einsum("gjlhxd,hm->gjlmxd", both, spread_full, precision=lax.Precision.HIGHEST)
        return (grad_query, folded)

    grad_query, grad_pairs = lax.map(
        attend_back,
        (grouped(query_here), grouped(window_pairs), grouped(allowed), logsum, grouped(grad_here)),
    )
    grad_pairs = grad_pairs.reshape(seqs, reach + 1, span, local_heads, 2, head_dim)
    carried = grad_pairs[:, reach]
    for hop in range(reach - 1, -1, -1):
        carried = (
            passed_along(carried.astype(jnp.bfloat16), "blk", -1).astype(carried.dtype)
            + grad_pairs[:, hop]
        )
    grad_query = rotate(grad_query.reshape(seqs, span, local_heads, head_dim), query_pos, -1.0)
    grad_query = grad_query.astype(jnp.bfloat16).reshape(seqs, span, local_heads * head_dim)
    grad_queries_pre = lax.all_to_all(grad_query, "head", split_axis=1, concat_axis=2, tiled=True)
    grad_pair_tok = lax.all_to_all(
        carried.reshape(seqs, span, local_heads * 2 * head_dim).astype(jnp.bfloat16),
        "head",
        split_axis=1,
        concat_axis=2,
        tiled=True,
    ).astype(jnp.float32)
    grad_pair_tok = grad_pair_tok.reshape(seqs, per_device, groups, local_heads, 2, head_dim)
    grad_pair_heads = jnp.einsum(
        "scgmxd,gmk->sckxd",
        grad_pair_tok,
        sender.astype(jnp.float32),
        precision=lax.Precision.HIGHEST,
    )
    grad_keys_pre = (
        rotate(grad_pair_heads[:, :, :, 0], token_pos, -1.0)
        .astype(jnp.bfloat16)
        .reshape(seqs, per_device, kv_heads * head_dim)
    )
    grad_values_pre = (
        grad_pair_heads[:, :, :, 1]
        .astype(jnp.bfloat16)
        .reshape(seqs, per_device, kv_heads * head_dim)
    )
    grad_in_query, gd_query, gu_query = project_back(
        normed, low_query, grad_queries_pre, w_query, down_query, up_query
    )
    grad_in_key, gd_key, gu_key = project_back(
        normed, low_key, grad_keys_pre, w_keyval[0], down_keyval[:, 0], up_keyval[:, 0]
    )
    grad_in_value, gd_value, gu_value = project_back(
        normed, low_value, grad_values_pre, w_keyval[1], down_keyval[:, 1], up_keyval[:, 1]
    )
    grad_normed = grad_in_query + grad_in_key + grad_in_value
    input_grad = (grad_middle + first_norm_back(grad_normed)[0]).astype(jnp.bfloat16)
    chooser = (
        adapter_index[:, None] == jnp.arange(query_down.shape[0], dtype=jnp.int32)[None, :]
    ).astype(jnp.float32)

    def per_adapter(per_sequence):
        return jnp.einsum("sa,s...->a...", chooser, per_sequence, precision=lax.Precision.HIGHEST)

    sums = lax.psum(
        (
            per_adapter(gd_query),
            per_adapter(gu_query),
            per_adapter(jnp.stack([gd_key, gd_value], axis=1)),
            per_adapter(jnp.stack([gu_key, gu_value], axis=1)),
            per_adapter(gd_output),
            per_adapter(gu_output),
            per_adapter(jnp.stack([gd_gate, gd_up], axis=1)),
            per_adapter(jnp.stack([gu_gate, gu_up], axis=1)),
            per_adapter(gd_ffdown),
            per_adapter(gu_ffdown),
        ),
        ("blk", "head"),
    )
    return (
        output,
        input_grad,
        sums[0],
        sums[1],
        sums[2],
        sums[3],
        sums[4],
        sums[5],
        sums[6],
        sums[7],
        sums[8],
        sums[9],
    )


MESH = pl.DeviceIdType.MESH
F32 = jnp.float32
BF16 = jnp.bfloat16
TILE = 128
ANYWHERE = pl.BlockSpec(memory_space=pl.ANY)


def dot(left, right, left_dim=1, right_dim=0):
    return lax.dot_general(
        left, right, (((left_dim,), (right_dim,)), ((), ())), preferred_element_type=F32
    )


def place():
    blk, head = lax.axis_index("blk"), lax.axis_index("head")
    return blk // 2, blk % 2, head // 2, head % 2


def device(z, x, y, core):
    return (z * 2 + x, y * 2 + core)


FLIPS = ((0, 0), (0, 1), (1, 0), (1, 1))
BZ, BH, LINE, PY, PX, CO = range(6)
END, EX, EXW, PACK, NORM, PAIRS, KEYS, GIVE, GET, QUERY, ATT0, ATT1, ATT2 = range(6, 19)
TOKENS, GRADS = range(2)


def remote(source, target, out, into, other):
    return pltpu.make_async_remote_copy(
        src_ref=source,
        dst_ref=target,
        send_sem=out,
        recv_sem=into,
        device_id=other,
        device_id_type=MESH,
    )


class Spread:
    def __init__(self, sources, target, lines, sems, planes=(), shares=None):
        self.sources, self.target, self.lines = sources, target, lines
        self.planes, self.shares = planes, shares or {}
        self.z, self.x, self.y, self.core = place()
        self.z_in, self.x_in, self.y_in, self.d_in, self.c_in = sems[:5]
        self.z_out, self.x_out, self.y_out, self.d_out, self.c_out = sems[5:10]

    @staticmethod
    def semaphores(parts, lines):
        dma = pltpu.SemaphoreType.DMA
        return [
            dma((parts, lines, 4)),
            dma((parts, lines)),
            dma((parts, lines)),
            dma((parts, lines, 2)),
            dma((parts, lines, 4)),
            dma((parts, 2, lines, 4)),
            dma((parts, lines)),
            dma((parts, lines)),
            dma((parts, lines, 2)),
            dma((parts, lines, 4)),
        ]

    def inside(self, z):
        return (z >= 0) & (z < self.lines)

    def slot(self, part, z, flip_x=0, flip_y=0):
        return self.target(part, z, (self.x + flip_x) % 2, (self.y + flip_y) % 2, self.core)

    def along_z(self, part, source, z, side, flip_x=0, flip_y=0):
        which = flip_x * 2 + flip_y
        return remote(
            source,
            self.slot(part, z, flip_x, flip_y),
            self.z_out.at[part, (side + 1) // 2, z, which],
            self.z_in.at[part, z, which],
            device(self.z + side, self.x, self.y, self.core),
        )

    def along_x(self, part, source, z):
        return remote(
            source,
            self.slot(part, z),
            self.x_out.at[part, z],
            self.x_in.at[part, z],
            device(self.z, 1 - self.x, self.y, self.core),
        )

    def along_y(self, part, source, z):
        return remote(
            source,
            self.slot(part, z),
            self.y_out.at[part, z],
            self.y_in.at[part, z],
            device(self.z, self.x, 1 - self.y, self.core),
        )

    def across(self, part, source, z, flip_x, flip_y):
        which = flip_x * 2 + flip_y
        return remote(
            source,
            self.slot(part, z, flip_x, flip_y),
            self.c_out.at[part, z, which],
            self.c_in.at[part, z, which],
            device(self.z, self.x, self.y, 1 - self.core),
        )

    def piece(self, part, ref, which):
        if ref.shape[0] < 32:
            size = ref.shape[1] // 2
            return ref.at[:, pl.ds(which * size, size)]
        count = ref.shape[0]
        first = int(count * self.shares.get(part, 0.5) + 15) // 16 * 16
        return ref.at[pl.ds(0, first)] if which == 0 else ref.at[pl.ds(first, count - first)]

    def diagonal(self, part, z, which):
        if which == 0:
            ref = self.slot(part, z, 0, 1)
            other = device(self.z, 1 - self.x, self.y, self.core)
        else:
            ref = self.slot(part, z, 1, 0)
            other = device(self.z, self.x, 1 - self.y, self.core)
        ref = self.piece(part, ref, which)
        return remote(ref, ref, self.d_out.at[part, z, which], self.d_in.at[part, z, which], other)

    def arrived(self, ref, out, into):
        remote(ref, ref, out, into, device(self.z, self.x, self.y, 1 - self.core)).wait_recv()

    def toward(self, part, source, z, flip_x, flip_y, sides=(1, -1)):
        for side in sides:

            @pl.when(self.inside(self.z + side))
            def _():
                self.along_z(part, source, z, side, flip_x, flip_y).start()

    def hand_on(self, part, source, z):
        self.along_x(part, source, z).start()
        self.along_y(part, source, z).start()
        self.across(part, source, z, 0, 0).start()

    def begin_line(self, part):
        self.toward(part, self.sources[part], self.z, 0, 0)

    def begin_plane(self, part):
        self.hand_on(part, self.sources[part], self.z)

    def line_step(self, part, distance, side):
        z = self.z - side * distance

        @pl.when(self.inside(z))
        def _():
            for flip_x, flip_y in FLIPS if part in self.planes else FLIPS[:1]:
                ref = self.slot(part, z, flip_x, flip_y)
                which = flip_x * 2 + flip_y
                self.arrived(ref, self.z_out.at[part, 0, z, which], self.z_in.at[part, z, which])
                self.toward(part, ref, z, flip_x, flip_y, (side,))
                if part in self.planes:
                    self.across(part, ref, z, flip_x, flip_y).start()
            if part not in self.planes:
                self.hand_on(part, ref, z)

    def y_step(self, part, z):
        ref = self.slot(part, z, 0, 1)
        self.arrived(ref, self.y_out.at[part, z], self.y_in.at[part, z])
        self.diagonal(part, z, 0).start()
        self.across(part, ref, z, 0, 1).start()
        if part in self.planes:
            self.toward(part, ref, z, 0, 1)

    def x_step(self, part, z):
        ref = self.slot(part, z, 1, 0)
        self.arrived(ref, self.x_out.at[part, z], self.x_in.at[part, z])
        self.diagonal(part, z, 1).start()
        self.across(part, ref, z, 1, 0).start()
        if part in self.planes:
            self.toward(part, ref, z, 1, 0)

    def corner_step(self, part, z):
        ref = self.slot(part, z, 1, 1)
        for which in (0, 1):
            self.arrived(
                self.piece(part, ref, which),
                self.d_out.at[part, z, which],
                self.d_in.at[part, z, which],
            )
        self.across(part, ref, z, 1, 1).start()
        if part in self.planes:
            self.toward(part, ref, z, 1, 1)

    def sent(self, part, z):
        mine = self.slot(part, z)
        self.along_x(part, mine, z).wait_send()
        self.along_y(part, mine, z).wait_send()
        self.diagonal(part, z, 0).wait_send()
        self.diagonal(part, z, 1).wait_send()

    def end(self, part):
        for z in range(self.lines):
            for flip_x, flip_y in FLIPS:
                which = flip_x * 2 + flip_y
                x, y = (self.x + flip_x) % 2, (self.y + flip_y) % 2
                self.arrived(
                    self.target(part, z, x, y, 1 - self.core),
                    self.c_out.at[part, z, which],
                    self.c_in.at[part, z, which],
                )
                mine = self.slot(part, z, flip_x, flip_y)
                self.across(part, mine, z, flip_x, flip_y).wait_send()
                if part not in self.planes and which > 0:
                    continue
                for side in (1, -1):

                    @pl.when(self.inside(self.z + side) & ((self.z - z) * side >= 0))
                    def _():
                        self.along_z(part, mine, z, side, flip_x, flip_y).wait_send()

            if part not in self.planes:
                self.sent(part, z)
        if part in self.planes:
            self.sent(part, self.z)

    def at(self, distance, run):
        if distance == 0:
            run(self.z)
            return
        for side in (1, -1):
            pl.when(self.inside(self.z - side * distance))(
                functools.partial(run, self.z - side * distance)
            )

    def do(self, kind, part, distance=0, side=0):
        if kind == BZ:
            self.begin_line(part)
        elif kind == BH:
            self.begin_plane(part)
        elif kind == LINE:
            self.line_step(part, distance, side)
        else:
            run = {PY: self.y_step, PX: self.x_step, CO: self.corner_step}[kind]
            self.at(distance, functools.partial(run, part))

    def all_steps(self, part):
        result = []
        for stage in range(1, self.lines + 2):
            steps = []
            if stage < self.lines:
                steps += [(LINE, part, stage, 1), (LINE, part, stage, -1)]
            if stage >= 2:
                steps += [(CO, part, stage - 2)]
            if stage <= self.lines:
                steps += [(PY, part, stage - 1), (PX, part, stage - 1)]
            result += [functools.partial(self.do, *step) for step in steps]
        return result


def paired(own, other, core):
    own, other = own.astype(F32), other.astype(F32)
    return [jnp.where(core == 0, own, other), jnp.where(core == 0, other, own)]


def in_pairs(array):
    half = array.shape[1] // 2
    size = 2 * KV_HEADS * HEAD_DIM // 4
    keys = jnp.concatenate([array[:, :size], array[:, half : half + size]], axis=1)
    values = jnp.concatenate(
        [array[:, size : 2 * size], array[:, half + size : half + 2 * size]], axis=1
    )
    pieces = []
    for head in range(KV_HEADS):
        cut = slice(head * HEAD_DIM, (head + 1) * HEAD_DIM)
        pieces += [keys[:, cut], values[:, cut]]
    return jnp.concatenate(pieces, axis=1)


def windows(blocks, span, low_part):
    reach = WINDOW + TILE
    fixed = [(0, (block + 1) * span) for block in range(WINDOW // span)]
    offset = TILE * (low_part // 2 + 1) - reach
    return fixed, reach, offset


def tiles_of(ref, flipped):
    lane = lax.broadcasted_iota(jnp.int32, (ref.shape[0], TILE), 1)
    result = []
    for slot in range(4):
        tile = ref[:, slot // 2 * TILE : (slot // 2 + 1) * TILE].astype(F32)
        if (slot % 2 == 0) == flipped:
            tile = pltpu.roll(tile, HEAD_DIM, 1)
        keep = lane >= HEAD_DIM if flipped else lane < HEAD_DIM
        result.append(jnp.where(keep, tile, 0.0).astype(BF16))
    return result


def joined(rows, flipped):
    span = rows.shape[0] // 4
    heads = [rows[slot * span : (slot + 1) * span] for slot in range(4)]
    lane = lax.broadcasted_iota(jnp.int32, (span, TILE), 1)
    result = []
    for first, second in ((heads[0], heads[1]), (heads[2], heads[3])):
        if flipped:
            first = pltpu.roll(first, HEAD_DIM, 1)
        else:
            second = pltpu.roll(second, HEAD_DIM, 1)
        result.append(jnp.where(lane < HEAD_DIM, first, second))
    return result


def bias_of(limits_ref, block, start, count):
    key = start + lax.broadcasted_iota(jnp.int32, (count, TILE), 0)
    least = limits_ref[0, pl.ds(block, 1), :]
    most = limits_ref[1, pl.ds(block, 1), :]
    self_pos = limits_ref[2, pl.ds(block, 1), :]
    allowed = ((key >= least) & (key <= most)) | (key == self_pos)
    bias = jnp.where(allowed, 0.0, MASKED)
    return jnp.concatenate([bias, bias], axis=1)


def each_block(blocks, body, between=lambda: None):
    span = 4 * HEAD_DIM
    fixed, reach, offset = windows(blocks, span, lax.axis_index("head"))
    for block, (start, count) in enumerate(fixed):
        body(block, start, count)
    between()

    @pl.loop(len(fixed), blocks)
    def _(block):
        body(block, pl.multiple_of(block * span + offset, TILE), reach)


def meet(others):
    barrier = pltpu.get_barrier_semaphore()
    for other in others:
        pl.semaphore_signal(barrier, inc=1, device_id=other, device_id_type=MESH)
    pl.semaphore_wait(barrier, len(others))


def along(count):
    blk, head = lax.axis_index("blk"), lax.axis_index("head")
    return [((blk + ahead) % count, head) for ahead in range(1, count)]


def beside():
    z, x, y, core = place()
    return [
        device(z, x, y, 1 - core),
        device(z, x, 1 - y, core),
        device(z, x, 1 - y, 1 - core),
    ]


class Exchange:
    def __init__(self, source, target, size, out, into, local):
        count = target.shape[0]
        blk, head = lax.axis_index("blk"), lax.axis_index("head")
        self.own = pltpu.make_async_copy(source.at[pl.ds(blk * size, size)], target.at[blk], local)
        self.copies, self.arrivals = [], []
        for at, (other, _) in enumerate(along(count)):
            self.copies.append(
                remote(
                    source.at[pl.ds(other * size, size)],
                    target.at[blk],
                    out.at[at],
                    into.at[at],
                    (other, head),
                )
            )
            giver = (blk + count - 1 - at) % count
            self.arrivals.append(
                remote(target.at[giver], target.at[giver], out.at[at], into.at[at], (other, head))
            )

    def start(self):
        self.own.start()
        for copy in self.copies:
            copy.start()

    def wait(self):
        for copy in self.arrivals:
            copy.wait_recv()
        for copy in self.copies:
            copy.wait_send()
        self.own.wait()


class Quarters:
    def __init__(self, terms, low, got, out, into):
        z, x, y, core = place()
        self.size = low.shape[1] // 4
        self.terms, self.low, self.got = terms, low, got
        self.mine = pl.ds((y * 2 + core) * self.size, self.size)
        self.copies = []
        for at, (flip_y, flip_core) in enumerate(((0, 1), (1, 0), (1, 1))):
            other_y, other_core = (y + flip_y) % 2, (core + flip_core) % 2
            theirs = pl.ds((other_y * 2 + other_core) * self.size, self.size)
            self.copies.append(
                remote(
                    low.at[:, theirs],
                    got.at[at],
                    out.at[at],
                    into.at[at],
                    device(z, x, other_y, other_core),
                )
            )

    def start(self):
        self.low[...] = self.terms[...].astype(BF16)
        for copy in self.copies:
            copy.start()

    def total(self):
        for copy in self.copies:
            copy.wait_recv()
        total = self.terms[:, self.mine]
        for at in range(3):
            total = total + self.got[at].astype(F32)
        return total.astype(BF16)

    def end(self):
        for copy in self.copies:
            copy.wait_send()


def turned(tile, cosine, sine, only_low=False):
    lane = lax.broadcasted_iota(jnp.int32, tile.shape, 1)
    half = HEAD_DIM // 2
    partner = jnp.where(
        lane % HEAD_DIM < half, pltpu.roll(tile, TILE - half, 1), pltpu.roll(tile, half, 1)
    )
    result = tile * cosine + partner * sine
    return jnp.where(lane < HEAD_DIM, result, tile) if only_low else result


def attend_back_kernel(
    lines,
    limits_ref,
    q_ref,
    kv_ref,
    lse_ref,
    grad_ref,
    turn_ref,
    output_ref,
    terms_ref,
    dqkv_ref,
    moved_ref,
    shared_ref,
    q_rows,
    g_rows,
    kv_turned,
    total,
    pair_low,
    pair_got,
    kept,
    y_low,
    y_got,
    low,
    got,
    shard,
    pair_out,
    pair_in,
    y_out,
    y_in,
    move_out,
    move_in,
    four_out,
    four_in,
    local,
    *sems,
):
    blocks, span = q_rows.shape[0], q_rows.shape[2]
    width = q_ref.shape[1]
    groups = width // (2 * TILE)
    scale = HEAD_DIM**-0.5
    z, x, y, core = place()
    size = shard.shape[1]

    def target(part, z, x, y, core):
        return shared_ref.at[z * 2 + x, :, pl.ds((y * 2 + core) * size, size)]

    spread = Spread([shard], target, lines, sems)
    meet(along(blocks) + beside())
    exchange = Exchange(output_ref, moved_ref, span, move_out, move_in, local.at[0])
    quarters = Quarters(terms_ref, low, got, four_out, four_in)
    quarters.start()
    own = pltpu.make_async_copy(shard, target(0, z, x, y, core), local.at[1])

    def gather_start():
        shard[...] = quarters.total()
        own.start()
        spread.begin_line(0)
        spread.begin_plane(0)

    steps = spread.all_steps(0)

    def some(count):
        def run():
            for _ in range(count):
                steps.pop(0)()

        return run

    later = [None, gather_start, some(4), some(3), some(4), exchange.start]
    later += [some(3), some(3), some(1)]

    def pump():
        if later:
            step = later.pop(0)
            if step is not None:
                step()

    def pair_copy(m):
        return remote(
            pair_low.at[m, 1 - core],
            pair_got.at[m],
            pair_out.at[m],
            pair_in.at[m],
            device(z, x, y, 1 - core),
        )

    def y_copy(m):
        return remote(
            y_low.at[m], y_got.at[m], y_out.at[m], y_in.at[m], device(z, x, 1 - y, core)
        )

    def give(m):
        whole = total[...].reshape(blocks, 4, span, TILE)
        for at in range(4):
            pair_low[m, at % 2, at // 2] = whole[:, at].astype(BF16)
        spot = total.reshape(blocks, 4, span, TILE)
        for at in range(2):
            kept[m, at] = spot[:, at * 2 + core]
        pair_copy(m).start()

    def add_pair(m):
        pair_copy(m).wait_recv()
        y_low[m] = (kept[m, 1 - y] + pair_got[m, 1 - y].astype(F32)).astype(BF16)
        y_copy(m).start()

    def add_y(m):
        y_copy(m).wait_recv()
        tile = kept[m, y] + pair_got[m, y].astype(F32) + y_got[m].astype(F32)
        tile = turned(tile.reshape(blocks * span, TILE), turn_ref[0], -turn_ref[1], True)
        at = width + m * TILE
        dqkv_ref[:, at : at + TILE] = tile.astype(BF16)

    for m in range(groups):
        columns = slice(m * 2 * TILE, (m + 1) * 2 * TILE)
        tile = slice(m * TILE, (m + 1) * TILE)
        for slot, rows in enumerate(tiles_of(q_ref[:, columns], False)):
            q_rows[:, slot] = (rows * BF16(scale)).reshape(blocks, span, TILE)
        for slot, rows in enumerate(tiles_of(grad_ref[:, columns], True)):
            g_rows[:, slot] = rows.reshape(blocks, span, TILE)
        kv_turned[...] = kv_ref[:, tile].astype(F32).T.astype(BF16)
        total[...] = jnp.zeros_like(total)

        def body(block, start, count):
            keys = pl.ds(start, count)
            queries = q_rows[block].reshape(4 * span, TILE)
            grads = g_rows[block].reshape(4 * span, TILE)
            scores = dot(kv_ref[keys, tile], queries, 1, 1)
            scores = scores + bias_of(limits_ref, block, start, count)
            probs = jnp.exp(scores - lse_ref[m, pl.ds(block, 1), :])
            grad_probs = dot(kv_ref[keys, tile], grads, 1, 1)
            inner = jnp.sum(probs * grad_probs, axis=0, keepdims=True)
            grad_scores = (probs * (grad_probs - inner)).astype(BF16)
            total[keys, :] += dot(grad_scores, queries) + dot(probs.astype(BF16), grads)
            grad_q = (dot(kv_turned[:, keys], grad_scores) * scale).T
            rows = pl.ds(block * span, span)
            cosine, sine = turn_ref[0, rows, :], -turn_ref[1, rows, :]
            for at, part in enumerate(joined(grad_q, False)):
                at = m * 2 * TILE + at * TILE
                dqkv_ref[rows, at : at + TILE] = turned(part, cosine, sine).astype(BF16)

        each_block(blocks, body, pump)
        pump()
        give(m)
        if m >= 1:
            add_pair(m - 1)
        if m >= 2:
            add_y(m - 2)
    while later:
        pump()
    add_pair(groups - 1)
    add_y(groups - 2)
    spread.end(0)
    own.wait()
    exchange.wait()
    quarters.end()
    add_y(groups - 1)
    for m in range(groups):
        pair_copy(m).wait_send()
        y_copy(m).wait_send()


def attend_back(limits, queries, pairs, lse, grads, turn, output, terms):
    rows, width = queries.shape
    blocks = limits.shape[1]
    span = rows // blocks
    groups = width // (2 * TILE)
    rank, total = terms.shape
    seqs = lax.axis_size("blk")
    each = pltpu.VMEM((blocks, 4, span, TILE), BF16)
    dma = pltpu.SemaphoreType.DMA
    vmem = pl.BlockSpec(memory_space=pltpu.VMEM)
    shape = jax.ShapeDtypeStruct
    return pl.pallas_call(
        functools.partial(attend_back_kernel, seqs // 2),
        out_shape=[
            shape((rows, width + pairs.shape[1]), BF16),
            shape((seqs, span, width), BF16),
            shape((seqs, rank, total), BF16),
        ],
        in_specs=[vmem] * 8,
        out_specs=[vmem, ANYWHERE, ANYWHERE],
        scratch_shapes=[
            each,
            each,
            pltpu.VMEM((TILE, pairs.shape[0]), BF16),
            pltpu.VMEM((pairs.shape[0], TILE), F32),
            pltpu.VMEM((groups, 2, 2, blocks, span, TILE), BF16),
            pltpu.VMEM((groups, 2, blocks, span, TILE), BF16),
            pltpu.VMEM((groups, 2, blocks, span, TILE), F32),
            pltpu.VMEM((groups, blocks, span, TILE), BF16),
            pltpu.VMEM((groups, blocks, span, TILE), BF16),
            pltpu.VMEM((rank, total), BF16),
            pltpu.VMEM((3, rank, total // 4), BF16),
            pltpu.VMEM((rank, total // 4), BF16),
            dma((groups,)),
            dma((groups,)),
            dma((groups,)),
            dma((groups,)),
            dma((seqs - 1,)),
            dma((seqs - 1,)),
            dma((3,)),
            dma((3,)),
            dma((2,)),
            *Spread.semaphores(1, seqs // 2),
        ],
        compiler_params=pltpu.CompilerParams(
            collective_id=1, has_side_effects=True, vmem_limit_bytes=56 << 20
        ),
    )(limits, queries, pairs, lse, grads, turn, output, terms)


def first_back_kernel(
    lines,
    dqkv_ref,
    weight_ref,
    down_ref,
    up_ref,
    normed_ref,
    low_ref,
    middle_ref,
    flat_ref,
    inverse_ref,
    gain_ref,
    moved_ref,
    shared_ref,
    result,
    terms,
    low,
    got,
    shard,
    move_out,
    move_in,
    four_out,
    four_in,
    local,
    *sems,
):
    blocks, span = moved_ref.shape[:2]
    z, x, y, core = place()
    size = shard.shape[1]
    rank = down_ref.shape[0] // 3
    width = flat_ref.shape[1]

    def target(part, z, x, y, core):
        return shared_ref.at[z * 2 + x, :, pl.ds((y * 2 + core) * size, size)]

    spread = Spread([shard], target, lines, sems)
    meet(along(blocks) + beside())
    grad_low = (ADAPTER_SCALE * dot(dqkv_ref[...], up_ref[...], 1, 1)).astype(BF16)
    grad_up = ADAPTER_SCALE * dot(low_ref[...], dqkv_ref[...], 0, 0)
    grad_down = dot(grad_low, normed_ref[...], 0, 0)
    terms[:, :width] = grad_up[:rank, :width]
    at = width
    while at < dqkv_ref.shape[1]:
        lane = lax.broadcasted_iota(jnp.int32, (rank, TILE), 1)
        terms[:, at : at + TILE] = jnp.where(
            lane < HEAD_DIM,
            grad_up[rank : 2 * rank, at : at + TILE],
            grad_up[2 * rank :, at : at + TILE],
        )
        at += TILE
    for which in range(3):
        terms[:, at : at + width] = grad_down[which * rank : (which + 1) * rank]
        at += width
    if at < terms.shape[1]:
        terms[:, at:] = jnp.zeros((rank, terms.shape[1] - at), F32)
    quarters = Quarters(terms, low, got, four_out, four_in)
    quarters.start()
    own = pltpu.make_async_copy(shard, target(0, z, x, y, core), local.at[1])
    exchange = Exchange(result, moved_ref, span, move_out, move_in, local.at[0])
    grad = dot(dqkv_ref[...], weight_ref[...], 1, 1) + dot(grad_low, down_ref[...])
    shard[...] = quarters.total()
    own.start()
    spread.begin_line(0)
    spread.begin_plane(0)
    weighted = grad * gain_ref[...]
    flat, inverse = flat_ref[...].astype(F32), inverse_ref[...]
    mean = jnp.mean(flat * weighted, axis=1, keepdims=True)
    grad = middle_ref[...] + inverse * weighted - flat * (inverse * inverse * inverse * mean)
    result[...] = grad.astype(BF16)
    steps = spread.all_steps(0)
    for step in steps[:11]:
        step()
    exchange.start()
    for step in steps[11:]:
        step()
    spread.end(0)
    own.wait()
    quarters.end()
    exchange.wait()


def first_back(grad_qkv, weight, down, up, normed, low, middle, flat, inverse, gain):
    rows, width = flat.shape
    rank = down.shape[0] // 3
    seqs, heads = lax.axis_size("blk"), lax.axis_size("head")
    total = 3 * width + weight.shape[1]
    total += -total % (2 * heads * TILE)
    dma = pltpu.SemaphoreType.DMA
    vmem = pl.BlockSpec(memory_space=pltpu.VMEM)
    shape = jax.ShapeDtypeStruct
    return pl.pallas_call(
        functools.partial(first_back_kernel, seqs // 2),
        out_shape=[
            shape((seqs, rows // seqs, width), BF16),
            shape((seqs, rank, total), BF16),
        ],
        in_specs=[vmem] * 10,
        out_specs=[ANYWHERE, ANYWHERE],
        scratch_shapes=[
            pltpu.VMEM((rows, width), BF16),
            pltpu.VMEM((rank, total), F32),
            pltpu.VMEM((rank, total), BF16),
            pltpu.VMEM((3, rank, total // 4), BF16),
            pltpu.VMEM((rank, total // 4), BF16),
            dma((seqs - 1,)),
            dma((seqs - 1,)),
            dma((3,)),
            dma((3,)),
            dma((2,)),
            *Spread.semaphores(1, seqs // 2),
        ],
        compiler_params=pltpu.CompilerParams(
            collective_id=2, has_side_effects=True, vmem_limit_bytes=56 << 20
        ),
    )(grad_qkv, weight, down, up, normed, low, middle, flat, inverse, gain.reshape(1, -1))


def placed_kernel(sizes, width, holder_ref, early_ref, late_ref, *outs):
    q_down, q_up, kv_down, kv_up, o_down, o_up, gu_down, gu_up, ff_down, ff_up = outs
    cuts = np.cumsum([0] + sizes)
    early = [slice(int(begin), int(end)) for begin, end in zip(cuts[:-1], cuts[1:])]
    for out, cut in zip((o_down, o_up), early[:2]):
        out[0] = early_ref[0, :, cut].astype(F32)
    for which in range(2):
        gu_down[0, which] = early_ref[0, :, early[2 + which]].astype(F32)
        gu_up[0, which] = early_ref[0, :, early[4 + which]].astype(F32)
    for out, cut in zip((ff_down, ff_up), early[6:]):
        out[0] = early_ref[0, :, cut].astype(F32)
    q_up[0] = late_ref[0, :, :width].astype(F32)
    narrow = KV_HEADS * HEAD_DIM
    pairs = late_ref[0, :, width : width + 2 * narrow].astype(F32)
    for which in range(2):
        pieces = [
            pairs[:, (2 * head + which) * HEAD_DIM : (2 * head + which + 1) * HEAD_DIM]
            for head in range(KV_HEADS)
        ]
        kv_up[0, which] = jnp.concatenate(pieces, axis=1)
    at = width + 2 * narrow
    q_down[0] = late_ref[0, :, at : at + width].astype(F32)
    for which in range(2):
        at += width
        kv_down[0, which] = late_ref[0, :, at : at + width].astype(F32)


def placed(holder, early, late, sizes, width):
    adapters, rank = early.shape[:2]
    hidden = sizes[4]
    narrow = KV_HEADS * HEAD_DIM
    shapes = [
        (rank, width),
        (rank, width),
        (2, rank, width),
        (2, rank, narrow),
        (rank, width),
        (rank, width),
        (2, rank, width),
        (2, rank, hidden),
        (rank, hidden),
        (rank, width),
    ]

    def whole(shape):
        return pl.BlockSpec((1,) + shape, lambda a, held: (a,) + (0,) * len(shape))

    return pl.pallas_call(
        functools.partial(placed_kernel, sizes, width),
        grid_spec=pltpu.PrefetchScalarGridSpec(
            num_scalar_prefetch=1,
            grid=(adapters,),
            in_specs=[
                pl.BlockSpec((1, rank, early.shape[2]), lambda a, held: (held[a], 0, 0)),
                pl.BlockSpec((1, rank, late.shape[2]), lambda a, held: (held[a], 0, 0)),
            ],
            out_specs=[whole(shape) for shape in shapes],
        ),
        out_shape=[jax.ShapeDtypeStruct((adapters,) + shape, F32) for shape in shapes],
    )(holder, early, late)


def norm_of(values, gain):
    inverse = lax.rsqrt(jnp.mean(values * values, axis=-1, keepdims=True) + EPSILON)
    return (values * inverse * gain).astype(BF16), inverse


def norm_back(values, inverse, gain, grad):
    weighted = grad * gain
    mean = jnp.mean(values * weighted, axis=-1, keepdims=True)
    return inverse * weighted - values * (inverse * inverse * inverse * mean)


def lowered(inputs, down):
    return dot(inputs, down, 1, 1).astype(BF16)


def front_kernel(lines, *refs):
    (
        tokens,
        out_grad,
        query,
        keyval,
        output,
        gateup,
        down,
        limits_ref,
        turn_ref,
        d_qkv_ref,
        u_qkv_ref,
        gain_ref,
        w_qkv,
        w_output,
        w_gateup,
        w_down,
        flat_ref,
        grad_ref,
        normed_ref,
        inverse_ref,
        low_ref,
        q_ref,
        pairs_ref,
        out_ref,
        lse_ref,
    ) = refs[:25]
    got_query, got_keyval, got_output, got_down, my_query, my_keyval, my_output, my_down = refs[25:33]
    all_keyval, first_weights, q_rows, kv_turned = refs[33:37]
    pair_out, pair_in, local, move_out, move_in, share_out, share_in = refs[37:44]
    rows, deep = my_query.shape[0], my_down.shape[0]
    wide, mixed = my_output.shape[1], my_keyval.shape[1]
    span, hidden = gateup.shape[1:]
    width = w_output.shape[1]
    blocks, part_rows = flat_ref.shape[:2]
    groups = width // (2 * TILE)

    def target(part, z, x, y, core):
        blk, head = z * 2 + x, y * 2 + core
        if part == 0:
            return all_keyval.at[pl.ds(blk * 2 * rows + core * rows, rows), pl.ds(y * mixed, mixed)]
        if part == 1:
            return first_weights.at[
                pl.ds(blk * 2 * rows + core * rows, rows), pl.ds(y * wide, wide)
            ]
        if part == 2:
            return w_output.at[pl.ds(blk * 2 * rows + core * rows, rows), pl.ds(y * wide, wide)]
        if part == 5:
            return w_down.at[pl.ds(blk * 2 * deep + core * deep, deep), pl.ds(y * wide, wide)]
        return w_gateup.at[part - 3, pl.ds(blk * span, span), pl.ds(head * hidden, hidden)]

    sources = [my_keyval, my_query, my_output, gateup.at[0], gateup.at[1], my_down]
    spread = Spread(sources, target, lines, refs[44:], FRONT_PLANES, FRONT_SHARES)
    z, x, y, core = place()
    head = y * 2 + core
    meet(along(blocks) + beside())
    sibling = device(z, x, y, 1 - core)
    theirs = pl.ds((1 - core) * rows, rows)
    swaps = [
        remote(keyval.at[:, theirs], got_keyval, pair_out.at[0], pair_in.at[0], sibling),
        remote(query.at[theirs], got_query, pair_out.at[1], pair_in.at[1], sibling),
        remote(output.at[theirs], got_output, pair_out.at[2], pair_in.at[2], sibling),
        remote(
            down.at[pl.ds((1 - core) * deep, deep)], got_down, pair_out.at[3], pair_in.at[3], sibling
        ),
    ]
    for swap in swaps:
        swap.start()
    arrive = Exchange(tokens, flat_ref, part_rows, move_out.at[0], move_in.at[0], local.at[7])
    later_grad = Exchange(out_grad, grad_ref, part_rows, move_out.at[1], move_in.at[1], local.at[8])
    own = [
        pltpu.make_async_copy(sources[part], target(part, z, x, y, core), local.at[part])
        for part in range(6)
    ]

    mine = pl.ds(core * rows, rows)
    kv_ref = pairs_ref.reshape(blocks * pairs_ref.shape[1], pairs_ref.shape[2])
    cosine, sine = turn_ref[0], turn_ref[1]
    here = pl.ds(head * part_rows, part_rows)
    weights_out = pltpu.make_async_copy(first_weights, w_qkv, local.at[6])
    shares = []
    for at, (flip_y, other) in enumerate(((0, device(z, x, 1 - y, core)), (0, sibling), (1, sibling))):
        source_head = ((y + flip_y) % 2) * 2 + core
        ref = pairs_ref.at[:, pl.ds(source_head * part_rows, part_rows)]
        shares.append(remote(ref, ref, share_out.at[at], share_in.at[at], other))

    def share_arrived(at, from_y, from_core):
        ref = pairs_ref.at[:, pl.ds((from_y * 2 + from_core) * part_rows, part_rows)]
        remote(ref, ref, share_out.at[at], share_in.at[at], sibling).wait_recv()

    def first(columns):
        return dot(normed_ref[...], first_weights[:, columns]) + ADAPTER_SCALE * dot(
            low_ref[...], u_qkv_ref[:, columns]
        )

    def pack_first():
        swaps[0].wait_recv()
        pieces = paired(keyval[0, mine, :], got_keyval[0], core)
        pieces += paired(keyval[1, mine, :], got_keyval[1], core)
        filled = sum(p.shape[1] for p in pieces)
        pieces.append(jnp.zeros((rows, mixed - filled), F32))
        my_keyval[...] = jnp.concatenate(pieces, axis=1).astype(BF16)
        swaps[1].wait_recv()
        my_query[...] = jnp.concatenate(
            paired(query[mine, :], got_query[...], core), axis=1
        ).astype(BF16)

    def pack_others():
        swaps[2].wait_recv()
        my_output[...] = jnp.concatenate(
            paired(output[mine, :], got_output[...], core), axis=1
        ).astype(BF16)
        swaps[3].wait_recv()
        my_down[...] = jnp.concatenate(
            paired(down[pl.ds(core * deep, deep), :], got_down[...], core), axis=1
        ).astype(BF16)

    def norm_first():
        flat = flat_ref[...].reshape(blocks * part_rows, width).astype(F32)
        normed, inverse = norm_of(flat, gain_ref[...])
        normed_ref[...] = normed
        inverse_ref[...] = inverse
        low_ref[...] = lowered(normed, d_qkv_ref[...])

    def pair_weights():
        own[0].wait()
        first_weights[:, width:] = in_pairs(all_keyval[...].astype(F32)).astype(BF16)

    def make_pairs():
        for m in range(groups):
            at = width + m * TILE
            tile = turned(first(slice(at, at + TILE)), cosine, sine, True).astype(BF16)
            pairs_ref[:, here, m * TILE : (m + 1) * TILE] = tile.reshape(blocks, part_rows, TILE)

    def give_pairs():
        shares[0].start()
        shares[1].start()

    def get_pairs():
        share_arrived(0, 1 - y, core)
        shares[2].start()
        share_arrived(1, y, 1 - core)
        share_arrived(2, 1 - y, 1 - core)

    def make_queries(m):
        if m == 0:
            own[1].wait()
            weights_out.start()
        both = first(slice(m * 2 * TILE, (m + 1) * 2 * TILE))
        for at in range(2):
            tile = turned(both[:, at * TILE : (at + 1) * TILE], cosine, sine).astype(BF16)
            q_ref[:, (2 * m + at) * TILE : (2 * m + at + 1) * TILE] = tile

    def body(m, block, start, count):
        tile = slice(m * TILE, (m + 1) * TILE)
        queries = q_rows[block].reshape(4 * part_rows, TILE)
        scores = dot(kv_ref[pl.ds(start, count), tile], queries, 1, 1)
        scores = scores + bias_of(limits_ref, block, start, count)
        top = jnp.max(scores, axis=0, keepdims=True)
        shifted = jnp.exp(scores - top)
        total = jnp.sum(shifted, axis=0, keepdims=True)
        result = dot(kv_turned[:, pl.ds(start, count)], shifted.astype(BF16))
        lse_ref[m, pl.ds(block, 1), :] = top + jnp.log(total)
        result = (result / total).T
        for at, part in enumerate(joined(result, True)):
            at = m * 2 * TILE + at * TILE
            out_ref[pl.ds(block * part_rows, part_rows), at : at + TILE] = part.astype(BF16)

    fixed, reach, offset = windows(blocks, 4 * part_rows, head)

    def attend_start(m):
        columns = slice(m * 2 * TILE, (m + 1) * 2 * TILE)
        for slot, part in enumerate(tiles_of(q_ref[:, columns], False)):
            q_rows[:, slot] = (part * BF16(HEAD_DIM**-0.5)).reshape(blocks, part_rows, TILE)
        kv_turned[...] = kv_ref[:, m * TILE : (m + 1) * TILE].astype(F32).T.astype(BF16)
        for block in range(2):
            body(m, block, *fixed[block])

    def attend_middle(m):
        for block in range(2, len(fixed)):
            body(m, block, *fixed[block])

    def attend_end(m):
        @pl.loop(len(fixed), blocks)
        def _(block):
            body(m, block, pl.multiple_of(block * 4 * part_rows + offset, TILE), reach)

    exchanges = (arrive, later_grad)
    run = {
        END: spread.end,
        EX: lambda which: exchanges[which].start(),
        EXW: lambda which: exchanges[which].wait(),
        PACK: lambda which: (pack_first, pack_others)[which](),
        NORM: norm_first,
        PAIRS: pair_weights,
        KEYS: make_pairs,
        GIVE: give_pairs,
        GET: get_pairs,
        QUERY: make_queries,
        ATT0: attend_start,
        ATT1: attend_middle,
        ATT2: attend_end,
    }
    for kind, *rest in FRONT_ORDER:
        if kind in run:
            run[kind](*rest)
        else:
            spread.do(kind, *rest)
            if kind == BH:
                own[rest[0]].start()
    for part in range(2, 6):
        own[part].wait()
    weights_out.wait()
    for copy in swaps + shares:
        copy.wait_send()


FRONT_PLANES = (2,)
FRONT_SHARES = {3: 0.4, 4: 0.4}
FRONT_ORDER = (
    (BH, 3), (BZ, 4), (BH, 4), (PACK, 0), (BZ, 0), (BZ, 1), (LINE, 0, 1, 1), (LINE, 0, 1, -1),
    (LINE, 0, 2, 1), (BH, 0), (LINE, 1, 1, 1), (PX, 3, 0), (BZ, 3), (LINE, 1, 1, -1), (PY, 0, 1),
    (LINE, 0, 2, -1), (LINE, 0, 3, 1), (PX, 0, 1), (EX, TOKENS), (LINE, 1, 2, 1), (PX, 4, 0),
    (LINE, 0, 3, -1), (PACK, 1), (BH, 5), (BH, 2), (PY, 0, 3), (PY, 1, 1), (LINE, 1, 3, -1),
    (BH, 1), (LINE, 1, 2, -1), (PX, 1, 1), (PY, 0, 2), (PY, 1, 0), (BZ, 5), (PX, 0, 0),
    (PY, 0, 0), (LINE, 3, 1, -1), (LINE, 1, 3, 1), (PX, 0, 2), (LINE, 3, 1, 1), (PX, 5, 0),
    (PY, 1, 2), (CO, 0, 1), (PX, 1, 2), (CO, 0, 0), (PX, 0, 3), (PX, 1, 0), (CO, 1, 1),
    (CO, 0, 2), (PY, 5, 0), (EXW, TOKENS), (PY, 4, 0), (PY, 2, 0), (NORM,), (CO, 0, 3),
    (PX, 2, 0), (PX, 1, 3), (PY, 1, 3), (LINE, 3, 2, -1), (END, 0), (LINE, 3, 2, 1), (PAIRS,),
    (KEYS,), (GIVE,), (CO, 1, 0), (CO, 1, 2), (LINE, 4, 1, -1), (CO, 1, 3), (END, 1), (BZ, 2),
    (CO, 4, 0), (LINE, 3, 3, -1), (LINE, 5, 1, -1), (QUERY, 0), (CO, 2, 0), (LINE, 4, 1, 1),
    (QUERY, 1), (QUERY, 2), (QUERY, 3), (PY, 3, 1), (QUERY, 4), (LINE, 3, 3, 1), (LINE, 5, 1, 1),
    (LINE, 4, 2, -1), (GET,), (LINE, 4, 2, 1), (ATT0, 0), (EX, GRADS), (ATT1, 0), (ATT2, 0),
    (ATT0, 1), (LINE, 4, 3, -1), (PX, 3, 3), (ATT1, 1), (LINE, 5, 2, 1), (ATT2, 1), (ATT0, 2),
    (LINE, 4, 3, 1), (LINE, 5, 2, -1), (ATT1, 2), (PX, 3, 2), (PY, 4, 1), (ATT2, 2), (ATT0, 3),
    (ATT1, 3), (ATT2, 3), (ATT0, 4), (ATT1, 4), (ATT2, 4), (LINE, 5, 3, -1), (LINE, 2, 1, -1),
    (PY, 5, 1), (CO, 5, 0), (PX, 3, 1), (LINE, 2, 1, 1), (PX, 4, 1), (PY, 3, 0), (PY, 3, 2),
    (PX, 5, 2), (PY, 3, 3), (LINE, 5, 3, 1), (PX, 4, 3), (PX, 4, 2), (PX, 5, 1), (CO, 4, 1),
    (PY, 4, 2), (LINE, 2, 2, -1), (LINE, 2, 2, 1), (PY, 5, 3), (PY, 4, 3), (LINE, 2, 3, 1),
    (PX, 5, 3), (PY, 5, 2), (LINE, 2, 3, -1), (CO, 3, 0), (CO, 5, 1), (CO, 4, 2), (CO, 3, 1),
    (CO, 4, 3), (END, 2), (CO, 3, 3), (CO, 3, 2), (END, 3), (CO, 5, 3), (CO, 5, 2), (END, 4),
    (END, 5), (EXW, GRADS),
)


def front(tokens, out_grad, weights, limits, turn, down, up, gain):
    query, keyval, output, gateup, w_down = weights
    seqs, part, width = tokens.shape
    rows, wide = query.shape
    deep = w_down.shape[0]
    blks, heads = lax.axis_size("blk"), lax.axis_size("head")
    narrow = keyval.shape[2]
    mixed = -(-4 * narrow // TILE) * TILE
    double = heads * narrow * 2
    groups = width // (2 * TILE)
    dma = pltpu.SemaphoreType.DMA
    vmem = pl.BlockSpec(memory_space=pltpu.VMEM)
    shape = jax.ShapeDtypeStruct
    return pl.pallas_call(
        functools.partial(front_kernel, blks // 2),
        out_shape=[
            shape((blks * rows, heads * wide + double), BF16),
            shape((blks * rows, heads * wide), BF16),
            shape((2, blks * rows, heads * gateup.shape[2]), BF16),
            shape((blks * deep, heads * wide), BF16),
            shape((seqs, part, width), BF16),
            shape((seqs, part, width), BF16),
            shape((seqs * part, width), BF16),
            shape((seqs * part, 1), F32),
            shape((seqs * part, down.shape[0]), BF16),
            shape((seqs * part, width), BF16),
            shape((seqs, heads * part, double), BF16),
            shape((seqs * part, width), BF16),
            shape((groups, seqs, 2 * TILE), F32),
        ],
        in_specs=[ANYWHERE, ANYWHERE, vmem, vmem, vmem, ANYWHERE] + [vmem] * 6,
        out_specs=[ANYWHERE] * 4 + [vmem, ANYWHERE] + [vmem] * 7,
        scratch_shapes=[
            pltpu.VMEM((rows // 2, wide), BF16),
            pltpu.VMEM((2, rows // 2, narrow), BF16),
            pltpu.VMEM((rows // 2, wide), BF16),
            pltpu.VMEM((deep // 2, wide), BF16),
            pltpu.VMEM((rows // 2, 2 * wide), BF16),
            pltpu.VMEM((rows // 2, mixed), BF16),
            pltpu.VMEM((rows // 2, 2 * wide), BF16),
            pltpu.VMEM((deep // 2, 2 * wide), BF16),
            pltpu.VMEM((blks * rows, heads // 2 * mixed), BF16),
            pltpu.VMEM((blks * rows, heads * wide + double), BF16),
            pltpu.VMEM((seqs, 4, part, TILE), BF16),
            pltpu.VMEM((TILE, seqs * heads * part), BF16),
            dma((4,)),
            dma((4,)),
            dma((9,)),
            dma((2, seqs - 1)),
            dma((2, seqs - 1)),
            dma((3,)),
            dma((3,)),
            *Spread.semaphores(6, blks // 2),
        ],
        compiler_params=pltpu.CompilerParams(
            collective_id=0, has_side_effects=True, vmem_limit_bytes=56 << 20
        ),
    )(
        tokens.reshape(seqs * part, width),
        out_grad.reshape(seqs * part, width),
        query,
        keyval,
        output,
        gateup,
        w_down,
        limits,
        turn,
        down,
        up,
        gain.reshape(1, -1),
    )


def feed_kernel(
    attended_ref,
    flat_ref,
    grad_ref,
    w_output_ref,
    w_gateup_ref,
    w_down_ref,
    d_output_ref,
    u_output_ref,
    d_gateup_ref,
    u_gateup_ref,
    d_ffdown_ref,
    u_ffdown_ref,
    gain_ref,
    output_ref,
    grad_middle_ref,
    grad_mixed_ref,
    terms_ref,
    middle,
    normed,
    result,
    grad_normed,
    low_output,
    low_gate,
    low_up,
    low_down,
    grad_low_down,
    grad_low_gate,
    grad_low_up,
):
    step = pl.program_id(0)
    rows, width = attended_ref.shape
    chunk = w_down_ref.shape[0]
    hidden = chunk * pl.num_programs(0)

    @pl.when(step == 0)
    def _():
        attended = attended_ref[...]
        low_output[...] = lowered(attended, d_output_ref[...])
        branch = dot(attended, w_output_ref[...])
        branch = branch + ADAPTER_SCALE * dot(low_output[...], u_output_ref[...])
        middle[...] = flat_ref[...].astype(F32) + branch
        normed[...] = norm_of(middle[...], gain_ref[...])[0]
        low_gate[...] = lowered(normed[...], d_gateup_ref[0])
        low_up[...] = lowered(normed[...], d_gateup_ref[1])
        grad_low_down[...] = (ADAPTER_SCALE * dot(grad_ref[...], u_ffdown_ref[...], 1, 1)).astype(
            BF16
        )
        for ref in (result, grad_normed, low_down, grad_low_gate, grad_low_up):
            ref[...] = jnp.zeros_like(ref)

    inputs = normed[...]
    w_gate, w_up = w_gateup_ref[0], w_gateup_ref[1]
    u_gate, u_up = u_gateup_ref[0], u_gateup_ref[1]
    gate = dot(inputs, w_gate) + ADAPTER_SCALE * dot(low_gate[...], u_gate)
    upward = dot(inputs, w_up) + ADAPTER_SCALE * dot(low_up[...], u_up)
    grad_act = dot(grad_ref[...], w_down_ref[...], 1, 1) + dot(grad_low_down[...], d_ffdown_ref[...])
    sigma = 1.0 / (1.0 + jnp.exp(-gate))
    silu = gate * sigma
    activated = (silu * upward).astype(BF16)
    grad_gate = (grad_act * upward * (sigma * (1.0 + gate * (1.0 - sigma)))).astype(BF16)
    grad_up = (grad_act * silu).astype(BF16)
    result[...] += dot(activated, w_down_ref[...])
    grad_normed[...] += dot(grad_gate, w_gate, 1, 1) + dot(grad_up, w_up, 1, 1)
    low_down[...] += dot(activated, d_ffdown_ref[...], 1, 1)
    grad_low_gate[...] += dot(grad_gate, u_gate, 1, 1)
    grad_low_up[...] += dot(grad_up, u_up, 1, 1)
    at = 4 * width + step * chunk
    spot = pl.ds(pl.multiple_of(at, TILE), chunk)
    terms_ref[:, spot] = ADAPTER_SCALE * dot(low_gate[...], grad_gate, 0, 0)
    spot = pl.ds(pl.multiple_of(at + hidden, TILE), chunk)
    terms_ref[:, spot] = ADAPTER_SCALE * dot(low_up[...], grad_up, 0, 0)
    spot = pl.ds(pl.multiple_of(at + 2 * hidden, TILE), chunk)
    terms_ref[:, spot] = dot(grad_low_down[...], activated, 0, 0)

    @pl.when(step == pl.num_programs(0) - 1)
    def _():
        low = low_down[...].astype(BF16)
        branch = result[...] + ADAPTER_SCALE * dot(low, u_ffdown_ref[...])
        output_ref[...] = (middle[...] + branch).astype(BF16)
        at = 4 * width + 3 * hidden
        terms_ref[:, at : at + width] = ADAPTER_SCALE * dot(low, grad_ref[...], 0, 0)
        if at + width < terms_ref.shape[1]:
            terms_ref[:, at + width :] = jnp.zeros(
                (terms_ref.shape[0], terms_ref.shape[1] - at - width), F32
            )
        low_g = (ADAPTER_SCALE * grad_low_gate[...]).astype(BF16)
        low_u = (ADAPTER_SCALE * grad_low_up[...]).astype(BF16)
        terms_ref[:, 2 * width : 3 * width] = dot(low_g, normed[...], 0, 0)
        terms_ref[:, 3 * width : 4 * width] = dot(low_u, normed[...], 0, 0)
        grad = grad_normed[...] + dot(low_g, d_gateup_ref[0]) + dot(low_u, d_gateup_ref[1])
        inverse = norm_of(middle[...], gain_ref[...])[1]
        grad = grad_ref[...].astype(F32) + norm_back(middle[...], inverse, gain_ref[...], grad)
        grad_middle_ref[...] = grad
        grad = grad.astype(BF16)
        low = (ADAPTER_SCALE * dot(grad, u_output_ref[...], 1, 1)).astype(BF16)
        mixed = dot(grad, w_output_ref[...], 1, 1) + dot(low, d_output_ref[...])
        grad_mixed_ref[...] = mixed.astype(BF16)
        terms_ref[:, :width] = dot(low, attended_ref[...], 0, 0)
        terms_ref[:, width : 2 * width] = ADAPTER_SCALE * dot(low_output[...], grad, 0, 0)


def feed(attended, flat, grad, w_output, w_gateup, w_down, factors, gain):
    rows, width = flat.shape
    hidden = w_down.shape[0]
    chunk = 4 * TILE
    rank = factors[0].shape[0]
    total = 5 * width + 3 * hidden
    total += -total % (2 * 4 * TILE)
    d_output, u_output, d_gateup, u_gateup, d_ffdown, u_ffdown = factors
    shape = jax.ShapeDtypeStruct

    def whole(array):
        return pl.BlockSpec(array.shape, lambda f: (0,) * len(array.shape))

    gain = gain.reshape(1, -1)
    outs = [
        shape((rows, width), BF16),
        shape((rows, width), F32),
        shape((rows, width), BF16),
        shape((rank, total), F32),
    ]
    return pl.pallas_call(
        feed_kernel,
        grid=(hidden // chunk,),
        out_shape=outs,
        in_specs=[
            whole(attended),
            whole(flat),
            whole(grad),
            whole(w_output),
            pl.BlockSpec((2, width, chunk), lambda f: (0, 0, f)),
            pl.BlockSpec((chunk, width), lambda f: (f, 0)),
            whole(d_output),
            whole(u_output),
            whole(d_gateup),
            pl.BlockSpec((2, rank, chunk), lambda f: (0, 0, f)),
            pl.BlockSpec((rank, chunk), lambda f: (0, f)),
            whole(u_ffdown),
            whole(gain),
        ],
        out_specs=[whole(out) for out in outs],
        scratch_shapes=[
            pltpu.VMEM((rows, width), F32),
            pltpu.VMEM((rows, width), BF16),
            pltpu.VMEM((rows, width), F32),
            pltpu.VMEM((rows, width), F32),
            pltpu.VMEM((rows, rank), BF16),
            pltpu.VMEM((rows, rank), BF16),
            pltpu.VMEM((rows, rank), BF16),
            pltpu.VMEM((rows, rank), F32),
            pltpu.VMEM((rows, rank), BF16),
            pltpu.VMEM((rows, rank), F32),
            pltpu.VMEM((rows, rank), F32),
        ],
        compiler_params=pltpu.CompilerParams(vmem_limit_bytes=56 << 20),
    )(
        attended,
        flat,
        grad,
        w_output,
        w_gateup,
        w_down,
        d_output,
        u_output,
        d_gateup,
        u_gateup,
        d_ffdown,
        u_ffdown,
        gain,
    )


def prepare_kernel(
    adapters_ref,
    where_ref,
    freqs_ref,
    segment_ref,
    real_ref,
    query_down,
    query_up,
    keyval_down,
    keyval_up,
    output_down,
    output_up,
    gateup_down,
    gateup_up,
    ffdown_down,
    ffdown_up,
    limits_ref,
    turn_ref,
    d_qkv,
    u_qkv,
    d_output,
    u_output,
    d_gateup,
    u_gateup,
    d_ffdown,
    u_ffdown,
):
    seq, head = where_ref[0], where_ref[1]
    blocks, part = limits_ref.shape[1], limits_ref.shape[2] // 2
    span = segment_ref.shape[1] // blocks
    rank, width = query_up.shape[1:]
    for out, ref in ((d_output, output_down), (u_output, output_up), (d_gateup, gateup_down)):
        out[...] = ref[0]
    for out, ref in ((u_gateup, gateup_up), (d_ffdown, ffdown_down), (u_ffdown, ffdown_up)):
        out[...] = ref[0]
    d_qkv[:rank] = query_down[0]
    d_qkv[rank : 2 * rank] = keyval_down[0, 0]
    d_qkv[2 * rank :] = keyval_down[0, 1]
    u_qkv[...] = jnp.zeros_like(u_qkv)
    u_qkv[:rank, :width] = query_up[0]
    nil = jnp.zeros((rank, HEAD_DIM), F32)
    for which in range(2):
        ups, pieces = keyval_up[0, which].astype(F32), []
        for m in range(KV_HEADS):
            piece = ups[:, m * HEAD_DIM : (m + 1) * HEAD_DIM]
            pieces += [piece, nil] if which == 0 else [nil, piece]
        u_qkv[(1 + which) * rank : (2 + which) * rank, width:] = jnp.concatenate(
            pieces, axis=1
        ).astype(BF16)
    segment = segment_ref[pl.ds(seq, 1), :].astype(F32)
    length = jnp.sum(real_ref[pl.ds(seq, 1), :], axis=1, keepdims=True)
    column = jnp.broadcast_to(segment, (TILE, segment.shape[1])).T
    lane = lax.broadcasted_iota(jnp.int32, (1, TILE), 1)
    for block in range(blocks):
        mine = segment[:, block * span : (block + 1) * span]
        mine = pltpu.roll(jnp.broadcast_to(mine, (8, span)), span - head * part, 1)[:1, :TILE]
        twin = pltpu.roll(jnp.broadcast_to(mine, (8, TILE)), part, 1)[:1]
        mine = jnp.where(lane < part, mine, twin)
        before = jnp.sum((column < mine).astype(F32), axis=0, keepdims=True).astype(jnp.int32)
        position = block * span + head * part + lane % part
        limits_ref[0, block : block + 1, :] = jnp.maximum(position - (WINDOW - 1), before)
        limits_ref[1, block : block + 1, :] = jnp.minimum(position, length - 1)
        limits_ref[2, block : block + 1, :] = position
    shape = (part, TILE)
    row = lax.broadcasted_iota(jnp.int32, shape, 0)
    lanes = lax.broadcasted_iota(jnp.int32, shape, 1)
    sign = jnp.where(lanes % HEAD_DIM < HEAD_DIM // 2, -1.0, 1.0)
    for block in range(blocks):
        angle = (block * span + head * part + row).astype(F32) * freqs_ref[...]
        turn_ref[0, block * part : (block + 1) * part, :] = jnp.cos(angle)
        turn_ref[1, block * part : (block + 1) * part, :] = sign * jnp.sin(angle)


def prepare(adapter_index, seq, head, segment_ids, real_mask, factors, part):
    seqs = adapter_index.shape[0]
    rank, width = factors[1].shape[1:]
    freqs = ROPE_BASE ** (-(jnp.arange(HEAD_DIM // 2, dtype=F32) * 2.0) / HEAD_DIM)
    freqs = jnp.tile(freqs, 2 * TILE // HEAD_DIM)[None, :]
    double = 2 * factors[3].shape[3]
    shapes = [
        ((3, seqs, 2 * part), jnp.int32),
        ((2, seqs * part, TILE), F32),
        ((3 * rank, width), BF16),
        ((3 * rank, width + double), BF16),
    ] + [(factor.shape[1:], BF16) for factor in factors[4:]]

    def whole(shape):
        return pl.BlockSpec(shape, lambda i, adapters, where: (0,) * len(shape))

    def one(shape):
        return pl.BlockSpec(
            (1,) + shape, lambda i, adapters, where: (adapters[where[0]],) + (0,) * len(shape)
        )

    return pl.pallas_call(
        prepare_kernel,
        grid_spec=pltpu.PrefetchScalarGridSpec(
            num_scalar_prefetch=2,
            grid=(1,),
            in_specs=[whole(freqs.shape), whole(segment_ids.shape), whole(real_mask.shape)]
            + [one(factor.shape[1:]) for factor in factors],
            out_specs=[whole(shape) for shape, _ in shapes],
        ),
        out_shape=[jax.ShapeDtypeStruct(shape, dtype) for shape, dtype in shapes],
    )(adapter_index, jnp.stack([seq, head]).astype(jnp.int32), freqs, segment_ids, real_mask, *factors)


def by_sequence(
    tokens,
    attn_gain,
    ffn_gain,
    query_weight,
    keyval_weight,
    output_weight,
    gateup_weight,
    down_weight,
    query_down,
    query_up,
    keyval_down,
    keyval_up,
    output_down,
    output_up,
    gateup_down,
    gateup_up,
    ffdown_down,
    ffdown_up,
    segment_ids,
    real_mask,
    adapter_index,
    out_grad,
):
    seqs, part, width = tokens.shape
    groups = lax.axis_size("head")
    seq, head_pos = lax.axis_index("blk"), lax.axis_index("head")
    rows = seqs * part
    span = groups * part
    rank = query_up.shape[1]
    limits, turn, d_qkv, u_qkv, *factors = prepare(
        adapter_index,
        seq,
        head_pos,
        segment_ids,
        real_mask,
        (
            query_down.swapaxes(1, 2),
            query_up,
            keyval_down.swapaxes(2, 3),
            keyval_up,
            output_down.swapaxes(1, 2),
            output_up,
            gateup_down.swapaxes(2, 3),
            gateup_up,
            ffdown_down.swapaxes(1, 2),
            ffdown_up,
        ),
        part,
    )
    (
        w_qkv,
        w_output,
        w_gateup,
        w_down,
        flat,
        grad_flat,
        normed,
        inverse1,
        low_qkv,
        queries,
        pairs,
        attended,
        lse,
    ) = front(
        tokens,
        out_grad,
        (query_weight, keyval_weight, output_weight, gateup_weight, down_weight),
        limits,
        turn,
        d_qkv,
        u_qkv,
        attn_gain,
    )
    flat, grad_flat = flat.reshape(rows, width), grad_flat.reshape(rows, width)
    pairs = pairs.reshape(seqs * span, pairs.shape[2])
    output, grad_middle, grad_mixed, early = feed(
        attended,
        flat,
        grad_flat,
        w_output,
        w_gateup,
        w_down,
        factors,
        ffn_gain,
    )
    hidden = w_down.shape[0]
    sizes = [width] * 4 + [hidden] * 3 + [width]
    grad_qkv, output, early = attend_back(
        limits, queries, pairs, lse, grad_mixed, turn, output, early
    )
    input_grad, late = first_back(
        grad_qkv, w_qkv, d_qkv, u_qkv, normed, low_qkv, grad_middle, flat, inverse1, attn_gain
    )
    adapters = jnp.arange(query_down.shape[0], dtype=jnp.int32)
    holder = jnp.argmax(adapter_index[None, :] == adapters[:, None], axis=1).astype(jnp.int32)
    found = placed(holder, early, late, sizes, width)
    return (
        output,
        input_grad,
        found[0].swapaxes(1, 2),
        found[1],
        found[2].swapaxes(2, 3),
        found[3],
        found[4].swapaxes(1, 2),
        found[5],
        found[6].swapaxes(2, 3),
        found[7],
        found[8].swapaxes(1, 2),
        found[9],
    )


def solution(mesh):
    in_specs = (
        P(None, ("blk", "head"), None),
        P(),
        P(),
        P("blk", "head"),
        P(None, "blk", "head"),
        P("blk", "head"),
        P(None, "blk", "head"),
        P("blk", "head"),
        P(),
        P(),
        P(),
        P(),
        P(),
        P(),
        P(),
        P(),
        P(),
        P(),
        P(),
        P(),
        P(),
        P(None, ("blk", "head"), None),
    )
    out_specs = (
        P(None, ("blk", "head"), None),
        P(None, ("blk", "head"), None),
        P(),
        P(),
        P(),
        P(),
        P(),
        P(),
        P(),
        P(),
        P(),
        P(),
    )

    def chosen(tokens, *rest):
        if mesh.shape["blk"] == tokens.shape[0] == 8 and mesh.shape["head"] == 4:
            return by_sequence(tokens, *rest)
        return on_device(tokens, *rest)

    return jax.shard_map(
        chosen, mesh=mesh, in_specs=in_specs, out_specs=out_specs, check_vma=False
    )
```

```python
import functools
import math

import jax
import jax.numpy as jnp
import numpy as np
from jax import lax
from jax.experimental import pallas as pl
from jax.experimental.pallas import tpu as pltpu
from jax.sharding import PartitionSpec as P

HEADS = 20
KV_HEADS = 5
HEAD_DIM = 64
WINDOW = 1024


EPSILON = 1e-05
ROPE_BASE = 10000.0
ADAPTER_SCALE = 2.0
MASKED = -1e30


def passed_along(value, axis, steps):
    count = lax.axis_size(axis)
    initial, last = (max(0, -steps), min(count, count - steps))
    return lax.ppermute(value, axis, [(source, source + steps) for source in range(initial, last)])


def rms_scale(values, gain):
    return values * lax.rsqrt(jnp.mean(values * values, axis=-1, keepdims=True) + EPSILON) * gain


def rotate(values, positions, sign):
    half = values.shape[-1] // 2
    freqs = ROPE_BASE ** (-(jnp.arange(half, dtype=jnp.float32) * 2.0) / values.shape[-1])
    angles = positions.astype(jnp.float32)[:, None] * freqs[None, :]
    cosine = jnp.cos(angles)[:, None, :]
    sine = sign * jnp.sin(angles)[:, None, :]
    first = values[..., :half]
    second = values[..., half:]
    return jnp.concatenate(
        [first * cosine - second * sine, second * cosine + first * sine], axis=-1
    )


def gated(gate, upward):
    return jax.nn.silu(gate) * upward


def project(inputs, weight, down, up):
    lowered = jnp.einsum("sci,sir->scr", inputs, down, preferred_element_type=jnp.float32).astype(
        jnp.bfloat16
    )
    extra = ADAPTER_SCALE * jnp.einsum(
        "scr,sro->sco", lowered, up, preferred_element_type=jnp.float32
    )
    return (
        jnp.einsum("sci,io->sco", inputs, weight, preferred_element_type=jnp.float32) + extra,
        lowered,
    )


def project_back(inputs, lowered, grad_out, weight, down, up):
    grad_up = ADAPTER_SCALE * jnp.einsum(
        "scr,sco->sro", lowered, grad_out, preferred_element_type=jnp.float32
    )
    grad_low = (
        ADAPTER_SCALE * jnp.einsum("sco,sro->scr", grad_out, up, preferred_element_type=jnp.float32)
    ).astype(jnp.bfloat16)
    grad_down = jnp.einsum("sci,scr->sir", inputs, grad_low, preferred_element_type=jnp.float32)
    grad_in = jnp.einsum("sco,io->sci", grad_out, weight, preferred_element_type=jnp.float32)
    grad_in = grad_in + jnp.einsum(
        "scr,sir->sci", grad_low, down, preferred_element_type=jnp.float32
    )
    return (grad_in, grad_down, grad_up)


def on_device(
    tokens,
    attn_gain,
    ffn_gain,
    query_weight,
    keyval_weight,
    output_weight,
    gateup_weight,
    down_weight,
    query_down,
    query_up,
    keyval_down,
    keyval_up,
    output_down,
    output_up,
    gateup_down,
    gateup_up,
    ffdown_down,
    ffdown_up,
    segment_ids,
    real_mask,
    adapter_index,
    out_grad,
):
    seqs, per_device, width = tokens.shape
    groups = lax.axis_size("head")
    head_pos = lax.axis_index("head")
    blk_pos = lax.axis_index("blk")
    span = groups * per_device
    heads = HEADS
    head_dim = HEAD_DIM
    kv_heads = KV_HEADS
    local_heads = heads // groups
    share = heads // kv_heads
    reach = (WINDOW - 2) // span + 1
    scale = 1.0 / math.sqrt(head_dim)
    rows_a, rows_b, rows_c, rows_d, rows_e = (
        lax.all_gather(query_weight, "blk", axis=0, tiled=True),
        lax.all_gather(keyval_weight, "blk", axis=1, tiled=True),
        lax.all_gather(output_weight, "blk", axis=0, tiled=True),
        lax.all_gather(gateup_weight, "blk", axis=1, tiled=True),
        lax.all_gather(down_weight, "blk", axis=0, tiled=True),
    )
    w_query, w_keyval, w_output, w_gateup, w_down = (
        lax.all_gather(rows_a, "head", axis=1, tiled=True),
        lax.all_gather(rows_b, "head", axis=2, tiled=True),
        lax.all_gather(rows_c, "head", axis=1, tiled=True),
        lax.all_gather(rows_d, "head", axis=2, tiled=True),
        lax.all_gather(rows_e, "head", axis=1, tiled=True),
    )
    down_query = query_down[adapter_index]
    up_query = query_up[adapter_index]
    down_keyval = keyval_down[adapter_index]
    up_keyval = keyval_up[adapter_index]
    down_output = output_down[adapter_index]
    up_output = output_up[adapter_index]
    down_gateup = gateup_down[adapter_index]
    up_gateup = gateup_up[adapter_index]
    down_ffdown = ffdown_down[adapter_index]
    up_ffdown = ffdown_up[adapter_index]

    def first_norm(values):
        return rms_scale(values, attn_gain)

    def second_norm(values):
        return rms_scale(values, ffn_gain)

    flat = tokens.astype(jnp.float32)
    normed_full, first_norm_back = jax.vjp(first_norm, flat)
    normed = normed_full.astype(jnp.bfloat16)
    queries_pre, low_query = project(normed, w_query, down_query, up_query)
    keys_pre, low_key = project(normed, w_keyval[0], down_keyval[:, 0], up_keyval[:, 0])
    values_pre, low_value = project(normed, w_keyval[1], down_keyval[:, 1], up_keyval[:, 1])
    token_pos = (blk_pos * groups + head_pos) * per_device + jnp.arange(per_device, dtype=jnp.int32)
    queries = rotate(queries_pre.reshape(seqs, per_device, heads, head_dim), token_pos, 1.0).astype(
        jnp.bfloat16
    )
    keys = rotate(keys_pre.reshape(seqs, per_device, kv_heads, head_dim), token_pos, 1.0).astype(
        jnp.bfloat16
    )
    values = values_pre.reshape(seqs, per_device, kv_heads, head_dim).astype(jnp.bfloat16)
    owner = np.array(
        [
            [(group * local_heads + slot) // share for slot in range(local_heads)]
            for group in range(groups)
        ]
    )
    slot_of = jnp.arange(local_heads, dtype=jnp.int32)
    sender = jnp.asarray(
        (owner[:, :, None] == np.arange(kv_heads)[None, None, :]).astype(np.float32), jnp.bfloat16
    )
    spread = (slot_of[:, None] == jnp.arange(local_heads, dtype=jnp.int32)[None, :]).astype(
        jnp.bfloat16
    )
    pair = jnp.stack([keys, values], axis=3)
    outgoing = jnp.einsum(
        "sckxd,gmk->scgmxd", pair, sender, preferred_element_type=jnp.float32
    ).astype(jnp.bfloat16)
    outgoing = outgoing.reshape(seqs, per_device, groups, local_heads * 2 * head_dim)
    query_send = queries.reshape(seqs, per_device, groups, local_heads * head_dim)
    query_here, pair_here = (
        lax.all_to_all(query_send, "head", split_axis=2, concat_axis=1, tiled=True),
        lax.all_to_all(outgoing, "head", split_axis=2, concat_axis=1, tiled=True),
    )
    query_here = query_here.reshape(seqs, span, local_heads, head_dim)
    pair_here = pair_here.reshape(seqs, span, local_heads, 2, head_dim)
    received = [pair_here]
    moving = pair_here
    for hop in range(reach):
        moving = passed_along(moving, "blk", 1)
        received.append(moving)
    window_pairs = jnp.stack(received, axis=1)
    query_pos = blk_pos * span + jnp.arange(span, dtype=jnp.int32)
    key_pos = (blk_pos - jnp.arange(reach + 1, dtype=jnp.int32))[:, None] * span + jnp.arange(
        span, dtype=jnp.int32
    )[None, :]
    safe_pos = jnp.clip(key_pos, 0, segment_ids.shape[1] - 1)
    query_segment = lax.dynamic_slice_in_dim(segment_ids, blk_pos * span, span, 1)
    key_segment = segment_ids[:, safe_pos]
    key_real = real_mask[:, safe_pos]
    distance = query_pos[:, None, None] - key_pos[None]
    allowed = (key_pos[None] >= 0) & (distance >= 0) & (distance < WINDOW)
    allowed = allowed & (query_segment[:, :, None, None] == key_segment[:, None])
    allowed = allowed & ((key_real[:, None] == 1) | (distance[None] == 0))
    batch = 1
    target = max(1, 512 // span)
    for option in range(1, seqs + 1):
        if seqs % option == 0 and option <= target:
            batch = option
    count = seqs // batch

    def grouped(array):
        return array.reshape((count, batch) + array.shape[1:])

    def scores_of(query_part, pair_part, allowed_part):
        keys_wide = jnp.einsum(
            "gjlmd,hm->gjlhd", pair_part[:, :, :, :, 0], spread, preferred_element_type=jnp.float32
        ).astype(jnp.bfloat16)
        values_wide = jnp.einsum(
            "gjlmd,hm->gjlhd", pair_part[:, :, :, :, 1], spread, preferred_element_type=jnp.float32
        ).astype(jnp.bfloat16)
        raw = (
            jnp.einsum(
                "gqhd,gjlhd->ghqjl", query_part, keys_wide, preferred_element_type=jnp.float32
            )
            * scale
        )
        raw = jnp.where(allowed_part[:, None], raw, MASKED)
        return (raw, keys_wide, values_wide)

    def attend(pieces):
        query_part, pair_part, allowed_part = pieces
        raw, keys_wide, values_wide = scores_of(query_part, pair_part, allowed_part)
        top = jnp.max(raw, axis=(3, 4), keepdims=True)
        shifted = jnp.exp(raw - top)
        total = jnp.sum(shifted, axis=(3, 4), keepdims=True)
        probs_low = (shifted / total).astype(jnp.bfloat16)
        result = jnp.einsum(
            "ghqjl,gjlhd->gqhd", probs_low, values_wide, preferred_element_type=jnp.float32
        )
        return (result.astype(jnp.bfloat16), top + jnp.log(total))

    attended, logsum = lax.map(
        attend, (grouped(query_here), grouped(window_pairs), grouped(allowed))
    )
    mixed = lax.all_to_all(
        attended.reshape(seqs, span, local_heads * head_dim),
        "head",
        split_axis=1,
        concat_axis=2,
        tiled=True,
    )
    branch_attn, low_output = project(mixed, w_output, down_output, up_output)
    middle = flat + branch_attn
    normed2_full, second_norm_back = jax.vjp(second_norm, middle)
    normed2 = normed2_full.astype(jnp.bfloat16)
    gate, low_gate = project(normed2, w_gateup[0], down_gateup[:, 0], up_gateup[:, 0])
    upward, low_upward = project(normed2, w_gateup[1], down_gateup[:, 1], up_gateup[:, 1])
    activated_full, gated_back = jax.vjp(gated, gate, upward)
    activated = activated_full.astype(jnp.bfloat16)
    branch_ffn, low_ffdown = project(activated, w_down, down_ffdown, up_ffdown)
    output = (middle + branch_ffn).astype(jnp.bfloat16)
    grad_activated, gd_ffdown, gu_ffdown = project_back(
        activated, low_ffdown, out_grad, w_down, down_ffdown, up_ffdown
    )
    grad_gate, grad_upward = gated_back(grad_activated)
    grad_in_gate, gd_gate, gu_gate = project_back(
        normed2,
        low_gate,
        grad_gate.astype(jnp.bfloat16),
        w_gateup[0],
        down_gateup[:, 0],
        up_gateup[:, 0],
    )
    grad_in_up, gd_up, gu_up = project_back(
        normed2,
        low_upward,
        grad_upward.astype(jnp.bfloat16),
        w_gateup[1],
        down_gateup[:, 1],
        up_gateup[:, 1],
    )
    grad_middle = out_grad.astype(jnp.float32) + second_norm_back(grad_in_gate + grad_in_up)[0]
    grad_mixed, gd_output, gu_output = project_back(
        mixed, low_output, grad_middle.astype(jnp.bfloat16), w_output, down_output, up_output
    )
    grad_send = grad_mixed.astype(jnp.bfloat16).reshape(
        seqs, per_device, groups, local_heads * head_dim
    )
    grad_here = lax.all_to_all(grad_send, "head", split_axis=2, concat_axis=1, tiled=True).reshape(
        seqs, span, local_heads, head_dim
    )
    spread_full = spread.astype(jnp.float32)

    def attend_back(pieces):
        query_part, pair_part, allowed_part, logsum_part, grad_part = pieces
        raw, keys_wide, values_wide = scores_of(query_part, pair_part, allowed_part)
        probs = jnp.exp(raw - logsum_part)
        probs_low = probs.astype(jnp.bfloat16)
        grad_probs = jnp.einsum(
            "gqhd,gjlhd->ghqjl", grad_part, values_wide, preferred_element_type=jnp.float32
        )
        inner = jnp.sum(probs * grad_probs, axis=(3, 4), keepdims=True)
        grad_raw = (probs * (grad_probs - inner)).astype(jnp.bfloat16)
        grad_query = scale * jnp.einsum(
            "ghqjl,gjlhd->gqhd", grad_raw, keys_wide, preferred_element_type=jnp.float32
        )
        grad_keys = scale * jnp.einsum(
            "ghqjl,gqhd->gjlhd", grad_raw, query_part, preferred_element_type=jnp.float32
        )
        grad_values = jnp.einsum(
            "ghqjl,gqhd->gjlhd", probs_low, grad_part, preferred_element_type=jnp.float32
        )
        both = jnp.stack([grad_keys, grad_values], axis=4)
        folded = jnp.einsum("gjlhxd,hm->gjlmxd", both, spread_full, precision=lax.Precision.HIGHEST)
        return (grad_query, folded)

    grad_query, grad_pairs = lax.map(
        attend_back,
        (grouped(query_here), grouped(window_pairs), grouped(allowed), logsum, grouped(grad_here)),
    )
    grad_pairs = grad_pairs.reshape(seqs, reach + 1, span, local_heads, 2, head_dim)
    carried = grad_pairs[:, reach]
    for hop in range(reach - 1, -1, -1):
        carried = (
            passed_along(carried.astype(jnp.bfloat16), "blk", -1).astype(carried.dtype)
            + grad_pairs[:, hop]
        )
    grad_query = rotate(grad_query.reshape(seqs, span, local_heads, head_dim), query_pos, -1.0)
    grad_query = grad_query.astype(jnp.bfloat16).reshape(seqs, span, local_heads * head_dim)
    grad_queries_pre = lax.all_to_all(grad_query, "head", split_axis=1, concat_axis=2, tiled=True)
    grad_pair_tok = lax.all_to_all(
        carried.reshape(seqs, span, local_heads * 2 * head_dim).astype(jnp.bfloat16),
        "head",
        split_axis=1,
        concat_axis=2,
        tiled=True,
    ).astype(jnp.float32)
    grad_pair_tok = grad_pair_tok.reshape(seqs, per_device, groups, local_heads, 2, head_dim)
    grad_pair_heads = jnp.einsum(
        "scgmxd,gmk->sckxd",
        grad_pair_tok,
        sender.astype(jnp.float32),
        precision=lax.Precision.HIGHEST,
    )
    grad_keys_pre = (
        rotate(grad_pair_heads[:, :, :, 0], token_pos, -1.0)
        .astype(jnp.bfloat16)
        .reshape(seqs, per_device, kv_heads * head_dim)
    )
    grad_values_pre = (
        grad_pair_heads[:, :, :, 1]
        .astype(jnp.bfloat16)
        .reshape(seqs, per_device, kv_heads * head_dim)
    )
    grad_in_query, gd_query, gu_query = project_back(
        normed, low_query, grad_queries_pre, w_query, down_query, up_query
    )
    grad_in_key, gd_key, gu_key = project_back(
        normed, low_key, grad_keys_pre, w_keyval[0], down_keyval[:, 0], up_keyval[:, 0]
    )
    grad_in_value, gd_value, gu_value = project_back(
        normed, low_value, grad_values_pre, w_keyval[1], down_keyval[:, 1], up_keyval[:, 1]
    )
    grad_normed = grad_in_query + grad_in_key + grad_in_value
    input_grad = (grad_middle + first_norm_back(grad_normed)[0]).astype(jnp.bfloat16)
    chooser = (
        adapter_index[:, None] == jnp.arange(query_down.shape[0], dtype=jnp.int32)[None, :]
    ).astype(jnp.float32)

    def per_adapter(per_sequence):
        return jnp.einsum("sa,s...->a...", chooser, per_sequence, precision=lax.Precision.HIGHEST)

    sums = lax.psum(
        (
            per_adapter(gd_query),
            per_adapter(gu_query),
            per_adapter(jnp.stack([gd_key, gd_value], axis=1)),
            per_adapter(jnp.stack([gu_key, gu_value], axis=1)),
            per_adapter(gd_output),
            per_adapter(gu_output),
            per_adapter(jnp.stack([gd_gate, gd_up], axis=1)),
            per_adapter(jnp.stack([gu_gate, gu_up], axis=1)),
            per_adapter(gd_ffdown),
            per_adapter(gu_ffdown),
        ),
        ("blk", "head"),
    )
    return (
        output,
        input_grad,
        sums[0],
        sums[1],
        sums[2],
        sums[3],
        sums[4],
        sums[5],
        sums[6],
        sums[7],
        sums[8],
        sums[9],
    )


MESH = pl.DeviceIdType.MESH
F32 = jnp.float32
BF16 = jnp.bfloat16
TILE = 128
ANYWHERE = pl.BlockSpec(memory_space=pl.ANY)


def dot(left, right, left_dim=1, right_dim=0):
    return lax.dot_general(
        left, right, (((left_dim,), (right_dim,)), ((), ())), preferred_element_type=F32
    )


def place():
    blk, head = lax.axis_index("blk"), lax.axis_index("head")
    return blk // 2, blk % 2, head // 2, head % 2


def device(z, x, y, core):
    return (z * 2 + x, y * 2 + core)


FLIPS = ((0, 0), (0, 1), (1, 0), (1, 1))
BZ, BH, LINE, PY, PX, CO = range(6)
END, EX, EXW, PACK, NORM, PAIRS, KEYS, GIVE, GET, QUERY, ATT0, ATT1, ATT2 = range(6, 19)
TOKENS, GRADS = range(2)


def remote(source, target, out, into, other):
    return pltpu.make_async_remote_copy(
        src_ref=source,
        dst_ref=target,
        send_sem=out,
        recv_sem=into,
        device_id=other,
        device_id_type=MESH,
    )


class Spread:
    def __init__(self, sources, target, lines, sems, planes=(), shares=None):
        self.sources, self.target, self.lines = sources, target, lines
        self.planes, self.shares = planes, shares or {}
        self.z, self.x, self.y, self.core = place()
        self.z_in, self.x_in, self.y_in, self.d_in, self.c_in = sems[:5]
        self.z_out, self.x_out, self.y_out, self.d_out, self.c_out = sems[5:10]

    @staticmethod
    def semaphores(parts, lines):
        dma = pltpu.SemaphoreType.DMA
        return [
            dma((parts, lines, 4)),
            dma((parts, lines)),
            dma((parts, lines)),
            dma((parts, lines, 2)),
            dma((parts, lines, 4)),
            dma((parts, 2, lines, 4)),
            dma((parts, lines)),
            dma((parts, lines)),
            dma((parts, lines, 2)),
            dma((parts, lines, 4)),
        ]

    def inside(self, z):
        return (z >= 0) & (z < self.lines)

    def slot(self, part, z, flip_x=0, flip_y=0):
        return self.target(part, z, (self.x + flip_x) % 2, (self.y + flip_y) % 2, self.core)

    def along_z(self, part, source, z, side, flip_x=0, flip_y=0):
        which = flip_x * 2 + flip_y
        return remote(
            source,
            self.slot(part, z, flip_x, flip_y),
            self.z_out.at[part, (side + 1) // 2, z, which],
            self.z_in.at[part, z, which],
            device(self.z + side, self.x, self.y, self.core),
        )

    def along_x(self, part, source, z):
        return remote(
            source,
            self.slot(part, z),
            self.x_out.at[part, z],
            self.x_in.at[part, z],
            device(self.z, 1 - self.x, self.y, self.core),
        )

    def along_y(self, part, source, z):
        return remote(
            source,
            self.slot(part, z),
            self.y_out.at[part, z],
            self.y_in.at[part, z],
            device(self.z, self.x, 1 - self.y, self.core),
        )

    def across(self, part, source, z, flip_x, flip_y):
        which = flip_x * 2 + flip_y
        return remote(
            source,
            self.slot(part, z, flip_x, flip_y),
            self.c_out.at[part, z, which],
            self.c_in.at[part, z, which],
            device(self.z, self.x, self.y, 1 - self.core),
        )

    def piece(self, part, ref, which):
        if ref.shape[0] < 32:
            size = ref.shape[1] // 2
            return ref.at[:, pl.ds(which * size, size)]
        count = ref.shape[0]
        first = int(count * self.shares.get(part, 0.5) + 15) // 16 * 16
        return ref.at[pl.ds(0, first)] if which == 0 else ref.at[pl.ds(first, count - first)]

    def diagonal(self, part, z, which):
        if which == 0:
            ref = self.slot(part, z, 0, 1)
            other = device(self.z, 1 - self.x, self.y, self.core)
        else:
            ref = self.slot(part, z, 1, 0)
            other = device(self.z, self.x, 1 - self.y, self.core)
        ref = self.piece(part, ref, which)
        return remote(ref, ref, self.d_out.at[part, z, which], self.d_in.at[part, z, which], other)

    def arrived(self, ref, out, into):
        remote(ref, ref, out, into, device(self.z, self.x, self.y, 1 - self.core)).wait_recv()

    def toward(self, part, source, z, flip_x, flip_y, sides=(1, -1)):
        for side in sides:

            @pl.when(self.inside(self.z + side))
            def _():
                self.along_z(part, source, z, side, flip_x, flip_y).start()

    def hand_on(self, part, source, z):
        self.along_x(part, source, z).start()
        self.along_y(part, source, z).start()
        self.across(part, source, z, 0, 0).start()

    def begin_line(self, part):
        self.toward(part, self.sources[part], self.z, 0, 0)

    def begin_plane(self, part):
        self.hand_on(part, self.sources[part], self.z)

    def line_step(self, part, distance, side):
        z = self.z - side * distance

        @pl.when(self.inside(z))
        def _():
            for flip_x, flip_y in FLIPS if part in self.planes else FLIPS[:1]:
                ref = self.slot(part, z, flip_x, flip_y)
                which = flip_x * 2 + flip_y
                self.arrived(ref, self.z_out.at[part, 0, z, which], self.z_in.at[part, z, which])
                self.toward(part, ref, z, flip_x, flip_y, (side,))
                if part in self.planes:
                    self.across(part, ref, z, flip_x, flip_y).start()
            if part not in self.planes:
                self.hand_on(part, ref, z)

    def y_step(self, part, z):
        ref = self.slot(part, z, 0, 1)
        self.arrived(ref, self.y_out.at[part, z], self.y_in.at[part, z])
        self.diagonal(part, z, 0).start()
        self.across(part, ref, z, 0, 1).start()
        if part in self.planes:
            self.toward(part, ref, z, 0, 1)

    def x_step(self, part, z):
        ref = self.slot(part, z, 1, 0)
        self.arrived(ref, self.x_out.at[part, z], self.x_in.at[part, z])
        self.diagonal(part, z, 1).start()
        self.across(part, ref, z, 1, 0).start()
        if part in self.planes:
            self.toward(part, ref, z, 1, 0)

    def corner_step(self, part, z):
        ref = self.slot(part, z, 1, 1)
        for which in (0, 1):
            self.arrived(
                self.piece(part, ref, which),
                self.d_out.at[part, z, which],
                self.d_in.at[part, z, which],
            )
        self.across(part, ref, z, 1, 1).start()
        if part in self.planes:
            self.toward(part, ref, z, 1, 1)

    def sent(self, part, z):
        mine = self.slot(part, z)
        self.along_x(part, mine, z).wait_send()
        self.along_y(part, mine, z).wait_send()
        self.diagonal(part, z, 0).wait_send()
        self.diagonal(part, z, 1).wait_send()

    def end(self, part):
        for z in range(self.lines):
            for flip_x, flip_y in FLIPS:
                which = flip_x * 2 + flip_y
                x, y = (self.x + flip_x) % 2, (self.y + flip_y) % 2
                self.arrived(
                    self.target(part, z, x, y, 1 - self.core),
                    self.c_out.at[part, z, which],
                    self.c_in.at[part, z, which],
                )
                mine = self.slot(part, z, flip_x, flip_y)
                self.across(part, mine, z, flip_x, flip_y).wait_send()
                if part not in self.planes and which > 0:
                    continue
                for side in (1, -1):

                    @pl.when(self.inside(self.z + side) & ((self.z - z) * side >= 0))
                    def _():
                        self.along_z(part, mine, z, side, flip_x, flip_y).wait_send()

            if part not in self.planes:
                self.sent(part, z)
        if part in self.planes:
            self.sent(part, self.z)

    def at(self, distance, run):
        if distance == 0:
            run(self.z)
            return
        for side in (1, -1):
            pl.when(self.inside(self.z - side * distance))(
                functools.partial(run, self.z - side * distance)
            )

    def do(self, kind, part, distance=0, side=0):
        if kind == BZ:
            self.begin_line(part)
        elif kind == BH:
            self.begin_plane(part)
        elif kind == LINE:
            self.line_step(part, distance, side)
        else:
            run = {PY: self.y_step, PX: self.x_step, CO: self.corner_step}[kind]
            self.at(distance, functools.partial(run, part))

    def all_steps(self, part):
        result = []
        for stage in range(1, self.lines + 2):
            steps = []
            if stage < self.lines:
                steps += [(LINE, part, stage, 1), (LINE, part, stage, -1)]
            if stage >= 2:
                steps += [(CO, part, stage - 2)]
            if stage <= self.lines:
                steps += [(PY, part, stage - 1), (PX, part, stage - 1)]
            result += [functools.partial(self.do, *step) for step in steps]
        return result


def paired(own, other, core):
    own, other = own.astype(F32), other.astype(F32)
    return [jnp.where(core == 0, own, other), jnp.where(core == 0, other, own)]


def in_pairs(array):
    half = array.shape[1] // 2
    size = 2 * KV_HEADS * HEAD_DIM // 4
    keys = jnp.concatenate([array[:, :size], array[:, half : half + size]], axis=1)
    values = jnp.concatenate(
        [array[:, size : 2 * size], array[:, half + size : half + 2 * size]], axis=1
    )
    pieces = []
    for head in range(KV_HEADS):
        cut = slice(head * HEAD_DIM, (head + 1) * HEAD_DIM)
        pieces += [keys[:, cut], values[:, cut]]
    return jnp.concatenate(pieces, axis=1)


def windows(blocks, span, low_part):
    reach = WINDOW + TILE
    fixed = [(0, (block + 1) * span) for block in range(WINDOW // span)]
    offset = TILE * (low_part // 2 + 1) - reach
    return fixed, reach, offset


def tiles_of(ref, flipped):
    lane = lax.broadcasted_iota(jnp.int32, (ref.shape[0], TILE), 1)
    result = []
    for slot in range(4):
        tile = ref[:, slot // 2 * TILE : (slot // 2 + 1) * TILE].astype(F32)
        if (slot % 2 == 0) == flipped:
            tile = pltpu.roll(tile, HEAD_DIM, 1)
        keep = lane >= HEAD_DIM if flipped else lane < HEAD_DIM
        result.append(jnp.where(keep, tile, 0.0).astype(BF16))
    return result


def joined(rows, flipped):
    span = rows.shape[0] // 4
    heads = [rows[slot * span : (slot + 1) * span] for slot in range(4)]
    lane = lax.broadcasted_iota(jnp.int32, (span, TILE), 1)
    result = []
    for first, second in ((heads[0], heads[1]), (heads[2], heads[3])):
        if flipped:
            first = pltpu.roll(first, HEAD_DIM, 1)
        else:
            second = pltpu.roll(second, HEAD_DIM, 1)
        result.append(jnp.where(lane < HEAD_DIM, first, second))
    return result


def bias_of(limits_ref, block, start, count):
    key = start + lax.broadcasted_iota(jnp.int32, (count, TILE), 0)
    least = limits_ref[0, pl.ds(block, 1), :]
    most = limits_ref[1, pl.ds(block, 1), :]
    self_pos = limits_ref[2, pl.ds(block, 1), :]
    allowed = ((key >= least) & (key <= most)) | (key == self_pos)
    bias = jnp.where(allowed, 0.0, MASKED)
    return jnp.concatenate([bias, bias], axis=1)


def each_block(blocks, body, between=lambda: None):
    span = 4 * HEAD_DIM
    fixed, reach, offset = windows(blocks, span, lax.axis_index("head"))
    for block, (start, count) in enumerate(fixed):
        body(block, start, count)
    between()

    @pl.loop(len(fixed), blocks)
    def _(block):
        body(block, pl.multiple_of(block * span + offset, TILE), reach)


def meet(others):
    barrier = pltpu.get_barrier_semaphore()
    for other in others:
        pl.semaphore_signal(barrier, inc=1, device_id=other, device_id_type=MESH)
    pl.semaphore_wait(barrier, len(others))


def along(count):
    blk, head = lax.axis_index("blk"), lax.axis_index("head")
    return [((blk + ahead) % count, head) for ahead in range(1, count)]


def beside():
    z, x, y, core = place()
    return [
        device(z, x, y, 1 - core),
        device(z, x, 1 - y, core),
        device(z, x, 1 - y, 1 - core),
    ]


class Exchange:
    def __init__(self, source, target, size, out, into, local):
        count = target.shape[0]
        blk, head = lax.axis_index("blk"), lax.axis_index("head")
        self.own = pltpu.make_async_copy(source.at[pl.ds(blk * size, size)], target.at[blk], local)
        self.copies, self.arrivals = [], []
        for at, (other, _) in enumerate(along(count)):
            self.copies.append(
                remote(
                    source.at[pl.ds(other * size, size)],
                    target.at[blk],
                    out.at[at],
                    into.at[at],
                    (other, head),
                )
            )
            giver = (blk + count - 1 - at) % count
            self.arrivals.append(
                remote(target.at[giver], target.at[giver], out.at[at], into.at[at], (other, head))
            )

    def start(self):
        self.own.start()
        for copy in self.copies:
            copy.start()

    def wait(self):
        for copy in self.arrivals:
            copy.wait_recv()
        for copy in self.copies:
            copy.wait_send()
        self.own.wait()


class Quarters:
    def __init__(self, terms, low, got, out, into):
        z, x, y, core = place()
        self.size = low.shape[1] // 4
        self.terms, self.low, self.got = terms, low, got
        self.mine = pl.ds((y * 2 + core) * self.size, self.size)
        self.copies = []
        for at, (flip_y, flip_core) in enumerate(((0, 1), (1, 0), (1, 1))):
            other_y, other_core = (y + flip_y) % 2, (core + flip_core) % 2
            theirs = pl.ds((other_y * 2 + other_core) * self.size, self.size)
            self.copies.append(
                remote(
                    low.at[:, theirs],
                    got.at[at],
                    out.at[at],
                    into.at[at],
                    device(z, x, other_y, other_core),
                )
            )

    def start(self):
        self.low[...] = self.terms[...].astype(BF16)
        for copy in self.copies:
            copy.start()

    def total(self):
        for copy in self.copies:
            copy.wait_recv()
        total = self.terms[:, self.mine]
        for at in range(3):
            total = total + self.got[at].astype(F32)
        return total.astype(BF16)

    def end(self):
        for copy in self.copies:
            copy.wait_send()


def turned(tile, cosine, sine, only_low=False):
    lane = lax.broadcasted_iota(jnp.int32, tile.shape, 1)
    half = HEAD_DIM // 2
    partner = jnp.where(
        lane % HEAD_DIM < half, pltpu.roll(tile, TILE - half, 1), pltpu.roll(tile, half, 1)
    )
    result = tile * cosine + partner * sine
    return jnp.where(lane < HEAD_DIM, result, tile) if only_low else result


def attend_back_kernel(
    lines,
    limits_ref,
    q_from,
    kv_from,
    lse_ref,
    grad_from,
    turn_ref,
    output_ref,
    terms_ref,
    dqkv_ref,
    moved_ref,
    shared_ref,
    q_rows,
    g_rows,
    kv_turned,
    total,
    pair_low,
    pair_got,
    kept,
    y_low,
    y_got,
    low,
    got,
    shard,
    pair_out,
    pair_in,
    y_out,
    y_in,
    move_out,
    move_in,
    four_out,
    four_in,
    local,
    q_ref,
    kv_ref,
    grad_ref,
    load,
    *sems,
):
    blocks, span = q_rows.shape[0], q_rows.shape[2]
    width = q_ref.shape[1]
    groups = width // (2 * TILE)
    scale = HEAD_DIM**-0.5
    z, x, y, core = place()
    size = shard.shape[1]

    def target(part, z, x, y, core):
        return shared_ref.at[z * 2 + x, :, pl.ds((y * 2 + core) * size, size)]

    spread = Spread([shard], target, lines, sems)
    loads = [
        pltpu.make_async_copy(source, held, load.at[at])
        for at, (source, held) in enumerate(
            ((q_from, q_ref), (kv_from, kv_ref), (grad_from, grad_ref))
        )
    ]
    for copy in loads:
        copy.start()
    meet(along(blocks) + beside())
    exchange = Exchange(output_ref, moved_ref, span, move_out, move_in, local.at[0])
    quarters = Quarters(terms_ref, low, got, four_out, four_in)
    quarters.start()
    own = pltpu.make_async_copy(shard, target(0, z, x, y, core), local.at[1])

    def gather_start():
        shard[...] = quarters.total()
        own.start()
        spread.begin_line(0)
        spread.begin_plane(0)

    steps = spread.all_steps(0)

    def some(count):
        def run():
            for _ in range(count):
                steps.pop(0)()

        return run

    later = [None, gather_start, some(4), some(3), some(4), exchange.start]
    later += [some(3), some(3), some(1)]

    def pump():
        if later:
            step = later.pop(0)
            if step is not None:
                step()

    def pair_copy(m):
        return remote(
            pair_low.at[m, 1 - core],
            pair_got.at[m],
            pair_out.at[m],
            pair_in.at[m],
            device(z, x, y, 1 - core),
        )

    def y_copy(m):
        return remote(
            y_low.at[m], y_got.at[m], y_out.at[m], y_in.at[m], device(z, x, 1 - y, core)
        )

    def give(m):
        whole = total[...].reshape(blocks, 4, span, TILE)
        for at in range(4):
            pair_low[m, at % 2, at // 2] = whole[:, at].astype(BF16)
        spot = total.reshape(blocks, 4, span, TILE)
        for at in range(2):
            kept[m, at] = spot[:, at * 2 + core]
        pair_copy(m).start()

    def add_pair(m):
        pair_copy(m).wait_recv()
        y_low[m] = (kept[m, 1 - y] + pair_got[m, 1 - y].astype(F32)).astype(BF16)
        y_copy(m).start()

    def add_y(m):
        y_copy(m).wait_recv()
        tile = kept[m, y] + pair_got[m, y].astype(F32) + y_got[m].astype(F32)
        tile = turned(tile.reshape(blocks * span, TILE), turn_ref[0], -turn_ref[1], True)
        at = width + m * TILE
        dqkv_ref[:, at : at + TILE] = tile.astype(BF16)

    for copy in loads:
        copy.wait()
    for m in range(groups):
        columns = slice(m * 2 * TILE, (m + 1) * 2 * TILE)
        tile = slice(m * TILE, (m + 1) * TILE)
        for slot, rows in enumerate(tiles_of(q_ref[:, columns], False)):
            q_rows[:, slot] = (rows * BF16(scale)).reshape(blocks, span, TILE)
        for slot, rows in enumerate(tiles_of(grad_ref[:, columns], True)):
            g_rows[:, slot] = rows.reshape(blocks, span, TILE)
        kv_turned[...] = kv_ref[:, tile].astype(F32).T.astype(BF16)
        total[...] = jnp.zeros_like(total)

        def body(block, start, count):
            keys = pl.ds(start, count)
            queries = q_rows[block].reshape(4 * span, TILE)
            grads = g_rows[block].reshape(4 * span, TILE)
            scores = dot(kv_ref[keys, tile], queries, 1, 1)
            scores = scores + bias_of(limits_ref, block, start, count)
            probs = jnp.exp(scores - lse_ref[m, pl.ds(block, 1), :])
            grad_probs = dot(kv_ref[keys, tile], grads, 1, 1)
            inner = jnp.sum(probs * grad_probs, axis=0, keepdims=True)
            grad_scores = (probs * (grad_probs - inner)).astype(BF16)
            total[keys, :] += dot(grad_scores, queries) + dot(probs.astype(BF16), grads)
            grad_q = (dot(kv_turned[:, keys], grad_scores) * scale).T
            rows = pl.ds(block * span, span)
            cosine, sine = turn_ref[0, rows, :], -turn_ref[1, rows, :]
            for at, part in enumerate(joined(grad_q, False)):
                at = m * 2 * TILE + at * TILE
                dqkv_ref[rows, at : at + TILE] = turned(part, cosine, sine).astype(BF16)

        each_block(blocks, body, pump)
        pump()
        give(m)
        if m >= 1:
            add_pair(m - 1)
        if m >= 2:
            add_y(m - 2)
    while later:
        pump()
    add_pair(groups - 1)
    add_y(groups - 2)
    spread.end(0)
    own.wait()
    exchange.wait()
    quarters.end()
    add_y(groups - 1)
    for m in range(groups):
        pair_copy(m).wait_send()
        y_copy(m).wait_send()


def attend_back(limits, queries, pairs, lse, grads, turn, output, terms):
    rows, width = queries.shape
    blocks = limits.shape[1]
    span = rows // blocks
    groups = width // (2 * TILE)
    rank, total = terms.shape
    seqs = lax.axis_size("blk")
    each = pltpu.VMEM((blocks, 4, span, TILE), BF16)
    dma = pltpu.SemaphoreType.DMA
    vmem = pl.BlockSpec(memory_space=pltpu.VMEM)
    shape = jax.ShapeDtypeStruct
    return pl.pallas_call(
        functools.partial(attend_back_kernel, seqs // 2),
        out_shape=[
            shape((rows, width + pairs.shape[1]), BF16),
            shape((seqs, span, width), BF16),
            shape((seqs, rank, total), BF16),
        ],
        in_specs=[vmem, ANYWHERE, ANYWHERE, vmem, ANYWHERE, vmem, ANYWHERE, vmem],
        out_specs=[vmem, ANYWHERE, ANYWHERE],
        scratch_shapes=[
            each,
            each,
            pltpu.VMEM((TILE, pairs.shape[0]), BF16),
            pltpu.VMEM((pairs.shape[0], TILE), F32),
            pltpu.VMEM((groups, 2, 2, blocks, span, TILE), BF16),
            pltpu.VMEM((groups, 2, blocks, span, TILE), BF16),
            pltpu.VMEM((groups, 2, blocks, span, TILE), F32),
            pltpu.VMEM((groups, blocks, span, TILE), BF16),
            pltpu.VMEM((groups, blocks, span, TILE), BF16),
            pltpu.VMEM((rank, total), BF16),
            pltpu.VMEM((3, rank, total // 4), BF16),
            pltpu.VMEM((rank, total // 4), BF16),
            dma((groups,)),
            dma((groups,)),
            dma((groups,)),
            dma((groups,)),
            dma((seqs - 1,)),
            dma((seqs - 1,)),
            dma((3,)),
            dma((3,)),
            dma((2,)),
            pltpu.VMEM(queries.shape, BF16),
            pltpu.VMEM(pairs.shape, BF16),
            pltpu.VMEM(grads.shape, BF16),
            dma((3,)),
            *Spread.semaphores(1, seqs // 2),
        ],
        compiler_params=pltpu.CompilerParams(
            collective_id=1, has_side_effects=True, vmem_limit_bytes=56 << 20
        ),
    )(limits, queries, pairs, lse, grads, turn, output, terms)


def first_back_kernel(
    lines,
    dqkv_ref,
    weight_from,
    down_ref,
    up_ref,
    normed_from,
    low_ref,
    middle_from,
    flat_from,
    inverse_ref,
    gain_ref,
    moved_ref,
    shared_ref,
    result,
    terms,
    low,
    got,
    shard,
    move_out,
    move_in,
    four_out,
    four_in,
    local,
    normed_ref,
    weight_ref,
    middle_ref,
    flat_ref,
    load,
    *sems,
):
    blocks, span = moved_ref.shape[:2]
    z, x, y, core = place()
    size = shard.shape[1]
    rank = down_ref.shape[0] // 3
    width = flat_ref.shape[1]

    def target(part, z, x, y, core):
        return shared_ref.at[z * 2 + x, :, pl.ds((y * 2 + core) * size, size)]

    spread = Spread([shard], target, lines, sems)
    loads = [
        pltpu.make_async_copy(source, held, load.at[at])
        for at, (source, held) in enumerate(
            (
                (normed_from, normed_ref),
                (weight_from, weight_ref),
                (middle_from, middle_ref),
                (flat_from, flat_ref),
            )
        )
    ]
    for copy in loads:
        copy.start()
    meet(along(blocks) + beside())
    grad_low = (ADAPTER_SCALE * dot(dqkv_ref[...], up_ref[...], 1, 1)).astype(BF16)
    grad_up = ADAPTER_SCALE * dot(low_ref[...], dqkv_ref[...], 0, 0)
    loads[0].wait()
    grad_down = dot(grad_low, normed_ref[...], 0, 0)
    terms[:, :width] = grad_up[:rank, :width]
    at = width
    while at < dqkv_ref.shape[1]:
        lane = lax.broadcasted_iota(jnp.int32, (rank, TILE), 1)
        terms[:, at : at + TILE] = jnp.where(
            lane < HEAD_DIM,
            grad_up[rank : 2 * rank, at : at + TILE],
            grad_up[2 * rank :, at : at + TILE],
        )
        at += TILE
    for which in range(3):
        terms[:, at : at + width] = grad_down[which * rank : (which + 1) * rank]
        at += width
    if at < terms.shape[1]:
        terms[:, at:] = jnp.zeros((rank, terms.shape[1] - at), F32)
    quarters = Quarters(terms, low, got, four_out, four_in)
    quarters.start()
    own = pltpu.make_async_copy(shard, target(0, z, x, y, core), local.at[1])
    exchange = Exchange(result, moved_ref, span, move_out, move_in, local.at[0])
    loads[1].wait()
    grad = dot(dqkv_ref[...], weight_ref[...], 1, 1) + dot(grad_low, down_ref[...])
    shard[...] = quarters.total()
    own.start()
    spread.begin_line(0)
    spread.begin_plane(0)
    loads[2].wait()
    loads[3].wait()
    weighted = grad * gain_ref[...]
    flat, inverse = flat_ref[...].astype(F32), inverse_ref[...]
    mean = jnp.mean(flat * weighted, axis=1, keepdims=True)
    grad = middle_ref[...] + inverse * weighted - flat * (inverse * inverse * inverse * mean)
    result[...] = grad.astype(BF16)
    steps = spread.all_steps(0)
    for step in steps[:11]:
        step()
    exchange.start()
    for step in steps[11:]:
        step()
    spread.end(0)
    own.wait()
    quarters.end()
    exchange.wait()


def first_back(grad_qkv, weight, down, up, normed, low, middle, flat, inverse, gain):
    rows, width = flat.shape
    rank = down.shape[0] // 3
    seqs, heads = lax.axis_size("blk"), lax.axis_size("head")
    total = 3 * width + weight.shape[1]
    total += -total % (2 * heads * TILE)
    dma = pltpu.SemaphoreType.DMA
    vmem = pl.BlockSpec(memory_space=pltpu.VMEM)
    shape = jax.ShapeDtypeStruct
    return pl.pallas_call(
        functools.partial(first_back_kernel, seqs // 2),
        out_shape=[
            shape((seqs, rows // seqs, width), BF16),
            shape((seqs, rank, total), BF16),
        ],
        in_specs=[
            vmem,
            ANYWHERE,
            vmem,
            vmem,
            ANYWHERE,
            vmem,
            ANYWHERE,
            ANYWHERE,
            vmem,
            vmem,
        ],
        out_specs=[ANYWHERE, ANYWHERE],
        scratch_shapes=[
            pltpu.VMEM((rows, width), BF16),
            pltpu.VMEM((rank, total), F32),
            pltpu.VMEM((rank, total), BF16),
            pltpu.VMEM((3, rank, total // 4), BF16),
            pltpu.VMEM((rank, total // 4), BF16),
            dma((seqs - 1,)),
            dma((seqs - 1,)),
            dma((3,)),
            dma((3,)),
            dma((2,)),
            pltpu.VMEM(normed.shape, BF16),
            pltpu.VMEM(weight.shape, BF16),
            pltpu.VMEM(middle.shape, F32),
            pltpu.VMEM(flat.shape, BF16),
            dma((4,)),
            *Spread.semaphores(1, seqs // 2),
        ],
        compiler_params=pltpu.CompilerParams(
            collective_id=2, has_side_effects=True, vmem_limit_bytes=56 << 20
        ),
    )(grad_qkv, weight, down, up, normed, low, middle, flat, inverse, gain.reshape(1, -1))


def placed_kernel(sizes, width, holder_ref, early_ref, late_ref, *outs):
    q_down, q_up, kv_down, kv_up, o_down, o_up, gu_down, gu_up, ff_down, ff_up = outs
    cuts = np.cumsum([0] + sizes)
    early = [slice(int(begin), int(end)) for begin, end in zip(cuts[:-1], cuts[1:])]
    for out, cut in zip((o_down, o_up), early[:2]):
        out[0] = early_ref[0, :, cut].astype(F32)
    for which in range(2):
        gu_down[0, which] = early_ref[0, :, early[2 + which]].astype(F32)
        gu_up[0, which] = early_ref[0, :, early[4 + which]].astype(F32)
    for out, cut in zip((ff_down, ff_up), early[6:]):
        out[0] = early_ref[0, :, cut].astype(F32)
    q_up[0] = late_ref[0, :, :width].astype(F32)
    narrow = KV_HEADS * HEAD_DIM
    pairs = late_ref[0, :, width : width + 2 * narrow].astype(F32)
    for which in range(2):
        pieces = [
            pairs[:, (2 * head + which) * HEAD_DIM : (2 * head + which + 1) * HEAD_DIM]
            for head in range(KV_HEADS)
        ]
        kv_up[0, which] = jnp.concatenate(pieces, axis=1)
    at = width + 2 * narrow
    q_down[0] = late_ref[0, :, at : at + width].astype(F32)
    for which in range(2):
        at += width
        kv_down[0, which] = late_ref[0, :, at : at + width].astype(F32)


def placed(holder, early, late, sizes, width):
    adapters, rank = early.shape[:2]
    hidden = sizes[4]
    narrow = KV_HEADS * HEAD_DIM
    shapes = [
        (rank, width),
        (rank, width),
        (2, rank, width),
        (2, rank, narrow),
        (rank, width),
        (rank, width),
        (2, rank, width),
        (2, rank, hidden),
        (rank, hidden),
        (rank, width),
    ]

    def whole(shape):
        return pl.BlockSpec((1,) + shape, lambda a, held: (a,) + (0,) * len(shape))

    return pl.pallas_call(
        functools.partial(placed_kernel, sizes, width),
        grid_spec=pltpu.PrefetchScalarGridSpec(
            num_scalar_prefetch=1,
            grid=(adapters,),
            in_specs=[
                pl.BlockSpec((1, rank, early.shape[2]), lambda a, held: (held[a], 0, 0)),
                pl.BlockSpec((1, rank, late.shape[2]), lambda a, held: (held[a], 0, 0)),
            ],
            out_specs=[whole(shape) for shape in shapes],
        ),
        out_shape=[jax.ShapeDtypeStruct((adapters,) + shape, F32) for shape in shapes],
    )(holder, early, late)


def norm_of(values, gain):
    inverse = lax.rsqrt(jnp.mean(values * values, axis=-1, keepdims=True) + EPSILON)
    return (values * inverse * gain).astype(BF16), inverse


def norm_back(values, inverse, gain, grad):
    weighted = grad * gain
    mean = jnp.mean(values * weighted, axis=-1, keepdims=True)
    return inverse * weighted - values * (inverse * inverse * inverse * mean)


def lowered(inputs, down):
    return dot(inputs, down, 1, 1).astype(BF16)


def front_kernel(lines, *refs):
    (
        tokens,
        out_grad,
        query,
        keyval,
        output,
        gateup,
        down,
        limits_ref,
        turn_ref,
        d_qkv_ref,
        u_qkv_ref,
        gain_ref,
        w_qkv,
        w_output,
        w_gateup,
        w_down,
        flat_ref,
        grad_ref,
        normed_ref,
        inverse_ref,
        low_ref,
        q_ref,
        pairs_ref,
        out_ref,
        lse_ref,
    ) = refs[:25]
    got_query, got_keyval, got_output, got_down, my_query, my_keyval, my_output, my_down = refs[25:33]
    all_keyval, first_weights, q_rows, kv_turned = refs[33:37]
    pair_out, pair_in, local, move_out, move_in, share_out, share_in = refs[37:44]
    rows, deep = my_query.shape[0], my_down.shape[0]
    wide, mixed = my_output.shape[1], my_keyval.shape[1]
    span, hidden = gateup.shape[1:]
    width = w_output.shape[1]
    blocks, part_rows = flat_ref.shape[:2]
    groups = width // (2 * TILE)

    def target(part, z, x, y, core):
        blk, head = z * 2 + x, y * 2 + core
        if part == 0:
            return all_keyval.at[pl.ds(blk * 2 * rows + core * rows, rows), pl.ds(y * mixed, mixed)]
        if part == 1:
            return first_weights.at[
                pl.ds(blk * 2 * rows + core * rows, rows), pl.ds(y * wide, wide)
            ]
        if part == 2:
            return w_output.at[pl.ds(blk * 2 * rows + core * rows, rows), pl.ds(y * wide, wide)]
        if part == 5:
            return w_down.at[pl.ds(blk * 2 * deep + core * deep, deep), pl.ds(y * wide, wide)]
        return w_gateup.at[part - 3, pl.ds(blk * span, span), pl.ds(head * hidden, hidden)]

    sources = [my_keyval, my_query, my_output, gateup.at[0], gateup.at[1], my_down]
    spread = Spread(sources, target, lines, refs[44:], FRONT_PLANES, FRONT_SHARES)
    z, x, y, core = place()
    head = y * 2 + core
    meet(along(blocks) + beside())
    sibling = device(z, x, y, 1 - core)
    theirs = pl.ds((1 - core) * rows, rows)
    swaps = [
        remote(keyval.at[:, theirs], got_keyval, pair_out.at[0], pair_in.at[0], sibling),
        remote(query.at[theirs], got_query, pair_out.at[1], pair_in.at[1], sibling),
        remote(output.at[theirs], got_output, pair_out.at[2], pair_in.at[2], sibling),
        remote(
            down.at[pl.ds((1 - core) * deep, deep)], got_down, pair_out.at[3], pair_in.at[3], sibling
        ),
    ]
    for swap in swaps:
        swap.start()
    arrive = Exchange(tokens, flat_ref, part_rows, move_out.at[0], move_in.at[0], local.at[7])
    later_grad = Exchange(out_grad, grad_ref, part_rows, move_out.at[1], move_in.at[1], local.at[8])
    own = [
        pltpu.make_async_copy(sources[part], target(part, z, x, y, core), local.at[part])
        for part in range(6)
    ]

    mine = pl.ds(core * rows, rows)
    kv_ref = pairs_ref.reshape(blocks * pairs_ref.shape[1], pairs_ref.shape[2])
    cosine, sine = turn_ref[0], turn_ref[1]
    here = pl.ds(head * part_rows, part_rows)
    weights_out = pltpu.make_async_copy(first_weights, w_qkv, local.at[6])
    shares = []
    for at, (flip_y, other) in enumerate(((0, device(z, x, 1 - y, core)), (0, sibling), (1, sibling))):
        source_head = ((y + flip_y) % 2) * 2 + core
        ref = pairs_ref.at[:, pl.ds(source_head * part_rows, part_rows)]
        shares.append(remote(ref, ref, share_out.at[at], share_in.at[at], other))

    def share_arrived(at, from_y, from_core):
        ref = pairs_ref.at[:, pl.ds((from_y * 2 + from_core) * part_rows, part_rows)]
        remote(ref, ref, share_out.at[at], share_in.at[at], sibling).wait_recv()

    def first(columns):
        return dot(normed_ref[...], first_weights[:, columns]) + ADAPTER_SCALE * dot(
            low_ref[...], u_qkv_ref[:, columns]
        )

    def pack_first():
        swaps[0].wait_recv()
        pieces = paired(keyval[0, mine, :], got_keyval[0], core)
        pieces += paired(keyval[1, mine, :], got_keyval[1], core)
        filled = sum(p.shape[1] for p in pieces)
        pieces.append(jnp.zeros((rows, mixed - filled), F32))
        my_keyval[...] = jnp.concatenate(pieces, axis=1).astype(BF16)
        swaps[1].wait_recv()
        my_query[...] = jnp.concatenate(
            paired(query[mine, :], got_query[...], core), axis=1
        ).astype(BF16)

    def pack_others():
        swaps[2].wait_recv()
        my_output[...] = jnp.concatenate(
            paired(output[mine, :], got_output[...], core), axis=1
        ).astype(BF16)
        swaps[3].wait_recv()
        my_down[...] = jnp.concatenate(
            paired(down[pl.ds(core * deep, deep), :], got_down[...], core), axis=1
        ).astype(BF16)

    def norm_first():
        flat = flat_ref[...].reshape(blocks * part_rows, width).astype(F32)
        normed, inverse = norm_of(flat, gain_ref[...])
        normed_ref[...] = normed
        inverse_ref[...] = inverse
        low_ref[...] = lowered(normed, d_qkv_ref[...])

    def pair_weights():
        own[0].wait()
        first_weights[:, width:] = in_pairs(all_keyval[...].astype(F32)).astype(BF16)

    def make_pairs():
        for m in range(groups):
            at = width + m * TILE
            tile = turned(first(slice(at, at + TILE)), cosine, sine, True).astype(BF16)
            pairs_ref[:, here, m * TILE : (m + 1) * TILE] = tile.reshape(blocks, part_rows, TILE)

    def give_pairs():
        shares[0].start()
        shares[1].start()

    def get_pairs():
        share_arrived(0, 1 - y, core)
        shares[2].start()
        share_arrived(1, y, 1 - core)
        share_arrived(2, 1 - y, 1 - core)

    def make_queries(m):
        if m == 0:
            own[1].wait()
            weights_out.start()
        both = first(slice(m * 2 * TILE, (m + 1) * 2 * TILE))
        for at in range(2):
            tile = turned(both[:, at * TILE : (at + 1) * TILE], cosine, sine).astype(BF16)
            q_ref[:, (2 * m + at) * TILE : (2 * m + at + 1) * TILE] = tile

    def body(m, block, start, count):
        tile = slice(m * TILE, (m + 1) * TILE)
        queries = q_rows[block].reshape(4 * part_rows, TILE)
        scores = dot(kv_ref[pl.ds(start, count), tile], queries, 1, 1)
        scores = scores + bias_of(limits_ref, block, start, count)
        top = jnp.max(scores, axis=0, keepdims=True)
        shifted = jnp.exp(scores - top)
        total = jnp.sum(shifted, axis=0, keepdims=True)
        result = dot(kv_turned[:, pl.ds(start, count)], shifted.astype(BF16))
        lse_ref[m, pl.ds(block, 1), :] = top + jnp.log(total)
        result = (result / total).T
        for at, part in enumerate(joined(result, True)):
            at = m * 2 * TILE + at * TILE
            out_ref[pl.ds(block * part_rows, part_rows), at : at + TILE] = part.astype(BF16)

    fixed, reach, offset = windows(blocks, 4 * part_rows, head)

    def attend_start(m):
        columns = slice(m * 2 * TILE, (m + 1) * 2 * TILE)
        for slot, part in enumerate(tiles_of(q_ref[:, columns], False)):
            q_rows[:, slot] = (part * BF16(HEAD_DIM**-0.5)).reshape(blocks, part_rows, TILE)
        kv_turned[...] = kv_ref[:, m * TILE : (m + 1) * TILE].astype(F32).T.astype(BF16)
        for block in range(2):
            body(m, block, *fixed[block])

    def attend_middle(m):
        for block in range(2, len(fixed)):
            body(m, block, *fixed[block])

    def attend_end(m):
        @pl.loop(len(fixed), blocks)
        def _(block):
            body(m, block, pl.multiple_of(block * 4 * part_rows + offset, TILE), reach)

    exchanges = (arrive, later_grad)
    run = {
        END: spread.end,
        EX: lambda which: exchanges[which].start(),
        EXW: lambda which: exchanges[which].wait(),
        PACK: lambda which: (pack_first, pack_others)[which](),
        NORM: norm_first,
        PAIRS: pair_weights,
        KEYS: make_pairs,
        GIVE: give_pairs,
        GET: get_pairs,
        QUERY: make_queries,
        ATT0: attend_start,
        ATT1: attend_middle,
        ATT2: attend_end,
    }
    for kind, *rest in FRONT_ORDER:
        if kind in run:
            run[kind](*rest)
        else:
            spread.do(kind, *rest)
            if kind == BH:
                own[rest[0]].start()
    for part in range(2, 6):
        own[part].wait()
    weights_out.wait()
    for copy in swaps + shares:
        copy.wait_send()


FRONT_PLANES = (2,)
FRONT_SHARES = {3: 0.4, 4: 0.4}
FRONT_ORDER = (
    (BH, 3), (BZ, 4), (BH, 4), (PACK, 0), (BZ, 0), (BZ, 1), (LINE, 0, 1, 1), (LINE, 0, 1, -1),
    (LINE, 0, 2, 1), (BH, 0), (LINE, 1, 1, 1), (PX, 3, 0), (BZ, 3), (LINE, 1, 1, -1), (PY, 0, 1),
    (LINE, 0, 2, -1), (LINE, 0, 3, 1), (PX, 0, 1), (EX, TOKENS), (LINE, 1, 2, 1), (PX, 4, 0),
    (LINE, 0, 3, -1), (PACK, 1), (BH, 5), (BH, 2), (PY, 0, 3), (PY, 1, 1), (LINE, 1, 3, -1),
    (BH, 1), (LINE, 1, 2, -1), (PX, 1, 1), (PY, 0, 2), (PY, 1, 0), (BZ, 5), (PX, 0, 0),
    (PY, 0, 0), (LINE, 3, 1, -1), (LINE, 1, 3, 1), (PX, 0, 2), (LINE, 3, 1, 1), (PX, 5, 0),
    (PY, 1, 2), (CO, 0, 1), (PX, 1, 2), (CO, 0, 0), (PX, 0, 3), (PX, 1, 0), (CO, 1, 1),
    (CO, 0, 2), (PY, 5, 0), (EXW, TOKENS), (PY, 4, 0), (PY, 2, 0), (NORM,), (CO, 0, 3),
    (PX, 2, 0), (PX, 1, 3), (PY, 1, 3), (LINE, 3, 2, -1), (END, 0), (LINE, 3, 2, 1), (PAIRS,),
    (KEYS,), (GIVE,), (CO, 1, 0), (CO, 1, 2), (LINE, 4, 1, -1), (CO, 1, 3), (END, 1), (BZ, 2),
    (CO, 4, 0), (LINE, 3, 3, -1), (LINE, 5, 1, -1), (QUERY, 0), (CO, 2, 0), (LINE, 4, 1, 1),
    (QUERY, 1), (QUERY, 2), (QUERY, 3), (PY, 3, 1), (QUERY, 4), (LINE, 3, 3, 1), (LINE, 5, 1, 1),
    (LINE, 4, 2, -1), (GET,), (LINE, 4, 2, 1), (ATT0, 0), (EX, GRADS), (ATT1, 0), (ATT2, 0),
    (ATT0, 1), (LINE, 4, 3, -1), (PX, 3, 3), (ATT1, 1), (LINE, 5, 2, 1), (ATT2, 1), (ATT0, 2),
    (LINE, 4, 3, 1), (LINE, 5, 2, -1), (ATT1, 2), (PX, 3, 2), (PY, 4, 1), (ATT2, 2), (ATT0, 3),
    (ATT1, 3), (ATT2, 3), (ATT0, 4), (ATT1, 4), (ATT2, 4), (LINE, 5, 3, -1), (LINE, 2, 1, -1),
    (PY, 5, 1), (CO, 5, 0), (PX, 3, 1), (LINE, 2, 1, 1), (PX, 4, 1), (PY, 3, 0), (PY, 3, 2),
    (PX, 5, 2), (PY, 3, 3), (LINE, 5, 3, 1), (PX, 4, 3), (PX, 4, 2), (PX, 5, 1), (CO, 4, 1),
    (PY, 4, 2), (LINE, 2, 2, -1), (LINE, 2, 2, 1), (PY, 5, 3), (PY, 4, 3), (LINE, 2, 3, 1),
    (PX, 5, 3), (PY, 5, 2), (LINE, 2, 3, -1), (CO, 3, 0), (CO, 5, 1), (CO, 4, 2), (CO, 3, 1),
    (CO, 4, 3), (END, 2), (CO, 3, 3), (CO, 3, 2), (END, 3), (CO, 5, 3), (CO, 5, 2), (END, 4),
    (END, 5), (EXW, GRADS),
)


def front(tokens, out_grad, weights, limits, turn, down, up, gain):
    query, keyval, output, gateup, w_down = weights
    seqs, part, width = tokens.shape
    rows, wide = query.shape
    deep = w_down.shape[0]
    blks, heads = lax.axis_size("blk"), lax.axis_size("head")
    narrow = keyval.shape[2]
    mixed = -(-4 * narrow // TILE) * TILE
    double = heads * narrow * 2
    groups = width // (2 * TILE)
    dma = pltpu.SemaphoreType.DMA
    vmem = pl.BlockSpec(memory_space=pltpu.VMEM)
    shape = jax.ShapeDtypeStruct
    return pl.pallas_call(
        functools.partial(front_kernel, blks // 2),
        out_shape=[
            shape((blks * rows, heads * wide + double), BF16),
            shape((blks * rows, heads * wide), BF16),
            shape((2, blks * rows, heads * gateup.shape[2]), BF16),
            shape((blks * deep, heads * wide), BF16),
            shape((seqs, part, width), BF16),
            shape((seqs, part, width), BF16),
            shape((seqs * part, width), BF16),
            shape((seqs * part, 1), F32),
            shape((seqs * part, down.shape[0]), BF16),
            shape((seqs * part, width), BF16),
            shape((seqs, heads * part, double), BF16),
            shape((seqs * part, width), BF16),
            shape((groups, seqs, 2 * TILE), F32),
        ],
        in_specs=[ANYWHERE, ANYWHERE, vmem, vmem, vmem, ANYWHERE] + [vmem] * 6,
        out_specs=[ANYWHERE] * 4 + [vmem, ANYWHERE] + [vmem] * 7,
        scratch_shapes=[
            pltpu.VMEM((rows // 2, wide), BF16),
            pltpu.VMEM((2, rows // 2, narrow), BF16),
            pltpu.VMEM((rows // 2, wide), BF16),
            pltpu.VMEM((deep // 2, wide), BF16),
            pltpu.VMEM((rows // 2, 2 * wide), BF16),
            pltpu.VMEM((rows // 2, mixed), BF16),
            pltpu.VMEM((rows // 2, 2 * wide), BF16),
            pltpu.VMEM((deep // 2, 2 * wide), BF16),
            pltpu.VMEM((blks * rows, heads // 2 * mixed), BF16),
            pltpu.VMEM((blks * rows, heads * wide + double), BF16),
            pltpu.VMEM((seqs, 4, part, TILE), BF16),
            pltpu.VMEM((TILE, seqs * heads * part), BF16),
            dma((4,)),
            dma((4,)),
            dma((9,)),
            dma((2, seqs - 1)),
            dma((2, seqs - 1)),
            dma((3,)),
            dma((3,)),
            *Spread.semaphores(6, blks // 2),
        ],
        compiler_params=pltpu.CompilerParams(
            collective_id=0, has_side_effects=True, vmem_limit_bytes=56 << 20
        ),
    )(
        tokens.reshape(seqs * part, width),
        out_grad.reshape(seqs * part, width),
        query,
        keyval,
        output,
        gateup,
        w_down,
        limits,
        turn,
        down,
        up,
        gain.reshape(1, -1),
    )


def feed_kernel(
    attended_ref,
    flat_ref,
    grad_ref,
    w_output_ref,
    w_gateup_ref,
    w_down_ref,
    d_output_ref,
    u_output_ref,
    d_gateup_ref,
    u_gateup_ref,
    d_ffdown_ref,
    u_ffdown_ref,
    gain_ref,
    output_ref,
    grad_middle_ref,
    grad_mixed_ref,
    terms_ref,
    middle,
    normed,
    result,
    grad_normed,
    low_output,
    low_gate,
    low_up,
    low_down,
    grad_low_down,
    grad_low_gate,
    grad_low_up,
):
    step = pl.program_id(0)
    rows, width = attended_ref.shape
    chunk = w_down_ref.shape[0]
    hidden = chunk * pl.num_programs(0)

    @pl.when(step == 0)
    def _():
        attended = attended_ref[...]
        low_output[...] = lowered(attended, d_output_ref[...])
        branch = dot(attended, w_output_ref[...])
        branch = branch + ADAPTER_SCALE * dot(low_output[...], u_output_ref[...])
        middle[...] = flat_ref[...].astype(F32) + branch
        normed[...] = norm_of(middle[...], gain_ref[...])[0]
        low_gate[...] = lowered(normed[...], d_gateup_ref[0])
        low_up[...] = lowered(normed[...], d_gateup_ref[1])
        grad_low_down[...] = (ADAPTER_SCALE * dot(grad_ref[...], u_ffdown_ref[...], 1, 1)).astype(
            BF16
        )
        for ref in (result, grad_normed, low_down, grad_low_gate, grad_low_up):
            ref[...] = jnp.zeros_like(ref)

    inputs = normed[...]
    w_gate, w_up = w_gateup_ref[0], w_gateup_ref[1]
    u_gate, u_up = u_gateup_ref[0], u_gateup_ref[1]
    gate = dot(inputs, w_gate) + ADAPTER_SCALE * dot(low_gate[...], u_gate)
    upward = dot(inputs, w_up) + ADAPTER_SCALE * dot(low_up[...], u_up)
    grad_act = dot(grad_ref[...], w_down_ref[...], 1, 1) + dot(grad_low_down[...], d_ffdown_ref[...])
    sigma = 1.0 / (1.0 + jnp.exp(-gate))
    silu = gate * sigma
    activated = (silu * upward).astype(BF16)
    grad_gate = (grad_act * upward * (sigma * (1.0 + gate * (1.0 - sigma)))).astype(BF16)
    grad_up = (grad_act * silu).astype(BF16)
    result[...] += dot(activated, w_down_ref[...])
    grad_normed[...] += dot(grad_gate, w_gate, 1, 1) + dot(grad_up, w_up, 1, 1)
    low_down[...] += dot(activated, d_ffdown_ref[...], 1, 1)
    grad_low_gate[...] += dot(grad_gate, u_gate, 1, 1)
    grad_low_up[...] += dot(grad_up, u_up, 1, 1)
    at = 4 * width + step * chunk
    spot = pl.ds(pl.multiple_of(at, TILE), chunk)
    terms_ref[:, spot] = ADAPTER_SCALE * dot(low_gate[...], grad_gate, 0, 0)
    spot = pl.ds(pl.multiple_of(at + hidden, TILE), chunk)
    terms_ref[:, spot] = ADAPTER_SCALE * dot(low_up[...], grad_up, 0, 0)
    spot = pl.ds(pl.multiple_of(at + 2 * hidden, TILE), chunk)
    terms_ref[:, spot] = dot(grad_low_down[...], activated, 0, 0)

    @pl.when(step == pl.num_programs(0) - 1)
    def _():
        low = low_down[...].astype(BF16)
        branch = result[...] + ADAPTER_SCALE * dot(low, u_ffdown_ref[...])
        output_ref[...] = (middle[...] + branch).astype(BF16)
        at = 4 * width + 3 * hidden
        terms_ref[:, at : at + width] = ADAPTER_SCALE * dot(low, grad_ref[...], 0, 0)
        if at + width < terms_ref.shape[1]:
            terms_ref[:, at + width :] = jnp.zeros(
                (terms_ref.shape[0], terms_ref.shape[1] - at - width), F32
            )
        low_g = (ADAPTER_SCALE * grad_low_gate[...]).astype(BF16)
        low_u = (ADAPTER_SCALE * grad_low_up[...]).astype(BF16)
        terms_ref[:, 2 * width : 3 * width] = dot(low_g, normed[...], 0, 0)
        terms_ref[:, 3 * width : 4 * width] = dot(low_u, normed[...], 0, 0)
        grad = grad_normed[...] + dot(low_g, d_gateup_ref[0]) + dot(low_u, d_gateup_ref[1])
        inverse = norm_of(middle[...], gain_ref[...])[1]
        grad = grad_ref[...].astype(F32) + norm_back(middle[...], inverse, gain_ref[...], grad)
        grad_middle_ref[...] = grad
        grad = grad.astype(BF16)
        low = (ADAPTER_SCALE * dot(grad, u_output_ref[...], 1, 1)).astype(BF16)
        mixed = dot(grad, w_output_ref[...], 1, 1) + dot(low, d_output_ref[...])
        grad_mixed_ref[...] = mixed.astype(BF16)
        terms_ref[:, :width] = dot(low, attended_ref[...], 0, 0)
        terms_ref[:, width : 2 * width] = ADAPTER_SCALE * dot(low_output[...], grad, 0, 0)


def feed(attended, flat, grad, w_output, w_gateup, w_down, factors, gain):
    rows, width = flat.shape
    hidden = w_down.shape[0]
    chunk = 4 * TILE
    rank = factors[0].shape[0]
    total = 5 * width + 3 * hidden
    total += -total % (2 * 4 * TILE)
    d_output, u_output, d_gateup, u_gateup, d_ffdown, u_ffdown = factors
    shape = jax.ShapeDtypeStruct

    def whole(array):
        return pl.BlockSpec(array.shape, lambda f: (0,) * len(array.shape))

    gain = gain.reshape(1, -1)
    outs = [
        shape((rows, width), BF16),
        shape((rows, width), F32),
        shape((rows, width), BF16),
        shape((rank, total), F32),
    ]
    return pl.pallas_call(
        feed_kernel,
        grid=(hidden // chunk,),
        out_shape=outs,
        in_specs=[
            whole(attended),
            whole(flat),
            whole(grad),
            whole(w_output),
            pl.BlockSpec((2, width, chunk), lambda f: (0, 0, f)),
            pl.BlockSpec((chunk, width), lambda f: (f, 0)),
            whole(d_output),
            whole(u_output),
            whole(d_gateup),
            pl.BlockSpec((2, rank, chunk), lambda f: (0, 0, f)),
            pl.BlockSpec((rank, chunk), lambda f: (0, f)),
            whole(u_ffdown),
            whole(gain),
        ],
        out_specs=[whole(out) for out in outs],
        scratch_shapes=[
            pltpu.VMEM((rows, width), F32),
            pltpu.VMEM((rows, width), BF16),
            pltpu.VMEM((rows, width), F32),
            pltpu.VMEM((rows, width), F32),
            pltpu.VMEM((rows, rank), BF16),
            pltpu.VMEM((rows, rank), BF16),
            pltpu.VMEM((rows, rank), BF16),
            pltpu.VMEM((rows, rank), F32),
            pltpu.VMEM((rows, rank), BF16),
            pltpu.VMEM((rows, rank), F32),
            pltpu.VMEM((rows, rank), F32),
        ],
        compiler_params=pltpu.CompilerParams(vmem_limit_bytes=56 << 20),
    )(
        attended,
        flat,
        grad,
        w_output,
        w_gateup,
        w_down,
        d_output,
        u_output,
        d_gateup,
        u_gateup,
        d_ffdown,
        u_ffdown,
        gain,
    )


def prepare_kernel(
    adapters_ref,
    where_ref,
    freqs_ref,
    segment_ref,
    real_ref,
    query_down,
    query_up,
    keyval_down,
    keyval_up,
    output_down,
    output_up,
    gateup_down,
    gateup_up,
    ffdown_down,
    ffdown_up,
    limits_ref,
    turn_ref,
    d_qkv,
    u_qkv,
    d_output,
    u_output,
    d_gateup,
    u_gateup,
    d_ffdown,
    u_ffdown,
):
    seq, head = where_ref[0], where_ref[1]
    blocks, part = limits_ref.shape[1], limits_ref.shape[2] // 2
    span = segment_ref.shape[1] // blocks
    rank, width = query_up.shape[1:]
    for out, ref in ((d_output, output_down), (u_output, output_up), (d_gateup, gateup_down)):
        out[...] = ref[0]
    for out, ref in ((u_gateup, gateup_up), (d_ffdown, ffdown_down), (u_ffdown, ffdown_up)):
        out[...] = ref[0]
    d_qkv[:rank] = query_down[0]
    d_qkv[rank : 2 * rank] = keyval_down[0, 0]
    d_qkv[2 * rank :] = keyval_down[0, 1]
    u_qkv[...] = jnp.zeros_like(u_qkv)
    u_qkv[:rank, :width] = query_up[0]
    nil = jnp.zeros((rank, HEAD_DIM), F32)
    for which in range(2):
        ups, pieces = keyval_up[0, which].astype(F32), []
        for m in range(KV_HEADS):
            piece = ups[:, m * HEAD_DIM : (m + 1) * HEAD_DIM]
            pieces += [piece, nil] if which == 0 else [nil, piece]
        u_qkv[(1 + which) * rank : (2 + which) * rank, width:] = jnp.concatenate(
            pieces, axis=1
        ).astype(BF16)
    segment = segment_ref[pl.ds(seq, 1), :].astype(F32)
    length = jnp.sum(real_ref[pl.ds(seq, 1), :], axis=1, keepdims=True)
    column = jnp.broadcast_to(segment, (TILE, segment.shape[1])).T
    lane = lax.broadcasted_iota(jnp.int32, (1, TILE), 1)
    for block in range(blocks):
        mine = segment[:, block * span : (block + 1) * span]
        mine = pltpu.roll(jnp.broadcast_to(mine, (8, span)), span - head * part, 1)[:1, :TILE]
        twin = pltpu.roll(jnp.broadcast_to(mine, (8, TILE)), part, 1)[:1]
        mine = jnp.where(lane < part, mine, twin)
        before = jnp.sum((column < mine).astype(F32), axis=0, keepdims=True).astype(jnp.int32)
        position = block * span + head * part + lane % part
        limits_ref[0, block : block + 1, :] = jnp.maximum(position - (WINDOW - 1), before)
        limits_ref[1, block : block + 1, :] = jnp.minimum(position, length - 1)
        limits_ref[2, block : block + 1, :] = position
    shape = (part, TILE)
    row = lax.broadcasted_iota(jnp.int32, shape, 0)
    lanes = lax.broadcasted_iota(jnp.int32, shape, 1)
    sign = jnp.where(lanes % HEAD_DIM < HEAD_DIM // 2, -1.0, 1.0)
    for block in range(blocks):
        angle = (block * span + head * part + row).astype(F32) * freqs_ref[...]
        turn_ref[0, block * part : (block + 1) * part, :] = jnp.cos(angle)
        turn_ref[1, block * part : (block + 1) * part, :] = sign * jnp.sin(angle)


def prepare(adapter_index, seq, head, segment_ids, real_mask, factors, part):
    seqs = adapter_index.shape[0]
    rank, width = factors[1].shape[1:]
    freqs = ROPE_BASE ** (-(jnp.arange(HEAD_DIM // 2, dtype=F32) * 2.0) / HEAD_DIM)
    freqs = jnp.tile(freqs, 2 * TILE // HEAD_DIM)[None, :]
    double = 2 * factors[3].shape[3]
    shapes = [
        ((3, seqs, 2 * part), jnp.int32),
        ((2, seqs * part, TILE), F32),
        ((3 * rank, width), BF16),
        ((3 * rank, width + double), BF16),
    ] + [(factor.shape[1:], BF16) for factor in factors[4:]]

    def whole(shape):
        return pl.BlockSpec(shape, lambda i, adapters, where: (0,) * len(shape))

    def one(shape):
        return pl.BlockSpec(
            (1,) + shape, lambda i, adapters, where: (adapters[where[0]],) + (0,) * len(shape)
        )

    return pl.pallas_call(
        prepare_kernel,
        grid_spec=pltpu.PrefetchScalarGridSpec(
            num_scalar_prefetch=2,
            grid=(1,),
            in_specs=[whole(freqs.shape), whole(segment_ids.shape), whole(real_mask.shape)]
            + [one(factor.shape[1:]) for factor in factors],
            out_specs=[whole(shape) for shape, _ in shapes],
        ),
        out_shape=[jax.ShapeDtypeStruct(shape, dtype) for shape, dtype in shapes],
    )(adapter_index, jnp.stack([seq, head]).astype(jnp.int32), freqs, segment_ids, real_mask, *factors)


def by_sequence(
    tokens,
    attn_gain,
    ffn_gain,
    query_weight,
    keyval_weight,
    output_weight,
    gateup_weight,
    down_weight,
    query_down,
    query_up,
    keyval_down,
    keyval_up,
    output_down,
    output_up,
    gateup_down,
    gateup_up,
    ffdown_down,
    ffdown_up,
    segment_ids,
    real_mask,
    adapter_index,
    out_grad,
):
    seqs, part, width = tokens.shape
    groups = lax.axis_size("head")
    seq, head_pos = lax.axis_index("blk"), lax.axis_index("head")
    rows = seqs * part
    span = groups * part
    rank = query_up.shape[1]
    limits, turn, d_qkv, u_qkv, *factors = prepare(
        adapter_index,
        seq,
        head_pos,
        segment_ids,
        real_mask,
        (
            query_down.swapaxes(1, 2),
            query_up,
            keyval_down.swapaxes(2, 3),
            keyval_up,
            output_down.swapaxes(1, 2),
            output_up,
            gateup_down.swapaxes(2, 3),
            gateup_up,
            ffdown_down.swapaxes(1, 2),
            ffdown_up,
        ),
        part,
    )
    (
        w_qkv,
        w_output,
        w_gateup,
        w_down,
        flat,
        grad_flat,
        normed,
        inverse1,
        low_qkv,
        queries,
        pairs,
        attended,
        lse,
    ) = front(
        tokens,
        out_grad,
        (query_weight, keyval_weight, output_weight, gateup_weight, down_weight),
        limits,
        turn,
        d_qkv,
        u_qkv,
        attn_gain,
    )
    flat, grad_flat = flat.reshape(rows, width), grad_flat.reshape(rows, width)
    pairs = pairs.reshape(seqs * span, pairs.shape[2])
    output, grad_middle, grad_mixed, early = feed(
        attended,
        flat,
        grad_flat,
        w_output,
        w_gateup,
        w_down,
        factors,
        ffn_gain,
    )
    hidden = w_down.shape[0]
    sizes = [width] * 4 + [hidden] * 3 + [width]
    grad_qkv, output, early = attend_back(
        limits, queries, pairs, lse, grad_mixed, turn, output, early
    )
    input_grad, late = first_back(
        grad_qkv, w_qkv, d_qkv, u_qkv, normed, low_qkv, grad_middle, flat, inverse1, attn_gain
    )
    adapters = jnp.arange(query_down.shape[0], dtype=jnp.int32)
    holder = jnp.argmax(adapter_index[None, :] == adapters[:, None], axis=1).astype(jnp.int32)
    found = placed(holder, early, late, sizes, width)
    return (
        output,
        input_grad,
        found[0].swapaxes(1, 2),
        found[1],
        found[2].swapaxes(2, 3),
        found[3],
        found[4].swapaxes(1, 2),
        found[5],
        found[6].swapaxes(2, 3),
        found[7],
        found[8].swapaxes(1, 2),
        found[9],
    )


def solution(mesh):
    in_specs = (
        P(None, ("blk", "head"), None),
        P(),
        P(),
        P("blk", "head"),
        P(None, "blk", "head"),
        P("blk", "head"),
        P(None, "blk", "head"),
        P("blk", "head"),
        P(),
        P(),
        P(),
        P(),
        P(),
        P(),
        P(),
        P(),
        P(),
        P(),
        P(),
        P(),
        P(),
        P(None, ("blk", "head"), None),
    )
    out_specs = (
        P(None, ("blk", "head"), None),
        P(None, ("blk", "head"), None),
        P(),
        P(),
        P(),
        P(),
        P(),
        P(),
        P(),
        P(),
        P(),
        P(),
    )

    def chosen(tokens, *rest):
        if mesh.shape["blk"] == tokens.shape[0] == 8 and mesh.shape["head"] == 4:
            return by_sequence(tokens, *rest)
        return on_device(tokens, *rest)

    return jax.shard_map(
        chosen, mesh=mesh, in_specs=in_specs, out_specs=out_specs, check_vma=False
    )
```
